32 devices in a mesh: row: 4 (over z), col: 2 (over y), depth: 4 (over x, core).
Axes of the slice: x: 2, y: 2, z: 4, core: 2. Of those that a mesh axis runs over, the one named last changes fastest.
Arguments:
- tokens: bfloat16 [768, 8192], P('col', 'depth'), may hold values from -6 to 6
- weight: bfloat16 [4096, 3, 8192], P(('row', 'col'), None, 'depth'), may hold values from -0.0625 to 0.0625
- taps: float32 [7, 256], P(None, 'row'), may hold values from -3 to 3
- upstream: bfloat16 [768, 4096], P(('col', 'depth'), 'row'), may hold values from -6 to 6
Outputs:
- output: bfloat16 [768, 4096], P(('col', 'depth'), 'row')
- grad_tokens: bfloat16 [768, 8192], P('col', 'depth')
- grad_weight: float32 [4096, 3, 8192], P(('row', 'col'), None, 'depth')
- grad_taps: float32 [7, 256], P(None, 'row')
The draws below stay inside these ranges and needn't reach their ends.
All inputs are finite; a program needn't handle non-finite values.
Results may differ from the reference program's by a relative error of at most 0.034.
Values may be sent and summed in bfloat16 or wider, within the bound.
No kernel may reach another device: no remote copies, remote signals or barrier semaphores. Data moves between devices by JAX's collectives and lax.ppermute only.
A program may use at most 128 MiB of HBM per device.

```python
import jax
import jax.numpy as jnp
from jax import lax

D = 8192
C = 4096
GROUP = 16
KT = 7
GROUPS = 256
GROUP_TOK = 384
TOKENS = 768
N_COL = 2


def block_scale(key, shape, cuts, least, high):
    loudness = 1.0
    for axis_at, parts in cuts:
        draws = jax.random.uniform(jax.random.fold_in(jax.random.fold_in(key, 6), axis_at), (parts,), jnp.float32, least / len(cuts), high / len(cuts))
        loudness = loudness * jnp.repeat(jnp.exp(draws), shape[axis_at] // parts).reshape((-1,) + (1,) * (len(shape) - 1 - axis_at))
    return loudness


def centred(key, dims, scale, bound, shards=(), dtype=jnp.bfloat16):
    loudness = block_scale(key, dims, shards, -0.22, 0.18) if shards else 1.0
    result = jax.random.normal(key, dims, jnp.float32) * scale * loudness
    return jnp.minimum(jnp.maximum(result, -bound), bound).astype(dtype)


def setup_inputs(seed: int = 0) -> dict:
    seeds = jax.random.split(jax.random.key(seed), 5)
    return {
        "tokens": centred(seeds[0], (TOKENS, D), 1.0, 6.0, ((0, 2), (1, 4))),
        "weight": centred(seeds[1], (C, 3, D), D ** -0.5, 0.0625, ((0, 8), (2, 4))),
        "taps": centred(seeds[2], (KT, GROUPS), 0.5, 3.0, ((1, 4),), jnp.float32),
        "upstream": centred(seeds[3], (TOKENS, C), 1.0, 6.0, ((0, 8), (1, 4))),
    }


def causal_filter(padded, spread, length):
    total = jnp.zeros((length, padded.shape[1]), jnp.float32)
    for offset in range(KT):
        first_row = KT - 1 - offset
        total = total + spread[offset] * padded[first_row:first_row + length]
    return total


def reference(tokens, weight, taps, upstream):
    flat_weight = jnp.transpose(weight, (1, 0, 2)).reshape(3 * C, D)
    projected = jnp.dot(tokens, flat_weight.T, preferred_element_type=jnp.float32)
    rounded = lax.optimization_barrier(projected.astype(jnp.bfloat16)).astype(jnp.float32)
    rounded = rounded.reshape(TOKENS, 3, C)
    query_part = rounded[:, 0, :]
    key_part = rounded[:, 1, :]
    value_part = rounded[:, 2, :]
    mixed = key_part * value_part
    spread = jnp.repeat(taps.astype(jnp.float32), GROUP, axis=1)
    padded = jnp.concatenate([jnp.zeros((KT - 1, C), jnp.float32), mixed], 0)
    filtered = causal_filter(padded, spread, TOKENS)
    output = (query_part * filtered).astype(jnp.bfloat16)
    upstream_f = upstream.astype(jnp.float32)
    grad_query = upstream_f * filtered
    grad_filtered = upstream_f * query_part
    padded_grad = jnp.concatenate([grad_filtered, jnp.zeros((KT - 1, C), jnp.float32)], 0)
    grad_mixed = jnp.zeros((TOKENS, C), jnp.float32)
    for offset in range(KT):
        grad_mixed = grad_mixed + spread[offset] * padded_grad[offset:offset + TOKENS]
    grad_key = grad_mixed * value_part
    grad_value = grad_mixed * key_part
    grad_proj = jnp.stack([grad_query, grad_key, grad_value], axis=1).astype(jnp.bfloat16)
    tap_rows = []
    for offset in range(KT):
        first_row = KT - 1 - offset
        summed = jnp.sum(grad_filtered * padded[first_row:first_row + TOKENS], axis=0)
        tap_rows.append(summed.reshape(GROUPS, GROUP).sum(axis=1))
    grad_taps = jnp.stack(tap_rows, 0)
    flat_grad = grad_proj.reshape(TOKENS, 3 * C)
    grad_flat_w = jnp.zeros((3 * C, D), jnp.float32)
    for block in range(N_COL):
        grad_rows = flat_grad[block * GROUP_TOK:(block + 1) * GROUP_TOK]
        token_rows = tokens[block * GROUP_TOK:(block + 1) * GROUP_TOK]
        partial_w = jnp.dot(grad_rows.T, token_rows, preferred_element_type=jnp.float32)
        partial_w = lax.optimization_barrier(partial_w.astype(jnp.bfloat16)).astype(jnp.float32)
        grad_flat_w = grad_flat_w + partial_w
    grad_weight = jnp.transpose(grad_flat_w.reshape(3, C, D), (1, 0, 2))
    grad_tokens = jnp.dot(flat_grad, flat_weight, preferred_element_type=jnp.float32).astype(jnp.bfloat16)
    return output, grad_tokens, grad_weight, grad_taps
```

```python
import functools

import jax
import jax.numpy as jnp
from jax import lax
from jax.experimental import pallas as pl
from jax.experimental.pallas import tpu as pltpu
from jax.sharding import PartitionSpec as P

GROUP = 16
KT = 7
PAD = 8
LANES = 128
VMEM_LIMIT = 48 * 1024 * 1024


def swap(value, axis, flip):
    count = lax.axis_size(axis)
    return lax.ppermute(value, axis, [(i, i ^ flip) for i in range(count)])


def params():
    return pltpu.CompilerParams(vmem_limit_bytes=VMEM_LIMIT)


def project_kernel(place, x_ref, w_ref, keep_ref, send_ref, *, count, width):
    stream = pl.program_id(0)
    core = place[0] % 2
    x = x_ref[...]
    nt = (((1,), (1,)), ((), ()))
    if width % LANES == 0:
        whole = lax.dot_general(x, w_ref[0], nt, preferred_element_type=jnp.float32).astype(jnp.bfloat16)
        blocks = [whole[:, j * width : (j + 1) * width] for j in range(count)]
    else:
        blocks = [
            lax.dot_general(
                x, w_ref[0, j * width : (j + 1) * width, :], nt, preferred_element_type=jnp.float32
            ).astype(jnp.bfloat16)
            for j in range(count)
        ]
    for mine in range(2):

        @pl.when(core == mine)
        def _():
            for j in range(count):
                at = (j ^ place[0]) // 2
                if j % 2 == mine:
                    keep_ref[at, stream] = blocks[j]
                else:
                    send_ref[at, stream] = blocks[j]


def project(place, x, w, count):
    tok, feat = x.shape
    streams, channels, _ = w.shape
    width = channels // count
    part = jax.ShapeDtypeStruct((count // 2, streams, tok, width), jnp.bfloat16)
    spec = pl.BlockSpec((count // 2, streams, tok, width), lambda s, _: (0, 0, 0, 0))
    return pl.pallas_call(
        functools.partial(project_kernel, count=count, width=width),
        grid_spec=pltpu.PrefetchScalarGridSpec(
            num_scalar_prefetch=1,
            grid=(streams,),
            in_specs=[
                pl.BlockSpec((tok, feat), lambda s, _: (0, 0)),
                pl.BlockSpec((1, channels, feat), lambda s, _: (s, 0, 0)),
            ],
            out_specs=[spec, spec],
        ),
        out_shape=[part, part],
        compiler_params=params(),
        cost_estimate=pl.CostEstimate(
            flops=2 * tok * feat * channels * streams,
            bytes_accessed=2 * (tok * feat + channels * streams * feat + tok * channels * streams),
            transcendentals=0,
        ),
        name="project",
    )(place, x, w)


def middle_kernel(place, taps_ref, up_ref, *refs, groups, terms, tile):
    part_refs = refs[: groups * terms]
    grad_ref, out_ref, grad_taps_ref, q_s, k_s, v_s, mixed_s, gf_s = refs[groups * terms :]
    col = place[1]
    tok = part_refs[0].shape[2]
    width = part_refs[0].shape[3]
    total = groups * tok
    mixed_s[0:PAD, :] = jnp.zeros((PAD, width), jnp.float32)
    gf_s[total : total + PAD, :] = jnp.zeros((PAD, width), jnp.float32)
    for k in range(groups):
        start = (col ^ k) * tok
        for i in range(tok // tile):
            inside = slice(i * tile, (i + 1) * tile)
            rows = pl.ds(pl.multiple_of(start + i * tile, tile), tile)
            streams = []
            for s in range(3):
                acc = None
                for ref in part_refs[k * terms : (k + 1) * terms]:
                    term = ref[0, s, inside, :].astype(jnp.float32)
                    acc = term if acc is None else acc + term
                streams.append(acc.astype(jnp.bfloat16).astype(jnp.float32))
            query, key, value = streams
            q_s[rows, :] = query
            k_s[rows, :] = key
            v_s[rows, :] = value
            mixed_s[pl.ds(pl.multiple_of(start + i * tile + PAD, PAD), tile), :] = key * value
            gf_s[rows, :] = up_ref[rows, :].astype(jnp.float32) * query
    taps = taps_ref[...]
    sums = [jnp.zeros((8, width), jnp.float32) for _ in range(KT)]
    for a in range(groups):
        for i in range(tok // tile):
            first = a * tok + i * tile
            rows = slice(first, first + tile)
            inside = slice(i * tile, (i + 1) * tile)
            gf = gf_s[rows, :]
            filtered = jnp.zeros((tile, width), jnp.float32)
            grad_mixed = jnp.zeros((tile, width), jnp.float32)
            for j in range(KT):
                shifted = mixed_s[first + PAD - j : first + PAD - j + tile, :]
                filtered = filtered + taps[j : j + 1, :] * shifted
                sums[j] = sums[j] + (gf * shifted).reshape(tile // 8, 8, width).sum(axis=0)
                grad_mixed = grad_mixed + taps[j : j + 1, :] * gf_s[first + j : first + j + tile, :]
            out_ref[rows, :] = (q_s[rows, :] * filtered).astype(jnp.bfloat16)
            at = col ^ a
            grad_ref[at, 0, inside, :] = (up_ref[rows, :].astype(jnp.float32) * filtered).astype(jnp.bfloat16)
            grad_ref[at, 1, inside, :] = (grad_mixed * v_s[rows, :]).astype(jnp.bfloat16)
            grad_ref[at, 2, inside, :] = (grad_mixed * k_s[rows, :]).astype(jnp.bfloat16)
    for j in range(KT):
        grad_taps_ref[j : j + 1, :] = sums[j].sum(axis=0, keepdims=True)
    grad_taps_ref[KT : KT + 1, :] = jnp.zeros((1, width), jnp.float32)


def middle(place, taps, up, parts):
    groups, terms = len(parts), len(parts[0])
    _, _, tok, width = parts[0][0].shape
    total = groups * tok
    whole = lambda *shape: pl.BlockSpec(shape, lambda i, _: (0,) * len(shape))
    return pl.pallas_call(
        functools.partial(middle_kernel, groups=groups, terms=terms, tile=64),
        grid_spec=pltpu.PrefetchScalarGridSpec(
            num_scalar_prefetch=1,
            grid=(1,),
            in_specs=[whole(KT, width), whole(total, width)] + [whole(1, 3, tok, width)] * (groups * terms),
            out_specs=[whole(groups, 3, tok, width), whole(total, width), whole(8, width)],
            scratch_shapes=[pltpu.VMEM((total, width), jnp.float32)] * 3
            + [pltpu.VMEM((total + PAD, width), jnp.float32)] * 2,
        ),
        out_shape=[
            jax.ShapeDtypeStruct((groups, 3, tok, width), jnp.bfloat16),
            jax.ShapeDtypeStruct((total, width), jnp.bfloat16),
            jax.ShapeDtypeStruct((8, width), jnp.float32),
        ],
        compiler_params=params(),
        cost_estimate=pl.CostEstimate(
            flops=60 * total * width,
            bytes_accessed=2 * total * width * (3 * terms + 5),
            transcendentals=0,
        ),
        name="middle",
    )(place, taps, up, *[term for terms_of in parts for term in terms_of])


def assemble(place, grad_refs, whole_s, width):
    for r, ref in enumerate(grad_refs):
        at = pl.multiple_of((place[0] ^ r) * width, width)
        for k in range(ref.shape[0]):
            for s in range(3):
                tok = ref.shape[2]
                whole_s[s, k * tok : (k + 1) * tok, pl.ds(at, width)] = ref[k, s]


def input_grad_kernel(place, *refs, width, count):
    grad_refs = refs[:count]
    w_ref, out_ref = refs[count : count + 2]
    acc = jnp.zeros(out_ref.shape, jnp.float32)
    if width % LANES == 0:
        whole_s = refs[count + 2]

        @pl.when(pl.program_id(0) == 0)
        def _():
            assemble(place, grad_refs, whole_s, width)

        for s in range(3):
            acc = acc + jnp.dot(whole_s[s], w_ref[s], preferred_element_type=jnp.float32)
    else:
        for r, ref in enumerate(grad_refs):
            rows = pl.ds(pl.multiple_of((place[0] ^ r) * width, width), width)
            for s in range(3):
                acc = acc + jnp.dot(ref[0, s], w_ref[s, rows, :], preferred_element_type=jnp.float32)
    out_ref[...] = acc.astype(jnp.bfloat16)


def input_grad(place, grads, w, k):
    count = len(grads)
    _, _, tok, width = grads[0].shape
    streams, channels, feat = w.shape
    step = min(512, feat)
    wide = width % LANES == 0
    return pl.pallas_call(
        functools.partial(input_grad_kernel, width=width, count=count),
        grid_spec=pltpu.PrefetchScalarGridSpec(
            num_scalar_prefetch=1,
            grid=(feat // step,),
            in_specs=[pl.BlockSpec((1, streams, tok, width), lambda i, _: (k, 0, 0, 0))] * count
            + [pl.BlockSpec((streams, channels, step), lambda i, _: (0, 0, i))],
            out_specs=pl.BlockSpec((tok, step), lambda i, _: (0, i)),
            scratch_shapes=[pltpu.VMEM((streams, tok, channels), jnp.bfloat16)] if wide else [],
        ),
        out_shape=jax.ShapeDtypeStruct((tok, feat), jnp.bfloat16),
        compiler_params=params(),
        cost_estimate=pl.CostEstimate(
            flops=2 * tok * feat * channels * streams,
            bytes_accessed=2 * (tok * feat + channels * streams * feat + tok * channels * streams),
            transcendentals=0,
        ),
        name="input_grad",
    )(place, *grads, w)


def weight_grad_kernel(place, *refs, width, count, groups):
    grad_refs = refs[:count]
    x_refs = refs[count : count + groups]
    out_ref = refs[count + groups]
    tn = (((0,), (0,)), ((), ()))
    tok = x_refs[0].shape[0]
    s = pl.program_id(0)
    if width % LANES == 0:
        whole_s = refs[count + groups + 1]

        @pl.when((pl.program_id(0) == 0) & (pl.program_id(1) == 0))
        def _():
            assemble(place, grad_refs, whole_s, width)

        acc = None
        for k in range(groups):
            rows = slice(k * tok, (k + 1) * tok)
            term = lax.dot_general(whole_s[s, rows, :], x_refs[k][...], tn, preferred_element_type=jnp.float32)
            acc = term if acc is None else acc + term
        out_ref[0] = acc
    else:
        for r, ref in enumerate(grad_refs):
            acc = None
            for k in range(groups):
                term = lax.dot_general(ref[k, 0], x_refs[k][...], tn, preferred_element_type=jnp.float32)
                acc = term if acc is None else acc + term
            out_ref[0, pl.ds(pl.multiple_of((place[0] ^ r) * width, width), width), :] = acc


def weight_grad(place, grads, xs):
    count, groups = len(grads), len(xs)
    _, streams, tok, width = grads[0].shape
    feat = xs[0].shape[1]
    channels = width * count
    step = min(512, feat)
    wide = width % LANES == 0
    return pl.pallas_call(
        functools.partial(weight_grad_kernel, width=width, count=count, groups=groups),
        grid_spec=pltpu.PrefetchScalarGridSpec(
            num_scalar_prefetch=1,
            grid=(streams, feat // step),
            in_specs=[
                pl.BlockSpec((groups, streams, tok, width), lambda s, i, _: (0, 0, 0, 0))
                if wide
                else pl.BlockSpec((groups, 1, tok, width), lambda s, i, _: (0, s, 0, 0))
            ]
            * count
            + [pl.BlockSpec((tok, step), lambda s, i, _: (0, i))] * groups,
            out_specs=pl.BlockSpec((1, channels, step), lambda s, i, _: (s, 0, i)),
            scratch_shapes=[pltpu.VMEM((streams, groups * tok, channels), jnp.bfloat16)] if wide else [],
        ),
        out_shape=jax.ShapeDtypeStruct((streams, channels, feat), jnp.float32),
        compiler_params=params(),
        cost_estimate=pl.CostEstimate(
            flops=2 * groups * tok * feat * channels * streams,
            bytes_accessed=4 * channels * streams * feat + 2 * groups * tok * (feat + channels * streams),
            transcendentals=0,
        ),
        name="weight_grad",
    )(place, *grads, *xs)


def on_device(tokens, weight, taps, upstream):
    n_col = lax.axis_size("col")
    n_depth = lax.axis_size("depth")
    both = ("col", "depth")
    depth_at = lax.axis_index("depth")
    col_at = lax.axis_index("col")
    place = jnp.stack([depth_at, col_at]).astype(jnp.int32)
    w = jnp.transpose(weight, (1, 0, 2))
    own_groups = w.shape[1] // n_depth // GROUP
    xs = [tokens] + [swap(tokens, "col", k) for k in range(1, n_col)]
    up = lax.all_to_all(upstream, both, split_axis=1, concat_axis=0, tiled=True)
    first_group = (col_at * n_depth + depth_at) * own_groups
    own_taps = jnp.repeat(lax.dynamic_slice_in_dim(taps, first_group, own_groups, axis=1), GROUP, axis=1)
    parts = []
    for x in xs:
        keep, send = project(place, x, w, n_depth)
        near = swap(send, "depth", 1)
        terms = [keep, near]
        for r in range(2, n_depth, 2):
            pair = (keep[r // 2].astype(jnp.float32) + near[r // 2].astype(jnp.float32)).astype(jnp.bfloat16)
            terms.append(swap(pair[None], "depth", r))
        parts.append(terms)
    grad_own, output, tap_sums = middle(place, own_taps, up, parts)
    grads = [grad_own, swap(grad_own, "depth", 1)]
    for r in range(2, n_depth, 2):
        far = swap(grad_own, "depth", r)
        grads += [far, swap(far, "depth", 1)]
    total = None
    for k in range(1, n_col):
        term = swap(input_grad(place, grads, w, k), "col", k).astype(jnp.float32)
        total = term if total is None else total + term
    partial_in = input_grad(place, grads, w, 0).astype(jnp.float32) + total
    grad_tokens = lax.psum(partial_in.astype(jnp.bfloat16), "row")
    grad_weight = jnp.transpose(weight_grad(place, grads, xs), (1, 0, 2))
    output = lax.all_to_all(output, both, split_axis=0, concat_axis=1, tiled=True)
    own_grad_taps = tap_sums[:KT].reshape(KT, own_groups, GROUP).sum(axis=2)
    grad_taps = lax.all_gather(own_grad_taps, both, axis=1, tiled=True)
    return (output, grad_tokens, grad_weight, grad_taps)


def solution(mesh):
    in_specs = (
        P("col", "depth"),
        P(("row", "col"), None, "depth"),
        P(None, "row"),
        P(("col", "depth"), "row"),
    )
    out_specs = (
        P(("col", "depth"), "row"),
        P("col", "depth"),
        P(("row", "col"), None, "depth"),
        P(None, "row"),
    )
    return jax.shard_map(
        on_device, mesh=mesh, in_specs=in_specs, out_specs=out_specs, check_vma=False
    )
```

```python
import functools

import jax
import jax.numpy as jnp
from jax import lax
from jax.experimental import pallas as pl
from jax.experimental.pallas import tpu as pltpu
from jax.sharding import PartitionSpec as P

GROUP = 16
KT = 7
PAD = 8
LANES = 128
VMEM_LIMIT = 48 * 1024 * 1024


def swap(value, axis, flip):
    count = lax.axis_size(axis)
    return lax.ppermute(value, axis, [(i, i ^ flip) for i in range(count)])


def params():
    return pltpu.CompilerParams(vmem_limit_bytes=VMEM_LIMIT)


def project_kernel(place, *refs, pieces, count, width):
    x_refs = refs[:pieces]
    w_ref, keep_ref, send_ref = refs[pieces : pieces + 3]
    stream = pl.program_id(0)
    core = place[0] % 2
    if pieces == 1:
        x = x_refs[0][...]
    else:
        x_out = refs[pieces + 3]
        third = x_refs[0].shape[0]
        parity = place[2] % 2

        @pl.when(stream == 0)
        def _():
            x_out[pl.ds(pl.multiple_of(parity * third, third), third), :] = x_refs[0][...]
            x_out[pl.ds(pl.multiple_of((1 - parity) * third, third), third), :] = x_refs[1][...]
            x_out[2 * third :, :] = x_refs[2][...]

        x = x_out[...]
    nt = (((1,), (1,)), ((), ()))
    if width % LANES == 0:
        whole = lax.dot_general(x, w_ref[0], nt, preferred_element_type=jnp.float32).astype(jnp.bfloat16)
        blocks = [whole[:, j * width : (j + 1) * width] for j in range(count)]
    else:
        blocks = [
            lax.dot_general(
                x, w_ref[0, j * width : (j + 1) * width, :], nt, preferred_element_type=jnp.float32
            ).astype(jnp.bfloat16)
            for j in range(count)
        ]
    for mine in range(2):

        @pl.when(core == mine)
        def _():
            for j in range(count):
                at = (j ^ place[0]) // 2
                if j % 2 == mine:
                    keep_ref[at, stream] = blocks[j]
                else:
                    send_ref[at, stream] = blocks[j]


def project(place, xs, w, count):
    tok, feat = sum(x.shape[0] for x in xs), xs[0].shape[1]
    streams, channels, _ = w.shape
    width = channels // count
    part = jax.ShapeDtypeStruct((count // 2, streams, tok, width), jnp.bfloat16)
    spec = pl.BlockSpec((count // 2, streams, tok, width), lambda s, _: (0, 0, 0, 0))
    joined = len(xs) > 1
    outs = pl.pallas_call(
        functools.partial(project_kernel, pieces=len(xs), count=count, width=width),
        grid_spec=pltpu.PrefetchScalarGridSpec(
            num_scalar_prefetch=1,
            grid=(streams,),
            in_specs=[pl.BlockSpec(x.shape, lambda s, _: (0, 0)) for x in xs]
            + [pl.BlockSpec((1, channels, feat), lambda s, _: (s, 0, 0))],
            out_specs=[spec, spec] + [pl.BlockSpec((tok, feat), lambda s, _: (0, 0))] * joined,
        ),
        out_shape=[part, part] + [jax.ShapeDtypeStruct((tok, feat), jnp.bfloat16)] * joined,
        compiler_params=params(),
        cost_estimate=pl.CostEstimate(
            flops=2 * tok * feat * channels * streams,
            bytes_accessed=2 * (tok * feat + channels * streams * feat + tok * channels * streams),
            transcendentals=0,
        ),
        name="project",
    )(place, *xs, w)
    return outs[0], outs[1], outs[2] if joined else xs[0]


def middle_kernel(place, taps_ref, up_ref, *refs, groups, terms, tile):
    part_refs = refs[: groups * terms]
    grad_refs = refs[groups * terms : groups * terms + groups]
    out_ref, q_s, k_s, v_s, mixed_s, gf_s, far_s = refs[groups * terms + groups :]
    col = place[1]
    tok = part_refs[0].shape[2]
    width = part_refs[0].shape[3]
    total = groups * tok
    mixed_s[0:PAD, :] = jnp.zeros((PAD, width), jnp.float32)
    gf_s[total : total + PAD, :] = jnp.zeros((PAD, width), jnp.float32)
    for k in range(groups):
        start = (col ^ k) * tok
        for i in range(tok // tile):
            inside = slice(i * tile, (i + 1) * tile)
            rows = pl.ds(pl.multiple_of(start + i * tile, tile), tile)
            streams = []
            for s in range(3):
                acc = None
                for ref in part_refs[k * terms : (k + 1) * terms]:
                    term = ref[0, s, inside, :].astype(jnp.float32)
                    acc = term if acc is None else acc + term
                streams.append(acc.astype(jnp.bfloat16).astype(jnp.float32))
            query, key, value = streams
            q_s[rows, :] = query
            k_s[rows, :] = key
            v_s[rows, :] = value
            mixed_s[pl.ds(pl.multiple_of(start + i * tile + PAD, PAD), tile), :] = key * value
            gf_s[rows, :] = up_ref[rows, :].astype(jnp.float32) * query
    taps = taps_ref[...]
    sums = [jnp.zeros((8, width), jnp.float32) for _ in range(KT)]
    for a in range(groups):
        for i in range(tok // tile):
            first = a * tok + i * tile
            rows = slice(first, first + tile)
            inside = slice(i * tile, (i + 1) * tile)
            gf = gf_s[rows, :]
            filtered = jnp.zeros((tile, width), jnp.float32)
            grad_mixed = jnp.zeros((tile, width), jnp.float32)
            for j in range(KT):
                shifted = mixed_s[first + PAD - j : first + PAD - j + tile, :]
                filtered = filtered + taps[j : j + 1, :] * shifted
                sums[j] = sums[j] + (gf * shifted).reshape(tile // 8, 8, width).sum(axis=0)
                grad_mixed = grad_mixed + taps[j : j + 1, :] * gf_s[first + j : first + j + tile, :]
            out_ref[first // tile, 0:tile, :] = (q_s[rows, :] * filtered).astype(jnp.bfloat16)
            at = col ^ a
            far_s[at, 0, inside, :] = (up_ref[rows, :].astype(jnp.float32) * filtered).astype(jnp.bfloat16)
            far_s[at, 1, inside, :] = (grad_mixed * v_s[rows, :]).astype(jnp.bfloat16)
            far_s[at, 2, inside, :] = (grad_mixed * k_s[rows, :]).astype(jnp.bfloat16)
    for k in range(groups):
        grad_refs[k][...] = far_s[k]
    rest = jnp.concatenate(
        [sums[j].sum(axis=0, keepdims=True) for j in range(KT)] + [jnp.zeros((1, width), jnp.float32)], axis=0
    )
    terms_of = []
    for _ in range(3):
        term = rest.astype(jnp.bfloat16).astype(jnp.float32)
        rest = rest - term
        terms_of.append(term)
    packed = jnp.concatenate(terms_of + [jnp.zeros((8, width), jnp.float32)], axis=0).astype(jnp.bfloat16)
    for i in range(out_ref.shape[0]):
        out_ref[i, tile : tile + 32, :] = packed


def middle(place, taps, up, parts, tile):
    groups, terms = len(parts), len(parts[0])
    _, _, tok, width = parts[0][0].shape
    total = groups * tok
    whole = lambda *shape: pl.BlockSpec(shape, lambda i, _: (0,) * len(shape))
    outs = pl.pallas_call(
        functools.partial(middle_kernel, groups=groups, terms=terms, tile=tile),
        grid_spec=pltpu.PrefetchScalarGridSpec(
            num_scalar_prefetch=1,
            grid=(1,),
            in_specs=[whole(KT, width), whole(total, width)] + [whole(1, 3, tok, width)] * (groups * terms),
            out_specs=[whole(3, tok, width)] * groups + [whole(total // tile, tile + 32, width)],
            scratch_shapes=[pltpu.VMEM((total, width), jnp.float32)] * 3
            + [pltpu.VMEM((total + PAD, width), jnp.float32)] * 2
            + [pltpu.VMEM((groups, 3, tok, width), jnp.bfloat16)],
        ),
        out_shape=[jax.ShapeDtypeStruct((3, tok, width), jnp.bfloat16)] * groups
        + [jax.ShapeDtypeStruct((total // tile, tile + 32, width), jnp.bfloat16)],
        compiler_params=params(),
        cost_estimate=pl.CostEstimate(
            flops=60 * total * width,
            bytes_accessed=2 * total * width * (3 * terms + 5),
            transcendentals=0,
        ),
        name="middle",
    )(place, taps, up, *[term for terms_of in parts for term in terms_of])
    return outs[:groups], outs[groups]


def assemble_kernel(place, *refs):
    grad_refs, out_ref = refs[:-1], refs[-1]
    width = grad_refs[0].shape[2]
    for r, ref in enumerate(grad_refs):
        at = pl.multiple_of((place[0] ^ r) * width, width)
        for s in range(3):
            out_ref[s, :, pl.ds(at, width)] = ref[s]


def assemble(place, grads):
    streams, tok, width = grads[0].shape
    out = jax.ShapeDtypeStruct((streams, tok, width * len(grads)), jnp.bfloat16)
    return pl.pallas_call(
        assemble_kernel,
        grid_spec=pltpu.PrefetchScalarGridSpec(
            num_scalar_prefetch=1,
            grid=(1,),
            in_specs=[pl.BlockSpec(grads[0].shape, lambda i, _: (0, 0, 0))] * len(grads),
            out_specs=pl.BlockSpec(out.shape, lambda i, _: (0, 0, 0)),
        ),
        out_shape=out,
        compiler_params=params(),
        cost_estimate=pl.CostEstimate(flops=0, bytes_accessed=4 * out.size, transcendentals=0),
        name="assemble",
    )(place, *grads)


def input_grad_kernel(place, *refs, width):
    grad_refs, w_ref, out_ref = refs[:-2], refs[-2], refs[-1]
    acc = jnp.zeros(out_ref.shape, jnp.float32)
    for r, ref in enumerate(grad_refs):
        for s in range(3):
            if len(grad_refs) == 1:
                rows = w_ref[s]
            else:
                rows = w_ref[s, pl.ds(pl.multiple_of((place[0] ^ r) * width, width), width), :]
            acc = acc + jnp.dot(ref[s], rows, preferred_element_type=jnp.float32)
    out_ref[...] = acc.astype(jnp.bfloat16)


def input_grad(place, grads, w, chunk, chunks):
    streams, tok, width = grads[0].shape
    _, channels, feat = w.shape
    step = feat // chunks
    return pl.pallas_call(
        functools.partial(input_grad_kernel, width=width),
        grid_spec=pltpu.PrefetchScalarGridSpec(
            num_scalar_prefetch=1,
            grid=(1,),
            in_specs=[pl.BlockSpec((streams, tok, width), lambda i, _: (0, 0, 0))] * len(grads)
            + [pl.BlockSpec((streams, channels, step), lambda i, _: (0, 0, chunk))],
            out_specs=pl.BlockSpec((tok, step), lambda i, _: (0, 0)),
        ),
        out_shape=jax.ShapeDtypeStruct((tok, step), jnp.bfloat16),
        compiler_params=params(),
        cost_estimate=pl.CostEstimate(
            flops=2 * tok * step * channels * streams,
            bytes_accessed=2 * (tok * step + channels * streams * step + tok * channels * streams),
            transcendentals=0,
        ),
        name="input_grad",
    )(place, *grads, w)


def weight_grad_kernel(place, *refs, groups, wide, chained):
    refs = refs[chained:]
    grad_refs = refs[:groups]
    x_refs = refs[groups : 2 * groups]
    out_ref = refs[2 * groups]
    tok, step = x_refs[0].shape
    width = grad_refs[0].shape[2]
    if wide:
        turned = refs[2 * groups + 1]

        @pl.when(pl.program_id(0) == 0)
        def _():
            for k in range(groups):
                for s in range(3):
                    turned[s * width : (s + 1) * width, k * tok : (k + 1) * tok] = grad_refs[k][s].T

        acc = None
        for k in range(groups):
            term = jnp.dot(
                turned[:, k * tok : (k + 1) * tok], x_refs[k][...], preferred_element_type=jnp.float32
            )
            acc = term if acc is None else acc + term
        for s in range(3):
            out_ref[s] = acc[s * width : (s + 1) * width, :]
    else:
        tn = (((0,), (0,)), ((), ()))
        for s in range(3):
            acc = None
            for k in range(groups):
                term = lax.dot_general(grad_refs[k][s], x_refs[k][...], tn, preferred_element_type=jnp.float32)
                acc = term if acc is None else acc + term
            out_ref[s] = acc


def weight_grad(place, earlier, grads, xs, r, count):
    groups = len(xs)
    streams, tok, width = grads[0].shape
    feat = xs[0].shape[1]
    channels = width * count
    step = min(512, feat)
    wide = width % LANES == 0
    chained = earlier is not None
    return pl.pallas_call(
        functools.partial(weight_grad_kernel, groups=groups, wide=wide, chained=chained),
        grid_spec=pltpu.PrefetchScalarGridSpec(
            num_scalar_prefetch=1,
            grid=(feat // step,),
            in_specs=[pl.BlockSpec(memory_space=pl.ANY)] * chained
            + [pl.BlockSpec((streams, tok, width), lambda i, _: (0, 0, 0))] * groups
            + [pl.BlockSpec((tok, step), lambda i, _: (0, i))] * groups,
            out_specs=pl.BlockSpec((streams, width, step), lambda i, at: (0, at[0] ^ r, i)),
            scratch_shapes=[pltpu.VMEM((streams * width, groups * tok), jnp.bfloat16)] if wide else [],
        ),
        out_shape=jax.ShapeDtypeStruct((streams, channels, feat), jnp.float32),
        input_output_aliases={1: 0} if chained else {},
        compiler_params=params(),
        cost_estimate=pl.CostEstimate(
            flops=2 * groups * tok * feat * width * streams,
            bytes_accessed=4 * width * streams * feat + 2 * groups * tok * (feat + width * streams),
            transcendentals=0,
        ),
        name="weight_grad",
    )(place, *([earlier] if chained else []), *grads, *xs)


def added(first, second):
    return (first.astype(jnp.float32) + second.astype(jnp.float32)).astype(jnp.bfloat16)


def sum_along_row(value):
    count = lax.axis_size("row")
    if count % 2:
        return lax.psum(value, "row")
    at = lax.axis_index("row")
    half = count // 2
    last = count - 1
    for i in range(half - 1):
        value = added(value, lax.ppermute(value, "row", [(i, i + 1), (last - i, last - i - 1)]))
    value = added(value, lax.ppermute(value, "row", [(half - 1, half), (half, half - 1)]))
    for i in reversed(range(half - 1)):
        outer = lax.ppermute(value, "row", [(i + 1, i), (last - i - 1, last - i)])
        value = jnp.where((at == i) | (at == last - i), outer, value)
    return value


def fetch_tokens(tokens, k):
    tok = tokens.shape[0]
    if tok % 48 or lax.axis_size("row") % 2:
        return [swap(tokens, "col", k)]
    third = tok // 3
    parity = lax.axis_index("row") % 2
    mine = swap(lax.dynamic_slice_in_dim(tokens, parity * third, third, axis=0), "col", k)
    return [mine, swap(mine, "row", 1), swap(tokens[2 * third :], "col", k)]


def on_device(tokens, weight, taps, upstream):
    n_col = lax.axis_size("col")
    n_depth = lax.axis_size("depth")
    both = ("col", "depth")
    local_tok = upstream.shape[0]
    depth_at = lax.axis_index("depth")
    col_at = lax.axis_index("col")
    place = jnp.stack([depth_at, col_at, lax.axis_index("row")]).astype(jnp.int32)
    w = jnp.transpose(weight, (1, 0, 2))
    width = w.shape[1] // n_depth
    own_groups = width // GROUP
    pieces = [fetch_tokens(tokens, k) for k in range(1, n_col)]
    up = lax.all_to_all(upstream, both, split_axis=1, concat_axis=0, tiled=True)
    own_tokens, up = lax.optimization_barrier((tokens, up))
    first_group = (col_at * n_depth + depth_at) * own_groups
    own_taps = jnp.repeat(lax.dynamic_slice_in_dim(taps, first_group, own_groups, axis=1), GROUP, axis=1)
    parts, xs = [], []
    for x_pieces in [[own_tokens]] + pieces:
        keep, send, x = project(place, x_pieces, w, n_depth)
        xs.append(x)
        near = swap(send, "depth", 1)
        terms = [keep, near]
        for r in range(2, n_depth, 2):
            terms.append(swap(added(keep[r // 2], near[r // 2])[None], "depth", r))
        parts.append(terms)
    own_grads, blocks = middle(place, own_taps, up, parts, local_tok)
    grads = [None] * n_col
    for k in reversed(range(n_col)):
        grads[k] = [own_grads[k], swap(own_grads[k], "depth", 1)]
        for r in range(2, n_depth, 2):
            far = swap(own_grads[k], "depth", r)
            grads[k] += [far, swap(far, "depth", 1)]
    chunks = 4
    lhs = [[assemble(place, of)] if width % LANES == 0 else of for of in grads]
    sent = [
        [swap(input_grad(place, lhs[k], w, c, chunks), "col", k) for c in range(chunks)] for k in range(1, n_col)
    ]
    done = []
    for c in range(chunks):
        total = input_grad(place, lhs[0], w, c, chunks).astype(jnp.float32)
        for of in sent:
            total = total + of[c].astype(jnp.float32)
        done.append(sum_along_row(total.astype(jnp.bfloat16)))
    grad_tokens = jnp.concatenate(done, axis=1)
    grad_weight = None
    for r in range(n_depth):
        grad_weight = weight_grad(place, grad_weight, [of[r] for of in grads], xs, r, n_depth)
    grad_weight = jnp.transpose(grad_weight, (1, 0, 2))
    blocks = lax.all_to_all(blocks, both, split_axis=0, concat_axis=0, tiled=True)
    output = jnp.transpose(blocks[:, :local_tok], (1, 0, 2)).reshape(local_tok, -1)
    sums = blocks[:, local_tok : local_tok + 24].astype(jnp.float32).reshape(-1, 3, 8, own_groups, GROUP)
    grad_taps = sums.sum(axis=(1, 4))[:, :KT].transpose(1, 0, 2).reshape(KT, -1)
    return (output, grad_tokens, grad_weight, grad_taps)


def solution(mesh):
    in_specs = (
        P("col", "depth"),
        P(("row", "col"), None, "depth"),
        P(None, "row"),
        P(("col", "depth"), "row"),
    )
    out_specs = (
        P(("col", "depth"), "row"),
        P("col", "depth"),
        P(("row", "col"), None, "depth"),
        P(None, "row"),
    )
    return jax.shard_map(
        on_device, mesh=mesh, in_specs=in_specs, out_specs=out_specs, check_vma=False
    )
```

```python
import functools

import jax
import jax.numpy as jnp
from jax import lax
from jax.experimental import pallas as pl
from jax.experimental.pallas import tpu as pltpu
from jax.sharding import PartitionSpec as P

GROUP = 16
KT = 7
PAD = 8
LANES = 128
MIB = 1024 * 1024
SMALL = pl.CostEstimate(flops=1, bytes_accessed=1, transcendentals=0)


def swap(value, axis, flip):
    count = lax.axis_size(axis)
    return lax.ppermute(value, axis, [(i, i ^ flip) for i in range(count)])


def after(value, *earlier):
    return lax.optimization_barrier((value, *earlier))[0]


def resident(shape, width):
    if width % LANES == 0:
        return pl.BlockSpec(memory_space=pltpu.VMEM)
    return pl.BlockSpec(tuple(shape), lambda *_: (0,) * len(shape))


def params(mib, width):
    return pltpu.CompilerParams(vmem_limit_bytes=(mib if width % LANES == 0 else 48) * MIB)


def project_kernel(place, *refs, pieces, count, width):
    x_refs = refs[:pieces]
    w_ref, keep_ref, send_ref = refs[pieces : pieces + 3]
    stream = pl.program_id(0)
    core = place[0] % 2
    if pieces == 1:
        x = x_refs[0][...]
    else:
        x_out = refs[pieces + 3]
        third = x_refs[0].shape[0]
        parity = place[2] % 2

        @pl.when(stream == 0)
        def _():
            x_out[pl.ds(pl.multiple_of(parity * third, third), third), :] = x_refs[0][...]
            x_out[pl.ds(pl.multiple_of((1 - parity) * third, third), third), :] = x_refs[1][...]
            x_out[2 * third :, :] = x_refs[2][...]

        x = x_out[...]
    nt = (((1,), (1,)), ((), ()))
    if width % LANES == 0:
        whole = lax.dot_general(x, w_ref[stream], nt, preferred_element_type=jnp.float32).astype(jnp.bfloat16)
        blocks = [whole[:, j * width : (j + 1) * width] for j in range(count)]
    else:
        blocks = [
            lax.dot_general(
                x, w_ref[0, j * width : (j + 1) * width, :], nt, preferred_element_type=jnp.float32
            ).astype(jnp.bfloat16)
            for j in range(count)
        ]
    for mine in range(2):

        @pl.when(core == mine)
        def _():
            for j in range(count):
                at = (j ^ place[0]) // 2
                if j % 2 == mine:
                    keep_ref[at, stream] = blocks[j]
                else:
                    send_ref[at, stream] = blocks[j]


def project(place, xs, w, count):
    tok, feat = sum(x.shape[0] for x in xs), xs[0].shape[1]
    streams, channels, _ = w.shape
    width = channels // count
    part = jax.ShapeDtypeStruct((count // 2, streams, tok, width), jnp.bfloat16)
    wide = width % LANES == 0
    spec = resident(part.shape, width)
    joined = len(xs) > 1
    outs = pl.pallas_call(
        functools.partial(project_kernel, pieces=len(xs), count=count, width=width),
        grid_spec=pltpu.PrefetchScalarGridSpec(
            num_scalar_prefetch=1,
            grid=(streams,),
            in_specs=[resident(x.shape, width) for x in xs]
            + [resident(w.shape, width) if wide else pl.BlockSpec((1, channels, feat), lambda s, _: (s, 0, 0))],
            out_specs=[spec, spec] + [resident((tok, feat), width)] * joined,
        ),
        out_shape=[part, part] + [jax.ShapeDtypeStruct((tok, feat), jnp.bfloat16)] * joined,
        compiler_params=params(24, width),
        cost_estimate=SMALL,
        name="project",
    )(place, *xs, w)
    return outs[0], outs[1], outs[2] if joined else xs[0]


def middle_kernel(place, taps_ref, up_ref, *refs, groups, terms, tile):
    part_refs = refs[: groups * terms]
    grad_refs = refs[groups * terms : groups * terms + groups]
    out_ref, q_s, k_s, v_s, mixed_s, gf_s, far_s = refs[groups * terms + groups :]
    col = place[1]
    tok = part_refs[0].shape[2]
    width = part_refs[0].shape[3]
    total = groups * tok
    mixed_s[0:PAD, :] = jnp.zeros((PAD, width), jnp.float32)
    gf_s[total : total + PAD, :] = jnp.zeros((PAD, width), jnp.float32)
    for k in range(groups):
        start = (col ^ k) * tok
        for i in range(tok // tile):
            inside = slice(i * tile, (i + 1) * tile)
            rows = pl.ds(pl.multiple_of(start + i * tile, tile), tile)
            streams = []
            for s in range(3):
                acc = None
                for ref in part_refs[k * terms : (k + 1) * terms]:
                    term = ref[0, s, inside, :].astype(jnp.float32)
                    acc = term if acc is None else acc + term
                streams.append(acc.astype(jnp.bfloat16).astype(jnp.float32))
            query, key, value = streams
            q_s[rows, :] = query
            k_s[rows, :] = key
            v_s[rows, :] = value
            mixed_s[pl.ds(pl.multiple_of(start + i * tile + PAD, PAD), tile), :] = key * value
            gf_s[rows, :] = up_ref[rows, :].astype(jnp.float32) * query
    taps = taps_ref[...]
    sums = [jnp.zeros((8, width), jnp.float32) for _ in range(KT)]
    for a in range(groups):
        for i in range(tok // tile):
            first = a * tok + i * tile
            rows = slice(first, first + tile)
            inside = slice(i * tile, (i + 1) * tile)
            gf = gf_s[rows, :]
            filtered = jnp.zeros((tile, width), jnp.float32)
            grad_mixed = jnp.zeros((tile, width), jnp.float32)
            for j in range(KT):
                shifted = mixed_s[first + PAD - j : first + PAD - j + tile, :]
                filtered = filtered + taps[j : j + 1, :] * shifted
                sums[j] = sums[j] + (gf * shifted).reshape(tile // 8, 8, width).sum(axis=0)
                grad_mixed = grad_mixed + taps[j : j + 1, :] * gf_s[first + j : first + j + tile, :]
            out_ref[first // tile, 0:tile, :] = (q_s[rows, :] * filtered).astype(jnp.bfloat16)
            at = col ^ a
            far_s[at, 0, inside, :] = (up_ref[rows, :].astype(jnp.float32) * filtered).astype(jnp.bfloat16)
            far_s[at, 1, inside, :] = (grad_mixed * v_s[rows, :]).astype(jnp.bfloat16)
            far_s[at, 2, inside, :] = (grad_mixed * k_s[rows, :]).astype(jnp.bfloat16)
    for k in range(groups):
        grad_refs[k][...] = far_s[k]
    rest = jnp.concatenate(
        [sums[j].sum(axis=0, keepdims=True) for j in range(KT)] + [jnp.zeros((1, width), jnp.float32)], axis=0
    )
    terms_of = []
    for _ in range(3):
        term = rest.astype(jnp.bfloat16).astype(jnp.float32)
        rest = rest - term
        terms_of.append(term)
    packed = jnp.concatenate(terms_of + [jnp.zeros((8, width), jnp.float32)], axis=0).astype(jnp.bfloat16)
    for i in range(out_ref.shape[0]):
        out_ref[i, tile : tile + 32, :] = packed


def middle(place, taps, up, parts, tile):
    groups, terms = len(parts), len(parts[0])
    _, _, tok, width = parts[0][0].shape
    total = groups * tok
    whole = lambda *shape: resident(shape, width)
    outs = pl.pallas_call(
        functools.partial(middle_kernel, groups=groups, terms=terms, tile=tile),
        grid_spec=pltpu.PrefetchScalarGridSpec(
            num_scalar_prefetch=1,
            grid=(1,),
            in_specs=[whole(KT, width), whole(total, width)]
            + [
                whole(1, 3, tok, width) if width % LANES == 0 else pl.BlockSpec((1, 3, tok, width), lambda *_: (0,) * 4)
            ]
            * (groups * terms),
            out_specs=[whole(3, tok, width)] * groups + [whole(total // tile, tile + 32, width)],
            scratch_shapes=[pltpu.VMEM((total, width), jnp.float32)] * 3
            + [pltpu.VMEM((total + PAD, width), jnp.float32)] * 2
            + [pltpu.VMEM((groups, 3, tok, width), jnp.bfloat16)],
        ),
        out_shape=[jax.ShapeDtypeStruct((3, tok, width), jnp.bfloat16)] * groups
        + [jax.ShapeDtypeStruct((total // tile, tile + 32, width), jnp.bfloat16)],
        compiler_params=params(16, width),
        cost_estimate=SMALL,
        name="middle",
    )(place, taps, up, *[term for terms_of in parts for term in terms_of])
    return outs[:groups], outs[groups]


def assemble_kernel(place, *refs):
    grad_refs, out_ref = refs[:-1], refs[-1]
    width = grad_refs[0].shape[2]
    for r, ref in enumerate(grad_refs):
        for s in range(3):
            at = pl.multiple_of((s * len(grad_refs) + (place[0] ^ r)) * width, width)
            out_ref[:, pl.ds(at, width)] = ref[s]


def assemble(place, grads):
    streams, tok, width = grads[0].shape
    out = jax.ShapeDtypeStruct((tok, streams * width * len(grads)), jnp.bfloat16)
    return pl.pallas_call(
        assemble_kernel,
        grid_spec=pltpu.PrefetchScalarGridSpec(
            num_scalar_prefetch=1,
            grid=(1,),
            in_specs=[resident(grads[0].shape, width)] * len(grads),
            out_specs=resident(out.shape, width),
        ),
        out_shape=out,
        compiler_params=params(12, width),
        cost_estimate=SMALL,
        name="assemble",
    )(place, *grads)


def input_grad_kernel(place, *refs, terms, width, first):
    grad_refs, w_ref, out_refs = refs[:terms], refs[terms], refs[terms + 1 :]
    step = out_refs[0].shape[1]
    if terms == 1:
        columns = pl.ds(pl.multiple_of((first + pl.program_id(0)) * step, step), step)
        acc = jnp.dot(
            grad_refs[0][...], w_ref[:, :, columns].reshape(-1, step), preferred_element_type=jnp.float32
        )
    else:
        acc = jnp.zeros(out_refs[0].shape, jnp.float32)
        for r, ref in enumerate(grad_refs):
            rows = pl.ds(pl.multiple_of((place[0] ^ r) * width, width), width)
            for s in range(3):
                acc = acc + jnp.dot(ref[s], w_ref[s, rows, :], preferred_element_type=jnp.float32)
    acc = acc.astype(jnp.bfloat16)
    for i, out_ref in enumerate(out_refs):

        @pl.when(pl.program_id(0) == i)
        def _():
            out_ref[...] = acc


def input_grad(place, grads, w, first, last, chunks):
    tok = grads[0].shape[-2]
    streams, channels, feat = w.shape
    step = feat // chunks
    width = channels if len(grads) == 1 else grads[0].shape[-1]
    return pl.pallas_call(
        functools.partial(input_grad_kernel, terms=len(grads), width=width, first=first),
        grid_spec=pltpu.PrefetchScalarGridSpec(
            num_scalar_prefetch=1,
            grid=(last - first,),
            in_specs=[resident(g.shape, width) for g in grads]
            + [
                resident(w.shape, width)
                if len(grads) == 1
                else pl.BlockSpec((streams, channels, step), lambda i, _: (0, 0, first + i))
            ],
            out_specs=[resident((tok, step), width)] * (last - first),
        ),
        out_shape=[jax.ShapeDtypeStruct((tok, step), jnp.bfloat16)] * (last - first),
        compiler_params=params(16, width),
        cost_estimate=SMALL,
        name="input_grad",
    )(place, *grads, w)


def weight_grad_kernel(place, *refs, chained, groups, wide, r):
    refs = refs[chained:]
    grad_refs = refs[: 2 * groups]
    x_refs = refs[2 * groups : 3 * groups]
    out_ref = refs[3 * groups]
    tok, step = x_refs[0].shape[0], out_ref.shape[2]
    width = grad_refs[0].shape[2]
    if wide:
        turned = refs[3 * groups + 1]

        @pl.when(pl.program_id(0) == 0)
        def _():
            for side in range(2):
                for s in range(3):
                    at = pl.multiple_of(((place[0] ^ r ^ side) % 2 + 2 * s) * width, width)
                    for k in range(groups):
                        turned[pl.ds(at, width), k * tok : (k + 1) * tok] = grad_refs[side * groups + k][s].T

        acc = None
        columns = pl.ds(pl.multiple_of(pl.program_id(0) * step, step), step)
        for k in range(groups):
            term = jnp.dot(
                turned[:, k * tok : (k + 1) * tok], x_refs[k][:, columns], preferred_element_type=jnp.float32
            )
            acc = term if acc is None else acc + term
        for s in range(3):
            out_ref[s] = acc[2 * s * width : 2 * (s + 1) * width, :]
    else:
        tn = (((0,), (0,)), ((), ()))
        for side in range(2):
            at = pl.multiple_of((place[0] ^ r ^ side) % 2 * width, width)
            for s in range(3):
                acc = None
                for k in range(groups):
                    term = lax.dot_general(
                        grad_refs[side * groups + k][s], x_refs[k][...], tn, preferred_element_type=jnp.float32
                    )
                    acc = term if acc is None else acc + term
                out_ref[s, pl.ds(at, width), :] = acc


def weight_grad(place, filled, grads, xs, r, count):
    groups = len(xs)
    streams, tok, width = grads[0].shape
    feat = xs[0].shape[1]
    channels = width * count
    step = min(512, feat)
    wide = width % LANES == 0
    chained = filled is not None
    return pl.pallas_call(
        functools.partial(weight_grad_kernel, chained=chained, groups=groups, wide=wide, r=r),
        grid_spec=pltpu.PrefetchScalarGridSpec(
            num_scalar_prefetch=1,
            grid=(feat // step,),
            in_specs=[pl.BlockSpec(memory_space=pl.ANY)] * chained
            + [resident((streams, tok, width), width)] * (2 * groups)
            + [resident((tok, feat), width) if wide else pl.BlockSpec((tok, step), lambda i, _: (0, i))] * groups,
            out_specs=pl.BlockSpec((streams, 2 * width, step), lambda i, at: (0, (at[0] ^ r) // 2, i)),
            scratch_shapes=[pltpu.VMEM((2 * streams * width, groups * tok), jnp.bfloat16)] if wide else [],
        ),
        out_shape=jax.ShapeDtypeStruct((streams, channels, feat), jnp.float32),
        input_output_aliases={1: 0} if chained else {},
        compiler_params=params(20, width),
        cost_estimate=SMALL,
        name="weight_grad",
    )(place, *([filled] if chained else []), *grads, *xs)


def added(first, second):
    return (first.astype(jnp.float32) + second.astype(jnp.float32)).astype(jnp.bfloat16)


def line_hops():
    count = lax.axis_size("row")
    half, last = count // 2, count - 1
    at = lax.axis_index("row")

    def inward(i):
        perm = [(i, i + 1), (last - i, last - i - 1)]
        return lambda value: lax.ppermute(value, "row", perm), added

    def across():
        perm = [(half - 1, half), (half, half - 1)]
        return lambda value: lax.ppermute(value, "row", perm), added

    def outward(i):
        perm = [(i + 1, i), (last - i - 1, last - i)]
        outer = (at == i) | (at == last - i)
        return lambda value: lax.ppermute(value, "row", perm), lambda value, got: jnp.where(outer, got, value)

    if count % 2:
        return [(lambda value: lax.psum(value, "row"), lambda value, got: got)]
    return [inward(i) for i in range(half - 1)] + [across()] + [outward(i) for i in reversed(range(half - 1))]


def first_pieces(tokens, k):
    tok = tokens.shape[0]
    if tok % 48 or lax.axis_size("row") % 2:
        return [swap(tokens, "col", k)]
    third = tok // 3
    parity = lax.axis_index("row") % 2
    return [swap(lax.dynamic_slice_in_dim(tokens, parity * third, third, axis=0), "col", k)]


def other_pieces(tokens, first, k):
    third = first[0].shape[0]
    if third == tokens.shape[0]:
        return first
    return first + [swap(first[0], "row", 1), swap(after(tokens[2 * third :], *first), "col", k)]


def on_device(tokens, weight, taps, upstream):
    n_col = lax.axis_size("col")
    n_depth = lax.axis_size("depth")
    both = ("col", "depth")
    local_tok = upstream.shape[0]
    depth_at = lax.axis_index("depth")
    col_at = lax.axis_index("col")
    place = jnp.stack([depth_at, col_at, lax.axis_index("row")]).astype(jnp.int32)
    w = jnp.transpose(weight, (1, 0, 2))
    width = w.shape[1] // n_depth
    own_groups = width // GROUP
    first_group = (col_at * n_depth + depth_at) * own_groups
    own_taps = jnp.repeat(lax.dynamic_slice_in_dim(taps, first_group, own_groups, axis=1), GROUP, axis=1)

    def project_and_sum(x_pieces, *earlier):
        keep, send, x = project(place, x_pieces, w, n_depth)
        near = swap(after(send, *earlier) if earlier else send, "depth", 1)
        pairs = [added(keep[r // 2], near[r // 2])[None] for r in range(2, n_depth, 2)]
        fars = [swap(pair, "depth", 2 * i + 2) for i, pair in enumerate(pairs)]
        return x, [keep, near] + fars, pairs, fars

    first = [first_pieces(tokens, k) for k in range(1, n_col)]
    x, terms, pairs, fars = project_and_sum([after(tokens, own_taps)], *[piece for of in first for piece in of])
    xs, parts = [x], [terms]
    up = lax.all_to_all(after(upstream, *pairs), both, split_axis=1, concat_axis=0, tiled=True)
    for k in range(1, n_col):
        x_pieces = other_pieces(tokens, first[k - 1], k)
        x_pieces[-1] = after(x_pieces[-1], up, *fars)
        x, terms, pairs, fars = project_and_sum(x_pieces)
        xs.append(x)
        parts.append(terms)
    own_grads, blocks = middle(place, own_taps, up, parts, local_tok)
    nears = [swap(own, "depth", 1) for own in own_grads]
    grads = [None] * n_col
    ready = []
    for k in reversed(range(n_col)):
        own = own_grads[k]
        fars = [swap(after(own, *ready) if ready else own, "depth", r) for r in range(2, n_depth, 2)]
        fars = [after(far, *nears) for far in fars]
        grads[k] = [own, nears[k]]
        for far in fars:
            grads[k] += [far, swap(far, "depth", 1)]
        ready = grads[k][2:]
    chunks = 4
    lhs = [[assemble(place, of)] if width % LANES == 0 else of for of in grads]
    sent = []
    for k in range(1, n_col):
        head = input_grad(place, lhs[k], w, 0, 1, chunks)
        behind = [after(lhs[k][0], *head)] + lhs[k][1:]
        tail = input_grad(place, behind, w, 1, chunks, chunks)
        sent.append([swap(part, "col", k) for part in list(head) + list(tail)])
        lhs[0][0] = after(lhs[0][0], tail[0])
    own_part = list(input_grad(place, lhs[0], w, 0, 1, chunks))
    hops = line_hops()
    done = [None] * chunks
    flying = [None] * chunks
    token = None
    filled = None
    for slot in range(chunks + len(hops)):
        for c in range(chunks):
            h = slot - c
            if h == 0:
                value = own_part[c] if token is None else after(own_part[c], token)
                total = value.astype(jnp.float32)
                for of in sent:
                    total = total + of[c].astype(jnp.float32)
                done[c] = total.astype(jnp.bfloat16)
            elif 0 < h <= len(hops):
                done[c] = hops[h - 1][1](after(done[c], token), flying[c])
            else:
                continue
            token = done[c]
            if h < len(hops):
                flying[c] = hops[h][0](done[c])
        if slot == 0:
            behind = [after(lhs[0][0], token)] + lhs[0][1:]
            own_part += input_grad(place, behind, w, 1, chunks, chunks)
            token = after(token, own_part[1])
        if 0 < slot <= n_depth // 2:
            r = n_depth - 2 * slot
            of = [group[i] for i in (r, r + 1) for group in grads]
            filled = weight_grad(place, filled, [after(of[0], token)] + of[1:], xs, r, n_depth)
            token = after(token, filled)
        if slot == chunks - 1:
            blocks = lax.all_to_all(after(blocks, token), both, split_axis=0, concat_axis=0, tiled=True)
    grad_tokens = jnp.concatenate(done, axis=1)
    grad_weight = jnp.transpose(filled, (1, 0, 2))
    output = jnp.transpose(blocks[:, :local_tok], (1, 0, 2)).reshape(local_tok, -1)
    sums = blocks[:, local_tok : local_tok + 24].astype(jnp.float32).reshape(-1, 3, 8, own_groups, GROUP)
    grad_taps = sums.sum(axis=(1, 4))[:, :KT].transpose(1, 0, 2).reshape(KT, -1)
    return (output, grad_tokens, grad_weight, grad_taps)


def solution(mesh):
    in_specs = (
        P("col", "depth"),
        P(("row", "col"), None, "depth"),
        P(None, "row"),
        P(("col", "depth"), "row"),
    )
    out_specs = (
        P(("col", "depth"), "row"),
        P("col", "depth"),
        P(("row", "col"), None, "depth"),
        P(None, "row"),
    )
    return jax.shard_map(
        on_device, mesh=mesh, in_specs=in_specs, out_specs=out_specs, check_vma=False
    )
```

```python
import functools

import jax
import jax.numpy as jnp
from jax import lax
from jax.experimental import pallas as pl
from jax.experimental.pallas import tpu as pltpu
from jax.sharding import PartitionSpec as P

GROUP = 16
KT = 7
PAD = 8
LANES = 128
MIB = 1024 * 1024
SMALL = pl.CostEstimate(flops=1, bytes_accessed=1, transcendentals=0)


def swap(value, axis, flip):
    count = lax.axis_size(axis)
    return lax.ppermute(value, axis, [(i, i ^ flip) for i in range(count)])


def after(value, *earlier):
    return lax.optimization_barrier((value, *earlier))[0]


def resident(shape, width):
    if width % LANES == 0:
        return pl.BlockSpec(memory_space=pltpu.VMEM)
    return pl.BlockSpec(tuple(shape), lambda *_: (0,) * len(shape), pipeline_mode=pl.Buffered(1))


def params(mib, width):
    return pltpu.CompilerParams(vmem_limit_bytes=(mib if width % LANES == 0 else 56) * MIB)


def project_kernel(place, *refs, pieces, count, width):
    x_refs = refs[:pieces]
    w_ref, keep_ref, send_ref = refs[pieces : pieces + 3]
    stream = pl.program_id(0)
    core = place[0] % 2
    if pieces == 1:
        x = x_refs[0][...]
    else:
        x_out = refs[pieces + 3]
        third = x_refs[0].shape[0]
        parity = place[2] % 2

        @pl.when(stream == 0)
        def _():
            x_out[pl.ds(pl.multiple_of(parity * third, third), third), :] = x_refs[0][...]
            x_out[pl.ds(pl.multiple_of((1 - parity) * third, third), third), :] = x_refs[1][...]
            x_out[2 * third :, :] = x_refs[2][...]

        x = x_out[...]
    nt = (((1,), (1,)), ((), ()))
    if width % LANES == 0:
        whole = lax.dot_general(x, w_ref[stream], nt, preferred_element_type=jnp.float32).astype(jnp.bfloat16)
        blocks = [whole[:, j * width : (j + 1) * width] for j in range(count)]
    else:
        blocks = [
            lax.dot_general(
                x, w_ref[0, j * width : (j + 1) * width, :], nt, preferred_element_type=jnp.float32
            ).astype(jnp.bfloat16)
            for j in range(count)
        ]
    for mine in range(2):

        @pl.when(core == mine)
        def _():
            for j in range(count):
                at = (j ^ place[0]) // 2
                if j % 2 == mine:
                    keep_ref[at, stream] = blocks[j]
                else:
                    send_ref[at, stream] = blocks[j]


def project(place, xs, w, count):
    tok, feat = sum(x.shape[0] for x in xs), xs[0].shape[1]
    streams, channels, _ = w.shape
    width = channels // count
    part = jax.ShapeDtypeStruct((count // 2, streams, tok, width), jnp.bfloat16)
    wide = width % LANES == 0
    spec = resident(part.shape, width)
    joined = len(xs) > 1
    outs = pl.pallas_call(
        functools.partial(project_kernel, pieces=len(xs), count=count, width=width),
        grid_spec=pltpu.PrefetchScalarGridSpec(
            num_scalar_prefetch=1,
            grid=(streams,),
            in_specs=[resident(x.shape, width) for x in xs]
            + [resident(w.shape, width) if wide else pl.BlockSpec((1, channels, feat), lambda s, _: (s, 0, 0))],
            out_specs=[spec, spec] + [resident((tok, feat), width)] * joined,
        ),
        out_shape=[part, part] + [jax.ShapeDtypeStruct((tok, feat), jnp.bfloat16)] * joined,
        compiler_params=params(10, width),
        cost_estimate=SMALL,
        name="project",
    )(place, *xs, w)
    return outs[0], outs[1], outs[2] if joined else xs[0]


def in_three(value):
    terms = []
    for _ in range(3):
        term = value.astype(jnp.bfloat16)
        value = value - term.astype(jnp.float32)
        terms.append(term)
    return terms


def split_kernel(place, up_ref, *out_refs):
    width = out_refs[0].shape[1]
    for r, ref in enumerate(out_refs):
        ref[...] = up_ref[:, pl.ds(pl.multiple_of((place[3] ^ r) * width, width), width)]


def split(place, up, count):
    tok, width = up.shape[0], up.shape[1] // count
    if width % LANES:
        blocks = jnp.transpose(up.reshape(tok, count, width), (1, 0, 2))
        return [lax.dynamic_index_in_dim(blocks, place[3] ^ r, 0, keepdims=False) for r in range(count)]
    return pl.pallas_call(
        split_kernel,
        grid_spec=pltpu.PrefetchScalarGridSpec(
            num_scalar_prefetch=1,
            grid=(1,),
            in_specs=[resident(up.shape, width)],
            out_specs=[resident((tok, width), width)] * count,
        ),
        out_shape=[jax.ShapeDtypeStruct((tok, width), jnp.bfloat16)] * count,
        compiler_params=params(4, width),
        cost_estimate=SMALL,
        name="split",
    )(place, up)


def join_kernel(place, _, *refs):
    block_refs, (out_ref, grad_taps_ref) = refs[:-2], refs[-2:]
    tok = out_ref.shape[0]
    width = block_refs[0].shape[1]
    groups = grad_taps_ref.shape[1]
    lane_group = lax.broadcasted_iota(jnp.int32, (width, groups), 0) // GROUP
    group = lax.broadcasted_iota(jnp.int32, (width, groups), 1)
    total = jnp.zeros((24, groups), jnp.float32)
    for r, ref in enumerate(block_refs):
        at = place[3] ^ r
        out_ref[:, pl.ds(pl.multiple_of(at * width, width), width)] = ref[0:tok, :]
        spread = (lane_group + at * (width // GROUP) == group).astype(jnp.bfloat16)
        total = total + jnp.dot(ref[tok : tok + 24, :], spread, preferred_element_type=jnp.float32)
    grad_taps_ref[...] = (total[0:8] + total[8:16] + total[16:24])[:KT]


def join(place, mark, blocks, tok, groups):
    count, width = len(blocks), blocks[0].shape[1]
    if width % LANES:
        whole = jnp.stack(blocks)[place[3] ^ jnp.arange(count)]
        output = jnp.transpose(whole[:, :tok], (1, 0, 2)).reshape(tok, -1)
        sums = whole[:, tok : tok + 24].astype(jnp.float32).reshape(count, 3, 8, width // GROUP, GROUP)
        return output, sums.sum(axis=(1, 4))[:, :KT].transpose(1, 0, 2).reshape(KT, -1)
    return pl.pallas_call(
        join_kernel,
        grid_spec=pltpu.PrefetchScalarGridSpec(
            num_scalar_prefetch=1,
            grid=(1,),
            in_specs=[pl.BlockSpec(memory_space=pl.ANY)] + [resident(blocks[0].shape, width)] * count,
            out_specs=[resident((tok, width * count), width), resident((KT, groups), width)],
        ),
        out_shape=[
            jax.ShapeDtypeStruct((tok, width * count), jnp.bfloat16),
            jax.ShapeDtypeStruct((KT, groups), jnp.float32),
        ],
        compiler_params=params(4, width),
        cost_estimate=SMALL,
        name="join",
    )(place, mark, *blocks)


def middle_kernel(place, taps_ref, *refs, devices, groups, terms, tile):
    up_refs, refs = refs[:devices], refs[devices:]
    part_refs = refs[: groups * terms]
    grad_refs = refs[groups * terms : groups * terms + groups]
    out_refs = refs[groups * terms + groups : groups * terms + groups + devices]
    up_s, out_s, q_s, k_s, v_s, mixed_s, gf_s, far_s = refs[groups * terms + groups + devices :]
    col = place[1]
    tok = part_refs[0].shape[2]
    width = part_refs[0].shape[3]
    total = groups * tok
    tap_groups = taps_ref.shape[1]
    for r, ref in enumerate(up_refs):
        rows = pl.ds(pl.multiple_of((place[3] ^ r) * tile, tile), tile)
        up_s[rows, :] = ref[...]
    lane_group = lax.broadcasted_iota(jnp.int32, (tap_groups, width), 1) // GROUP
    group = lax.broadcasted_iota(jnp.int32, (tap_groups, width), 0)
    spread = (lane_group + place[3] * (width // GROUP) == group).astype(jnp.bfloat16)
    taps = sum(jnp.dot(term, spread, preferred_element_type=jnp.float32) for term in in_three(taps_ref[...]))
    mixed_s[0:PAD, :] = jnp.zeros((PAD, width), jnp.float32)
    gf_s[total : total + PAD, :] = jnp.zeros((PAD, width), jnp.float32)
    for k in range(groups):
        start = (col ^ k) * tok
        for i in range(tok // tile):
            inside = slice(i * tile, (i + 1) * tile)
            rows = pl.ds(pl.multiple_of(start + i * tile, tile), tile)
            streams = []
            for s in range(3):
                acc = None
                for ref in part_refs[k * terms : (k + 1) * terms]:
                    term = ref[0, s, inside, :].astype(jnp.float32)
                    acc = term if acc is None else acc + term
                streams.append(acc.astype(jnp.bfloat16))
            q_s[rows, :], k_s[rows, :], v_s[rows, :] = streams
            query, key, value = [stream.astype(jnp.float32) for stream in streams]
            mixed_s[pl.ds(pl.multiple_of(start + i * tile + PAD, PAD), tile), :] = key * value
            gf_s[rows, :] = up_s[rows, :].astype(jnp.float32) * query
    sums = [jnp.zeros((8, width), jnp.float32) for _ in range(KT)]
    for a in range(groups):
        for i in range(tok // tile):
            first = a * tok + i * tile
            rows = slice(first, first + tile)
            inside = slice(i * tile, (i + 1) * tile)
            gf = gf_s[rows, :]
            filtered = jnp.zeros((tile, width), jnp.float32)
            grad_mixed = jnp.zeros((tile, width), jnp.float32)
            for j in range(KT):
                shifted = mixed_s[first + PAD - j : first + PAD - j + tile, :]
                filtered = filtered + taps[j : j + 1, :] * shifted
                sums[j] = sums[j] + (gf * shifted).reshape(tile // 8, 8, width).sum(axis=0)
                grad_mixed = grad_mixed + taps[j : j + 1, :] * gf_s[first + j : first + j + tile, :]
            out_s[first // tile] = (q_s[rows, :].astype(jnp.float32) * filtered).astype(jnp.bfloat16)
            at = col ^ a
            far_s[at, 0, inside, :] = (up_s[rows, :].astype(jnp.float32) * filtered).astype(jnp.bfloat16)
            far_s[at, 1, inside, :] = (grad_mixed * v_s[rows, :].astype(jnp.float32)).astype(jnp.bfloat16)
            far_s[at, 2, inside, :] = (grad_mixed * k_s[rows, :].astype(jnp.float32)).astype(jnp.bfloat16)
    for k in range(groups):
        grad_refs[k][...] = far_s[k]
    rest = jnp.concatenate(
        [sums[j].sum(axis=0, keepdims=True) for j in range(KT)] + [jnp.zeros((1, width), jnp.float32)], axis=0
    )
    terms_of = [term.astype(jnp.float32) for term in in_three(rest)]
    packed = jnp.concatenate(terms_of + [jnp.zeros((8, width), jnp.float32)], axis=0).astype(jnp.bfloat16)
    for r, ref in enumerate(out_refs):
        ref[0:tile, :] = out_s[place[3] ^ r]
        ref[tile : tile + 32, :] = packed


def middle(place, taps, ups, parts):
    groups, terms, devices = len(parts), len(parts[0]), len(ups)
    tile = ups[0].shape[0]
    _, _, tok, width = parts[0][0].shape
    total = groups * tok
    whole = lambda *shape: resident(shape, width)
    one = whole(1, 3, tok, width)
    outs = pl.pallas_call(
        functools.partial(middle_kernel, devices=devices, groups=groups, terms=terms, tile=tile),
        grid_spec=pltpu.PrefetchScalarGridSpec(
            num_scalar_prefetch=1,
            grid=(1,),
            in_specs=[whole(*taps.shape)] + [whole(tile, width)] * devices + [one] * (groups * terms),
            out_specs=[whole(3, tok, width)] * groups + [whole(tile + 32, width)] * devices,
            scratch_shapes=[
                pltpu.VMEM((total, width), jnp.bfloat16),
                pltpu.VMEM((devices, tile, width), jnp.bfloat16),
            ]
            + [pltpu.VMEM((total, width), jnp.bfloat16)] * 3
            + [pltpu.VMEM((total + PAD, width), jnp.float32)] * 2
            + [pltpu.VMEM((groups, 3, tok, width), jnp.bfloat16)],
        ),
        out_shape=[jax.ShapeDtypeStruct((3, tok, width), jnp.bfloat16)] * groups
        + [jax.ShapeDtypeStruct((tile + 32, width), jnp.bfloat16)] * devices,
        compiler_params=params(10, width),
        cost_estimate=SMALL,
        name="middle",
    )(place, taps, *ups, *[term for terms_of in parts for term in terms_of])
    return outs[:groups], outs[groups:]


def assemble_kernel(place, *refs):
    grad_refs, out_ref = refs[:-1], refs[-1]
    width = grad_refs[0].shape[2]
    for r, ref in enumerate(grad_refs):
        for s in range(3):
            at = pl.multiple_of((s * len(grad_refs) + (place[0] ^ r)) * width, width)
            out_ref[:, pl.ds(at, width)] = ref[s]


def assemble(place, grads):
    streams, tok, width = grads[0].shape
    out = jax.ShapeDtypeStruct((tok, streams * width * len(grads)), jnp.bfloat16)
    return pl.pallas_call(
        assemble_kernel,
        grid_spec=pltpu.PrefetchScalarGridSpec(
            num_scalar_prefetch=1,
            grid=(1,),
            in_specs=[resident(grads[0].shape, width)] * len(grads),
            out_specs=resident(out.shape, width),
        ),
        out_shape=out,
        compiler_params=params(4, width),
        cost_estimate=SMALL,
        name="assemble",
    )(place, *grads)


def input_grad_kernel(place, *refs, terms, width, first):
    grad_refs, w_ref, out_refs = refs[:terms], refs[terms], refs[terms + 1 :]
    step = out_refs[0].shape[1]
    if terms == 1:
        columns = pl.ds(pl.multiple_of((first + pl.program_id(0)) * step, step), step)
        acc = jnp.dot(
            grad_refs[0][...], w_ref[:, :, columns].reshape(-1, step), preferred_element_type=jnp.float32
        )
    else:
        acc = jnp.zeros(out_refs[0].shape, jnp.float32)
        for r, ref in enumerate(grad_refs):
            rows = pl.ds(pl.multiple_of((place[0] ^ r) * width, width), width)
            for s in range(3):
                acc = acc + jnp.dot(ref[s], w_ref[s, rows, :], preferred_element_type=jnp.float32)
    acc = acc.astype(jnp.bfloat16)
    for i, out_ref in enumerate(out_refs):

        @pl.when(pl.program_id(0) == i)
        def _():
            out_ref[...] = acc


def input_grad(place, grads, w, first, last, chunks):
    tok = grads[0].shape[-2]
    streams, channels, feat = w.shape
    step = feat // chunks
    width = channels if len(grads) == 1 else grads[0].shape[-1]
    return pl.pallas_call(
        functools.partial(input_grad_kernel, terms=len(grads), width=width, first=first),
        grid_spec=pltpu.PrefetchScalarGridSpec(
            num_scalar_prefetch=1,
            grid=(last - first,),
            in_specs=[resident(g.shape, width) for g in grads]
            + [
                resident(w.shape, width)
                if len(grads) == 1
                else pl.BlockSpec((streams, channels, step), lambda i, _: (0, 0, first + i))
            ],
            out_specs=[resident((tok, step), width)] * (last - first),
        ),
        out_shape=[jax.ShapeDtypeStruct((tok, step), jnp.bfloat16)] * (last - first),
        compiler_params=params(8, width),
        cost_estimate=SMALL,
        name="input_grad",
    )(place, *grads, w)


def weight_grad_kernel(place, *refs, chained, groups, wide, r):
    refs = refs[2 * chained :]
    grad_refs = refs[: 2 * groups]
    x_refs = refs[2 * groups : 3 * groups]
    out_ref, mark_ref = refs[3 * groups : 3 * groups + 2]
    mark_ref[...] = jnp.zeros(mark_ref.shape, jnp.float32)
    tok, step = x_refs[0].shape[0], out_ref.shape[2]
    width = grad_refs[0].shape[2]
    if wide:
        turned = refs[3 * groups + 2]

        @pl.when(pl.program_id(0) == 0)
        def _():
            for side in range(2):
                for s in range(3):
                    at = pl.multiple_of(((place[0] ^ r ^ side) % 2 + 2 * s) * width, width)
                    for k in range(groups):
                        turned[pl.ds(at, width), k * tok : (k + 1) * tok] = grad_refs[side * groups + k][s].T

        acc = None
        columns = pl.ds(pl.multiple_of(pl.program_id(0) * step, step), step)
        for k in range(groups):
            term = jnp.dot(
                turned[:, k * tok : (k + 1) * tok], x_refs[k][:, columns], preferred_element_type=jnp.float32
            )
            acc = term if acc is None else acc + term
        for s in range(3):
            out_ref[s] = acc[2 * s * width : 2 * (s + 1) * width, :]
    else:
        tn = (((0,), (0,)), ((), ()))
        for side in range(2):
            at = pl.multiple_of((place[0] ^ r ^ side) % 2 * width, width)
            for s in range(3):
                acc = None
                for k in range(groups):
                    term = lax.dot_general(
                        grad_refs[side * groups + k][s], x_refs[k][...], tn, preferred_element_type=jnp.float32
                    )
                    acc = term if acc is None else acc + term
                out_ref[s, pl.ds(at, width), :] = acc


def weight_grad(place, filled, grads, xs, r, count):
    groups = len(xs)
    streams, tok, width = grads[0].shape
    feat = xs[0].shape[1]
    channels = width * count
    step = min(512, feat)
    wide = width % LANES == 0
    chained = filled is not None
    return pl.pallas_call(
        functools.partial(weight_grad_kernel, chained=chained, groups=groups, wide=wide, r=r),
        grid_spec=pltpu.PrefetchScalarGridSpec(
            num_scalar_prefetch=1,
            grid=(feat // step,),
            in_specs=[pl.BlockSpec(memory_space=pl.ANY)] * (2 * chained)
            + [resident((streams, tok, width), width)] * (2 * groups)
            + [resident((tok, feat), width) if wide else pl.BlockSpec((tok, step), lambda i, _: (0, i))] * groups,
            out_specs=[
                pl.BlockSpec((streams, 2 * width, step), lambda i, at: (0, (at[0] ^ r) // 2, i)),
                resident((8, LANES), width),
            ],
            scratch_shapes=[pltpu.VMEM((2 * streams * width, groups * tok), jnp.bfloat16)] if wide else [],
        ),
        out_shape=[
            jax.ShapeDtypeStruct((streams, channels, feat), jnp.float32),
            jax.ShapeDtypeStruct((8, LANES), jnp.float32),
        ],
        input_output_aliases={1: 0} if chained else {},
        compiler_params=params(14, width),
        cost_estimate=SMALL,
        name="weight_grad",
    )(place, *(filled if chained else []), *grads, *xs)


def added(first, second):
    return (first.astype(jnp.float32) + second.astype(jnp.float32)).astype(jnp.bfloat16)


def first_pieces(tokens, k):
    tok = tokens.shape[0]
    if tok % 48 or lax.axis_size("row") % 2:
        return [swap(tokens, "col", k)]
    third = tok // 3
    parity = lax.axis_index("row") % 2
    return [swap(lax.dynamic_slice_in_dim(tokens, parity * third, third, axis=0), "col", k)]


def other_pieces(tokens, first, k):
    third = first[0].shape[0]
    if third == tokens.shape[0]:
        return first
    rest = after(tokens, lax.axis_index("row"))[2 * third :]
    return first + [swap(first[0], "row", 1), swap(after(rest, *first), "col", k)]


def on_device(tokens, weight, taps, upstream):
    n_col = lax.axis_size("col")
    n_depth = lax.axis_size("depth")
    both = ("col", "depth")
    local_tok = upstream.shape[0]
    depth_at = lax.axis_index("depth")
    col_at = lax.axis_index("col")
    row_at = lax.axis_index("row")
    place = jnp.stack([depth_at, col_at, row_at, col_at * n_depth + depth_at]).astype(jnp.int32)
    w = jnp.transpose(weight, (1, 0, 2))
    width = w.shape[1] // n_depth
    def project_and_sum(x_pieces, *earlier):
        keep, send, x = project(place, x_pieces, w, n_depth)
        near = swap(after(send, *earlier) if earlier else send, "depth", 1)
        pairs = [added(keep[r // 2], near[r // 2])[None] for r in range(2, n_depth, 2)]
        fars = [swap(pair, "depth", 2 * i + 2) for i, pair in enumerate(pairs)]
        return x, [keep, near] + fars, pairs, fars

    first = [first_pieces(tokens, k) for k in range(1, n_col)]
    x, terms, pairs, fars = project_and_sum([tokens], *[piece for of in first for piece in of])
    xs, parts = [x], [terms]
    ups = split(place, after(upstream, *pairs), n_col * n_depth)
    ups = [up if r == 0 else swap(up, both, r) for r, up in enumerate(ups)]
    for k in range(1, n_col):
        x_pieces = other_pieces(tokens, first[k - 1], k)
        x_pieces[-1] = after(x_pieces[-1], *ups, *fars)
        x, terms, pairs, fars = project_and_sum(x_pieces)
        xs.append(x)
        parts.append(terms)
    own_grads, blocks = middle(place, taps, ups, parts)
    nears = [swap(own, "depth", 1) for own in own_grads]
    grads = [None] * n_col
    ready = []
    for k in reversed(range(n_col)):
        own = own_grads[k]
        fars = [swap(after(own, *ready) if ready else own, "depth", r) for r in range(2, n_depth, 2)]
        fars = [after(far, *nears) for far in fars]
        grads[k] = [own, nears[k]]
        for far in fars:
            grads[k] += [far, swap(far, "depth", 1)]
        ready = grads[k][2:]
    chunks = 4
    lhs = [[assemble(place, of)] if width % LANES == 0 else of for of in grads]
    sent = []
    for k in range(1, n_col):
        head = input_grad(place, lhs[k], w, 0, 1, chunks)
        behind = [after(lhs[k][0], *head)] + lhs[k][1:]
        tail = input_grad(place, behind, w, 1, chunks, chunks)
        sent.append([swap(part, "col", k) for part in list(head) + list(tail)])
        lhs[0][0] = after(lhs[0][0], tail[0])
    own_part = list(input_grad(place, lhs[0], w, 0, 1, chunks))
    outer = (row_at == 0) | (row_at == 3)
    inward, across, summed, done = ([None] * chunks for _ in range(4))
    pair = cross = filled = None
    marks = []
    line = lax.axis_size("row") == 4
    for slot in range(chunks + 3):
        if slot < chunks:
            total = after(own_part[slot], *marks).astype(jnp.float32)
            for of in sent:
                total = total + of[slot].astype(jnp.float32)
            inward[slot] = total.astype(jnp.bfloat16)
            marks = [inward[slot]]
        if not line:
            if slot < chunks:
                done[slot] = lax.psum(inward[slot], "row")
        else:
            if 0 <= slot - 1 < chunks:
                across[slot - 1] = added(after(inward[slot - 1], *marks), pair)
                marks = [across[slot - 1]]
            if 0 <= slot - 2 < chunks:
                summed[slot - 2] = added(after(across[slot - 2], *marks), cross)
                marks = [summed[slot - 2]]
            if 0 <= slot - 3 < chunks:
                done[slot - 3] = jnp.where(outer, pair, summed[slot - 3])
            if slot < chunks + 2:
                out = summed[slot - 2] if slot >= 2 else inward[slot]
                pair = swap(jnp.where(outer, inward[slot], out) if slot < chunks else out, "row", 1)
            if 0 <= slot - 1 < chunks:
                cross = lax.ppermute(across[slot - 1], "row", [(1, 2), (2, 1)])
        if slot == 0:
            behind = [after(lhs[0][0], *marks)] + lhs[0][1:]
            own_part += input_grad(place, behind, w, 1, chunks, chunks)
            marks = [own_part[1]]
        if 0 < slot <= n_depth // 2:
            r = n_depth - 2 * slot
            of = [group[i] for i in (r, r + 1) for group in grads]
            filled = weight_grad(place, filled, [after(of[0], *marks)] + of[1:], xs, r, n_depth)
            marks = [filled[1]]
        if slot == chunks - 1:
            blocks = [
                block if r == 0 else swap(after(block, *marks), both, r) for r, block in enumerate(blocks)
            ]
    grad_tokens = jnp.concatenate(done, axis=1)
    grad_weight = jnp.transpose(filled[0], (1, 0, 2))
    output, grad_taps = join(place, filled[1], blocks, local_tok, taps.shape[1])
    return (output, grad_tokens, grad_weight, grad_taps)


def solution(mesh):
    in_specs = (
        P("col", "depth"),
        P(("row", "col"), None, "depth"),
        P(None, "row"),
        P(("col", "depth"), "row"),
    )
    out_specs = (
        P(("col", "depth"), "row"),
        P("col", "depth"),
        P(("row", "col"), None, "depth"),
        P(None, "row"),
    )
    return jax.shard_map(
        on_device, mesh=mesh, in_specs=in_specs, out_specs=out_specs, check_vma=False
    )
```

```python
import functools

import jax
import jax.numpy as jnp
from jax import lax
from jax.experimental import pallas as pl
from jax.experimental.pallas import tpu as pltpu
from jax.sharding import PartitionSpec as P

GROUP = 16
KT = 7
PAD = 8
LANES = 128
MIB = 1024 * 1024
SMALL = pl.CostEstimate(flops=1, bytes_accessed=1, transcendentals=0)


def swap(value, axis, flip):
    count = lax.axis_size(axis)
    return lax.ppermute(value, axis, [(i, i ^ flip) for i in range(count)])


def after(value, *earlier):
    return lax.optimization_barrier((value, *earlier))[0]


def resident(shape, width):
    if width % LANES == 0:
        return pl.BlockSpec(memory_space=pltpu.VMEM)
    return pl.BlockSpec(tuple(shape), lambda *_: (0,) * len(shape), pipeline_mode=pl.Buffered(1))


def params(mib, width):
    return pltpu.CompilerParams(vmem_limit_bytes=(mib if width % LANES == 0 else 56) * MIB)


def project_kernel(place, *refs, pieces, count, width):
    x_refs = refs[:pieces]
    w_ref, keep_ref, send_ref = refs[pieces : pieces + 3]
    stream = pl.program_id(0)
    core = place[0] % 2
    if pieces == 1:
        x = x_refs[0][...]
    else:
        x_out = refs[pieces + 3]
        third = x_refs[0].shape[0]
        parity = place[2] % 2

        @pl.when(stream == 0)
        def _():
            x_out[pl.ds(pl.multiple_of(parity * third, third), third), :] = x_refs[0][...]
            x_out[pl.ds(pl.multiple_of((1 - parity) * third, third), third), :] = x_refs[1][...]
            x_out[2 * third :, :] = x_refs[2][...]

        x = x_out[...]
    nt = (((1,), (1,)), ((), ()))
    if width % LANES == 0:
        whole = lax.dot_general(x, w_ref[stream], nt, preferred_element_type=jnp.float32).astype(jnp.bfloat16)
        blocks = [whole[:, j * width : (j + 1) * width] for j in range(count)]
    else:
        blocks = [
            lax.dot_general(
                x, w_ref[0, j * width : (j + 1) * width, :], nt, preferred_element_type=jnp.float32
            ).astype(jnp.bfloat16)
            for j in range(count)
        ]
    for mine in range(2):

        @pl.when(core == mine)
        def _():
            for j in range(count):
                at = (j ^ place[0]) // 2
                if j % 2 == mine:
                    keep_ref[at, stream] = blocks[j]
                else:
                    send_ref[at, stream] = blocks[j]


def project(place, xs, w, count):
    tok, feat = sum(x.shape[0] for x in xs), xs[0].shape[1]
    streams, channels, _ = w.shape
    width = channels // count
    part = jax.ShapeDtypeStruct((count // 2, streams, tok, width), jnp.bfloat16)
    wide = width % LANES == 0
    spec = resident(part.shape, width)
    joined = len(xs) > 1
    outs = pl.pallas_call(
        functools.partial(project_kernel, pieces=len(xs), count=count, width=width),
        grid_spec=pltpu.PrefetchScalarGridSpec(
            num_scalar_prefetch=1,
            grid=(streams,),
            in_specs=[resident(x.shape, width) for x in xs]
            + [resident(w.shape, width) if wide else pl.BlockSpec((1, channels, feat), lambda s, _: (s, 0, 0))],
            out_specs=[spec, spec] + [resident((tok, feat), width)] * joined,
        ),
        out_shape=[part, part] + [jax.ShapeDtypeStruct((tok, feat), jnp.bfloat16)] * joined,
        compiler_params=params(10, width),
        cost_estimate=SMALL,
        name="project",
    )(place, *xs, w)
    return outs[0], outs[1], outs[2] if joined else xs[0]


def in_three(value):
    terms = []
    for _ in range(3):
        term = value.astype(jnp.bfloat16)
        value = value - term.astype(jnp.float32)
        terms.append(term)
    return terms


def split_kernel(place, up_ref, *out_refs):
    width = out_refs[0].shape[1]
    for r, ref in enumerate(out_refs):
        ref[...] = up_ref[:, pl.ds(pl.multiple_of((place[3] ^ r) * width, width), width)]


def split(place, up, count):
    tok, width = up.shape[0], up.shape[1] // count
    if width % LANES:
        blocks = jnp.transpose(up.reshape(tok, count, width), (1, 0, 2))
        return [lax.dynamic_index_in_dim(blocks, place[3] ^ r, 0, keepdims=False) for r in range(count)]
    return pl.pallas_call(
        split_kernel,
        grid_spec=pltpu.PrefetchScalarGridSpec(
            num_scalar_prefetch=1,
            grid=(1,),
            in_specs=[resident(up.shape, width)],
            out_specs=[resident((tok, width), width)] * count,
        ),
        out_shape=[jax.ShapeDtypeStruct((tok, width), jnp.bfloat16)] * count,
        compiler_params=params(4, width),
        cost_estimate=SMALL,
        name="split",
    )(place, up)


def join_kernel(place, _, *refs):
    block_refs, (out_ref, grad_taps_ref) = refs[:-2], refs[-2:]
    tok = out_ref.shape[0]
    width = block_refs[0].shape[1]
    groups = grad_taps_ref.shape[1]
    lane_group = lax.broadcasted_iota(jnp.int32, (width, groups), 0) // GROUP
    group = lax.broadcasted_iota(jnp.int32, (width, groups), 1)
    total = jnp.zeros((24, groups), jnp.float32)
    for r, ref in enumerate(block_refs):
        at = place[3] ^ r
        out_ref[:, pl.ds(pl.multiple_of(at * width, width), width)] = ref[0:tok, :]
        spread = (lane_group + at * (width // GROUP) == group).astype(jnp.bfloat16)
        total = total + jnp.dot(ref[tok : tok + 24, :], spread, preferred_element_type=jnp.float32)
    grad_taps_ref[...] = (total[0:8] + total[8:16] + total[16:24])[:KT]


def join(place, mark, blocks, tok, groups):
    count, width = len(blocks), blocks[0].shape[1]
    if width % LANES:
        whole = jnp.stack(blocks)[place[3] ^ jnp.arange(count)]
        output = jnp.transpose(whole[:, :tok], (1, 0, 2)).reshape(tok, -1)
        sums = whole[:, tok : tok + 24].astype(jnp.float32).reshape(count, 3, 8, width // GROUP, GROUP)
        return output, sums.sum(axis=(1, 4))[:, :KT].transpose(1, 0, 2).reshape(KT, -1)
    return pl.pallas_call(
        join_kernel,
        grid_spec=pltpu.PrefetchScalarGridSpec(
            num_scalar_prefetch=1,
            grid=(1,),
            in_specs=[pl.BlockSpec(memory_space=pl.ANY)] + [resident(blocks[0].shape, width)] * count,
            out_specs=[resident((tok, width * count), width), resident((KT, groups), width)],
        ),
        out_shape=[
            jax.ShapeDtypeStruct((tok, width * count), jnp.bfloat16),
            jax.ShapeDtypeStruct((KT, groups), jnp.float32),
        ],
        compiler_params=params(4, width),
        cost_estimate=SMALL,
        name="join",
    )(place, mark, *blocks)


def middle_kernel(place, taps_ref, *refs, devices, groups, terms, tile):
    up_refs, refs = refs[:devices], refs[devices:]
    part_refs = refs[: groups * terms]
    grad_refs = refs[groups * terms : groups * terms + groups]
    out_refs = refs[groups * terms + groups : groups * terms + groups + devices]
    up_s, out_s, q_s, k_s, v_s, mixed_s, gf_s, far_s = refs[groups * terms + groups + devices :]
    col = place[1]
    tok = part_refs[0].shape[2]
    width = part_refs[0].shape[3]
    total = groups * tok
    tap_groups = taps_ref.shape[1]
    for r, ref in enumerate(up_refs):
        rows = pl.ds(pl.multiple_of((place[3] ^ r) * tile, tile), tile)
        up_s[rows, :] = ref[...]
    lane_group = lax.broadcasted_iota(jnp.int32, (tap_groups, width), 1) // GROUP
    group = lax.broadcasted_iota(jnp.int32, (tap_groups, width), 0)
    spread = (lane_group + place[3] * (width // GROUP) == group).astype(jnp.bfloat16)
    taps = sum(jnp.dot(term, spread, preferred_element_type=jnp.float32) for term in in_three(taps_ref[...]))
    mixed_s[0:PAD, :] = jnp.zeros((PAD, width), jnp.float32)
    gf_s[total : total + PAD, :] = jnp.zeros((PAD, width), jnp.float32)
    for k in range(groups):
        start = (col ^ k) * tok
        for i in range(tok // tile):
            inside = slice(i * tile, (i + 1) * tile)
            rows = pl.ds(pl.multiple_of(start + i * tile, tile), tile)
            streams = []
            for s in range(3):
                acc = None
                for ref in part_refs[k * terms : (k + 1) * terms]:
                    term = ref[0, s, inside, :].astype(jnp.float32)
                    acc = term if acc is None else acc + term
                streams.append(acc.astype(jnp.bfloat16))
            q_s[rows, :], k_s[rows, :], v_s[rows, :] = streams
            query, key, value = [stream.astype(jnp.float32) for stream in streams]
            mixed_s[pl.ds(pl.multiple_of(start + i * tile + PAD, PAD), tile), :] = key * value
            gf_s[rows, :] = up_s[rows, :].astype(jnp.float32) * query
    sums = [jnp.zeros((8, width), jnp.float32) for _ in range(KT)]
    for a in range(groups):
        for i in range(tok // tile):
            first = a * tok + i * tile
            rows = slice(first, first + tile)
            inside = slice(i * tile, (i + 1) * tile)
            gf = gf_s[rows, :]
            filtered = jnp.zeros((tile, width), jnp.float32)
            grad_mixed = jnp.zeros((tile, width), jnp.float32)
            for j in range(KT):
                shifted = mixed_s[first + PAD - j : first + PAD - j + tile, :]
                filtered = filtered + taps[j : j + 1, :] * shifted
                sums[j] = sums[j] + (gf * shifted).reshape(tile // 8, 8, width).sum(axis=0)
                grad_mixed = grad_mixed + taps[j : j + 1, :] * gf_s[first + j : first + j + tile, :]
            out_s[first // tile] = (q_s[rows, :].astype(jnp.float32) * filtered).astype(jnp.bfloat16)
            at = col ^ a
            far_s[at, 0, inside, :] = (up_s[rows, :].astype(jnp.float32) * filtered).astype(jnp.bfloat16)
            far_s[at, 1, inside, :] = (grad_mixed * v_s[rows, :].astype(jnp.float32)).astype(jnp.bfloat16)
            far_s[at, 2, inside, :] = (grad_mixed * k_s[rows, :].astype(jnp.float32)).astype(jnp.bfloat16)
    for k in range(groups):
        grad_refs[k][...] = far_s[k]
    rest = jnp.concatenate(
        [sums[j].sum(axis=0, keepdims=True) for j in range(KT)] + [jnp.zeros((1, width), jnp.float32)], axis=0
    )
    terms_of = [term.astype(jnp.float32) for term in in_three(rest)]
    packed = jnp.concatenate(terms_of + [jnp.zeros((8, width), jnp.float32)], axis=0).astype(jnp.bfloat16)
    for r, ref in enumerate(out_refs):
        ref[0:tile, :] = out_s[place[3] ^ r]
        ref[tile : tile + 32, :] = packed


def middle(place, taps, ups, parts):
    groups, terms, devices = len(parts), len(parts[0]), len(ups)
    tile = ups[0].shape[0]
    _, _, tok, width = parts[0][0].shape
    total = groups * tok
    whole = lambda *shape: resident(shape, width)
    one = whole(1, 3, tok, width)
    outs = pl.pallas_call(
        functools.partial(middle_kernel, devices=devices, groups=groups, terms=terms, tile=tile),
        grid_spec=pltpu.PrefetchScalarGridSpec(
            num_scalar_prefetch=1,
            grid=(1,),
            in_specs=[whole(*taps.shape)] + [whole(tile, width)] * devices + [one] * (groups * terms),
            out_specs=[whole(3, tok, width)] * groups + [whole(tile + 32, width)] * devices,
            scratch_shapes=[
                pltpu.VMEM((total, width), jnp.bfloat16),
                pltpu.VMEM((devices, tile, width), jnp.bfloat16),
            ]
            + [pltpu.VMEM((total, width), jnp.bfloat16)] * 3
            + [pltpu.VMEM((total + PAD, width), jnp.float32)] * 2
            + [pltpu.VMEM((groups, 3, tok, width), jnp.bfloat16)],
        ),
        out_shape=[jax.ShapeDtypeStruct((3, tok, width), jnp.bfloat16)] * groups
        + [jax.ShapeDtypeStruct((tile + 32, width), jnp.bfloat16)] * devices,
        compiler_params=params(10, width),
        cost_estimate=SMALL,
        name="middle",
    )(place, taps, *ups, *[term for terms_of in parts for term in terms_of])
    return outs[:groups], outs[groups:]


def assemble_kernel(place, *refs):
    grad_refs, out_ref = refs[:-1], refs[-1]
    width = grad_refs[0].shape[2]
    for r, ref in enumerate(grad_refs):
        for s in range(3):
            at = pl.multiple_of((s * len(grad_refs) + (place[0] ^ r)) * width, width)
            out_ref[:, pl.ds(at, width)] = ref[s]


def assemble(place, grads):
    streams, tok, width = grads[0].shape
    out = jax.ShapeDtypeStruct((tok, streams * width * len(grads)), jnp.bfloat16)
    return pl.pallas_call(
        assemble_kernel,
        grid_spec=pltpu.PrefetchScalarGridSpec(
            num_scalar_prefetch=1,
            grid=(1,),
            in_specs=[resident(grads[0].shape, width)] * len(grads),
            out_specs=resident(out.shape, width),
        ),
        out_shape=out,
        compiler_params=params(4, width),
        cost_estimate=SMALL,
        name="assemble",
    )(place, *grads)


def input_grad_kernel(place, *refs, terms, width, first):
    grad_refs, w_ref, out_refs = refs[:terms], refs[terms], refs[terms + 1 :]
    step = out_refs[0].shape[1]
    if terms == 1:
        own = slice(first * step, (first + 1) * step) if len(out_refs) == 1 else slice(None)
        acc = jnp.dot(grad_refs[0][...], w_ref[:, :, own].reshape(-1, step), preferred_element_type=jnp.float32)
    else:
        acc = jnp.zeros(out_refs[0].shape, jnp.float32)
        for r, ref in enumerate(grad_refs):
            rows = pl.ds(pl.multiple_of((place[0] ^ r) * width, width), width)
            for s in range(3):
                acc = acc + jnp.dot(ref[s], w_ref[s, rows, :], preferred_element_type=jnp.float32)
    acc = acc.astype(jnp.bfloat16)
    for i, out_ref in enumerate(out_refs):

        @pl.when(pl.program_id(0) == i)
        def _():
            out_ref[...] = acc


def input_grad(place, grads, w, first, last, chunks):
    tok = grads[0].shape[-2]
    streams, channels, feat = w.shape
    step = feat // chunks
    width = channels if len(grads) == 1 else grads[0].shape[-1]
    return pl.pallas_call(
        functools.partial(input_grad_kernel, terms=len(grads), width=width, first=first),
        grid_spec=pltpu.PrefetchScalarGridSpec(
            num_scalar_prefetch=1,
            grid=(last - first,),
            in_specs=[resident(g.shape, width) for g in grads]
            + [
                resident(w.shape, width)
                if len(grads) == 1 and last - first == 1
                else pl.BlockSpec((streams, channels, step), lambda i, _: (0, 0, first + i))
            ],
            out_specs=[resident((tok, step), width)] * (last - first),
        ),
        out_shape=[jax.ShapeDtypeStruct((tok, step), jnp.bfloat16)] * (last - first),
        compiler_params=params(12, width),
        cost_estimate=SMALL,
        name="input_grad",
    )(place, *grads, w)


def weight_grad_kernel(place, *refs, chained, groups, wide, r):
    refs = refs[2 * chained :]
    grad_refs = refs[: 2 * groups]
    x_refs = refs[2 * groups : 3 * groups]
    out_ref, mark_ref = refs[3 * groups : 3 * groups + 2]
    mark_ref[...] = jnp.zeros(mark_ref.shape, jnp.float32)
    tok, step = x_refs[0].shape[0], out_ref.shape[2]
    width = grad_refs[0].shape[2]
    if wide:
        turned = refs[3 * groups + 2]

        @pl.when(pl.program_id(0) == 0)
        def _():
            for side in range(2):
                for s in range(3):
                    at = pl.multiple_of(((place[0] ^ r ^ side) % 2 + 2 * s) * width, width)
                    for k in range(groups):
                        turned[pl.ds(at, width), k * tok : (k + 1) * tok] = grad_refs[side * groups + k][s].T

        acc = None
        columns = pl.ds(pl.multiple_of(pl.program_id(0) * step, step), step)
        for k in range(groups):
            term = jnp.dot(
                turned[:, k * tok : (k + 1) * tok], x_refs[k][:, columns], preferred_element_type=jnp.float32
            )
            acc = term if acc is None else acc + term
        for s in range(3):
            out_ref[s] = acc[2 * s * width : 2 * (s + 1) * width, :]
    else:
        tn = (((0,), (0,)), ((), ()))
        for side in range(2):
            at = pl.multiple_of((place[0] ^ r ^ side) % 2 * width, width)
            for s in range(3):
                acc = None
                for k in range(groups):
                    term = lax.dot_general(
                        grad_refs[side * groups + k][s], x_refs[k][...], tn, preferred_element_type=jnp.float32
                    )
                    acc = term if acc is None else acc + term
                out_ref[s, pl.ds(at, width), :] = acc


def weight_grad(place, filled, grads, xs, r, count):
    groups = len(xs)
    streams, tok, width = grads[0].shape
    feat = xs[0].shape[1]
    channels = width * count
    step = min(512, feat)
    wide = width % LANES == 0
    chained = filled is not None
    return pl.pallas_call(
        functools.partial(weight_grad_kernel, chained=chained, groups=groups, wide=wide, r=r),
        grid_spec=pltpu.PrefetchScalarGridSpec(
            num_scalar_prefetch=1,
            grid=(feat // step,),
            in_specs=[pl.BlockSpec(memory_space=pl.ANY)] * (2 * chained)
            + [resident((streams, tok, width), width)] * (2 * groups)
            + [resident((tok, feat), width) if wide else pl.BlockSpec((tok, step), lambda i, _: (0, i))] * groups,
            out_specs=[
                pl.BlockSpec((streams, 2 * width, step), lambda i, at: (0, (at[0] ^ r) // 2, i)),
                resident((8, LANES), width),
            ],
            scratch_shapes=[pltpu.VMEM((2 * streams * width, groups * tok), jnp.bfloat16)] if wide else [],
        ),
        out_shape=[
            jax.ShapeDtypeStruct((streams, channels, feat), jnp.float32),
            jax.ShapeDtypeStruct((8, LANES), jnp.float32),
        ],
        input_output_aliases={1: 0} if chained else {},
        compiler_params=params(14, width),
        cost_estimate=SMALL,
        name="weight_grad",
    )(place, *(filled if chained else []), *grads, *xs)


def added(first, second):
    return (first.astype(jnp.float32) + second.astype(jnp.float32)).astype(jnp.bfloat16)


def first_pieces(tokens, k):
    tok = tokens.shape[0]
    if tok % 48 or lax.axis_size("row") % 2:
        return [swap(tokens, "col", k)]
    third = tok // 3
    parity = lax.axis_index("row") % 2
    return [swap(lax.dynamic_slice_in_dim(tokens, parity * third, third, axis=0), "col", k)]


def other_pieces(tokens, first, k):
    third = first[0].shape[0]
    if third == tokens.shape[0]:
        return first
    rest = after(tokens, lax.axis_index("row"))[2 * third :]
    return first + [swap(first[0], "row", 1), swap(after(rest, *first), "col", k)]


def on_device(tokens, weight, taps, upstream):
    n_col = lax.axis_size("col")
    n_depth = lax.axis_size("depth")
    both = ("col", "depth")
    local_tok = upstream.shape[0]
    depth_at = lax.axis_index("depth")
    col_at = lax.axis_index("col")
    row_at = lax.axis_index("row")
    place = jnp.stack([depth_at, col_at, row_at, col_at * n_depth + depth_at]).astype(jnp.int32)
    w = jnp.transpose(weight, (1, 0, 2))
    width = w.shape[1] // n_depth
    def project_and_sum(x_pieces, *earlier):
        keep, send, x = project(place, x_pieces, w, n_depth)
        near = swap(after(send, *earlier) if earlier else send, "depth", 1)
        pairs = [added(keep[r // 2], near[r // 2])[None] for r in range(2, n_depth, 2)]
        fars = [swap(pair, "depth", 2 * i + 2) for i, pair in enumerate(pairs)]
        return x, [keep, near] + fars, pairs, fars

    first = [first_pieces(tokens, k) for k in range(1, n_col)]
    x, terms, pairs, fars = project_and_sum([tokens], *[piece for of in first for piece in of])
    xs, parts = [x], [terms]
    for k in range(1, n_col):
        x_pieces = other_pieces(tokens, first[k - 1], k)
        x_pieces[-1] = after(x_pieces[-1], *fars)
        x, terms, pairs, fars = project_and_sum(x_pieces)
        xs.append(x)
        parts.append(terms)
    ups = split(place, after(upstream, *pairs), n_col * n_depth)
    ups = [up if r == 0 else swap(up, both, r) for r, up in enumerate(ups)]
    own_grads, blocks = middle(place, taps, ups, parts)
    near_blocks = [r for r in range(1, len(blocks)) if r % n_depth < 2]
    blocks = [swap(block, both, r) if r in near_blocks else block for r, block in enumerate(blocks)]
    nears = [swap(own, "depth", 1) for own in own_grads]
    beside = nears + [blocks[r] for r in near_blocks]
    chunks = 4
    grads = [None] * n_col
    ready = []
    sent = []
    for k in reversed(range(n_col)):
        fars = [swap(after(own_grads[k], *ready) if ready else own_grads[k], "depth", r) for r in range(2, n_depth, 2)]
        ready = fars
        if k > 0:
            fars = [after(far, *beside) for far in fars]
        elif sent:
            fars = [after(far, sent[-1][1][-1]) for far in fars]
        grads[k] = [own_grads[k], nears[k]]
        for far in fars:
            grads[k] += [far, swap(far, "depth", 1)]
        ready = grads[k][2:]
        lhs = [assemble(place, grads[k])] if width % LANES == 0 else grads[k]
        if k > 0:
            head = input_grad(place, lhs, w, 0, 1, chunks)
            behind = [after(lhs[0], *head)] + lhs[1:]
            tail = input_grad(place, behind, w, 1, chunks, chunks)
            parts_of = list(head) + list(tail)
            sent.append(([swap(part, "col", k) for part in parts_of], parts_of))
    sent = [of for of, _ in sent]
    own_part = list(input_grad(place, lhs, w, 0, 1, chunks))
    outer = (row_at == 0) | (row_at == 3)
    inward, across, summed, done = ([None] * chunks for _ in range(4))
    pair = cross = filled = None
    marks = []
    line = lax.axis_size("row") == 4
    for slot in range(chunks + 3):
        if slot < chunks:
            total = after(own_part[slot], *marks).astype(jnp.float32)
            for of in sent:
                total = total + of[slot].astype(jnp.float32)
            inward[slot] = total.astype(jnp.bfloat16)
            marks = [inward[slot]]
        if not line:
            if slot < chunks:
                done[slot] = lax.psum(inward[slot], "row")
        else:
            if 0 <= slot - 1 < chunks:
                across[slot - 1] = added(after(inward[slot - 1], *marks), pair)
                marks = [across[slot - 1]]
            if 0 <= slot - 2 < chunks:
                summed[slot - 2] = added(after(across[slot - 2], *marks), cross)
                marks = [summed[slot - 2]]
            if 0 <= slot - 3 < chunks:
                done[slot - 3] = jnp.where(outer, pair, summed[slot - 3])
            if slot < chunks + 2:
                out = summed[slot - 2] if slot >= 2 else inward[slot]
                pair = swap(jnp.where(outer, inward[slot], out) if slot < chunks else out, "row", 1)
            if 0 <= slot - 1 < chunks:
                cross = lax.ppermute(across[slot - 1], "row", [(0, 0), (1, 2), (2, 1), (3, 3)])
        if slot == 0:
            behind = [after(lhs[0], *marks)] + lhs[1:]
            own_part += input_grad(place, behind, w, 1, chunks, chunks)
            marks = [own_part[1]]
        if 0 < slot <= n_depth // 2:
            r = n_depth - 2 * slot
            of = [group[i] for i in (r, r + 1) for group in grads]
            filled = weight_grad(place, filled, [after(of[0], *marks)] + of[1:], xs, r, n_depth)
            marks = [filled[1]]
        if slot == chunks + 1:
            blocks = [
                block if r == 0 or r in near_blocks else swap(after(block, *marks), both, r)
                for r, block in enumerate(blocks)
            ]
    grad_tokens = jnp.concatenate(done, axis=1)
    grad_weight = jnp.transpose(filled[0], (1, 0, 2))
    output, grad_taps = join(place, filled[1], blocks, local_tok, taps.shape[1])
    return (output, grad_tokens, grad_weight, grad_taps)


def solution(mesh):
    in_specs = (
        P("col", "depth"),
        P(("row", "col"), None, "depth"),
        P(None, "row"),
        P(("col", "depth"), "row"),
    )
    out_specs = (
        P(("col", "depth"), "row"),
        P("col", "depth"),
        P(("row", "col"), None, "depth"),
        P(None, "row"),
    )
    return jax.shard_map(
        on_device, mesh=mesh, in_specs=in_specs, out_specs=out_specs, check_vma=False
    )
```

```python
import functools

import jax
import jax.numpy as jnp
from jax import lax
from jax.experimental import pallas as pl
from jax.experimental.pallas import tpu as pltpu
from jax.sharding import PartitionSpec as P

GROUP = 16
KT = 7
PAD = 8
LANES = 128
MIB = 1024 * 1024
SMALL = pl.CostEstimate(flops=1, bytes_accessed=1, transcendentals=0)


def swap(value, axis, flip):
    count = lax.axis_size(axis)
    return lax.ppermute(value, axis, [(i, i ^ flip) for i in range(count)])


def after(value, *earlier):
    return lax.optimization_barrier((value, *earlier))[0]


def resident(shape, width):
    if width % LANES == 0:
        return pl.BlockSpec(memory_space=pltpu.VMEM)
    return pl.BlockSpec(tuple(shape), lambda *_: (0,) * len(shape), pipeline_mode=pl.Buffered(1))


def params(mib, width):
    return pltpu.CompilerParams(vmem_limit_bytes=(mib if width % LANES == 0 else 56) * MIB)


def project_kernel(place, *refs, pieces, count, width):
    x_refs = refs[:pieces]
    w_ref, keep_ref, send_ref = refs[pieces : pieces + 3]
    stream = pl.program_id(0)
    core = place[0] % 2
    if pieces == 1:
        x = x_refs[0][...]
    else:
        x_out = refs[pieces + 3]
        third = x_refs[0].shape[0]
        parity = place[2] % 2

        @pl.when(stream == 0)
        def _():
            x_out[pl.ds(pl.multiple_of(parity * third, third), third), :] = x_refs[0][...]
            x_out[pl.ds(pl.multiple_of((1 - parity) * third, third), third), :] = x_refs[1][...]
            x_out[2 * third :, :] = x_refs[2][...]

        x = x_out[...]
    nt = (((1,), (1,)), ((), ()))
    if width % LANES == 0:
        whole = lax.dot_general(x, w_ref[stream], nt, preferred_element_type=jnp.float32).astype(jnp.bfloat16)
        blocks = [whole[:, j * width : (j + 1) * width] for j in range(count)]
    else:
        blocks = [
            lax.dot_general(
                x, w_ref[0, j * width : (j + 1) * width, :], nt, preferred_element_type=jnp.float32
            ).astype(jnp.bfloat16)
            for j in range(count)
        ]
    for mine in range(2):

        @pl.when(core == mine)
        def _():
            for j in range(count):
                at = (j ^ place[0]) // 2
                if j % 2 == mine:
                    keep_ref[at, stream] = blocks[j]
                else:
                    send_ref[at, stream] = blocks[j]


def project(place, xs, w, count):
    tok, feat = sum(x.shape[0] for x in xs), xs[0].shape[1]
    streams, channels, _ = w.shape
    width = channels // count
    part = jax.ShapeDtypeStruct((count // 2, streams, tok, width), jnp.bfloat16)
    wide = width % LANES == 0
    spec = resident(part.shape, width)
    joined = len(xs) > 1
    outs = pl.pallas_call(
        functools.partial(project_kernel, pieces=len(xs), count=count, width=width),
        grid_spec=pltpu.PrefetchScalarGridSpec(
            num_scalar_prefetch=1,
            grid=(streams,),
            in_specs=[resident(x.shape, width) for x in xs]
            + [resident(w.shape, width) if wide else pl.BlockSpec((1, channels, feat), lambda s, _: (s, 0, 0))],
            out_specs=[spec, spec] + [resident((tok, feat), width)] * joined,
        ),
        out_shape=[part, part] + [jax.ShapeDtypeStruct((tok, feat), jnp.bfloat16)] * joined,
        compiler_params=params(10, width),
        cost_estimate=SMALL,
        name="project",
    )(place, *xs, w)
    return outs[0], outs[1], outs[2] if joined else xs[0]


def in_three(value):
    terms = []
    for _ in range(3):
        term = value.astype(jnp.bfloat16)
        value = value - term.astype(jnp.float32)
        terms.append(term)
    return terms


def split_kernel(place, up_ref, *out_refs, n_depth):
    width = out_refs[0].shape[1]
    for k, ref in enumerate(out_refs):
        at = ((place[1] ^ k) * n_depth + place[0]) * width
        ref[...] = up_ref[:, pl.ds(pl.multiple_of(at, width), width)]


def split(place, up, n_col, n_depth):
    tok, width = up.shape[0], up.shape[1] // (n_col * n_depth)
    if width % LANES:
        blocks = up.reshape(tok, n_col * n_depth, width)
        at = [(place[1] ^ k) * n_depth + place[0] for k in range(n_col)]
        return [lax.dynamic_index_in_dim(blocks, i, 1, keepdims=False) for i in at]
    return pl.pallas_call(
        functools.partial(split_kernel, n_depth=n_depth),
        grid_spec=pltpu.PrefetchScalarGridSpec(
            num_scalar_prefetch=1,
            grid=(1,),
            in_specs=[resident(up.shape, width)],
            out_specs=[resident((tok, width), width)] * n_col,
        ),
        out_shape=[jax.ShapeDtypeStruct((tok, width), jnp.bfloat16)] * n_col,
        compiler_params=params(4, width),
        cost_estimate=SMALL,
        name="split",
    )(place, up)


def join_kernel(place, _, blocks_ref, out_ref, grad_taps_ref):
    n_depth, n_col, rows, width = blocks_ref.shape
    local, groups = out_ref.shape[0], grad_taps_ref.shape[1]
    lane_group = lax.broadcasted_iota(jnp.int32, (width, groups), 0) // GROUP
    group = lax.broadcasted_iota(jnp.int32, (width, groups), 1)
    total = jnp.zeros((24, groups), jnp.float32)
    mine = pl.ds(pl.multiple_of(place[0] * local, 16), local)
    for p in range(n_depth):
        for k in range(n_col):
            at = (place[1] ^ k) * n_depth + p
            out_ref[:, pl.ds(pl.multiple_of(at * width, width), width)] = blocks_ref[p, k, mine, :]
            spread = (lane_group + at * (width // GROUP) == group).astype(jnp.bfloat16)
            sums = blocks_ref[p, k, rows - 32 : rows - 8, :]
            total = total + jnp.dot(sums, spread, preferred_element_type=jnp.float32)
    grad_taps_ref[...] = (total[0:8] + total[8:16] + total[16:24])[:KT]


def join(place, mark, blocks, local, groups):
    n_depth, n_col, rows, width = blocks.shape
    if width % LANES:
        blocks = blocks[:, place[1] ^ jnp.arange(n_col)]
        mine = lax.dynamic_slice_in_dim(blocks, place[0] * local, local, axis=2)
        sums = blocks[:, :, rows - 32 : rows - 8].astype(jnp.float32)
        sums = sums.reshape(n_depth, n_col, 3, 8, width // GROUP, GROUP).sum(axis=(2, 5))[:, :, :KT]
        return (
            jnp.transpose(mine, (2, 1, 0, 3)).reshape(local, -1),
            jnp.transpose(sums, (2, 1, 0, 3)).reshape(KT, -1),
        )
    channels = n_depth * n_col * width
    return pl.pallas_call(
        join_kernel,
        grid_spec=pltpu.PrefetchScalarGridSpec(
            num_scalar_prefetch=1,
            grid=(1,),
            in_specs=[pl.BlockSpec(memory_space=pl.ANY), resident(blocks.shape, width)],
            out_specs=[resident((local, channels), width), resident((KT, groups), width)],
        ),
        out_shape=[
            jax.ShapeDtypeStruct((local, channels), jnp.bfloat16),
            jax.ShapeDtypeStruct((KT, groups), jnp.float32),
        ],
        compiler_params=params(4, width),
        cost_estimate=SMALL,
        name="join",
    )(place, mark, blocks)


def middle_kernel(place, taps_ref, *refs, groups, terms, tile):
    up_refs, refs = refs[:groups], refs[groups:]
    part_refs = refs[: groups * terms]
    grad_refs = refs[groups * terms : groups * terms + groups]
    out_refs = refs[groups * terms + groups : groups * terms + 2 * groups]
    up_s, out_s, q_s, k_s, v_s, mixed_s, gf_s, far_s = refs[groups * terms + 2 * groups :]
    col = place[1]
    tok = part_refs[0].shape[2]
    width = part_refs[0].shape[3]
    total = groups * tok
    tap_groups = taps_ref.shape[1]
    for k, ref in enumerate(up_refs):
        up_s[pl.ds(pl.multiple_of((col ^ k) * tok, tok), tok), :] = ref[...]
    lane_group = lax.broadcasted_iota(jnp.int32, (tap_groups, width), 1) // GROUP
    group = lax.broadcasted_iota(jnp.int32, (tap_groups, width), 0)
    spread = (lane_group + place[3] * (width // GROUP) == group).astype(jnp.bfloat16)
    taps = sum(jnp.dot(term, spread, preferred_element_type=jnp.float32) for term in in_three(taps_ref[...]))
    mixed_s[0:PAD, :] = jnp.zeros((PAD, width), jnp.float32)
    gf_s[total : total + PAD, :] = jnp.zeros((PAD, width), jnp.float32)
    for k in range(groups):
        start = (col ^ k) * tok
        for i in range(tok // tile):
            inside = slice(i * tile, (i + 1) * tile)
            rows = pl.ds(pl.multiple_of(start + i * tile, tile), tile)
            streams = []
            for s in range(3):
                acc = None
                for ref in part_refs[k * terms : (k + 1) * terms]:
                    term = ref[0, s, inside, :].astype(jnp.float32)
                    acc = term if acc is None else acc + term
                streams.append(acc.astype(jnp.bfloat16))
            q_s[rows, :], k_s[rows, :], v_s[rows, :] = streams
            query, key, value = [stream.astype(jnp.float32) for stream in streams]
            mixed_s[pl.ds(pl.multiple_of(start + i * tile + PAD, PAD), tile), :] = key * value
            gf_s[rows, :] = up_s[rows, :].astype(jnp.float32) * query
    sums = [jnp.zeros((8, width), jnp.float32) for _ in range(KT)]
    for a in range(groups):
        for i in range(tok // tile):
            first = a * tok + i * tile
            rows = slice(first, first + tile)
            inside = slice(i * tile, (i + 1) * tile)
            gf = gf_s[rows, :]
            filtered = jnp.zeros((tile, width), jnp.float32)
            grad_mixed = jnp.zeros((tile, width), jnp.float32)
            for j in range(KT):
                shifted = mixed_s[first + PAD - j : first + PAD - j + tile, :]
                filtered = filtered + taps[j : j + 1, :] * shifted
                sums[j] = sums[j] + (gf * shifted).reshape(tile // 8, 8, width).sum(axis=0)
                grad_mixed = grad_mixed + taps[j : j + 1, :] * gf_s[first + j : first + j + tile, :]
            out_s[a, inside, :] = (q_s[rows, :].astype(jnp.float32) * filtered).astype(jnp.bfloat16)
            at = col ^ a
            far_s[at, 0, inside, :] = (up_s[rows, :].astype(jnp.float32) * filtered).astype(jnp.bfloat16)
            far_s[at, 1, inside, :] = (grad_mixed * v_s[rows, :].astype(jnp.float32)).astype(jnp.bfloat16)
            far_s[at, 2, inside, :] = (grad_mixed * k_s[rows, :].astype(jnp.float32)).astype(jnp.bfloat16)
    for k in range(groups):
        grad_refs[k][...] = far_s[k]
    rest = jnp.concatenate(
        [sums[j].sum(axis=0, keepdims=True) for j in range(KT)] + [jnp.zeros((1, width), jnp.float32)], axis=0
    )
    terms_of = [term.astype(jnp.float32) for term in in_three(rest)]
    packed = jnp.concatenate(terms_of + [jnp.zeros((8, width), jnp.float32)], axis=0).astype(jnp.bfloat16)
    for k, ref in enumerate(out_refs):
        ref[0:tok, :] = out_s[col ^ k]
        ref[tok : tok + 32, :] = packed


def middle(place, taps, ups, parts, tile):
    groups, terms = len(parts), len(parts[0])
    _, _, tok, width = parts[0][0].shape
    total = groups * tok
    whole = lambda *shape: resident(shape, width)
    one = whole(1, 3, tok, width)
    outs = pl.pallas_call(
        functools.partial(middle_kernel, groups=groups, terms=terms, tile=tile),
        grid_spec=pltpu.PrefetchScalarGridSpec(
            num_scalar_prefetch=1,
            grid=(1,),
            in_specs=[whole(*taps.shape)] + [whole(tok, width)] * groups + [one] * (groups * terms),
            out_specs=[whole(3, tok, width)] * groups + [whole(tok + 32, width)] * groups,
            scratch_shapes=[
                pltpu.VMEM((total, width), jnp.bfloat16),
                pltpu.VMEM((groups, tok, width), jnp.bfloat16),
            ]
            + [pltpu.VMEM((total, width), jnp.bfloat16)] * 3
            + [pltpu.VMEM((total + PAD, width), jnp.float32)] * 2
            + [pltpu.VMEM((groups, 3, tok, width), jnp.bfloat16)],
        ),
        out_shape=[jax.ShapeDtypeStruct((3, tok, width), jnp.bfloat16)] * groups
        + [jax.ShapeDtypeStruct((tok + 32, width), jnp.bfloat16)] * groups,
        compiler_params=params(10, width),
        cost_estimate=SMALL,
        name="middle",
    )(place, taps, *ups, *[term for terms_of in parts for term in terms_of])
    return outs[:groups], outs[groups:]


def assemble_kernel(place, *refs):
    grad_refs, out_ref = refs[:-1], refs[-1]
    width = grad_refs[0].shape[2]
    for r, ref in enumerate(grad_refs):
        for s in range(3):
            at = pl.multiple_of((s * len(grad_refs) + (place[0] ^ r)) * width, width)
            out_ref[:, pl.ds(at, width)] = ref[s]


def assemble(place, grads):
    streams, tok, width = grads[0].shape
    out = jax.ShapeDtypeStruct((tok, streams * width * len(grads)), jnp.bfloat16)
    return pl.pallas_call(
        assemble_kernel,
        grid_spec=pltpu.PrefetchScalarGridSpec(
            num_scalar_prefetch=1,
            grid=(1,),
            in_specs=[resident(grads[0].shape, width)] * len(grads),
            out_specs=resident(out.shape, width),
        ),
        out_shape=out,
        compiler_params=params(4, width),
        cost_estimate=SMALL,
        name="assemble",
    )(place, *grads)


def input_grad_kernel(place, *refs, terms, width, first):
    grad_refs, w_ref, out_refs = refs[:terms], refs[terms], refs[terms + 1 :]
    step = out_refs[0].shape[1]
    if terms == 1:
        own = slice(first * step, (first + 1) * step) if len(out_refs) == 1 else slice(None)
        acc = jnp.dot(grad_refs[0][...], w_ref[:, :, own].reshape(-1, step), preferred_element_type=jnp.float32)
    else:
        acc = jnp.zeros(out_refs[0].shape, jnp.float32)
        for r, ref in enumerate(grad_refs):
            rows = pl.ds(pl.multiple_of((place[0] ^ r) * width, width), width)
            for s in range(3):
                acc = acc + jnp.dot(ref[s], w_ref[s, rows, :], preferred_element_type=jnp.float32)
    acc = acc.astype(jnp.bfloat16)
    for i, out_ref in enumerate(out_refs):

        @pl.when(pl.program_id(0) == i)
        def _():
            out_ref[...] = acc


def input_grad(place, grads, w, first, last, chunks):
    tok = grads[0].shape[-2]
    streams, channels, feat = w.shape
    step = feat // chunks
    width = channels if len(grads) == 1 else grads[0].shape[-1]
    return pl.pallas_call(
        functools.partial(input_grad_kernel, terms=len(grads), width=width, first=first),
        grid_spec=pltpu.PrefetchScalarGridSpec(
            num_scalar_prefetch=1,
            grid=(last - first,),
            in_specs=[resident(g.shape, width) for g in grads]
            + [
                resident(w.shape, width)
                if len(grads) == 1 and last - first == 1
                else pl.BlockSpec((streams, channels, step), lambda i, _: (0, 0, first + i))
            ],
            out_specs=[resident((tok, step), width)] * (last - first),
        ),
        out_shape=[jax.ShapeDtypeStruct((tok, step), jnp.bfloat16)] * (last - first),
        compiler_params=params(12, width),
        cost_estimate=SMALL,
        name="input_grad",
    )(place, *grads, w)


def weight_grad_kernel(place, *refs, chained, groups, wide, r):
    refs = refs[2 * chained :]
    grad_refs = refs[: 2 * groups]
    x_refs = refs[2 * groups : 3 * groups]
    out_ref, mark_ref = refs[3 * groups : 3 * groups + 2]
    mark_ref[...] = jnp.zeros(mark_ref.shape, jnp.float32)
    tok, step = x_refs[0].shape[0], out_ref.shape[2]
    width = grad_refs[0].shape[2]
    if wide:
        turned = refs[3 * groups + 2]

        @pl.when(pl.program_id(0) == 0)
        def _():
            for side in range(2):
                for s in range(3):
                    at = pl.multiple_of(((place[0] ^ r ^ side) % 2 + 2 * s) * width, width)
                    for k in range(groups):
                        turned[pl.ds(at, width), k * tok : (k + 1) * tok] = grad_refs[side * groups + k][s].T

        acc = None
        columns = pl.ds(pl.multiple_of(pl.program_id(0) * step, step), step)
        for k in range(groups):
            term = jnp.dot(
                turned[:, k * tok : (k + 1) * tok], x_refs[k][:, columns], preferred_element_type=jnp.float32
            )
            acc = term if acc is None else acc + term
        for s in range(3):
            out_ref[s] = acc[2 * s * width : 2 * (s + 1) * width, :]
    else:
        tn = (((0,), (0,)), ((), ()))
        for side in range(2):
            at = pl.multiple_of((place[0] ^ r ^ side) % 2 * width, width)
            for s in range(3):
                acc = None
                for k in range(groups):
                    term = lax.dot_general(
                        grad_refs[side * groups + k][s], x_refs[k][...], tn, preferred_element_type=jnp.float32
                    )
                    acc = term if acc is None else acc + term
                out_ref[s, pl.ds(at, width), :] = acc


def weight_grad(place, filled, grads, xs, r, count):
    groups = len(xs)
    streams, tok, width = grads[0].shape
    feat = xs[0].shape[1]
    channels = width * count
    step = min(512, feat)
    wide = width % LANES == 0
    chained = filled is not None
    return pl.pallas_call(
        functools.partial(weight_grad_kernel, chained=chained, groups=groups, wide=wide, r=r),
        grid_spec=pltpu.PrefetchScalarGridSpec(
            num_scalar_prefetch=1,
            grid=(feat // step,),
            in_specs=[pl.BlockSpec(memory_space=pl.ANY)] * (2 * chained)
            + [resident((streams, tok, width), width)] * (2 * groups)
            + [resident((tok, feat), width) if wide else pl.BlockSpec((tok, step), lambda i, _: (0, i))] * groups,
            out_specs=[
                pl.BlockSpec((streams, 2 * width, step), lambda i, at: (0, (at[0] ^ r) // 2, i)),
                resident((8, LANES), width),
            ],
            scratch_shapes=[pltpu.VMEM((2 * streams * width, groups * tok), jnp.bfloat16)] if wide else [],
        ),
        out_shape=[
            jax.ShapeDtypeStruct((streams, channels, feat), jnp.float32),
            jax.ShapeDtypeStruct((8, LANES), jnp.float32),
        ],
        input_output_aliases={1: 0} if chained else {},
        compiler_params=params(14, width),
        cost_estimate=SMALL,
        name="weight_grad",
    )(place, *(filled if chained else []), *grads, *xs)


def added(first, second):
    return (first.astype(jnp.float32) + second.astype(jnp.float32)).astype(jnp.bfloat16)


def first_pieces(tokens, k):
    tok = tokens.shape[0]
    if tok % 48 or lax.axis_size("row") % 2:
        return [swap(tokens, "col", k)]
    third = tok // 3
    parity = lax.axis_index("row") % 2
    return [swap(lax.dynamic_slice_in_dim(tokens, parity * third, third, axis=0), "col", k)]


def other_pieces(tokens, first, k):
    third = first[0].shape[0]
    if third == tokens.shape[0]:
        return first
    rest = after(tokens, lax.axis_index("row"))[2 * third :]
    return first + [swap(first[0], "row", 1), swap(after(rest, *first), "col", k)]


def on_device(tokens, weight, taps, upstream):
    n_col = lax.axis_size("col")
    n_depth = lax.axis_size("depth")
    local_tok = upstream.shape[0]
    depth_at = lax.axis_index("depth")
    col_at = lax.axis_index("col")
    row_at = lax.axis_index("row")
    place = jnp.stack([depth_at, col_at, row_at, col_at * n_depth + depth_at]).astype(jnp.int32)
    w = jnp.transpose(weight, (1, 0, 2))
    width = w.shape[1] // n_depth
    def project_and_sum(x_pieces, *earlier):
        keep, send, x = project(place, x_pieces, w, n_depth)
        near = swap(after(send, *earlier) if earlier else send, "depth", 1)
        pairs = [added(keep[r // 2], near[r // 2])[None] for r in range(2, n_depth, 2)]
        fars = [swap(pair, "depth", 2 * i + 2) for i, pair in enumerate(pairs)]
        return x, [keep, near] + fars, pairs, fars

    first = [first_pieces(tokens, k) for k in range(1, n_col)]
    x, terms, pairs, fars = project_and_sum([tokens], *[piece for of in first for piece in of])
    xs, parts = [x], [terms]
    group_up = lax.all_gather(upstream, "depth", axis=0, tiled=True)
    ups = split(place, after(group_up, *pairs), n_col, n_depth)
    for k in range(1, n_col):
        x_pieces = other_pieces(tokens, first[k - 1], k)
        x_pieces[-1] = after(x_pieces[-1], *fars, *ups)
        x, terms, pairs, fars = project_and_sum(x_pieces)
        xs.append(x)
        parts.append(terms)
    ups = [up if k == 0 else swap(up, "col", k) for k, up in enumerate(ups)]
    own_grads, blocks = middle(place, taps, ups, parts, local_tok)
    nears = [swap(own, "depth", 1) for own in own_grads]
    blocks = [block if k == 0 else swap(block, "col", k) for k, block in enumerate(blocks)]
    beside = nears + blocks[1:]
    chunks = 4
    grads = [None] * n_col
    ready = []
    sent = []
    for k in reversed(range(n_col)):
        fars = [swap(after(own_grads[k], *ready) if ready else own_grads[k], "depth", r) for r in range(2, n_depth, 2)]
        ready = fars
        if k > 0:
            fars = [after(far, *beside) for far in fars]
        elif sent:
            fars = [after(far, sent[-1][1][-1]) for far in fars]
        grads[k] = [own_grads[k], nears[k]]
        for far in fars:
            grads[k] += [far, swap(far, "depth", 1)]
        ready = grads[k][2:]
        lhs = [assemble(place, grads[k])] if width % LANES == 0 else grads[k]
        if k > 0:
            head = input_grad(place, lhs, w, 0, 1, chunks)
            behind = [after(lhs[0], *head)] + lhs[1:]
            tail = input_grad(place, behind, w, 1, chunks, chunks)
            parts_of = list(head) + list(tail)
            got = []
            for c, part in enumerate(parts_of):
                got.append(swap(part if c < 3 else after(part, got[c - 2]), "col", k))
            sent.append((got, parts_of))
    sent = [of for of, _ in sent]
    own_part = list(input_grad(place, lhs, w, 0, 1, chunks))
    outer = (row_at == 0) | (row_at == 3)
    blocks = lax.all_gather(after(jnp.stack(blocks), own_part[0]), "depth", axis=0)
    inward, across, summed, done = ([None] * chunks for _ in range(4))
    pair = cross = filled = None
    marks = []
    line = lax.axis_size("row") == 4
    for slot in range(chunks + 3):
        if slot < chunks:
            total = after(own_part[slot], *marks).astype(jnp.float32)
            for of in sent:
                total = total + of[slot].astype(jnp.float32)
            inward[slot] = total.astype(jnp.bfloat16)
            marks = [inward[slot]]
        if not line:
            if slot < chunks:
                done[slot] = lax.psum(inward[slot], "row")
        else:
            if 0 <= slot - 1 < chunks:
                across[slot - 1] = added(after(inward[slot - 1], *marks), pair)
                marks = [across[slot - 1]]
            if 0 <= slot - 2 < chunks:
                summed[slot - 2] = added(after(across[slot - 2], *marks), cross)
                marks = [summed[slot - 2]]
            if 0 <= slot - 3 < chunks:
                done[slot - 3] = jnp.where(outer, pair, summed[slot - 3])
            if slot < chunks + 2:
                out = summed[slot - 2] if slot >= 2 else inward[slot]
                pair = swap(jnp.where(outer, inward[slot], out) if slot < chunks else out, "row", 1)
            if 0 <= slot - 1 < chunks:
                cross = lax.ppermute(across[slot - 1], "row", [(0, 0), (1, 2), (2, 1), (3, 3)])
        if slot == 0:
            behind = [after(lhs[0], *marks)] + lhs[1:]
            own_part += input_grad(place, behind, w, 1, chunks, chunks)
            marks = [own_part[1]]
        if 0 < slot <= n_depth // 2:
            r = n_depth - 2 * slot
            of = [group[i] for i in (r, r + 1) for group in grads]
            filled = weight_grad(place, filled, [after(of[0], *marks)] + of[1:], xs, r, n_depth)
            marks = [filled[1]]
        if slot == chunks:
            marks.append(blocks)
    grad_tokens = jnp.concatenate(done, axis=1)
    grad_weight = jnp.transpose(filled[0], (1, 0, 2))
    output, grad_taps = join(place, filled[1], after(blocks, *marks), local_tok, taps.shape[1])
    return (output, grad_tokens, grad_weight, grad_taps)


def solution(mesh):
    in_specs = (
        P("col", "depth"),
        P(("row", "col"), None, "depth"),
        P(None, "row"),
        P(("col", "depth"), "row"),
    )
    out_specs = (
        P(("col", "depth"), "row"),
        P("col", "depth"),
        P(("row", "col"), None, "depth"),
        P(None, "row"),
    )
    return jax.shard_map(
        on_device, mesh=mesh, in_specs=in_specs, out_specs=out_specs, check_vma=False
    )
```

```python
import functools

import jax
import jax.numpy as jnp
from jax import lax
from jax.experimental import pallas as pl
from jax.experimental.pallas import tpu as pltpu
from jax.sharding import PartitionSpec as P

GROUP = 16
KT = 7
PAD = 8
LANES = 128
MIB = 1024 * 1024
SMALL = pl.CostEstimate(flops=1, bytes_accessed=1, transcendentals=0)


def swap(value, axis, flip):
    count = lax.axis_size(axis)
    return lax.ppermute(value, axis, [(i, i ^ flip) for i in range(count)])


def after(value, *earlier):
    return lax.optimization_barrier((value, *earlier))[0]


def resident(shape, width):
    if width % LANES == 0:
        return pl.BlockSpec(memory_space=pltpu.VMEM)
    return pl.BlockSpec(tuple(shape), lambda *_: (0,) * len(shape), pipeline_mode=pl.Buffered(1))


def params(mib, width):
    return pltpu.CompilerParams(vmem_limit_bytes=(mib if width % LANES == 0 else 56) * MIB)


def project_kernel(place, *refs, pieces, count, width):
    x_refs = refs[:pieces]
    w_ref, keep_ref, send_ref = refs[pieces : pieces + 3]
    stream = pl.program_id(0)
    core = place[0] % 2
    if pieces == 1:
        x = x_refs[0][...]
    else:
        x_out = refs[pieces + 3]
        third = x_refs[0].shape[0]
        parity = place[2] % 2

        @pl.when(stream == 0)
        def _():
            x_out[pl.ds(pl.multiple_of(parity * third, third), third), :] = x_refs[0][...]
            x_out[pl.ds(pl.multiple_of((1 - parity) * third, third), third), :] = x_refs[1][...]
            x_out[2 * third :, :] = x_refs[2][...]

        x = x_out[...]
    nt = (((1,), (1,)), ((), ()))
    if width % LANES == 0:
        whole = lax.dot_general(x, w_ref[stream], nt, preferred_element_type=jnp.float32).astype(jnp.bfloat16)
        blocks = [whole[:, j * width : (j + 1) * width] for j in range(count)]
    else:
        blocks = [
            lax.dot_general(
                x, w_ref[0, j * width : (j + 1) * width, :], nt, preferred_element_type=jnp.float32
            ).astype(jnp.bfloat16)
            for j in range(count)
        ]
    for mine in range(2):

        @pl.when(core == mine)
        def _():
            for j in range(count):
                at = (j ^ place[0]) // 2
                if j % 2 == mine:
                    keep_ref[at, stream] = blocks[j]
                else:
                    send_ref[at, stream] = blocks[j]


def project(place, xs, w, count):
    tok, feat = sum(x.shape[0] for x in xs), xs[0].shape[1]
    streams, channels, _ = w.shape
    width = channels // count
    part = jax.ShapeDtypeStruct((count // 2, streams, tok, width), jnp.bfloat16)
    wide = width % LANES == 0
    spec = resident(part.shape, width)
    joined = len(xs) > 1
    outs = pl.pallas_call(
        functools.partial(project_kernel, pieces=len(xs), count=count, width=width),
        grid_spec=pltpu.PrefetchScalarGridSpec(
            num_scalar_prefetch=1,
            grid=(streams,),
            in_specs=[resident(x.shape, width) for x in xs]
            + [resident(w.shape, width) if wide else pl.BlockSpec((1, channels, feat), lambda s, _: (s, 0, 0))],
            out_specs=[spec, spec] + [resident((tok, feat), width)] * joined,
        ),
        out_shape=[part, part] + [jax.ShapeDtypeStruct((tok, feat), jnp.bfloat16)] * joined,
        compiler_params=params(10, width),
        cost_estimate=SMALL,
        name="project",
    )(place, *xs, w)
    return outs[0], outs[1], outs[2] if joined else xs[0]


def in_three(value):
    terms = []
    for _ in range(3):
        term = value.astype(jnp.bfloat16)
        value = value - term.astype(jnp.float32)
        terms.append(term)
    return terms


def split_lanes_kernel(place, *refs, n_col):
    in_refs, out_refs = refs[:n_col], refs[n_col:]
    width = out_refs[0].shape[2]
    for r, ref in enumerate(out_refs):
        lanes = pl.ds(pl.multiple_of((place[0] ^ r) * width, width), width)
        for k in range(n_col):
            ref[k] = in_refs[k][:, lanes]


def split_rows_kernel(place, *refs, n_col):
    in_refs, out_refs = refs[:n_col], refs[n_col:]
    local = out_refs[0].shape[1] - 32
    for r, ref in enumerate(out_refs):
        rows = pl.ds(pl.multiple_of((place[0] ^ r) * local, 16), local)
        for k in range(n_col):
            ref[k, 0:local] = in_refs[k][rows, :]
            ref[k, local:] = in_refs[k][-32:, :]


def split(kernel, place, arrays, n_depth, shape):
    whole = (len(arrays),) + shape
    return pl.pallas_call(
        functools.partial(kernel, n_col=len(arrays)),
        grid_spec=pltpu.PrefetchScalarGridSpec(
            num_scalar_prefetch=1,
            grid=(1,),
            in_specs=[resident(value.shape, shape[1]) for value in arrays],
            out_specs=[resident(whole, shape[1])] * n_depth,
        ),
        out_shape=[jax.ShapeDtypeStruct(whole, jnp.bfloat16)] * n_depth,
        compiler_params=params(4, shape[1]),
        cost_estimate=SMALL,
        name="split",
    )(place, *arrays)


def split_lanes(place, arrays, n_depth):
    local, width = arrays[0].shape[0], arrays[0].shape[1] // n_depth
    if width % LANES:
        whole = jnp.stack(arrays)
        return [lax.dynamic_slice_in_dim(whole, (place[0] ^ r) * width, width, axis=2) for r in range(n_depth)]
    return split(split_lanes_kernel, place, arrays, n_depth, (local, width))


def split_rows(place, arrays, n_depth):
    local, width = (arrays[0].shape[0] - 32) // n_depth, arrays[0].shape[1]
    if width % LANES:
        whole = jnp.stack(arrays)
        return [
            jnp.concatenate(
                [lax.dynamic_slice_in_dim(whole, (place[0] ^ r) * local, local, axis=1), whole[:, -32:]], axis=1
            )
            for r in range(n_depth)
        ]
    return split(split_rows_kernel, place, arrays, n_depth, (local + 32, width))


def join_kernel(place, _, *refs):
    block_refs, (out_ref, grad_taps_ref) = refs[:-2], refs[-2:]
    n_depth = len(block_refs)
    n_col, _, width = block_refs[0].shape
    local, groups = out_ref.shape[0], grad_taps_ref.shape[1]
    lane_group = lax.broadcasted_iota(jnp.int32, (width, groups), 0) // GROUP
    group = lax.broadcasted_iota(jnp.int32, (width, groups), 1)
    total = jnp.zeros((24, groups), jnp.float32)
    for r, ref in enumerate(block_refs):
        for k in range(n_col):
            at = (place[1] ^ k) * n_depth + (place[0] ^ r)
            out_ref[:, pl.ds(pl.multiple_of(at * width, width), width)] = ref[k, 0:local, :]
            spread = (lane_group + at * (width // GROUP) == group).astype(jnp.bfloat16)
            total = total + jnp.dot(ref[k, local : local + 24, :], spread, preferred_element_type=jnp.float32)
    grad_taps_ref[...] = (total[0:8] + total[8:16] + total[16:24])[:KT]


def join(place, mark, blocks, groups):
    n_depth = len(blocks)
    n_col, rows, width = blocks[0].shape
    local = rows - 32
    if width % LANES:
        whole = jnp.stack(blocks)[place[0] ^ jnp.arange(n_depth)][:, place[1] ^ jnp.arange(n_col)]
        sums = whole[:, :, local : local + 24].astype(jnp.float32)
        sums = sums.reshape(n_depth, n_col, 3, 8, width // GROUP, GROUP).sum(axis=(2, 5))[:, :, :KT]
        return (
            jnp.transpose(whole[:, :, :local], (2, 1, 0, 3)).reshape(local, -1),
            jnp.transpose(sums, (2, 1, 0, 3)).reshape(KT, -1),
        )
    channels = n_depth * n_col * width
    return pl.pallas_call(
        join_kernel,
        grid_spec=pltpu.PrefetchScalarGridSpec(
            num_scalar_prefetch=1,
            grid=(1,),
            in_specs=[pl.BlockSpec(memory_space=pl.ANY)] + [resident(blocks[0].shape, width)] * n_depth,
            out_specs=[resident((local, channels), width), resident((KT, groups), width)],
        ),
        out_shape=[
            jax.ShapeDtypeStruct((local, channels), jnp.bfloat16),
            jax.ShapeDtypeStruct((KT, groups), jnp.float32),
        ],
        compiler_params=params(4, width),
        cost_estimate=SMALL,
        name="join",
    )(place, mark, *blocks)


def middle_kernel(place, taps_ref, *refs, devices, groups, terms, tile):
    up_refs, refs = refs[:devices], refs[devices:]
    part_refs = refs[: groups * terms]
    grad_refs = refs[groups * terms : groups * terms + groups]
    out_refs = refs[groups * terms + groups : groups * terms + 2 * groups]
    up_s, out_s, q_s, k_s, v_s, mixed_s, gf_s, far_s = refs[groups * terms + 2 * groups :]
    col = place[1]
    tok = part_refs[0].shape[2]
    width = part_refs[0].shape[3]
    total = groups * tok
    tap_groups = taps_ref.shape[1]
    for r, ref in enumerate(up_refs):
        for k in range(groups):
            at = (col ^ k) * tok + (place[0] ^ r) * tile
            up_s[pl.ds(pl.multiple_of(at, tile), tile), :] = ref[k]
    lane_group = lax.broadcasted_iota(jnp.int32, (tap_groups, width), 1) // GROUP
    group = lax.broadcasted_iota(jnp.int32, (tap_groups, width), 0)
    spread = (lane_group + place[3] * (width // GROUP) == group).astype(jnp.bfloat16)
    taps = sum(jnp.dot(term, spread, preferred_element_type=jnp.float32) for term in in_three(taps_ref[...]))
    mixed_s[0:PAD, :] = jnp.zeros((PAD, width), jnp.float32)
    gf_s[total : total + PAD, :] = jnp.zeros((PAD, width), jnp.float32)
    for k in range(groups):
        start = (col ^ k) * tok
        for i in range(tok // tile):
            inside = slice(i * tile, (i + 1) * tile)
            rows = pl.ds(pl.multiple_of(start + i * tile, tile), tile)
            streams = []
            for s in range(3):
                acc = None
                for ref in part_refs[k * terms : (k + 1) * terms]:
                    term = ref[0, s, inside, :].astype(jnp.float32)
                    acc = term if acc is None else acc + term
                streams.append(acc.astype(jnp.bfloat16))
            q_s[rows, :], k_s[rows, :], v_s[rows, :] = streams
            query, key, value = [stream.astype(jnp.float32) for stream in streams]
            mixed_s[pl.ds(pl.multiple_of(start + i * tile + PAD, PAD), tile), :] = key * value
            gf_s[rows, :] = up_s[rows, :].astype(jnp.float32) * query
    sums = [jnp.zeros((8, width), jnp.float32) for _ in range(KT)]
    for a in range(groups):
        for i in range(tok // tile):
            first = a * tok + i * tile
            rows = slice(first, first + tile)
            inside = slice(i * tile, (i + 1) * tile)
            gf = gf_s[rows, :]
            filtered = jnp.zeros((tile, width), jnp.float32)
            grad_mixed = jnp.zeros((tile, width), jnp.float32)
            for j in range(KT):
                shifted = mixed_s[first + PAD - j : first + PAD - j + tile, :]
                filtered = filtered + taps[j : j + 1, :] * shifted
                sums[j] = sums[j] + (gf * shifted).reshape(tile // 8, 8, width).sum(axis=0)
                grad_mixed = grad_mixed + taps[j : j + 1, :] * gf_s[first + j : first + j + tile, :]
            out_s[a, inside, :] = (q_s[rows, :].astype(jnp.float32) * filtered).astype(jnp.bfloat16)
            at = col ^ a
            far_s[at, 0, inside, :] = (up_s[rows, :].astype(jnp.float32) * filtered).astype(jnp.bfloat16)
            far_s[at, 1, inside, :] = (grad_mixed * v_s[rows, :].astype(jnp.float32)).astype(jnp.bfloat16)
            far_s[at, 2, inside, :] = (grad_mixed * k_s[rows, :].astype(jnp.float32)).astype(jnp.bfloat16)
    for k in range(groups):
        grad_refs[k][...] = far_s[k]
    rest = jnp.concatenate(
        [sums[j].sum(axis=0, keepdims=True) for j in range(KT)] + [jnp.zeros((1, width), jnp.float32)], axis=0
    )
    terms_of = [term.astype(jnp.float32) for term in in_three(rest)]
    packed = jnp.concatenate(terms_of + [jnp.zeros((8, width), jnp.float32)], axis=0).astype(jnp.bfloat16)
    for k, ref in enumerate(out_refs):
        ref[0:tok, :] = out_s[col ^ k]
        ref[tok : tok + 32, :] = packed


def middle(place, taps, ups, parts):
    groups, terms, devices = len(parts), len(parts[0]), len(ups)
    tile = ups[0].shape[1]
    _, _, tok, width = parts[0][0].shape
    total = groups * tok
    whole = lambda *shape: resident(shape, width)
    one = whole(1, 3, tok, width)
    outs = pl.pallas_call(
        functools.partial(middle_kernel, devices=devices, groups=groups, terms=terms, tile=tile),
        grid_spec=pltpu.PrefetchScalarGridSpec(
            num_scalar_prefetch=1,
            grid=(1,),
            in_specs=[whole(*taps.shape)] + [whole(*ups[0].shape)] * devices + [one] * (groups * terms),
            out_specs=[whole(3, tok, width)] * groups + [whole(tok + 32, width)] * groups,
            scratch_shapes=[
                pltpu.VMEM((total, width), jnp.bfloat16),
                pltpu.VMEM((groups, tok, width), jnp.bfloat16),
            ]
            + [pltpu.VMEM((total, width), jnp.bfloat16)] * 3
            + [pltpu.VMEM((total + PAD, width), jnp.float32)] * 2
            + [pltpu.VMEM((groups, 3, tok, width), jnp.bfloat16)],
        ),
        out_shape=[jax.ShapeDtypeStruct((3, tok, width), jnp.bfloat16)] * groups
        + [jax.ShapeDtypeStruct((tok + 32, width), jnp.bfloat16)] * groups,
        compiler_params=params(10, width),
        cost_estimate=SMALL,
        name="middle",
    )(place, taps, *ups, *[term for terms_of in parts for term in terms_of])
    return outs[:groups], outs[groups:]


def assemble_kernel(place, *refs):
    grad_refs, out_ref = refs[:-1], refs[-1]
    width = grad_refs[0].shape[2]
    for r, ref in enumerate(grad_refs):
        for s in range(3):
            at = pl.multiple_of((s * len(grad_refs) + (place[0] ^ r)) * width, width)
            out_ref[:, pl.ds(at, width)] = ref[s]


def assemble(place, grads):
    streams, tok, width = grads[0].shape
    out = jax.ShapeDtypeStruct((tok, streams * width * len(grads)), jnp.bfloat16)
    return pl.pallas_call(
        assemble_kernel,
        grid_spec=pltpu.PrefetchScalarGridSpec(
            num_scalar_prefetch=1,
            grid=(1,),
            in_specs=[resident(grads[0].shape, width)] * len(grads),
            out_specs=resident(out.shape, width),
        ),
        out_shape=out,
        compiler_params=params(4, width),
        cost_estimate=SMALL,
        name="assemble",
    )(place, *grads)


def input_grad_kernel(place, *refs, terms, width, first):
    grad_refs, w_ref, out_refs = refs[:terms], refs[terms], refs[terms + 1 :]
    step = out_refs[0].shape[1]
    if terms == 1:
        own = slice(first * step, (first + 1) * step) if len(out_refs) == 1 else slice(None)
        acc = jnp.dot(grad_refs[0][...], w_ref[:, :, own].reshape(-1, step), preferred_element_type=jnp.float32)
    else:
        acc = jnp.zeros(out_refs[0].shape, jnp.float32)
        for r, ref in enumerate(grad_refs):
            rows = pl.ds(pl.multiple_of((place[0] ^ r) * width, width), width)
            for s in range(3):
                acc = acc + jnp.dot(ref[s], w_ref[s, rows, :], preferred_element_type=jnp.float32)
    acc = acc.astype(jnp.bfloat16)
    for i, out_ref in enumerate(out_refs):

        @pl.when(pl.program_id(0) == i)
        def _():
            out_ref[...] = acc


def input_grad(place, grads, w, first, last, chunks):
    tok = grads[0].shape[-2]
    streams, channels, feat = w.shape
    step = feat // chunks
    width = channels if len(grads) == 1 else grads[0].shape[-1]
    return pl.pallas_call(
        functools.partial(input_grad_kernel, terms=len(grads), width=width, first=first),
        grid_spec=pltpu.PrefetchScalarGridSpec(
            num_scalar_prefetch=1,
            grid=(last - first,),
            in_specs=[resident(g.shape, width) for g in grads]
            + [
                resident(w.shape, width)
                if len(grads) == 1 and last - first == 1
                else pl.BlockSpec((streams, channels, step), lambda i, _: (0, 0, first + i))
            ],
            out_specs=[resident((tok, step), width)] * (last - first),
        ),
        out_shape=[jax.ShapeDtypeStruct((tok, step), jnp.bfloat16)] * (last - first),
        compiler_params=params(12, width),
        cost_estimate=SMALL,
        name="input_grad",
    )(place, *grads, w)


def weight_grad_kernel(place, *refs, chained, groups, wide, r):
    refs = refs[2 * chained :]
    grad_refs = refs[: 2 * groups]
    x_refs = refs[2 * groups : 3 * groups]
    out_ref, mark_ref = refs[3 * groups : 3 * groups + 2]
    mark_ref[...] = jnp.zeros(mark_ref.shape, jnp.float32)
    tok, step = x_refs[0].shape[0], out_ref.shape[2]
    width = grad_refs[0].shape[2]
    if wide:
        turned = refs[3 * groups + 2]

        @pl.when(pl.program_id(0) == 0)
        def _():
            for side in range(2):
                for s in range(3):
                    at = pl.multiple_of(((place[0] ^ r ^ side) % 2 + 2 * s) * width, width)
                    for k in range(groups):
                        turned[pl.ds(at, width), k * tok : (k + 1) * tok] = grad_refs[side * groups + k][s].T

        acc = None
        columns = pl.ds(pl.multiple_of(pl.program_id(0) * step, step), step)
        for k in range(groups):
            term = jnp.dot(
                turned[:, k * tok : (k + 1) * tok], x_refs[k][:, columns], preferred_element_type=jnp.float32
            )
            acc = term if acc is None else acc + term
        for s in range(3):
            out_ref[s] = acc[2 * s * width : 2 * (s + 1) * width, :]
    else:
        tn = (((0,), (0,)), ((), ()))
        for side in range(2):
            at = pl.multiple_of((place[0] ^ r ^ side) % 2 * width, width)
            for s in range(3):
                acc = None
                for k in range(groups):
                    term = lax.dot_general(
                        grad_refs[side * groups + k][s], x_refs[k][...], tn, preferred_element_type=jnp.float32
                    )
                    acc = term if acc is None else acc + term
                out_ref[s, pl.ds(at, width), :] = acc


def weight_grad(place, filled, grads, xs, r, count):
    groups = len(xs)
    streams, tok, width = grads[0].shape
    feat = xs[0].shape[1]
    channels = width * count
    step = min(512, feat)
    wide = width % LANES == 0
    chained = filled is not None
    return pl.pallas_call(
        functools.partial(weight_grad_kernel, chained=chained, groups=groups, wide=wide, r=r),
        grid_spec=pltpu.PrefetchScalarGridSpec(
            num_scalar_prefetch=1,
            grid=(feat // step,),
            in_specs=[pl.BlockSpec(memory_space=pl.ANY)] * (2 * chained)
            + [resident((streams, tok, width), width)] * (2 * groups)
            + [resident((tok, feat), width) if wide else pl.BlockSpec((tok, step), lambda i, _: (0, i))] * groups,
            out_specs=[
                pl.BlockSpec((streams, 2 * width, step), lambda i, at: (0, (at[0] ^ r) // 2, i)),
                resident((8, LANES), width),
            ],
            scratch_shapes=[pltpu.VMEM((2 * streams * width, groups * tok), jnp.bfloat16)] if wide else [],
        ),
        out_shape=[
            jax.ShapeDtypeStruct((streams, channels, feat), jnp.float32),
            jax.ShapeDtypeStruct((8, LANES), jnp.float32),
        ],
        input_output_aliases={1: 0} if chained else {},
        compiler_params=params(14, width),
        cost_estimate=SMALL,
        name="weight_grad",
    )(place, *(filled if chained else []), *grads, *xs)


def added(first, second):
    return (first.astype(jnp.float32) + second.astype(jnp.float32)).astype(jnp.bfloat16)


def first_pieces(tokens, k):
    tok = tokens.shape[0]
    if tok % 48 or lax.axis_size("row") % 2:
        return [swap(tokens, "col", k)]
    third = tok // 3
    parity = lax.axis_index("row") % 2
    return [swap(lax.dynamic_slice_in_dim(tokens, parity * third, third, axis=0), "col", k)]


def other_pieces(tokens, first, k):
    third = first[0].shape[0]
    if third == tokens.shape[0]:
        return first
    rest = after(tokens, lax.axis_index("row"))[2 * third :]
    return first + [swap(first[0], "row", 1), swap(after(rest, *first), "col", k)]


def on_device(tokens, weight, taps, upstream):
    n_col = lax.axis_size("col")
    n_depth = lax.axis_size("depth")
    local_tok = upstream.shape[0]
    depth_at = lax.axis_index("depth")
    col_at = lax.axis_index("col")
    row_at = lax.axis_index("row")
    place = jnp.stack([depth_at, col_at, row_at, col_at * n_depth + depth_at]).astype(jnp.int32)
    w = jnp.transpose(weight, (1, 0, 2))
    width = w.shape[1] // n_depth
    def project_and_sum(x_pieces, *earlier):
        keep, send, x = project(place, x_pieces, w, n_depth)
        near = swap(after(send, *earlier) if earlier else send, "depth", 1)
        pairs = [added(keep[r // 2], near[r // 2])[None] for r in range(2, n_depth, 2)]
        fars = [swap(pair, "depth", 2 * i + 2) for i, pair in enumerate(pairs)]
        return x, [keep, near] + fars, pairs, fars

    first = [first_pieces(tokens, k) for k in range(1, n_col)]
    span = width * n_depth
    col_ups = [lax.dynamic_slice_in_dim(upstream, (col_at ^ k) * span, span, axis=1) for k in range(n_col)]
    col_ups = [up if k == 0 else swap(up, "col", k) for k, up in enumerate(col_ups)]
    x, terms, pairs, fars = project_and_sum([tokens], *[piece for of in first for piece in of], *col_ups[1:])
    xs, parts = [x], [terms]
    ups = split_lanes(place, [after(col_ups[0], *pairs)] + col_ups[1:], n_depth)
    ups = [up if r == 0 else swap(up, "depth", r) for r, up in enumerate(ups)]
    for k in range(1, n_col):
        x_pieces = other_pieces(tokens, first[k - 1], k)
        x_pieces[-1] = after(x_pieces[-1], *fars, *ups[1:])
        x, terms, pairs, fars = project_and_sum(x_pieces)
        xs.append(x)
        parts.append(terms)
    own_grads, blocks = middle(place, taps, ups, parts)
    nears = [swap(own, "depth", 1) for own in own_grads]
    blocks = [block if k == 0 else swap(block, "col", k) for k, block in enumerate(blocks)]
    beside = nears + blocks[1:]
    chunks = 4
    grads = [None] * n_col
    ready = []
    sent = []
    for k in reversed(range(n_col)):
        fars = [swap(after(own_grads[k], *ready) if ready else own_grads[k], "depth", r) for r in range(2, n_depth, 2)]
        ready = fars
        if k > 0:
            fars = [after(far, *beside) for far in fars]
        elif sent:
            fars = [after(far, sent[-1][1][-1]) for far in fars]
        grads[k] = [own_grads[k], nears[k]]
        for far in fars:
            grads[k] += [far, swap(far, "depth", 1)]
        ready = grads[k][2:]
        lhs = [assemble(place, grads[k])] if width % LANES == 0 else grads[k]
        if k > 0:
            head = input_grad(place, lhs, w, 0, 1, chunks)
            behind = [after(lhs[0], *head)] + lhs[1:]
            tail = input_grad(place, behind, w, 1, chunks, chunks)
            parts_of = list(head) + list(tail)
            sent.append(([swap(part, "col", k) for part in parts_of[:3]], parts_of))
    held = [parts_of[3:] for _, parts_of in sent]
    sent = [of for of, _ in sent]
    own_part = list(input_grad(place, lhs, w, 0, 1, chunks))
    outer = (row_at == 0) | (row_at == 3)
    inward, across, summed, done = ([None] * chunks for _ in range(4))
    pair = cross = filled = None
    marks = []
    line = lax.axis_size("row") == 4
    for slot in range(chunks + 3):
        if slot < chunks:
            total = after(own_part[slot], *marks).astype(jnp.float32)
            for of in sent:
                total = total + of[slot].astype(jnp.float32)
            inward[slot] = total.astype(jnp.bfloat16)
            marks = [inward[slot]]
        if not line:
            if slot < chunks:
                done[slot] = lax.psum(inward[slot], "row")
                if slot + 3 < chunks:
                    for k, parts_of in enumerate(held):
                        sent[k].append(swap(parts_of[slot], "col", k + 1))
        else:
            if 0 <= slot - 1 < chunks:
                across[slot - 1] = added(after(inward[slot - 1], *marks), pair)
                marks = [across[slot - 1]]
                if slot + 2 < chunks:
                    for k, parts_of in enumerate(held):
                        sent[k].append(swap(after(parts_of[slot - 1], *marks), "col", k + 1))
            if 0 <= slot - 2 < chunks:
                summed[slot - 2] = added(after(across[slot - 2], *marks), cross)
                marks = [summed[slot - 2]]
            if 0 <= slot - 3 < chunks:
                done[slot - 3] = jnp.where(outer, pair, summed[slot - 3])
            if slot < chunks + 2:
                out = summed[slot - 2] if slot >= 2 else inward[slot]
                pair = swap(jnp.where(outer, inward[slot], out) if slot < chunks else out, "row", 1)
            if 0 <= slot - 1 < chunks:
                cross = lax.ppermute(across[slot - 1], "row", [(0, 0), (1, 2), (2, 1), (3, 3)])
        if slot == 0:
            behind = [after(lhs[0], *marks)] + lhs[1:]
            own_part += input_grad(place, behind, w, 1, chunks, chunks)
            marks = [own_part[1]]
        if 0 < slot <= n_depth // 2:
            r = n_depth - 2 * slot
            of = [group[i] for i in (r, r + 1) for group in grads]
            filled = weight_grad(place, filled, [after(of[0], *marks)] + of[1:], xs, r, n_depth)
            marks = [filled[1]]
        if slot == chunks - 1:
            blocks = split_rows(place, [after(blocks[0], *marks)] + blocks[1:], n_depth)
            blocks = [block if r == 0 else swap(block, "depth", r) for r, block in enumerate(blocks)]
            late = blocks[1:]
        if slot == chunks:
            marks += late
    grad_tokens = jnp.concatenate(done, axis=1)
    grad_weight = jnp.transpose(filled[0], (1, 0, 2))
    output, grad_taps = join(place, filled[1], [after(blocks[0], *marks)] + blocks[1:], taps.shape[1])
    return (output, grad_tokens, grad_weight, grad_taps)


def solution(mesh):
    in_specs = (
        P("col", "depth"),
        P(("row", "col"), None, "depth"),
        P(None, "row"),
        P(("col", "depth"), "row"),
    )
    out_specs = (
        P(("col", "depth"), "row"),
        P("col", "depth"),
        P(("row", "col"), None, "depth"),
        P(None, "row"),
    )
    return jax.shard_map(
        on_device, mesh=mesh, in_specs=in_specs, out_specs=out_specs, check_vma=False
    )
```

```python
import functools

import jax
import jax.numpy as jnp
from jax import lax
from jax.experimental import pallas as pl
from jax.experimental.pallas import tpu as pltpu
from jax.sharding import PartitionSpec as P

GROUP = 16
KT = 7
PAD = 8
LANES = 128
MIB = 1024 * 1024
SMALL = pl.CostEstimate(flops=1, bytes_accessed=1, transcendentals=0)


def swap(value, axis, flip):
    count = lax.axis_size(axis)
    return lax.ppermute(value, axis, [(i, i ^ flip) for i in range(count)])


def after(value, *earlier):
    return lax.optimization_barrier((value, *earlier))[0]


def resident(shape, width):
    if width % LANES == 0:
        return pl.BlockSpec(memory_space=pltpu.VMEM)
    return pl.BlockSpec(tuple(shape), lambda *_: (0,) * len(shape), pipeline_mode=pl.Buffered(1))


def params(mib, width):
    return pltpu.CompilerParams(vmem_limit_bytes=(mib if width % LANES == 0 else 56) * MIB)


def project_kernel(place, *refs, pieces, count, width):
    x_refs = refs[:pieces]
    w_ref, keep_ref, send_ref = refs[pieces : pieces + 3]
    stream = pl.program_id(0)
    core = place[0] % 2
    if pieces == 1:
        x = x_refs[0][...]
    else:
        x_out = refs[pieces + 3]
        third = x_refs[0].shape[0]
        parity = place[2] % 2

        @pl.when(stream == 0)
        def _():
            x_out[pl.ds(pl.multiple_of(parity * third, third), third), :] = x_refs[0][...]
            x_out[pl.ds(pl.multiple_of((1 - parity) * third, third), third), :] = x_refs[1][...]
            x_out[2 * third :, :] = x_refs[2][...]

        x = x_out[...]
    nt = (((1,), (1,)), ((), ()))
    if width % LANES == 0:
        whole = lax.dot_general(x, w_ref[stream], nt, preferred_element_type=jnp.float32).astype(jnp.bfloat16)
        blocks = [whole[:, j * width : (j + 1) * width] for j in range(count)]
    else:
        blocks = [
            lax.dot_general(
                x, w_ref[0, j * width : (j + 1) * width, :], nt, preferred_element_type=jnp.float32
            ).astype(jnp.bfloat16)
            for j in range(count)
        ]
    for mine in range(2):

        @pl.when(core == mine)
        def _():
            for j in range(count):
                at = (j ^ place[0]) // 2
                if j % 2 == mine:
                    keep_ref[at, stream] = blocks[j]
                else:
                    send_ref[at, stream] = blocks[j]


def project(place, xs, w, count):
    tok, feat = sum(x.shape[0] for x in xs), xs[0].shape[1]
    streams, channels, _ = w.shape
    width = channels // count
    part = jax.ShapeDtypeStruct((count // 2, streams, tok, width), jnp.bfloat16)
    wide = width % LANES == 0
    spec = resident(part.shape, width)
    joined = len(xs) > 1
    outs = pl.pallas_call(
        functools.partial(project_kernel, pieces=len(xs), count=count, width=width),
        grid_spec=pltpu.PrefetchScalarGridSpec(
            num_scalar_prefetch=1,
            grid=(streams,),
            in_specs=[resident(x.shape, width) for x in xs]
            + [resident(w.shape, width) if wide else pl.BlockSpec((1, channels, feat), lambda s, _: (s, 0, 0))],
            out_specs=[spec, spec] + [resident((tok, feat), width)] * joined,
        ),
        out_shape=[part, part] + [jax.ShapeDtypeStruct((tok, feat), jnp.bfloat16)] * joined,
        compiler_params=params(10, width),
        cost_estimate=SMALL,
        name="project",
    )(place, *xs, w)
    return outs[0], outs[1], outs[2] if joined else xs[0]


def in_three(value):
    terms = []
    for _ in range(3):
        term = value.astype(jnp.bfloat16)
        value = value - term.astype(jnp.float32)
        terms.append(term)
    return terms


def split_lanes_kernel(place, up_ref, *out_refs):
    n_depth, width = len(out_refs), out_refs[0].shape[2]
    for r, ref in enumerate(out_refs):
        for k in range(ref.shape[0]):
            at = ((place[1] ^ k) * n_depth + (place[0] ^ r)) * width
            ref[k] = up_ref[:, pl.ds(pl.multiple_of(at, width), width)]


def merge_rows_kernel(place, *refs, n_depth):
    in_refs, out_refs = refs[:n_depth], refs[n_depth:]
    local = in_refs[0].shape[1]
    for r, ref in enumerate(in_refs):
        for k, out_ref in enumerate(out_refs):
            out_ref[pl.ds(pl.multiple_of((place[0] ^ r) * local, 16), local), :] = ref[k]


def split_rows_kernel(place, *refs, n_col):
    in_refs, out_refs = refs[:n_col], refs[n_col:]
    local = out_refs[0].shape[1] - 32
    for r, ref in enumerate(out_refs):
        rows = pl.ds(pl.multiple_of((place[0] ^ r) * local, 16), local)
        for k in range(n_col):
            ref[k, 0:local] = in_refs[k][rows, :]
            ref[k, local:] = in_refs[k][-32:, :]


def rearrange(kernel, place, arrays, count, shape, name):
    width = shape[-1]
    return pl.pallas_call(
        kernel,
        grid_spec=pltpu.PrefetchScalarGridSpec(
            num_scalar_prefetch=1,
            grid=(1,),
            in_specs=[resident(value.shape, width) for value in arrays],
            out_specs=[resident(shape, width)] * count,
        ),
        out_shape=[jax.ShapeDtypeStruct(shape, jnp.bfloat16)] * count,
        compiler_params=params(4, width),
        cost_estimate=SMALL,
        name=name,
    )(place, *arrays)


def split_lanes(place, up, n_col, n_depth):
    local, width = up.shape[0], up.shape[1] // (n_col * n_depth)
    if width % LANES:
        blocks = up.reshape(local, n_col, n_depth, width)[:, place[1] ^ jnp.arange(n_col)]
        return [
            jnp.transpose(lax.dynamic_index_in_dim(blocks, place[0] ^ r, 2, keepdims=False), (1, 0, 2))
            for r in range(n_depth)
        ]
    return rearrange(split_lanes_kernel, place, [up], n_depth, (n_col, local, width), "split")


def merge_rows(place, pieces):
    n_depth = len(pieces)
    n_col, local, width = pieces[0].shape
    if width % LANES:
        whole = jnp.stack(pieces)[place[0] ^ jnp.arange(n_depth)]
        return list(jnp.transpose(whole, (1, 0, 2, 3)).reshape(n_col, n_depth * local, width))
    kernel = functools.partial(merge_rows_kernel, n_depth=n_depth)
    return list(rearrange(kernel, place, pieces, n_col, (n_depth * local, width), "merge"))


def split_rows(place, arrays, n_depth):
    local, width = (arrays[0].shape[0] - 32) // n_depth, arrays[0].shape[1]
    if width % LANES:
        whole = jnp.stack(arrays)
        return [
            jnp.concatenate(
                [lax.dynamic_slice_in_dim(whole, (place[0] ^ r) * local, local, axis=1), whole[:, -32:]], axis=1
            )
            for r in range(n_depth)
        ]
    kernel = functools.partial(split_rows_kernel, n_col=len(arrays))
    return rearrange(kernel, place, arrays, n_depth, (len(arrays), local + 32, width), "split")


def join_kernel(place, _, *refs):
    block_refs, (out_ref, grad_taps_ref) = refs[:-2], refs[-2:]
    n_depth = len(block_refs)
    n_col, _, width = block_refs[0].shape
    local, groups = out_ref.shape[0], grad_taps_ref.shape[1]
    lane_group = lax.broadcasted_iota(jnp.int32, (width, groups), 0) // GROUP
    group = lax.broadcasted_iota(jnp.int32, (width, groups), 1)
    total = jnp.zeros((24, groups), jnp.float32)
    for r, ref in enumerate(block_refs):
        for k in range(n_col):
            at = (place[1] ^ k) * n_depth + (place[0] ^ r)
            out_ref[:, pl.ds(pl.multiple_of(at * width, width), width)] = ref[k, 0:local, :]
            spread = (lane_group + at * (width // GROUP) == group).astype(jnp.bfloat16)
            total = total + jnp.dot(ref[k, local : local + 24, :], spread, preferred_element_type=jnp.float32)
    grad_taps_ref[...] = (total[0:8] + total[8:16] + total[16:24])[:KT]


def join(place, mark, blocks, groups):
    n_depth = len(blocks)
    n_col, rows, width = blocks[0].shape
    local = rows - 32
    if width % LANES:
        whole = jnp.stack(blocks)[place[0] ^ jnp.arange(n_depth)][:, place[1] ^ jnp.arange(n_col)]
        sums = whole[:, :, local : local + 24].astype(jnp.float32)
        sums = sums.reshape(n_depth, n_col, 3, 8, width // GROUP, GROUP).sum(axis=(2, 5))[:, :, :KT]
        return (
            jnp.transpose(whole[:, :, :local], (2, 1, 0, 3)).reshape(local, -1),
            jnp.transpose(sums, (2, 1, 0, 3)).reshape(KT, -1),
        )
    channels = n_depth * n_col * width
    return pl.pallas_call(
        join_kernel,
        grid_spec=pltpu.PrefetchScalarGridSpec(
            num_scalar_prefetch=1,
            grid=(1,),
            in_specs=[pl.BlockSpec(memory_space=pl.ANY)] + [resident(blocks[0].shape, width)] * n_depth,
            out_specs=[resident((local, channels), width), resident((KT, groups), width)],
        ),
        out_shape=[
            jax.ShapeDtypeStruct((local, channels), jnp.bfloat16),
            jax.ShapeDtypeStruct((KT, groups), jnp.float32),
        ],
        compiler_params=params(4, width),
        cost_estimate=SMALL,
        name="join",
    )(place, mark, *blocks)


def middle_kernel(place, taps_ref, *refs, groups, terms, tile):
    up_refs, refs = refs[:groups], refs[groups:]
    part_refs = refs[: groups * terms]
    grad_refs = refs[groups * terms : groups * terms + groups]
    out_refs = refs[groups * terms + groups : groups * terms + 2 * groups]
    up_s, out_s, q_s, k_s, v_s, mixed_s, gf_s, far_s = refs[groups * terms + 2 * groups :]
    col = place[1]
    tok = part_refs[0].shape[2]
    width = part_refs[0].shape[3]
    total = groups * tok
    tap_groups = taps_ref.shape[1]
    for k, ref in enumerate(up_refs):
        up_s[pl.ds(pl.multiple_of((col ^ k) * tok, tok), tok), :] = ref[...]
    lane_group = lax.broadcasted_iota(jnp.int32, (tap_groups, width), 1) // GROUP
    group = lax.broadcasted_iota(jnp.int32, (tap_groups, width), 0)
    spread = (lane_group + place[3] * (width // GROUP) == group).astype(jnp.bfloat16)
    taps = sum(jnp.dot(term, spread, preferred_element_type=jnp.float32) for term in in_three(taps_ref[...]))
    mixed_s[0:PAD, :] = jnp.zeros((PAD, width), jnp.float32)
    gf_s[total : total + PAD, :] = jnp.zeros((PAD, width), jnp.float32)
    for k in range(groups):
        start = (col ^ k) * tok
        for i in range(tok // tile):
            inside = slice(i * tile, (i + 1) * tile)
            rows = pl.ds(pl.multiple_of(start + i * tile, tile), tile)
            streams = []
            for s in range(3):
                acc = None
                for ref in part_refs[k * terms : (k + 1) * terms]:
                    term = ref[0, s, inside, :].astype(jnp.float32)
                    acc = term if acc is None else acc + term
                streams.append(acc.astype(jnp.bfloat16))
            q_s[rows, :], k_s[rows, :], v_s[rows, :] = streams
            query, key, value = [stream.astype(jnp.float32) for stream in streams]
            mixed_s[pl.ds(pl.multiple_of(start + i * tile + PAD, PAD), tile), :] = key * value
            gf_s[rows, :] = up_s[rows, :].astype(jnp.float32) * query
    sums = [jnp.zeros((8, width), jnp.float32) for _ in range(KT)]
    for a in range(groups):
        for i in range(tok // tile):
            first = a * tok + i * tile
            rows = slice(first, first + tile)
            inside = slice(i * tile, (i + 1) * tile)
            gf = gf_s[rows, :]
            filtered = jnp.zeros((tile, width), jnp.float32)
            grad_mixed = jnp.zeros((tile, width), jnp.float32)
            for j in range(KT):
                shifted = mixed_s[first + PAD - j : first + PAD - j + tile, :]
                filtered = filtered + taps[j : j + 1, :] * shifted
                sums[j] = sums[j] + (gf * shifted).reshape(tile // 8, 8, width).sum(axis=0)
                grad_mixed = grad_mixed + taps[j : j + 1, :] * gf_s[first + j : first + j + tile, :]
            out_s[a, inside, :] = (q_s[rows, :].astype(jnp.float32) * filtered).astype(jnp.bfloat16)
            at = col ^ a
            far_s[at, 0, inside, :] = (up_s[rows, :].astype(jnp.float32) * filtered).astype(jnp.bfloat16)
            far_s[at, 1, inside, :] = (grad_mixed * v_s[rows, :].astype(jnp.float32)).astype(jnp.bfloat16)
            far_s[at, 2, inside, :] = (grad_mixed * k_s[rows, :].astype(jnp.float32)).astype(jnp.bfloat16)
    for k in range(groups):
        grad_refs[k][...] = far_s[k]
    rest = jnp.concatenate(
        [sums[j].sum(axis=0, keepdims=True) for j in range(KT)] + [jnp.zeros((1, width), jnp.float32)], axis=0
    )
    terms_of = [term.astype(jnp.float32) for term in in_three(rest)]
    packed = jnp.concatenate(terms_of + [jnp.zeros((8, width), jnp.float32)], axis=0).astype(jnp.bfloat16)
    for k, ref in enumerate(out_refs):
        ref[0:tok, :] = out_s[col ^ k]
        ref[tok : tok + 32, :] = packed


def middle(place, taps, ups, parts, tile):
    groups, terms = len(parts), len(parts[0])
    _, _, tok, width = parts[0][0].shape
    total = groups * tok
    whole = lambda *shape: resident(shape, width)
    one = whole(1, 3, tok, width)
    outs = pl.pallas_call(
        functools.partial(middle_kernel, groups=groups, terms=terms, tile=tile),
        grid_spec=pltpu.PrefetchScalarGridSpec(
            num_scalar_prefetch=1,
            grid=(1,),
            in_specs=[whole(*taps.shape)] + [whole(tok, width)] * groups + [one] * (groups * terms),
            out_specs=[whole(3, tok, width)] * groups + [whole(tok + 32, width)] * groups,
            scratch_shapes=[
                pltpu.VMEM((total, width), jnp.bfloat16),
                pltpu.VMEM((groups, tok, width), jnp.bfloat16),
            ]
            + [pltpu.VMEM((total, width), jnp.bfloat16)] * 3
            + [pltpu.VMEM((total + PAD, width), jnp.float32)] * 2
            + [pltpu.VMEM((groups, 3, tok, width), jnp.bfloat16)],
        ),
        out_shape=[jax.ShapeDtypeStruct((3, tok, width), jnp.bfloat16)] * groups
        + [jax.ShapeDtypeStruct((tok + 32, width), jnp.bfloat16)] * groups,
        compiler_params=params(10, width),
        cost_estimate=SMALL,
        name="middle",
    )(place, taps, *ups, *[term for terms_of in parts for term in terms_of])
    return outs[:groups], outs[groups:]


def assemble_kernel(place, *refs):
    grad_refs, out_ref = refs[:-1], refs[-1]
    width = grad_refs[0].shape[2]
    for r, ref in enumerate(grad_refs):
        for s in range(3):
            at = pl.multiple_of((s * len(grad_refs) + (place[0] ^ r)) * width, width)
            out_ref[:, pl.ds(at, width)] = ref[s]


def assemble(place, grads):
    streams, tok, width = grads[0].shape
    out = jax.ShapeDtypeStruct((tok, streams * width * len(grads)), jnp.bfloat16)
    if width % LANES:
        whole = jnp.stack(grads)[place[0] ^ jnp.arange(len(grads))]
        return jnp.transpose(whole, (2, 1, 0, 3)).reshape(out.shape)
    return pl.pallas_call(
        assemble_kernel,
        grid_spec=pltpu.PrefetchScalarGridSpec(
            num_scalar_prefetch=1,
            grid=(1,),
            in_specs=[resident(grads[0].shape, width)] * len(grads),
            out_specs=resident(out.shape, width),
        ),
        out_shape=out,
        compiler_params=params(4, width),
        cost_estimate=SMALL,
        name="assemble",
    )(place, *grads)


def input_grad_kernel(grad_ref, w_ref, *out_refs, first):
    step = out_refs[0].shape[1]
    own = slice(first * step, (first + 1) * step) if len(out_refs) == 1 else slice(None)
    acc = jnp.dot(grad_ref[...], w_ref[:, :, own].reshape(-1, step), preferred_element_type=jnp.float32)
    acc = acc.astype(jnp.bfloat16)
    for i, out_ref in enumerate(out_refs):

        @pl.when(pl.program_id(0) == i)
        def _():
            out_ref[...] = acc


def input_grad(grad, w, first, last, chunks, width):
    tok = grad.shape[0]
    streams, channels, feat = w.shape
    step = feat // chunks
    count = last - first
    if width % LANES:
        rows = w[:, :, first * step : last * step].reshape(streams * channels, count * step)
        whole = jnp.dot(grad, rows, preferred_element_type=jnp.float32).astype(jnp.bfloat16)
        return [whole[:, i * step : (i + 1) * step] for i in range(count)]
    return list(
        pl.pallas_call(
            functools.partial(input_grad_kernel, first=first),
            grid=(count,),
            in_specs=[
                resident(grad.shape, width),
                resident(w.shape, width)
                if count == 1
                else pl.BlockSpec((streams, channels, step), lambda i: (0, 0, first + i)),
            ],
            out_specs=[resident((tok, step), width)] * count,
            out_shape=[jax.ShapeDtypeStruct((tok, step), jnp.bfloat16)] * count,
            compiler_params=params(12, width),
            cost_estimate=SMALL,
            name="input_grad",
        )(grad, w)
    )


def weight_grad_kernel(*refs, chained, groups, half):
    refs = refs[2 * chained :]
    grad_refs, x_refs = refs[:groups], refs[groups : 2 * groups]
    out_ref, mark_ref, turned = refs[2 * groups :]
    mark_ref[...] = jnp.zeros(mark_ref.shape, jnp.float32)
    streams, channels, step = out_ref.shape
    tok = x_refs[0].shape[0]

    @pl.when(pl.program_id(0) == 0)
    def _():
        for k in range(groups):
            for s in range(streams):
                at = (2 * s + half) * channels
                block = grad_refs[k][:, at : at + channels]
                turned[s * channels : (s + 1) * channels, k * tok : (k + 1) * tok] = block.T

    columns = pl.ds(pl.multiple_of(pl.program_id(0) * step, step), step)
    acc = None
    for k in range(groups):
        term = jnp.dot(turned[:, k * tok : (k + 1) * tok], x_refs[k][:, columns], preferred_element_type=jnp.float32)
        acc = term if acc is None else acc + term
    for s in range(streams):
        out_ref[s] = acc[s * channels : (s + 1) * channels, :]


def weight_grad(filled, grads, xs, half, streams, width):
    groups = len(xs)
    tok, feat = xs[0].shape
    channels = grads[0].shape[1] // streams
    chained = filled is not None
    if width % LANES:
        if chained:
            return filled
        terms = [
            lax.dot_general(grad, x, (((0,), (0,)), ((), ())), preferred_element_type=jnp.float32)
            for grad, x in zip(grads, xs)
        ]
        return sum(terms).reshape(streams, channels, feat), jnp.zeros((8, LANES), jnp.float32)
    step = min(512, feat)
    return pl.pallas_call(
        functools.partial(weight_grad_kernel, chained=chained, groups=groups, half=half),
        grid=(feat // step,),
        in_specs=[pl.BlockSpec(memory_space=pl.ANY)] * (2 * chained)
        + [resident(grads[0].shape, width)] * groups
        + [resident((tok, feat), width)] * groups,
        out_specs=[
            pl.BlockSpec((streams, channels // 2, step), lambda i: (0, half, i)),
            resident((8, LANES), width),
        ],
        scratch_shapes=[pltpu.VMEM((streams * channels // 2, groups * tok), jnp.bfloat16)],
        out_shape=[
            jax.ShapeDtypeStruct((streams, channels, feat), jnp.float32),
            jax.ShapeDtypeStruct((8, LANES), jnp.float32),
        ],
        input_output_aliases={0: 0} if chained else {},
        compiler_params=params(14, width),
        cost_estimate=SMALL,
        name="weight_grad",
    )(*(filled if chained else []), *grads, *xs)


def added(first, second):
    return (first.astype(jnp.float32) + second.astype(jnp.float32)).astype(jnp.bfloat16)


def first_pieces(tokens, k):
    tok = tokens.shape[0]
    if tok % 48 or lax.axis_size("row") % 2:
        return [swap(tokens, "col", k)]
    third = tok // 3
    parity = lax.axis_index("row") % 2
    return [swap(lax.dynamic_slice_in_dim(tokens, parity * third, third, axis=0), "col", k)]


def other_pieces(tokens, first, k):
    third = first[0].shape[0]
    if third == tokens.shape[0]:
        return first
    rest = after(tokens, lax.axis_index("row"))[2 * third :]
    return first + [swap(first[0], "row", 1), swap(after(rest, *first), "col", k)]


def on_device(tokens, weight, taps, upstream):
    n_col = lax.axis_size("col")
    n_depth = lax.axis_size("depth")
    local_tok = upstream.shape[0]
    depth_at = lax.axis_index("depth")
    col_at = lax.axis_index("col")
    row_at = lax.axis_index("row")
    place = jnp.stack([depth_at, col_at, row_at, col_at * n_depth + depth_at]).astype(jnp.int32)
    w = jnp.transpose(weight, (1, 0, 2))
    width = w.shape[1] // n_depth
    def project_and_sum(x_pieces, *earlier):
        keep, send, x = project(place, x_pieces, w, n_depth)
        near = swap(after(send, *earlier) if earlier else send, "depth", 1)
        pairs = [added(keep[r // 2], near[r // 2])[None] for r in range(2, n_depth, 2)]
        fars = [swap(pair, "depth", 2 * i + 2) for i, pair in enumerate(pairs)]
        return x, [keep, near] + fars, pairs, fars

    first = [first_pieces(tokens, k) for k in range(1, n_col)]
    ups = split_lanes(place, upstream, n_col, n_depth)
    ups = [up if r == 0 else swap(up, "depth", r) for r, up in enumerate(ups)]
    x, terms, pairs, fars = project_and_sum([tokens], *[piece for of in first for piece in of], *ups[1:])
    xs, parts = [x], [terms]
    for k in range(1, n_col):
        x_pieces = other_pieces(tokens, first[k - 1], k)
        x_pieces[-1] = after(x_pieces[-1], *fars)
        x, terms, pairs, fars = project_and_sum(x_pieces)
        xs.append(x)
        parts.append(terms)
    ups = merge_rows(place, [after(ups[0], *pairs)] + ups[1:])
    ups = [up if k == 0 else swap(up, "col", k) for k, up in enumerate(ups)]
    own_grads, blocks = middle(place, taps, ups, parts, local_tok)
    nears = [swap(own, "depth", 1) for own in own_grads]
    blocks = [block if k == 0 else swap(block, "col", k) for k, block in enumerate(blocks)]
    beside = nears + blocks[1:]
    chunks = 4
    grads = [None] * n_col
    ready = []
    sent = []
    lhs = [None] * n_col
    for k in reversed(range(n_col)):
        fars = [swap(after(own_grads[k], *ready) if ready else own_grads[k], "depth", r) for r in range(2, n_depth, 2)]
        ready = fars
        if k > 0:
            fars = [after(far, *beside) for far in fars]
        elif sent:
            fars = [after(far, sent[-1][1][-1]) for far in fars]
        grads[k] = [own_grads[k], nears[k]]
        for far in fars:
            grads[k] += [far, swap(far, "depth", 1)]
        ready = grads[k][2:]
        lhs[k] = assemble(place, grads[k])
        if k > 0:
            parts_of = input_grad(lhs[k], w, 0, 1, chunks, width)
            parts_of += input_grad(after(lhs[k], *parts_of), w, 1, chunks, chunks, width)
            sent.append(([swap(part, "col", k) for part in parts_of[:3]], parts_of))
    held = [parts_of[3:] for _, parts_of in sent]
    sent = [of for of, _ in sent]
    own_part = input_grad(lhs[0], w, 0, 1, chunks, width)
    outer = (row_at == 0) | (row_at == 3)
    line = lax.axis_size("row") == 4
    hopping = chunks - 1
    inward, across, summed, done = ([None] * chunks for _ in range(4))
    pair = cross = filled = None
    marks = []

    def with_sent(c):
        total = after(own_part[c], *marks).astype(jnp.float32)
        for of in sent:
            total = total + of[c].astype(jnp.float32)
        return total.astype(jnp.bfloat16)

    for slot in range(hopping + 3):
        if slot < hopping:
            inward[slot] = with_sent(slot)
            marks = [inward[slot]]
        if not line:
            if slot < hopping:
                done[slot] = lax.psum(inward[slot], "row")
        else:
            if 0 <= slot - 1 < hopping:
                across[slot - 1] = added(after(inward[slot - 1], *marks), pair)
                marks = [across[slot - 1]]
            if 0 <= slot - 2 < hopping:
                summed[slot - 2] = added(after(across[slot - 2], *marks), cross)
                marks = [summed[slot - 2]]
            if 0 <= slot - 3 < hopping:
                done[slot - 3] = jnp.where(outer, pair, summed[slot - 3])
            if slot < hopping + 2:
                out = summed[slot - 2] if slot >= 2 else inward[slot]
                pair = swap(jnp.where(outer, inward[slot], out) if slot < hopping else out, "row", 1)
            if 0 <= slot - 1 < hopping:
                cross = lax.ppermute(across[slot - 1], "row", [(0, 0), (1, 2), (2, 1), (3, 3)])
        if slot == 0:
            own_part += input_grad(after(lhs[0], *marks), w, 1, chunks, chunks, width)
            marks = [own_part[1]]
        if slot == 1:
            for k, parts_of in enumerate(held):
                sent[k] += [swap(after(part, *marks), "col", k + 1) for part in parts_of]
            blocks = split_rows(place, [after(blocks[0], *marks)] + blocks[1:], n_depth)
            blocks = [block if r == 0 else swap(block, "depth", r) for r, block in enumerate(blocks)]
            marks += blocks[1:]
        if slot == 2:
            last = with_sent(hopping)
            done[hopping] = lax.psum(last, "row")
            marks = [last]
        if slot >= hopping and slot < hopping + 2:
            filled = weight_grad(filled, [after(lhs[0], *marks)] + lhs[1:], xs, slot - hopping, 3, width)
            marks = [filled[1]]
    output, grad_taps = join(
        place, filled[1], [after(blocks[0], *marks, done[hopping])] + blocks[1:], taps.shape[1]
    )
    grad_tokens = jnp.concatenate(done, axis=1)
    grad_weight = jnp.transpose(filled[0], (1, 0, 2))
    return (output, grad_tokens, grad_weight, grad_taps)


def solution(mesh):
    in_specs = (
        P("col", "depth"),
        P(("row", "col"), None, "depth"),
        P(None, "row"),
        P(("col", "depth"), "row"),
    )
    out_specs = (
        P(("col", "depth"), "row"),
        P("col", "depth"),
        P(("row", "col"), None, "depth"),
        P(None, "row"),
    )
    return jax.shard_map(
        on_device, mesh=mesh, in_specs=in_specs, out_specs=out_specs, check_vma=False
    )
```

```python
import functools

import jax
import jax.numpy as jnp
from jax import lax
from jax.experimental import pallas as pl
from jax.experimental.pallas import tpu as pltpu
from jax.sharding import PartitionSpec as P

GROUP = 16
KT = 7
PAD = 8
LANES = 128
MIB = 1024 * 1024
SMALL = pl.CostEstimate(flops=1, bytes_accessed=1, transcendentals=0)


def swap(value, axis, flip):
    count = lax.axis_size(axis)
    return lax.ppermute(value, axis, [(i, i ^ flip) for i in range(count)])


def after(value, *earlier):
    return lax.optimization_barrier((value, *earlier))[0]


def resident(shape, width):
    if width % LANES == 0:
        return pl.BlockSpec(memory_space=pltpu.VMEM)
    return pl.BlockSpec(tuple(shape), lambda *_: (0,) * len(shape), pipeline_mode=pl.Buffered(1))


def params(mib, width):
    return pltpu.CompilerParams(vmem_limit_bytes=(mib if width % LANES == 0 else 56) * MIB)


def project_kernel(place, *refs, pieces, count, width):
    x_refs = refs[:pieces]
    w_ref, keep_ref, send_ref = refs[pieces : pieces + 3]
    stream = pl.program_id(0)
    core = place[0] % 2
    if pieces == 1:
        x = x_refs[0][...]
    else:
        x_out = refs[pieces + 3]
        third = x_refs[0].shape[0]
        parity = place[2] % 2

        @pl.when(stream == 0)
        def _():
            x_out[pl.ds(pl.multiple_of(parity * third, third), third), :] = x_refs[0][...]
            x_out[pl.ds(pl.multiple_of((1 - parity) * third, third), third), :] = x_refs[1][...]
            x_out[2 * third :, :] = x_refs[2][...]

        x = x_out[...]
    nt = (((1,), (1,)), ((), ()))
    if width % LANES == 0:
        whole = lax.dot_general(x, w_ref[stream], nt, preferred_element_type=jnp.float32).astype(jnp.bfloat16)
        blocks = [whole[:, j * width : (j + 1) * width] for j in range(count)]
    else:
        blocks = [
            lax.dot_general(
                x, w_ref[0, j * width : (j + 1) * width, :], nt, preferred_element_type=jnp.float32
            ).astype(jnp.bfloat16)
            for j in range(count)
        ]
    for mine in range(2):

        @pl.when(core == mine)
        def _():
            for j in range(count):
                at = (j ^ place[0]) // 2
                if j % 2 == mine:
                    keep_ref[at, stream] = blocks[j]
                else:
                    send_ref[at, stream] = blocks[j]


def project(place, xs, w, count):
    tok, feat = sum(x.shape[0] for x in xs), xs[0].shape[1]
    streams, channels, _ = w.shape
    width = channels // count
    part = jax.ShapeDtypeStruct((count // 2, streams, tok, width), jnp.bfloat16)
    wide = width % LANES == 0
    spec = resident(part.shape, width)
    joined = len(xs) > 1
    outs = pl.pallas_call(
        functools.partial(project_kernel, pieces=len(xs), count=count, width=width),
        grid_spec=pltpu.PrefetchScalarGridSpec(
            num_scalar_prefetch=1,
            grid=(streams,),
            in_specs=[resident(x.shape, width) for x in xs]
            + [resident(w.shape, width) if wide else pl.BlockSpec((1, channels, feat), lambda s, _: (s, 0, 0))],
            out_specs=[spec, spec] + [resident((tok, feat), width)] * joined,
        ),
        out_shape=[part, part] + [jax.ShapeDtypeStruct((tok, feat), jnp.bfloat16)] * joined,
        compiler_params=params(10, width),
        cost_estimate=SMALL,
        name="project",
    )(place, *xs, w)
    return outs[0], outs[1], outs[2] if joined else xs[0]


def in_three(value):
    terms = []
    for _ in range(3):
        term = value.astype(jnp.bfloat16)
        value = value - term.astype(jnp.float32)
        terms.append(term)
    return terms


def split_lanes_kernel(place, up_ref, *out_refs):
    n_depth, width = len(out_refs), out_refs[0].shape[2]
    for r, ref in enumerate(out_refs):
        for k in range(ref.shape[0]):
            at = ((place[1] ^ k) * n_depth + (place[0] ^ r)) * width
            ref[k] = up_ref[:, pl.ds(pl.multiple_of(at, width), width)]


def merge_rows_kernel(place, *refs, n_depth):
    in_refs, out_refs = refs[:n_depth], refs[n_depth:]
    local = in_refs[0].shape[1]
    for r, ref in enumerate(in_refs):
        for k, out_ref in enumerate(out_refs):
            out_ref[pl.ds(pl.multiple_of((place[0] ^ r) * local, 16), local), :] = ref[k]


def split_rows_kernel(place, *refs, n_col):
    in_refs, out_refs = refs[:n_col], refs[n_col:]
    local = out_refs[0].shape[1] - 32
    for r, ref in enumerate(out_refs):
        rows = pl.ds(pl.multiple_of((place[0] ^ r) * local, 16), local)
        for k in range(n_col):
            ref[k, 0:local] = in_refs[k][rows, :]
            ref[k, local:] = in_refs[k][-32:, :]


def rearrange(kernel, place, arrays, count, shape, name):
    width = shape[-1]
    return pl.pallas_call(
        kernel,
        grid_spec=pltpu.PrefetchScalarGridSpec(
            num_scalar_prefetch=1,
            grid=(1,),
            in_specs=[resident(value.shape, width) for value in arrays],
            out_specs=[resident(shape, width)] * count,
        ),
        out_shape=[jax.ShapeDtypeStruct(shape, jnp.bfloat16)] * count,
        compiler_params=params(4, width),
        cost_estimate=SMALL,
        name=name,
    )(place, *arrays)


def split_lanes(place, up, n_col, n_depth):
    local, width = up.shape[0], up.shape[1] // (n_col * n_depth)
    if width % LANES:
        blocks = up.reshape(local, n_col, n_depth, width)[:, place[1] ^ jnp.arange(n_col)]
        return [
            jnp.transpose(lax.dynamic_index_in_dim(blocks, place[0] ^ r, 2, keepdims=False), (1, 0, 2))
            for r in range(n_depth)
        ]
    return rearrange(split_lanes_kernel, place, [up], n_depth, (n_col, local, width), "split")


def merge_rows(place, pieces):
    n_depth = len(pieces)
    n_col, local, width = pieces[0].shape
    if width % LANES:
        whole = jnp.stack(pieces)[place[0] ^ jnp.arange(n_depth)]
        return list(jnp.transpose(whole, (1, 0, 2, 3)).reshape(n_col, n_depth * local, width))
    kernel = functools.partial(merge_rows_kernel, n_depth=n_depth)
    return list(rearrange(kernel, place, pieces, n_col, (n_depth * local, width), "merge"))


def split_rows(place, arrays, n_depth):
    local, width = (arrays[0].shape[0] - 32) // n_depth, arrays[0].shape[1]
    if width % LANES:
        whole = jnp.stack(arrays)
        return [
            jnp.concatenate(
                [lax.dynamic_slice_in_dim(whole, (place[0] ^ r) * local, local, axis=1), whole[:, -32:]], axis=1
            )
            for r in range(n_depth)
        ]
    kernel = functools.partial(split_rows_kernel, n_col=len(arrays))
    return rearrange(kernel, place, arrays, n_depth, (len(arrays), local + 32, width), "split")


def join_kernel(place, _, *refs):
    block_refs, (out_ref, grad_taps_ref) = refs[:-2], refs[-2:]
    n_depth = len(block_refs)
    n_col, _, width = block_refs[0].shape
    local, groups = out_ref.shape[0], grad_taps_ref.shape[1]
    lane_group = lax.broadcasted_iota(jnp.int32, (width, groups), 0) // GROUP
    group = lax.broadcasted_iota(jnp.int32, (width, groups), 1)
    total = jnp.zeros((24, groups), jnp.float32)
    for r, ref in enumerate(block_refs):
        for k in range(n_col):
            at = (place[1] ^ k) * n_depth + (place[0] ^ r)
            out_ref[:, pl.ds(pl.multiple_of(at * width, width), width)] = ref[k, 0:local, :]
            spread = (lane_group + at * (width // GROUP) == group).astype(jnp.bfloat16)
            total = total + jnp.dot(ref[k, local : local + 24, :], spread, preferred_element_type=jnp.float32)
    grad_taps_ref[...] = (total[0:8] + total[8:16] + total[16:24])[:KT]


def join(place, mark, blocks, groups):
    n_depth = len(blocks)
    n_col, rows, width = blocks[0].shape
    local = rows - 32
    if width % LANES:
        whole = jnp.stack(blocks)[place[0] ^ jnp.arange(n_depth)][:, place[1] ^ jnp.arange(n_col)]
        sums = whole[:, :, local : local + 24].astype(jnp.float32)
        sums = sums.reshape(n_depth, n_col, 3, 8, width // GROUP, GROUP).sum(axis=(2, 5))[:, :, :KT]
        return (
            jnp.transpose(whole[:, :, :local], (2, 1, 0, 3)).reshape(local, -1),
            jnp.transpose(sums, (2, 1, 0, 3)).reshape(KT, -1),
        )
    channels = n_depth * n_col * width
    return pl.pallas_call(
        join_kernel,
        grid_spec=pltpu.PrefetchScalarGridSpec(
            num_scalar_prefetch=1,
            grid=(1,),
            in_specs=[pl.BlockSpec(memory_space=pl.ANY)] + [resident(blocks[0].shape, width)] * n_depth,
            out_specs=[resident((local, channels), width), resident((KT, groups), width)],
        ),
        out_shape=[
            jax.ShapeDtypeStruct((local, channels), jnp.bfloat16),
            jax.ShapeDtypeStruct((KT, groups), jnp.float32),
        ],
        compiler_params=params(4, width),
        cost_estimate=SMALL,
        name="join",
    )(place, mark, *blocks)


def middle_kernel(place, taps_ref, *refs, groups, terms, tile):
    up_refs, refs = refs[:groups], refs[groups:]
    part_refs = refs[: groups * terms]
    grad_refs = refs[groups * terms : groups * terms + groups]
    out_refs = refs[groups * terms + groups : groups * terms + 2 * groups]
    up_s, out_s, q_s, k_s, v_s, mixed_s, gf_s, far_s = refs[groups * terms + 2 * groups :]
    col = place[1]
    tok = part_refs[0].shape[2]
    width = part_refs[0].shape[3]
    total = groups * tok
    tap_groups = taps_ref.shape[1]
    for k, ref in enumerate(up_refs):
        up_s[pl.ds(pl.multiple_of((col ^ k) * tok, tok), tok), :] = ref[...]
    lane_group = lax.broadcasted_iota(jnp.int32, (tap_groups, width), 1) // GROUP
    group = lax.broadcasted_iota(jnp.int32, (tap_groups, width), 0)
    spread = (lane_group + place[3] * (width // GROUP) == group).astype(jnp.bfloat16)
    taps = sum(jnp.dot(term, spread, preferred_element_type=jnp.float32) for term in in_three(taps_ref[...]))
    mixed_s[0:PAD, :] = jnp.zeros((PAD, width), jnp.float32)
    gf_s[total : total + PAD, :] = jnp.zeros((PAD, width), jnp.float32)
    for k in range(groups):
        start = (col ^ k) * tok
        for i in range(tok // tile):
            inside = slice(i * tile, (i + 1) * tile)
            rows = pl.ds(pl.multiple_of(start + i * tile, tile), tile)
            streams = []
            for s in range(3):
                acc = None
                for ref in part_refs[k * terms : (k + 1) * terms]:
                    term = ref[0, s, inside, :].astype(jnp.float32)
                    acc = term if acc is None else acc + term
                streams.append(acc.astype(jnp.bfloat16))
            q_s[rows, :], k_s[rows, :], v_s[rows, :] = streams
            query, key, value = [stream.astype(jnp.float32) for stream in streams]
            mixed_s[pl.ds(pl.multiple_of(start + i * tile + PAD, PAD), tile), :] = key * value
            gf_s[rows, :] = up_s[rows, :].astype(jnp.float32) * query
    sums = [jnp.zeros((8, width), jnp.float32) for _ in range(KT)]
    for a in range(groups):
        for i in range(tok // tile):
            first = a * tok + i * tile
            rows = slice(first, first + tile)
            inside = slice(i * tile, (i + 1) * tile)
            gf = gf_s[rows, :]
            filtered = jnp.zeros((tile, width), jnp.float32)
            grad_mixed = jnp.zeros((tile, width), jnp.float32)
            for j in range(KT):
                shifted = mixed_s[first + PAD - j : first + PAD - j + tile, :]
                filtered = filtered + taps[j : j + 1, :] * shifted
                sums[j] = sums[j] + (gf * shifted).reshape(tile // 8, 8, width).sum(axis=0)
                grad_mixed = grad_mixed + taps[j : j + 1, :] * gf_s[first + j : first + j + tile, :]
            out_s[a, inside, :] = (q_s[rows, :].astype(jnp.float32) * filtered).astype(jnp.bfloat16)
            at = col ^ a
            far_s[at, 0, inside, :] = (up_s[rows, :].astype(jnp.float32) * filtered).astype(jnp.bfloat16)
            far_s[at, 1, inside, :] = (grad_mixed * v_s[rows, :].astype(jnp.float32)).astype(jnp.bfloat16)
            far_s[at, 2, inside, :] = (grad_mixed * k_s[rows, :].astype(jnp.float32)).astype(jnp.bfloat16)
    for k in range(groups):
        grad_refs[k][...] = far_s[k]
    rest = jnp.concatenate(
        [sums[j].sum(axis=0, keepdims=True) for j in range(KT)] + [jnp.zeros((1, width), jnp.float32)], axis=0
    )
    terms_of = [term.astype(jnp.float32) for term in in_three(rest)]
    packed = jnp.concatenate(terms_of + [jnp.zeros((8, width), jnp.float32)], axis=0).astype(jnp.bfloat16)
    for k, ref in enumerate(out_refs):
        ref[0:tok, :] = out_s[col ^ k]
        ref[tok : tok + 32, :] = packed


def middle(place, taps, ups, parts, tile):
    groups, terms = len(parts), len(parts[0])
    _, _, tok, width = parts[0][0].shape
    total = groups * tok
    whole = lambda *shape: resident(shape, width)
    one = whole(1, 3, tok, width)
    outs = pl.pallas_call(
        functools.partial(middle_kernel, groups=groups, terms=terms, tile=tile),
        grid_spec=pltpu.PrefetchScalarGridSpec(
            num_scalar_prefetch=1,
            grid=(1,),
            in_specs=[whole(*taps.shape)] + [whole(tok, width)] * groups + [one] * (groups * terms),
            out_specs=[whole(3, tok, width)] * groups + [whole(tok + 32, width)] * groups,
            scratch_shapes=[
                pltpu.VMEM((total, width), jnp.bfloat16),
                pltpu.VMEM((groups, tok, width), jnp.bfloat16),
            ]
            + [pltpu.VMEM((total, width), jnp.bfloat16)] * 3
            + [pltpu.VMEM((total + PAD, width), jnp.float32)] * 2
            + [pltpu.VMEM((groups, 3, tok, width), jnp.bfloat16)],
        ),
        out_shape=[jax.ShapeDtypeStruct((3, tok, width), jnp.bfloat16)] * groups
        + [jax.ShapeDtypeStruct((tok + 32, width), jnp.bfloat16)] * groups,
        compiler_params=params(10, width),
        cost_estimate=SMALL,
        name="middle",
    )(place, taps, *ups, *[term for terms_of in parts for term in terms_of])
    return outs[:groups], outs[groups:]


def assemble_kernel(place, *refs):
    grad_refs, out_ref = refs[:-1], refs[-1]
    width = grad_refs[0].shape[2]
    for r, ref in enumerate(grad_refs):
        for s in range(3):
            at = pl.multiple_of((s * len(grad_refs) + (place[0] ^ r)) * width, width)
            out_ref[:, pl.ds(at, width)] = ref[s]


def assemble(place, grads):
    streams, tok, width = grads[0].shape
    out = jax.ShapeDtypeStruct((tok, streams * width * len(grads)), jnp.bfloat16)
    if width % LANES:
        whole = jnp.stack(grads)[place[0] ^ jnp.arange(len(grads))]
        return jnp.transpose(whole, (2, 1, 0, 3)).reshape(out.shape)
    return pl.pallas_call(
        assemble_kernel,
        grid_spec=pltpu.PrefetchScalarGridSpec(
            num_scalar_prefetch=1,
            grid=(1,),
            in_specs=[resident(grads[0].shape, width)] * len(grads),
            out_specs=resident(out.shape, width),
        ),
        out_shape=out,
        compiler_params=params(4, width),
        cost_estimate=SMALL,
        name="assemble",
    )(place, *grads)


def input_grad_kernel(grad_ref, w_ref, *out_refs, first):
    step = out_refs[0].shape[1]
    own = slice(first * step, (first + 1) * step) if len(out_refs) == 1 else slice(None)
    acc = jnp.dot(grad_ref[...], w_ref[:, :, own].reshape(-1, step), preferred_element_type=jnp.float32)
    acc = acc.astype(jnp.bfloat16)
    for i, out_ref in enumerate(out_refs):

        @pl.when(pl.program_id(0) == i)
        def _():
            out_ref[...] = acc


def input_grad(grad, w, first, last, chunks, width):
    tok = grad.shape[0]
    streams, channels, feat = w.shape
    step = feat // chunks
    count = last - first
    if width % LANES:
        rows = w[:, :, first * step : last * step].reshape(streams * channels, count * step)
        whole = jnp.dot(grad, rows, preferred_element_type=jnp.float32).astype(jnp.bfloat16)
        return [whole[:, i * step : (i + 1) * step] for i in range(count)]
    return list(
        pl.pallas_call(
            functools.partial(input_grad_kernel, first=first),
            grid=(count,),
            in_specs=[
                resident(grad.shape, width),
                resident(w.shape, width)
                if count == 1
                else pl.BlockSpec((streams, channels, step), lambda i: (0, 0, first + i)),
            ],
            out_specs=[resident((tok, step), width)] * count,
            out_shape=[jax.ShapeDtypeStruct((tok, step), jnp.bfloat16)] * count,
            compiler_params=params(12, width),
            cost_estimate=SMALL,
            name="input_grad",
        )(grad, w)
    )


def weight_grad_kernel(*refs, chained, groups, half):
    refs = refs[2 * chained :]
    grad_refs, x_refs = refs[:groups], refs[groups : 2 * groups]
    out_ref, mark_ref, turned = refs[2 * groups :]
    mark_ref[...] = jnp.zeros(mark_ref.shape, jnp.float32)
    streams, channels, step = out_ref.shape
    tok = x_refs[0].shape[0]

    @pl.when(pl.program_id(0) == 0)
    def _():
        for k in range(groups):
            for s in range(streams):
                at = (2 * s + half) * channels
                block = grad_refs[k][:, at : at + channels]
                turned[s * channels : (s + 1) * channels, k * tok : (k + 1) * tok] = block.T

    columns = pl.ds(pl.multiple_of(pl.program_id(0) * step, step), step)
    acc = None
    for k in range(groups):
        term = jnp.dot(turned[:, k * tok : (k + 1) * tok], x_refs[k][:, columns], preferred_element_type=jnp.float32)
        acc = term if acc is None else acc + term
    for s in range(streams):
        out_ref[s] = acc[s * channels : (s + 1) * channels, :]


def weight_grad(filled, grads, xs, half, streams, width):
    groups = len(xs)
    tok, feat = xs[0].shape
    channels = grads[0].shape[1] // streams
    chained = filled is not None
    if width % LANES:
        if chained:
            return filled
        terms = [
            lax.dot_general(grad, x, (((0,), (0,)), ((), ())), preferred_element_type=jnp.float32)
            for grad, x in zip(grads, xs)
        ]
        return sum(terms).reshape(streams, channels, feat), jnp.zeros((8, LANES), jnp.float32)
    step = min(512, feat)
    return pl.pallas_call(
        functools.partial(weight_grad_kernel, chained=chained, groups=groups, half=half),
        grid=(feat // step,),
        in_specs=[pl.BlockSpec(memory_space=pl.ANY)] * (2 * chained)
        + [resident(grads[0].shape, width)] * groups
        + [resident((tok, feat), width)] * groups,
        out_specs=[
            pl.BlockSpec((streams, channels // 2, step), lambda i: (0, half, i)),
            resident((8, LANES), width),
        ],
        scratch_shapes=[pltpu.VMEM((streams * channels // 2, groups * tok), jnp.bfloat16)],
        out_shape=[
            jax.ShapeDtypeStruct((streams, channels, feat), jnp.float32),
            jax.ShapeDtypeStruct((8, LANES), jnp.float32),
        ],
        input_output_aliases={0: 0} if chained else {},
        compiler_params=params(14, width),
        cost_estimate=SMALL,
        name="weight_grad",
    )(*(filled if chained else []), *grads, *xs)


def added(first, second):
    return (first.astype(jnp.float32) + second.astype(jnp.float32)).astype(jnp.bfloat16)


def cut_kernel(_, own_ref, last_ref, own_out, last_out):
    own_out[...] = own_ref[...]
    last_out[...] = last_ref[...]


def cut(place, tokens):
    tok, feat = tokens.shape
    if tok % 48 or lax.axis_size("row") % 2:
        return None
    third = tok // 3
    out = jax.ShapeDtypeStruct((third, feat), jnp.bfloat16)
    return pl.pallas_call(
        cut_kernel,
        grid_spec=pltpu.PrefetchScalarGridSpec(
            num_scalar_prefetch=1,
            grid=(1,),
            in_specs=[
                pl.BlockSpec((third, feat), lambda i, at: (at[2] % 2, 0)),
                pl.BlockSpec((third, feat), lambda i, at: (2, 0)),
            ],
            out_specs=[pl.BlockSpec(memory_space=pltpu.VMEM)] * 2,
        ),
        out_shape=[out, out],
        compiler_params=params(10, LANES),
        cost_estimate=SMALL,
        name="cut",
    )(place, tokens, tokens)


def put_kernel(place, *refs):
    pair_ref, summed_ref, out_ref = refs[-3:]
    outer = (place[2] == 0) | (place[2] == 3)

    @pl.when(outer)
    def _():
        out_ref[...] = pair_ref[...]

    @pl.when(jnp.logical_not(outer))
    def _():
        out_ref[...] = summed_ref[...]


def put(place, filled, pair, summed, chunk, feat):
    tok, step = pair.shape
    chained = filled is not None
    return pl.pallas_call(
        put_kernel,
        grid_spec=pltpu.PrefetchScalarGridSpec(
            num_scalar_prefetch=1,
            grid=(1,),
            in_specs=[pl.BlockSpec(memory_space=pl.ANY)] * chained + [resident((tok, step), LANES)] * 2,
            out_specs=pl.BlockSpec((tok, step), lambda i, _: (0, chunk)),
        ),
        out_shape=jax.ShapeDtypeStruct((tok, feat), jnp.bfloat16),
        input_output_aliases={1: 0} if chained else {},
        compiler_params=params(6, LANES),
        cost_estimate=SMALL,
        name="put",
    )(place, *([filled] if chained else []), pair, summed)


def on_device(tokens, weight, taps, upstream):
    n_col = lax.axis_size("col")
    n_depth = lax.axis_size("depth")
    local_tok = upstream.shape[0]
    depth_at = lax.axis_index("depth")
    col_at = lax.axis_index("col")
    row_at = lax.axis_index("row")
    place = jnp.stack([depth_at, col_at, row_at, col_at * n_depth + depth_at]).astype(jnp.int32)
    w = jnp.transpose(weight, (1, 0, 2))
    width = w.shape[1] // n_depth
    def project_and_sum(x_pieces, *earlier):
        keep, send, x = project(place, x_pieces, w, n_depth)
        near = swap(after(send, *earlier) if earlier else send, "depth", 1)
        pairs = [added(keep[r // 2], near[r // 2])[None] for r in range(2, n_depth, 2)]
        fars = [swap(pair, "depth", 2 * i + 2) for i, pair in enumerate(pairs)]
        return x, [keep, near] + fars, pairs, fars

    thirds = cut(place, tokens)
    first = [[swap(tokens if thirds is None else thirds[0], "col", k)] for k in range(1, n_col)]
    ups = split_lanes(place, upstream, n_col, n_depth)
    ups = [up if r == 0 else swap(up, "depth", r) for r, up in enumerate(ups)]
    x, terms, pairs, fars = project_and_sum([tokens], *[piece for of in first for piece in of], *ups[1:])
    xs, parts = [x], [terms]
    for k in range(1, n_col):
        x_pieces = first[k - 1]
        if thirds is not None:
            x_pieces += [swap(x_pieces[0], "row", 1), swap(after(thirds[1], *x_pieces), "col", k)]
        x_pieces[-1] = after(x_pieces[-1], *fars)
        x, terms, pairs, fars = project_and_sum(x_pieces)
        xs.append(x)
        parts.append(terms)
    ups = merge_rows(place, [after(ups[0], *pairs)] + ups[1:])
    ups = [up if k == 0 else swap(up, "col", k) for k, up in enumerate(ups)]
    own_grads, blocks = middle(place, taps, ups, parts, local_tok)
    nears = [swap(own, "depth", 1) for own in own_grads]
    blocks = [block if k == 0 else swap(block, "col", k) for k, block in enumerate(blocks)]
    beside = nears + blocks[1:]
    chunks = 4
    grads = [None] * n_col
    ready = []
    sent = []
    lhs = [None] * n_col
    for k in reversed(range(n_col)):
        fars = [swap(after(own_grads[k], *ready) if ready else own_grads[k], "depth", r) for r in range(2, n_depth, 2)]
        ready = fars
        if k > 0:
            fars = [after(far, *beside) for far in fars]
        elif sent:
            fars = [after(far, sent[-1][1][-1]) for far in fars]
        grads[k] = [own_grads[k], nears[k]]
        for far in fars:
            grads[k] += [far, swap(far, "depth", 1)]
        ready = grads[k][2:]
        lhs[k] = assemble(place, grads[k])
        if k > 0:
            parts_of = input_grad(lhs[k], w, 0, 1, chunks, width)
            parts_of += input_grad(after(lhs[k], *parts_of), w, 1, chunks, chunks, width)
            sent.append(([swap(part, "col", k) for part in parts_of[:3]], parts_of))
    held = [parts_of[3:] for _, parts_of in sent]
    sent = [of for of, _ in sent]
    own_part = input_grad(lhs[0], w, 0, 1, chunks, width)
    outer = (row_at == 0) | (row_at == 3)
    line = lax.axis_size("row") == 4
    inward, across, summed, done = ([None] * chunks for _ in range(4))
    pair = cross = filled = grad_tokens = None
    marks = []
    for slot in range(chunks + 3):
        if slot < chunks:
            total = after(own_part[slot], *marks).astype(jnp.float32)
            for of in sent:
                total = total + of[slot].astype(jnp.float32)
            inward[slot] = total.astype(jnp.bfloat16)
            marks = [inward[slot]]
        if not line:
            if slot < chunks:
                done[slot] = lax.psum(inward[slot], "row")
        else:
            if 0 <= slot - 1 < chunks:
                across[slot - 1] = added(after(inward[slot - 1], *marks), pair)
                marks = [across[slot - 1]]
            if 0 <= slot - 2 < chunks:
                summed[slot - 2] = added(after(across[slot - 2], *marks), cross)
                marks = [summed[slot - 2]]
            if 0 <= slot - 3 < chunks:
                grad_tokens = put(place, grad_tokens, pair, summed[slot - 3], slot - 3, tokens.shape[1])
            if slot < chunks + 2:
                out = summed[slot - 2] if slot >= 2 else inward[slot]
                pair = swap(jnp.where(outer, inward[slot], out) if slot < chunks else out, "row", 1)
            if 0 <= slot - 1 < chunks:
                cross = lax.ppermute(across[slot - 1], "row", [(0, 0), (1, 2), (2, 1), (3, 3)])
        if slot == 0:
            own_part += input_grad(after(lhs[0], *marks), w, 1, chunks, chunks, width)
            marks = [own_part[1]]
        if slot == 1:
            for k, parts_of in enumerate(held):
                sent[k] += [swap(after(part, *marks), "col", k + 1) for part in parts_of]
        if slot == 2:
            marks += [of[-1] for of in sent]
        if slot in (2, 3):
            filled = weight_grad(filled, [after(lhs[0], *marks)] + lhs[1:], xs, slot - 2, 3, width)
            marks = [filled[1]]
        if slot == chunks:
            blocks = split_rows(place, [after(blocks[0], *marks)] + blocks[1:], n_depth)
            blocks = [block if r == 0 else swap(block, "depth", r) for r, block in enumerate(blocks)]
            marks += blocks[1:]
    if not line:
        grad_tokens = jnp.concatenate(done, axis=1)
    output, grad_taps = join(place, filled[1], [after(blocks[0], *marks)] + blocks[1:], taps.shape[1])
    grad_weight = jnp.transpose(filled[0], (1, 0, 2))
    return (output, grad_tokens, grad_weight, grad_taps)


def solution(mesh):
    in_specs = (
        P("col", "depth"),
        P(("row", "col"), None, "depth"),
        P(None, "row"),
        P(("col", "depth"), "row"),
    )
    out_specs = (
        P(("col", "depth"), "row"),
        P("col", "depth"),
        P(("row", "col"), None, "depth"),
        P(None, "row"),
    )
    return jax.shard_map(
        on_device, mesh=mesh, in_specs=in_specs, out_specs=out_specs, check_vma=False
    )
```

```python
import functools

import jax
import jax.numpy as jnp
from jax import lax
from jax.experimental import pallas as pl
from jax.experimental.pallas import tpu as pltpu
from jax.sharding import PartitionSpec as P

GROUP = 16
KT = 7
PAD = 8
LANES = 128
MIB = 1024 * 1024
SMALL = pl.CostEstimate(flops=1, bytes_accessed=1, transcendentals=0)


def swap(value, axis, flip):
    count = lax.axis_size(axis)
    return lax.ppermute(value, axis, [(i, i ^ flip) for i in range(count)])


def after(value, *earlier):
    return lax.optimization_barrier((value, *earlier))[0]


def resident(shape, width):
    if width % LANES == 0:
        return pl.BlockSpec(memory_space=pltpu.VMEM)
    return pl.BlockSpec(tuple(shape), lambda *_: (0,) * len(shape), pipeline_mode=pl.Buffered(1))


def params(mib, width):
    return pltpu.CompilerParams(vmem_limit_bytes=(mib if width % LANES == 0 else 56) * MIB)


def project_kernel(place, *refs, pieces, count, width):
    x_refs = refs[:pieces]
    w_ref, keep_ref, send_ref = refs[pieces : pieces + 3]
    stream = pl.program_id(0)
    core = place[0] % 2
    if pieces == 1:
        x = x_refs[0][...]
    else:
        x_out = refs[pieces + 3]
        third = x_refs[0].shape[0]
        parity = place[2] % 2

        @pl.when(stream == 0)
        def _():
            x_out[pl.ds(pl.multiple_of(parity * third, third), third), :] = x_refs[0][...]
            x_out[pl.ds(pl.multiple_of((1 - parity) * third, third), third), :] = x_refs[1][...]
            x_out[2 * third :, :] = x_refs[2][...]

        x = x_out[...]
    nt = (((1,), (1,)), ((), ()))
    if width % LANES == 0:
        whole = lax.dot_general(x, w_ref[stream], nt, preferred_element_type=jnp.float32).astype(jnp.bfloat16)
        blocks = [whole[:, j * width : (j + 1) * width] for j in range(count)]
    else:
        blocks = [
            lax.dot_general(
                x, w_ref[0, j * width : (j + 1) * width, :], nt, preferred_element_type=jnp.float32
            ).astype(jnp.bfloat16)
            for j in range(count)
        ]
    for mine in range(2):

        @pl.when(core == mine)
        def _():
            for j in range(count):
                at = (j ^ place[0]) // 2
                if j % 2 == mine:
                    keep_ref[at, stream] = blocks[j]
                else:
                    send_ref[at, stream] = blocks[j]


def project(place, xs, w, count):
    tok, feat = sum(x.shape[0] for x in xs), xs[0].shape[1]
    streams, channels, _ = w.shape
    width = channels // count
    part = jax.ShapeDtypeStruct((count // 2, streams, tok, width), jnp.bfloat16)
    wide = width % LANES == 0
    spec = resident(part.shape, width)
    joined = len(xs) > 1
    outs = pl.pallas_call(
        functools.partial(project_kernel, pieces=len(xs), count=count, width=width),
        grid_spec=pltpu.PrefetchScalarGridSpec(
            num_scalar_prefetch=1,
            grid=(streams,),
            in_specs=[resident(x.shape, width) for x in xs]
            + [resident(w.shape, width) if wide else pl.BlockSpec((1, channels, feat), lambda s, _: (s, 0, 0))],
            out_specs=[spec, spec] + [resident((tok, feat), width)] * joined,
        ),
        out_shape=[part, part] + [jax.ShapeDtypeStruct((tok, feat), jnp.bfloat16)] * joined,
        compiler_params=params(10, width),
        cost_estimate=SMALL,
        name="project",
    )(place, *xs, w)
    return outs[0], outs[1], outs[2] if joined else xs[0]


def in_three(value):
    terms = []
    for _ in range(3):
        term = value.astype(jnp.bfloat16)
        value = value - term.astype(jnp.float32)
        terms.append(term)
    return terms


def split_lanes_kernel(place, up_ref, *out_refs):
    n_depth, width = len(out_refs), out_refs[0].shape[2]
    for r, ref in enumerate(out_refs):
        for k in range(ref.shape[0]):
            at = ((place[1] ^ k) * n_depth + (place[0] ^ r)) * width
            ref[k] = up_ref[:, pl.ds(pl.multiple_of(at, width), width)]


def merge_rows_kernel(place, *refs, n_depth):
    in_refs, out_refs = refs[:n_depth], refs[n_depth:]
    local = in_refs[0].shape[1]
    for r, ref in enumerate(in_refs):
        for k, out_ref in enumerate(out_refs):
            out_ref[pl.ds(pl.multiple_of((place[0] ^ r) * local, 16), local), :] = ref[k]


def split_rows_kernel(place, *refs, n_col):
    in_refs, out_refs = refs[:n_col], refs[n_col:]
    local = out_refs[0].shape[1] - 32
    for r, ref in enumerate(out_refs):
        rows = pl.ds(pl.multiple_of((place[0] ^ r) * local, 16), local)
        for k in range(n_col):
            ref[k, 0:local] = in_refs[k][rows, :]
            ref[k, local:] = in_refs[k][-32:, :]


def rearrange(kernel, place, arrays, count, shape, name):
    width = shape[-1]
    return pl.pallas_call(
        kernel,
        grid_spec=pltpu.PrefetchScalarGridSpec(
            num_scalar_prefetch=1,
            grid=(1,),
            in_specs=[resident(value.shape, width) for value in arrays],
            out_specs=[resident(shape, width)] * count,
        ),
        out_shape=[jax.ShapeDtypeStruct(shape, jnp.bfloat16)] * count,
        compiler_params=params(4, width),
        cost_estimate=SMALL,
        name=name,
    )(place, *arrays)


def split_lanes(place, up, n_col, n_depth):
    local, width = up.shape[0], up.shape[1] // (n_col * n_depth)
    if width % LANES:
        blocks = up.reshape(local, n_col, n_depth, width)[:, place[1] ^ jnp.arange(n_col)]
        return [
            jnp.transpose(lax.dynamic_index_in_dim(blocks, place[0] ^ r, 2, keepdims=False), (1, 0, 2))
            for r in range(n_depth)
        ]
    return rearrange(split_lanes_kernel, place, [up], n_depth, (n_col, local, width), "split")


def merge_rows(place, pieces):
    n_depth = len(pieces)
    n_col, local, width = pieces[0].shape
    if width % LANES:
        whole = jnp.stack(pieces)[place[0] ^ jnp.arange(n_depth)]
        return list(jnp.transpose(whole, (1, 0, 2, 3)).reshape(n_col, n_depth * local, width))
    kernel = functools.partial(merge_rows_kernel, n_depth=n_depth)
    return list(rearrange(kernel, place, pieces, n_col, (n_depth * local, width), "merge"))


def split_rows(place, arrays, n_depth):
    local, width = (arrays[0].shape[0] - 32) // n_depth, arrays[0].shape[1]
    if width % LANES:
        whole = jnp.stack(arrays)
        return [
            jnp.concatenate(
                [lax.dynamic_slice_in_dim(whole, (place[0] ^ r) * local, local, axis=1), whole[:, -32:]], axis=1
            )
            for r in range(n_depth)
        ]
    kernel = functools.partial(split_rows_kernel, n_col=len(arrays))
    return rearrange(kernel, place, arrays, n_depth, (len(arrays), local + 32, width), "split")


def join_kernel(place, _, *refs):
    block_refs, (out_ref, grad_taps_ref) = refs[:-2], refs[-2:]
    n_depth = len(block_refs)
    n_col, _, width = block_refs[0].shape
    local, groups = out_ref.shape[0], grad_taps_ref.shape[1]
    lane_group = lax.broadcasted_iota(jnp.int32, (width, groups), 0) // GROUP
    group = lax.broadcasted_iota(jnp.int32, (width, groups), 1)
    total = jnp.zeros((24, groups), jnp.float32)
    for r, ref in enumerate(block_refs):
        for k in range(n_col):
            at = (place[1] ^ k) * n_depth + (place[0] ^ r)
            out_ref[:, pl.ds(pl.multiple_of(at * width, width), width)] = ref[k, 0:local, :]
            spread = (lane_group + at * (width // GROUP) == group).astype(jnp.bfloat16)
            total = total + jnp.dot(ref[k, local : local + 24, :], spread, preferred_element_type=jnp.float32)
    grad_taps_ref[...] = (total[0:8] + total[8:16] + total[16:24])[:KT]


def join(place, mark, blocks, groups):
    n_depth = len(blocks)
    n_col, rows, width = blocks[0].shape
    local = rows - 32
    if width % LANES:
        whole = jnp.stack(blocks)[place[0] ^ jnp.arange(n_depth)][:, place[1] ^ jnp.arange(n_col)]
        sums = whole[:, :, local : local + 24].astype(jnp.float32)
        sums = sums.reshape(n_depth, n_col, 3, 8, width // GROUP, GROUP).sum(axis=(2, 5))[:, :, :KT]
        return (
            jnp.transpose(whole[:, :, :local], (2, 1, 0, 3)).reshape(local, -1),
            jnp.transpose(sums, (2, 1, 0, 3)).reshape(KT, -1),
        )
    channels = n_depth * n_col * width
    return pl.pallas_call(
        join_kernel,
        grid_spec=pltpu.PrefetchScalarGridSpec(
            num_scalar_prefetch=1,
            grid=(1,),
            in_specs=[pl.BlockSpec(memory_space=pl.ANY)] + [resident(blocks[0].shape, width)] * n_depth,
            out_specs=[resident((local, channels), width), resident((KT, groups), width)],
        ),
        out_shape=[
            jax.ShapeDtypeStruct((local, channels), jnp.bfloat16),
            jax.ShapeDtypeStruct((KT, groups), jnp.float32),
        ],
        compiler_params=params(4, width),
        cost_estimate=SMALL,
        name="join",
    )(place, mark, *blocks)


def middle_kernel(place, taps_ref, *refs, groups, terms, tile):
    up_refs, refs = refs[:groups], refs[groups:]
    part_refs = refs[: groups * terms]
    grad_refs = refs[groups * terms : groups * terms + groups]
    out_refs = refs[groups * terms + groups : groups * terms + 2 * groups]
    up_s, out_s, q_s, k_s, v_s, mixed_s, gf_s, far_s = refs[groups * terms + 2 * groups :]
    col = place[1]
    tok = part_refs[0].shape[2]
    width = part_refs[0].shape[3]
    total = groups * tok
    tap_groups = taps_ref.shape[1]
    for k, ref in enumerate(up_refs):
        up_s[pl.ds(pl.multiple_of((col ^ k) * tok, tok), tok), :] = ref[...]
    lane_group = lax.broadcasted_iota(jnp.int32, (tap_groups, width), 1) // GROUP
    group = lax.broadcasted_iota(jnp.int32, (tap_groups, width), 0)
    spread = (lane_group + place[3] * (width // GROUP) == group).astype(jnp.bfloat16)
    taps = sum(jnp.dot(term, spread, preferred_element_type=jnp.float32) for term in in_three(taps_ref[...]))
    mixed_s[0:PAD, :] = jnp.zeros((PAD, width), jnp.float32)
    gf_s[total : total + PAD, :] = jnp.zeros((PAD, width), jnp.float32)
    for k in range(groups):
        start = (col ^ k) * tok
        for i in range(tok // tile):
            inside = slice(i * tile, (i + 1) * tile)
            rows = pl.ds(pl.multiple_of(start + i * tile, tile), tile)
            streams = []
            for s in range(3):
                acc = None
                for ref in part_refs[k * terms : (k + 1) * terms]:
                    term = ref[0, s, inside, :].astype(jnp.float32)
                    acc = term if acc is None else acc + term
                streams.append(acc.astype(jnp.bfloat16))
            q_s[rows, :], k_s[rows, :], v_s[rows, :] = streams
            query, key, value = [stream.astype(jnp.float32) for stream in streams]
            mixed_s[pl.ds(pl.multiple_of(start + i * tile + PAD, PAD), tile), :] = key * value
            gf_s[rows, :] = up_s[rows, :].astype(jnp.float32) * query
    sums = [jnp.zeros((8, width), jnp.float32) for _ in range(KT)]
    for a in range(groups):
        for i in range(tok // tile):
            first = a * tok + i * tile
            rows = slice(first, first + tile)
            inside = slice(i * tile, (i + 1) * tile)
            gf = gf_s[rows, :]
            filtered = jnp.zeros((tile, width), jnp.float32)
            grad_mixed = jnp.zeros((tile, width), jnp.float32)
            for j in range(KT):
                shifted = mixed_s[first + PAD - j : first + PAD - j + tile, :]
                filtered = filtered + taps[j : j + 1, :] * shifted
                sums[j] = sums[j] + (gf * shifted).reshape(tile // 8, 8, width).sum(axis=0)
                grad_mixed = grad_mixed + taps[j : j + 1, :] * gf_s[first + j : first + j + tile, :]
            out_s[a, inside, :] = (q_s[rows, :].astype(jnp.float32) * filtered).astype(jnp.bfloat16)
            at = col ^ a
            far_s[at, 0, inside, :] = (up_s[rows, :].astype(jnp.float32) * filtered).astype(jnp.bfloat16)
            far_s[at, 1, inside, :] = (grad_mixed * v_s[rows, :].astype(jnp.float32)).astype(jnp.bfloat16)
            far_s[at, 2, inside, :] = (grad_mixed * k_s[rows, :].astype(jnp.float32)).astype(jnp.bfloat16)
    for k in range(groups):
        grad_refs[k][...] = far_s[k]
    rest = jnp.concatenate(
        [sums[j].sum(axis=0, keepdims=True) for j in range(KT)] + [jnp.zeros((1, width), jnp.float32)], axis=0
    )
    terms_of = [term.astype(jnp.float32) for term in in_three(rest)]
    packed = jnp.concatenate(terms_of + [jnp.zeros((8, width), jnp.float32)], axis=0).astype(jnp.bfloat16)
    for k, ref in enumerate(out_refs):
        ref[0:tok, :] = out_s[col ^ k]
        ref[tok : tok + 32, :] = packed


def middle(place, taps, ups, parts, tile):
    groups, terms = len(parts), len(parts[0])
    _, _, tok, width = parts[0][0].shape
    total = groups * tok
    whole = lambda *shape: resident(shape, width)
    one = whole(1, 3, tok, width)
    outs = pl.pallas_call(
        functools.partial(middle_kernel, groups=groups, terms=terms, tile=tile),
        grid_spec=pltpu.PrefetchScalarGridSpec(
            num_scalar_prefetch=1,
            grid=(1,),
            in_specs=[whole(*taps.shape)] + [whole(tok, width)] * groups + [one] * (groups * terms),
            out_specs=[whole(3, tok, width)] * groups + [whole(tok + 32, width)] * groups,
            scratch_shapes=[
                pltpu.VMEM((total, width), jnp.bfloat16),
                pltpu.VMEM((groups, tok, width), jnp.bfloat16),
            ]
            + [pltpu.VMEM((total, width), jnp.bfloat16)] * 3
            + [pltpu.VMEM((total + PAD, width), jnp.float32)] * 2
            + [pltpu.VMEM((groups, 3, tok, width), jnp.bfloat16)],
        ),
        out_shape=[jax.ShapeDtypeStruct((3, tok, width), jnp.bfloat16)] * groups
        + [jax.ShapeDtypeStruct((tok + 32, width), jnp.bfloat16)] * groups,
        compiler_params=params(10, width),
        cost_estimate=SMALL,
        name="middle",
    )(place, taps, *ups, *[term for terms_of in parts for term in terms_of])
    return outs[:groups], outs[groups:]


def assemble_kernel(place, *refs):
    grad_refs, out_ref = refs[:-1], refs[-1]
    width = grad_refs[0].shape[2]
    for r, ref in enumerate(grad_refs):
        for s in range(3):
            at = pl.multiple_of((s * len(grad_refs) + (place[0] ^ r)) * width, width)
            out_ref[:, pl.ds(at, width)] = ref[s]


def assemble(place, grads):
    streams, tok, width = grads[0].shape
    out = jax.ShapeDtypeStruct((tok, streams * width * len(grads)), jnp.bfloat16)
    if width % LANES:
        whole = jnp.stack(grads)[place[0] ^ jnp.arange(len(grads))]
        return jnp.transpose(whole, (2, 1, 0, 3)).reshape(out.shape)
    return pl.pallas_call(
        assemble_kernel,
        grid_spec=pltpu.PrefetchScalarGridSpec(
            num_scalar_prefetch=1,
            grid=(1,),
            in_specs=[resident(grads[0].shape, width)] * len(grads),
            out_specs=resident(out.shape, width),
        ),
        out_shape=out,
        compiler_params=params(4, width),
        cost_estimate=SMALL,
        name="assemble",
    )(place, *grads)


def input_grad_kernel(grad_ref, w_ref, out_ref, *, first):
    step = out_ref.shape[1]
    rows = w_ref[:, :, first * step : (first + 1) * step].reshape(-1, step)
    out_ref[...] = jnp.dot(grad_ref[...], rows, preferred_element_type=jnp.float32).astype(jnp.bfloat16)


def input_grads_kernel(grad_ref, w_ref, *refs, first):
    out_refs, (slots, sems) = refs[:-2], refs[-2:]
    step = out_refs[0].shape[1]

    def fetch(i):
        columns = pl.ds((first + i) * step, step)
        return pltpu.make_async_copy(w_ref.at[:, :, columns], slots.at[i % 2], sems.at[i % 2])

    fetch(0).start()
    for i, out_ref in enumerate(out_refs):
        if i + 1 < len(out_refs):
            fetch(i + 1).start()
        fetch(i).wait()
        rows = slots[i % 2].reshape(-1, step)
        out_ref[...] = jnp.dot(grad_ref[...], rows, preferred_element_type=jnp.float32).astype(jnp.bfloat16)


def input_grad(grad, w, first, last, chunks, width):
    tok = grad.shape[0]
    streams, channels, feat = w.shape
    step = feat // chunks
    count = last - first
    if width % LANES:
        rows = w[:, :, first * step : last * step].reshape(streams * channels, count * step)
        whole = jnp.dot(grad, rows, preferred_element_type=jnp.float32).astype(jnp.bfloat16)
        return [whole[:, i * step : (i + 1) * step] for i in range(count)]
    single = count == 1
    return list(
        pl.pallas_call(
            functools.partial(input_grad_kernel if single else input_grads_kernel, first=first),
            in_specs=[
                resident(grad.shape, width),
                pl.BlockSpec(memory_space=pltpu.VMEM if single else pltpu.HBM),
            ],
            out_specs=[resident((tok, step), width)] * count,
            out_shape=[jax.ShapeDtypeStruct((tok, step), jnp.bfloat16)] * count,
            scratch_shapes=[]
            if single
            else [pltpu.VMEM((2, streams, channels, step), jnp.bfloat16), pltpu.SemaphoreType.DMA((2,))],
            compiler_params=params(8, width),
            cost_estimate=SMALL,
            name="input_grad",
        )(grad, w)
    )


def weight_grad_kernel(*refs, chained, groups, half):
    refs = refs[2 * chained :]
    grad_refs, x_refs = refs[:groups], refs[groups : 2 * groups]
    out_ref, mark_ref, turned = refs[2 * groups :]
    mark_ref[...] = jnp.zeros(mark_ref.shape, jnp.float32)
    streams, channels, step = out_ref.shape
    tok = x_refs[0].shape[0]

    @pl.when(pl.program_id(0) == 0)
    def _():
        for k in range(groups):
            for s in range(streams):
                at = (2 * s + half) * channels
                block = grad_refs[k][:, at : at + channels]
                turned[s * channels : (s + 1) * channels, k * tok : (k + 1) * tok] = block.T

    columns = pl.ds(pl.multiple_of(pl.program_id(0) * step, step), step)
    acc = None
    for k in range(groups):
        term = jnp.dot(turned[:, k * tok : (k + 1) * tok], x_refs[k][:, columns], preferred_element_type=jnp.float32)
        acc = term if acc is None else acc + term
    for s in range(streams):
        out_ref[s] = acc[s * channels : (s + 1) * channels, :]


def weight_grad(filled, grads, xs, half, streams, width):
    groups = len(xs)
    tok, feat = xs[0].shape
    channels = grads[0].shape[1] // streams
    chained = filled is not None
    if width % LANES:
        if chained:
            return filled
        terms = [
            lax.dot_general(grad, x, (((0,), (0,)), ((), ())), preferred_element_type=jnp.float32)
            for grad, x in zip(grads, xs)
        ]
        return sum(terms).reshape(streams, channels, feat), jnp.zeros((8, LANES), jnp.float32)
    step = min(512, feat)
    return pl.pallas_call(
        functools.partial(weight_grad_kernel, chained=chained, groups=groups, half=half),
        grid=(feat // step,),
        in_specs=[pl.BlockSpec(memory_space=pl.ANY)] * (2 * chained)
        + [resident(grads[0].shape, width)] * groups
        + [resident((tok, feat), width)] * groups,
        out_specs=[
            pl.BlockSpec((streams, channels // 2, step), lambda i: (0, half, i)),
            resident((8, LANES), width),
        ],
        scratch_shapes=[pltpu.VMEM((streams * channels // 2, groups * tok), jnp.bfloat16)],
        out_shape=[
            jax.ShapeDtypeStruct((streams, channels, feat), jnp.float32),
            jax.ShapeDtypeStruct((8, LANES), jnp.float32),
        ],
        input_output_aliases={0: 0} if chained else {},
        compiler_params=params(14, width),
        cost_estimate=SMALL,
        name="weight_grad",
    )(*(filled if chained else []), *grads, *xs)


def added(first, second):
    return (first.astype(jnp.float32) + second.astype(jnp.float32)).astype(jnp.bfloat16)


def cut_kernel(_, own_ref, last_ref, own_out, last_out):
    own_out[...] = own_ref[...]
    last_out[...] = last_ref[...]


def cut(place, tokens):
    tok, feat = tokens.shape
    if tok % 48 or lax.axis_size("row") % 2:
        return None
    third = tok // 3
    out = jax.ShapeDtypeStruct((third, feat), jnp.bfloat16)
    return pl.pallas_call(
        cut_kernel,
        grid_spec=pltpu.PrefetchScalarGridSpec(
            num_scalar_prefetch=1,
            grid=(1,),
            in_specs=[
                pl.BlockSpec((third, feat), lambda i, at: (at[2] % 2, 0)),
                pl.BlockSpec((third, feat), lambda i, at: (2, 0)),
            ],
            out_specs=[pl.BlockSpec(memory_space=pltpu.VMEM)] * 2,
        ),
        out_shape=[out, out],
        compiler_params=params(10, LANES),
        cost_estimate=SMALL,
        name="cut",
    )(place, tokens, tokens)


def on_device(tokens, weight, taps, upstream):
    n_col = lax.axis_size("col")
    n_depth = lax.axis_size("depth")
    local_tok = upstream.shape[0]
    depth_at = lax.axis_index("depth")
    col_at = lax.axis_index("col")
    row_at = lax.axis_index("row")
    place = jnp.stack([depth_at, col_at, row_at, col_at * n_depth + depth_at]).astype(jnp.int32)
    w = jnp.transpose(weight, (1, 0, 2))
    width = w.shape[1] // n_depth
    def project_and_sum(x_pieces, *earlier):
        keep, send, x = project(place, x_pieces, w, n_depth)
        near = swap(after(send, *earlier) if earlier else send, "depth", 1)
        pairs = [added(keep[r // 2], near[r // 2])[None] for r in range(2, n_depth, 2)]
        fars = [swap(pair, "depth", 2 * i + 2) for i, pair in enumerate(pairs)]
        return x, [keep, near] + fars, pairs, fars

    thirds = cut(place, tokens)
    first = [[swap(tokens if thirds is None else thirds[0], "col", k)] for k in range(1, n_col)]
    ups = split_lanes(place, upstream, n_col, n_depth)
    ups = [up if r == 0 else swap(up, "depth", r) for r, up in enumerate(ups)]
    x, terms, pairs, fars = project_and_sum([tokens], *[piece for of in first for piece in of], *ups[1:])
    xs, parts = [x], [terms]
    for k in range(1, n_col):
        x_pieces = first[k - 1]
        if thirds is not None:
            x_pieces += [swap(x_pieces[0], "row", 1), swap(after(thirds[1], *x_pieces), "col", k)]
        x_pieces[-1] = after(x_pieces[-1], *fars)
        x, terms, pairs, fars = project_and_sum(x_pieces)
        xs.append(x)
        parts.append(terms)
    ups = merge_rows(place, [after(ups[0], *pairs)] + ups[1:])
    ups = [up if k == 0 else swap(up, "col", k) for k, up in enumerate(ups)]
    own_grads, blocks = middle(place, taps, ups, parts, local_tok)
    nears = [swap(own, "depth", 1) for own in own_grads]
    blocks = [block if k == 0 else swap(block, "col", k) for k, block in enumerate(blocks)]
    beside = nears + blocks[1:]
    chunks = 4
    grads = [None] * n_col
    ready = []
    sent = []
    lhs = [None] * n_col
    for k in reversed(range(n_col)):
        fars = [swap(after(own_grads[k], *ready) if ready else own_grads[k], "depth", r) for r in range(2, n_depth, 2)]
        ready = fars
        if k > 0:
            fars = [after(far, *beside) for far in fars]
        elif sent:
            fars = [after(far, sent[-1][1][-1]) for far in fars]
        grads[k] = [own_grads[k], nears[k]]
        for far in fars:
            grads[k] += [far, swap(far, "depth", 1)]
        ready = grads[k][2:]
        lhs[k] = assemble(place, grads[k])
        if k > 0:
            parts_of = input_grad(lhs[k], w, 0, 1, chunks, width)
            parts_of += input_grad(after(lhs[k], *parts_of), w, 1, chunks, chunks, width)
            sent.append(([swap(part, "col", k) for part in parts_of[:3]], parts_of))
    held = [parts_of[3:] for _, parts_of in sent]
    sent = [of for of, _ in sent]
    own_part = input_grad(lhs[0], w, 0, 1, chunks, width)
    outer = (row_at == 0) | (row_at == 3)
    line = lax.axis_size("row") == 4
    inward, across, summed, done = ([None] * chunks for _ in range(4))
    pair = cross = filled = None
    marks = []
    for slot in range(chunks + 3):
        if slot < chunks:
            total = after(own_part[slot], *marks).astype(jnp.float32)
            for of in sent:
                total = total + of[slot].astype(jnp.float32)
            inward[slot] = total.astype(jnp.bfloat16)
            marks = [inward[slot]]
        if not line:
            if slot < chunks:
                done[slot] = lax.psum(inward[slot], "row")
        else:
            if 0 <= slot - 1 < chunks:
                across[slot - 1] = added(after(inward[slot - 1], *marks), pair)
                marks = [across[slot - 1]]
            if 0 <= slot - 2 < chunks:
                summed[slot - 2] = added(after(across[slot - 2], *marks), cross)
                marks = [summed[slot - 2]]
            if 0 <= slot - 3 < chunks:
                done[slot - 3] = jnp.where(outer, pair, summed[slot - 3])
            if slot < chunks + 2:
                out = summed[slot - 2] if slot >= 2 else inward[slot]
                pair = swap(jnp.where(outer, inward[slot], out) if slot < chunks else out, "row", 1)
            if 0 <= slot - 1 < chunks:
                cross = lax.ppermute(across[slot - 1], "row", [(0, 0), (1, 2), (2, 1), (3, 3)])
        if slot == 0:
            own_part += input_grad(after(lhs[0], *marks), w, 1, chunks, chunks, width)
            marks = [own_part[1]]
            for k, parts_of in enumerate(held):
                sent[k] += [swap(after(part, *marks), "col", k + 1) for part in parts_of]
        if slot in (2, 3):
            filled = weight_grad(filled, [after(lhs[0], *marks)] + lhs[1:], xs, slot - 2, 3, width)
            marks = [filled[1]]
        if slot == chunks + 1:
            blocks = split_rows(place, [after(blocks[0], *marks)] + blocks[1:], n_depth)
            blocks = [block if r == 0 else swap(block, "depth", r) for r, block in enumerate(blocks)]
    grad_tokens = jnp.concatenate(done, axis=1)
    output, grad_taps = join(place, filled[1], [after(blocks[0], *marks)] + blocks[1:], taps.shape[1])
    grad_weight = jnp.transpose(filled[0], (1, 0, 2))
    return (output, grad_tokens, grad_weight, grad_taps)


def solution(mesh):
    in_specs = (
        P("col", "depth"),
        P(("row", "col"), None, "depth"),
        P(None, "row"),
        P(("col", "depth"), "row"),
    )
    out_specs = (
        P(("col", "depth"), "row"),
        P("col", "depth"),
        P(("row", "col"), None, "depth"),
        P(None, "row"),
    )
    return jax.shard_map(
        on_device, mesh=mesh, in_specs=in_specs, out_specs=out_specs, check_vma=False
    )
```

```python
import functools

import jax
import jax.numpy as jnp
from jax import lax
from jax.experimental import pallas as pl
from jax.experimental.pallas import tpu as pltpu
from jax.sharding import PartitionSpec as P

GROUP = 16
KT = 7
PAD = 8
LANES = 128
MIB = 1024 * 1024
SMALL = pl.CostEstimate(flops=1, bytes_accessed=1, transcendentals=0)


def swap(value, axis, flip):
    count = lax.axis_size(axis)
    return lax.ppermute(value, axis, [(i, i ^ flip) for i in range(count)])


def after(value, *earlier):
    return lax.optimization_barrier((value, *earlier))[0]


def resident(shape, width):
    if width % LANES == 0:
        return pl.BlockSpec(memory_space=pltpu.VMEM)
    return pl.BlockSpec(tuple(shape), lambda *_: (0,) * len(shape), pipeline_mode=pl.Buffered(1))


def params(mib, width):
    return pltpu.CompilerParams(vmem_limit_bytes=(mib if width % LANES == 0 else 56) * MIB)


def project_kernel(place, *refs, pieces, count, width):
    x_refs = refs[:pieces]
    w_ref, keep_ref, send_ref = refs[pieces : pieces + 3]
    stream = pl.program_id(0)
    core = place[0] % 2
    if pieces == 1:
        x = x_refs[0][...]
    else:
        x_out = refs[pieces + 3]
        third = x_refs[0].shape[0]
        parity = place[2] % 2

        @pl.when(stream == 0)
        def _():
            x_out[pl.ds(pl.multiple_of(parity * third, third), third), :] = x_refs[0][...]
            x_out[pl.ds(pl.multiple_of((1 - parity) * third, third), third), :] = x_refs[1][...]
            x_out[2 * third :, :] = x_refs[2][...]

        x = x_out[...]
    nt = (((1,), (1,)), ((), ()))
    if width % LANES == 0:
        whole = lax.dot_general(x, w_ref[stream], nt, preferred_element_type=jnp.float32).astype(jnp.bfloat16)
        blocks = [whole[:, j * width : (j + 1) * width] for j in range(count)]
    else:
        blocks = [
            lax.dot_general(
                x, w_ref[0, j * width : (j + 1) * width, :], nt, preferred_element_type=jnp.float32
            ).astype(jnp.bfloat16)
            for j in range(count)
        ]
    for mine in range(2):

        @pl.when(core == mine)
        def _():
            for j in range(count):
                at = (j ^ place[0]) // 2
                if j % 2 == mine:
                    keep_ref[at, stream] = blocks[j]
                else:
                    send_ref[at, stream] = blocks[j]


def project(place, xs, w, count):
    tok, feat = sum(x.shape[0] for x in xs), xs[0].shape[1]
    streams, channels, _ = w.shape
    width = channels // count
    part = jax.ShapeDtypeStruct((count // 2, streams, tok, width), jnp.bfloat16)
    wide = width % LANES == 0
    spec = resident(part.shape, width)
    joined = len(xs) > 1
    outs = pl.pallas_call(
        functools.partial(project_kernel, pieces=len(xs), count=count, width=width),
        grid_spec=pltpu.PrefetchScalarGridSpec(
            num_scalar_prefetch=1,
            grid=(streams,),
            in_specs=[resident(x.shape, width) for x in xs]
            + [resident(w.shape, width) if wide else pl.BlockSpec((1, channels, feat), lambda s, _: (s, 0, 0))],
            out_specs=[spec, spec] + [resident((tok, feat), width)] * joined,
        ),
        out_shape=[part, part] + [jax.ShapeDtypeStruct((tok, feat), jnp.bfloat16)] * joined,
        compiler_params=params(10, width),
        cost_estimate=SMALL,
        name="project",
    )(place, *xs, w)
    return outs[0], outs[1], outs[2] if joined else xs[0]


def in_three(value):
    terms = []
    for _ in range(3):
        term = value.astype(jnp.bfloat16)
        value = value - term.astype(jnp.float32)
        terms.append(term)
    return terms


def split_lanes_kernel(place, up_ref, *out_refs):
    n_depth, width = len(out_refs), out_refs[0].shape[2]
    for r, ref in enumerate(out_refs):
        for k in range(ref.shape[0]):
            at = ((place[1] ^ k) * n_depth + (place[0] ^ r)) * width
            ref[k] = up_ref[:, pl.ds(pl.multiple_of(at, width), width)]


def merge_rows_kernel(place, *refs, n_depth):
    in_refs, out_refs = refs[:n_depth], refs[n_depth:]
    local = in_refs[0].shape[1]
    for r, ref in enumerate(in_refs):
        for k, out_ref in enumerate(out_refs):
            out_ref[pl.ds(pl.multiple_of((place[0] ^ r) * local, 16), local), :] = ref[k]


def split_rows_kernel(place, *refs, n_col):
    in_refs, out_refs = refs[:n_col], refs[n_col:]
    local = out_refs[0].shape[1] - 32
    for r, ref in enumerate(out_refs):
        rows = pl.ds(pl.multiple_of((place[0] ^ r) * local, 16), local)
        for k in range(n_col):
            ref[k, 0:local] = in_refs[k][rows, :]
            ref[k, local:] = in_refs[k][-32:, :]


def rearrange(kernel, place, arrays, count, shape, name):
    width = shape[-1]
    return pl.pallas_call(
        kernel,
        grid_spec=pltpu.PrefetchScalarGridSpec(
            num_scalar_prefetch=1,
            grid=(1,),
            in_specs=[resident(value.shape, width) for value in arrays],
            out_specs=[resident(shape, width)] * count,
        ),
        out_shape=[jax.ShapeDtypeStruct(shape, jnp.bfloat16)] * count,
        compiler_params=params(4, width),
        cost_estimate=SMALL,
        name=name,
    )(place, *arrays)


def split_lanes(place, up, n_col, n_depth):
    local, width = up.shape[0], up.shape[1] // (n_col * n_depth)
    if width % LANES:
        blocks = up.reshape(local, n_col, n_depth, width)[:, place[1] ^ jnp.arange(n_col)]
        return [
            jnp.transpose(lax.dynamic_index_in_dim(blocks, place[0] ^ r, 2, keepdims=False), (1, 0, 2))
            for r in range(n_depth)
        ]
    return rearrange(split_lanes_kernel, place, [up], n_depth, (n_col, local, width), "split")


def merge_rows(place, pieces):
    n_depth = len(pieces)
    n_col, local, width = pieces[0].shape
    if width % LANES:
        whole = jnp.stack(pieces)[place[0] ^ jnp.arange(n_depth)]
        return list(jnp.transpose(whole, (1, 0, 2, 3)).reshape(n_col, n_depth * local, width))
    kernel = functools.partial(merge_rows_kernel, n_depth=n_depth)
    return list(rearrange(kernel, place, pieces, n_col, (n_depth * local, width), "merge"))


def split_rows(place, arrays, n_depth):
    local, width = (arrays[0].shape[0] - 32) // n_depth, arrays[0].shape[1]
    if width % LANES:
        whole = jnp.stack(arrays)
        return [
            jnp.concatenate(
                [lax.dynamic_slice_in_dim(whole, (place[0] ^ r) * local, local, axis=1), whole[:, -32:]], axis=1
            )
            for r in range(n_depth)
        ]
    kernel = functools.partial(split_rows_kernel, n_col=len(arrays))
    return rearrange(kernel, place, arrays, n_depth, (len(arrays), local + 32, width), "split")


def join_kernel(place, _, *refs):
    block_refs, (out_ref, grad_taps_ref) = refs[:-2], refs[-2:]
    n_depth = len(block_refs)
    n_col, _, width = block_refs[0].shape
    local, groups = out_ref.shape[0], grad_taps_ref.shape[1]
    lane_group = lax.broadcasted_iota(jnp.int32, (width, groups), 0) // GROUP
    group = lax.broadcasted_iota(jnp.int32, (width, groups), 1)
    total = jnp.zeros((24, groups), jnp.float32)
    for r, ref in enumerate(block_refs):
        for k in range(n_col):
            at = (place[1] ^ k) * n_depth + (place[0] ^ r)
            out_ref[:, pl.ds(pl.multiple_of(at * width, width), width)] = ref[k, 0:local, :]
            spread = (lane_group + at * (width // GROUP) == group).astype(jnp.bfloat16)
            total = total + jnp.dot(ref[k, local : local + 24, :], spread, preferred_element_type=jnp.float32)
    grad_taps_ref[...] = (total[0:8] + total[8:16] + total[16:24])[:KT]


def join(place, mark, blocks, groups):
    n_depth = len(blocks)
    n_col, rows, width = blocks[0].shape
    local = rows - 32
    if width % LANES:
        whole = jnp.stack(blocks)[place[0] ^ jnp.arange(n_depth)][:, place[1] ^ jnp.arange(n_col)]
        sums = whole[:, :, local : local + 24].astype(jnp.float32)
        sums = sums.reshape(n_depth, n_col, 3, 8, width // GROUP, GROUP).sum(axis=(2, 5))[:, :, :KT]
        return (
            jnp.transpose(whole[:, :, :local], (2, 1, 0, 3)).reshape(local, -1),
            jnp.transpose(sums, (2, 1, 0, 3)).reshape(KT, -1),
        )
    channels = n_depth * n_col * width
    return pl.pallas_call(
        join_kernel,
        grid_spec=pltpu.PrefetchScalarGridSpec(
            num_scalar_prefetch=1,
            grid=(1,),
            in_specs=[pl.BlockSpec(memory_space=pl.ANY)] + [resident(blocks[0].shape, width)] * n_depth,
            out_specs=[resident((local, channels), width), resident((KT, groups), width)],
        ),
        out_shape=[
            jax.ShapeDtypeStruct((local, channels), jnp.bfloat16),
            jax.ShapeDtypeStruct((KT, groups), jnp.float32),
        ],
        compiler_params=params(4, width),
        cost_estimate=SMALL,
        name="join",
    )(place, mark, *blocks)


def middle_kernel(place, taps_ref, *refs, groups, terms, tile):
    up_refs, refs = refs[:groups], refs[groups:]
    part_refs = refs[: groups * terms]
    grad_refs = refs[groups * terms : groups * terms + groups]
    out_refs = refs[groups * terms + groups : groups * terms + 2 * groups]
    up_s, out_s, q_s, k_s, v_s, mixed_s, gf_s, far_s = refs[groups * terms + 2 * groups :]
    col = place[1]
    tok = part_refs[0].shape[2]
    width = part_refs[0].shape[3]
    total = groups * tok
    tap_groups = taps_ref.shape[1]
    for k, ref in enumerate(up_refs):
        up_s[pl.ds(pl.multiple_of((col ^ k) * tok, tok), tok), :] = ref[...]
    lane_group = lax.broadcasted_iota(jnp.int32, (tap_groups, width), 1) // GROUP
    group = lax.broadcasted_iota(jnp.int32, (tap_groups, width), 0)
    spread = (lane_group + place[3] * (width // GROUP) == group).astype(jnp.bfloat16)
    taps = sum(jnp.dot(term, spread, preferred_element_type=jnp.float32) for term in in_three(taps_ref[...]))
    mixed_s[0:PAD, :] = jnp.zeros((PAD, width), jnp.float32)
    gf_s[total : total + PAD, :] = jnp.zeros((PAD, width), jnp.float32)
    for k in range(groups):
        start = (col ^ k) * tok
        for i in range(tok // tile):
            inside = slice(i * tile, (i + 1) * tile)
            rows = pl.ds(pl.multiple_of(start + i * tile, tile), tile)
            streams = []
            for s in range(3):
                acc = None
                for ref in part_refs[k * terms : (k + 1) * terms]:
                    term = ref[0, s, inside, :].astype(jnp.float32)
                    acc = term if acc is None else acc + term
                streams.append(acc.astype(jnp.bfloat16))
            q_s[rows, :], k_s[rows, :], v_s[rows, :] = streams
            query, key, value = [stream.astype(jnp.float32) for stream in streams]
            mixed_s[pl.ds(pl.multiple_of(start + i * tile + PAD, PAD), tile), :] = key * value
            gf_s[rows, :] = up_s[rows, :].astype(jnp.float32) * query
    sums = [jnp.zeros((8, width), jnp.float32) for _ in range(KT)]
    for a in range(groups):
        for i in range(tok // tile):
            first = a * tok + i * tile
            rows = slice(first, first + tile)
            inside = slice(i * tile, (i + 1) * tile)
            gf = gf_s[rows, :]
            filtered = jnp.zeros((tile, width), jnp.float32)
            grad_mixed = jnp.zeros((tile, width), jnp.float32)
            for j in range(KT):
                shifted = mixed_s[first + PAD - j : first + PAD - j + tile, :]
                filtered = filtered + taps[j : j + 1, :] * shifted
                sums[j] = sums[j] + (gf * shifted).reshape(tile // 8, 8, width).sum(axis=0)
                grad_mixed = grad_mixed + taps[j : j + 1, :] * gf_s[first + j : first + j + tile, :]
            out_s[a, inside, :] = (q_s[rows, :].astype(jnp.float32) * filtered).astype(jnp.bfloat16)
            at = col ^ a
            far_s[at, 0, inside, :] = (up_s[rows, :].astype(jnp.float32) * filtered).astype(jnp.bfloat16)
            far_s[at, 1, inside, :] = (grad_mixed * v_s[rows, :].astype(jnp.float32)).astype(jnp.bfloat16)
            far_s[at, 2, inside, :] = (grad_mixed * k_s[rows, :].astype(jnp.float32)).astype(jnp.bfloat16)
    for k in range(groups):
        grad_refs[k][...] = far_s[k]
    rest = jnp.concatenate(
        [sums[j].sum(axis=0, keepdims=True) for j in range(KT)] + [jnp.zeros((1, width), jnp.float32)], axis=0
    )
    terms_of = [term.astype(jnp.float32) for term in in_three(rest)]
    packed = jnp.concatenate(terms_of + [jnp.zeros((8, width), jnp.float32)], axis=0).astype(jnp.bfloat16)
    for k, ref in enumerate(out_refs):
        ref[0:tok, :] = out_s[col ^ k]
        ref[tok : tok + 32, :] = packed


def middle(place, taps, ups, parts, tile):
    groups, terms = len(parts), len(parts[0])
    _, _, tok, width = parts[0][0].shape
    total = groups * tok
    whole = lambda *shape: resident(shape, width)
    one = whole(1, 3, tok, width)
    outs = pl.pallas_call(
        functools.partial(middle_kernel, groups=groups, terms=terms, tile=tile),
        grid_spec=pltpu.PrefetchScalarGridSpec(
            num_scalar_prefetch=1,
            grid=(1,),
            in_specs=[whole(*taps.shape)] + [whole(tok, width)] * groups + [one] * (groups * terms),
            out_specs=[whole(3, tok, width)] * groups + [whole(tok + 32, width)] * groups,
            scratch_shapes=[
                pltpu.VMEM((total, width), jnp.bfloat16),
                pltpu.VMEM((groups, tok, width), jnp.bfloat16),
            ]
            + [pltpu.VMEM((total, width), jnp.bfloat16)] * 3
            + [pltpu.VMEM((total + PAD, width), jnp.float32)] * 2
            + [pltpu.VMEM((groups, 3, tok, width), jnp.bfloat16)],
        ),
        out_shape=[jax.ShapeDtypeStruct((3, tok, width), jnp.bfloat16)] * groups
        + [jax.ShapeDtypeStruct((tok + 32, width), jnp.bfloat16)] * groups,
        compiler_params=params(10, width),
        cost_estimate=SMALL,
        name="middle",
    )(place, taps, *ups, *[term for terms_of in parts for term in terms_of])
    return outs[:groups], outs[groups:]


def assemble_kernel(place, *refs):
    grad_refs, out_ref = refs[:-1], refs[-1]
    width = grad_refs[0].shape[2]
    for r, ref in enumerate(grad_refs):
        for s in range(3):
            at = pl.multiple_of((s * len(grad_refs) + (place[0] ^ r)) * width, width)
            out_ref[:, pl.ds(at, width)] = ref[s]


def assemble(place, grads):
    streams, tok, width = grads[0].shape
    out = jax.ShapeDtypeStruct((tok, streams * width * len(grads)), jnp.bfloat16)
    if width % LANES:
        whole = jnp.stack(grads)[place[0] ^ jnp.arange(len(grads))]
        return jnp.transpose(whole, (2, 1, 0, 3)).reshape(out.shape)
    return pl.pallas_call(
        assemble_kernel,
        grid_spec=pltpu.PrefetchScalarGridSpec(
            num_scalar_prefetch=1,
            grid=(1,),
            in_specs=[resident(grads[0].shape, width)] * len(grads),
            out_specs=resident(out.shape, width),
        ),
        out_shape=out,
        compiler_params=params(4, width),
        cost_estimate=SMALL,
        name="assemble",
    )(place, *grads)


def input_grad_kernel(grad_ref, w_ref, out_ref, *, first):
    step = out_ref.shape[1]
    rows = w_ref[:, :, first * step : (first + 1) * step].reshape(-1, step)
    out_ref[...] = jnp.dot(grad_ref[...], rows, preferred_element_type=jnp.float32).astype(jnp.bfloat16)


def input_grads_kernel(grad_ref, w_ref, *refs, first):
    out_refs, (slots, sems) = refs[:-2], refs[-2:]
    step = out_refs[0].shape[1]

    def fetch(i):
        columns = pl.ds((first + i) * step, step)
        return pltpu.make_async_copy(w_ref.at[:, :, columns], slots.at[i % 2], sems.at[i % 2])

    fetch(0).start()
    for i, out_ref in enumerate(out_refs):
        if i + 1 < len(out_refs):
            fetch(i + 1).start()
        fetch(i).wait()
        rows = slots[i % 2].reshape(-1, step)
        out_ref[...] = jnp.dot(grad_ref[...], rows, preferred_element_type=jnp.float32).astype(jnp.bfloat16)


def input_grad(grad, w, first, last, chunks, width):
    tok = grad.shape[0]
    streams, channels, feat = w.shape
    step = feat // chunks
    count = last - first
    if width % LANES:
        rows = w[:, :, first * step : last * step].reshape(streams * channels, count * step)
        whole = jnp.dot(grad, rows, preferred_element_type=jnp.float32).astype(jnp.bfloat16)
        return [whole[:, i * step : (i + 1) * step] for i in range(count)]
    single = count == 1
    return list(
        pl.pallas_call(
            functools.partial(input_grad_kernel if single else input_grads_kernel, first=first),
            in_specs=[
                resident(grad.shape, width),
                pl.BlockSpec(memory_space=pltpu.VMEM if single else pltpu.HBM),
            ],
            out_specs=[resident((tok, step), width)] * count,
            out_shape=[jax.ShapeDtypeStruct((tok, step), jnp.bfloat16)] * count,
            scratch_shapes=[]
            if single
            else [pltpu.VMEM((2, streams, channels, step), jnp.bfloat16), pltpu.SemaphoreType.DMA((2,))],
            compiler_params=params(8, width),
            cost_estimate=SMALL,
            name="input_grad",
        )(grad, w)
    )


def weight_grad_kernel(*refs, chained, groups, half):
    refs = refs[2 * chained :]
    grad_refs, x_refs = refs[:groups], refs[groups : 2 * groups]
    out_ref, mark_ref, turned = refs[2 * groups :]
    mark_ref[...] = jnp.zeros(mark_ref.shape, jnp.float32)
    streams, channels, step = out_ref.shape
    tok = x_refs[0].shape[0]

    @pl.when(pl.program_id(0) == 0)
    def _():
        for k in range(groups):
            for s in range(streams):
                at = (2 * s + half) * channels
                block = grad_refs[k][:, at : at + channels]
                turned[s * channels : (s + 1) * channels, k * tok : (k + 1) * tok] = block.T

    columns = pl.ds(pl.multiple_of(pl.program_id(0) * step, step), step)
    acc = None
    for k in range(groups):
        term = jnp.dot(turned[:, k * tok : (k + 1) * tok], x_refs[k][:, columns], preferred_element_type=jnp.float32)
        acc = term if acc is None else acc + term
    for s in range(streams):
        out_ref[s] = acc[s * channels : (s + 1) * channels, :]


def weight_grad(filled, grads, xs, half, streams, width):
    groups = len(xs)
    tok, feat = xs[0].shape
    channels = grads[0].shape[1] // streams
    chained = filled is not None
    if width % LANES:
        if chained:
            return filled
        terms = [
            lax.dot_general(grad, x, (((0,), (0,)), ((), ())), preferred_element_type=jnp.float32)
            for grad, x in zip(grads, xs)
        ]
        return sum(terms).reshape(streams, channels, feat), jnp.zeros((8, LANES), jnp.float32)
    step = min(512, feat)
    return pl.pallas_call(
        functools.partial(weight_grad_kernel, chained=chained, groups=groups, half=half),
        grid=(feat // step,),
        in_specs=[pl.BlockSpec(memory_space=pl.ANY)] * (2 * chained)
        + [resident(grads[0].shape, width)] * groups
        + [resident((tok, feat), width)] * groups,
        out_specs=[
            pl.BlockSpec((streams, channels // 2, step), lambda i: (0, half, i)),
            resident((8, LANES), width),
        ],
        scratch_shapes=[pltpu.VMEM((streams * channels // 2, groups * tok), jnp.bfloat16)],
        out_shape=[
            jax.ShapeDtypeStruct((streams, channels, feat), jnp.float32),
            jax.ShapeDtypeStruct((8, LANES), jnp.float32),
        ],
        input_output_aliases={0: 0} if chained else {},
        compiler_params=params(14, width),
        cost_estimate=SMALL,
        name="weight_grad",
    )(*(filled if chained else []), *grads, *xs)


def added(first, second):
    return (first.astype(jnp.float32) + second.astype(jnp.float32)).astype(jnp.bfloat16)


def cut_kernel(_, own_ref, last_ref, own_out, last_out):
    own_out[...] = own_ref[...]
    last_out[...] = last_ref[...]


def cut(place, tokens):
    tok, feat = tokens.shape
    if tok % 48 or lax.axis_size("row") % 2:
        return None
    third = tok // 3
    out = jax.ShapeDtypeStruct((third, feat), jnp.bfloat16)
    return pl.pallas_call(
        cut_kernel,
        grid_spec=pltpu.PrefetchScalarGridSpec(
            num_scalar_prefetch=1,
            grid=(1,),
            in_specs=[
                pl.BlockSpec((third, feat), lambda i, at: (at[2] % 2, 0)),
                pl.BlockSpec((third, feat), lambda i, at: (2, 0)),
            ],
            out_specs=[pl.BlockSpec(memory_space=pltpu.VMEM)] * 2,
        ),
        out_shape=[out, out],
        compiler_params=params(10, LANES),
        cost_estimate=SMALL,
        name="cut",
    )(place, tokens, tokens)


def on_device(tokens, weight, taps, upstream):
    n_col = lax.axis_size("col")
    n_depth = lax.axis_size("depth")
    local_tok = upstream.shape[0]
    depth_at = lax.axis_index("depth")
    col_at = lax.axis_index("col")
    row_at = lax.axis_index("row")
    place = jnp.stack([depth_at, col_at, row_at, col_at * n_depth + depth_at]).astype(jnp.int32)
    w = jnp.transpose(weight, (1, 0, 2))
    width = w.shape[1] // n_depth
    def project_and_sum(x_pieces, *earlier):
        keep, send, x = project(place, x_pieces, w, n_depth)
        near = swap(after(send, *earlier) if earlier else send, "depth", 1)
        pairs = [added(keep[r // 2], near[r // 2])[None] for r in range(2, n_depth, 2)]
        fars = [swap(pair, "depth", 2 * i + 2) for i, pair in enumerate(pairs)]
        return x, [keep, near] + fars, pairs, fars

    thirds = cut(place, tokens)
    first = [[swap(tokens if thirds is None else thirds[0], "col", k)] for k in range(1, n_col)]
    ups = split_lanes(place, upstream, n_col, n_depth)
    ups = [up if r == 0 else swap(up, "depth", r) for r, up in enumerate(ups)]
    x, terms, pairs, fars = project_and_sum([tokens], *[piece for of in first for piece in of], *ups[1:])
    xs, parts = [x], [terms]
    for k in range(1, n_col):
        x_pieces = first[k - 1]
        if thirds is not None:
            x_pieces += [swap(x_pieces[0], "row", 1), swap(after(thirds[1], *x_pieces), "col", k)]
        x_pieces[-1] = after(x_pieces[-1], *fars)
        x, terms, pairs, fars = project_and_sum(x_pieces)
        xs.append(x)
        parts.append(terms)
    ups = merge_rows(place, [after(ups[0], *pairs)] + ups[1:])
    ups = [up if k == 0 else swap(up, "col", k) for k, up in enumerate(ups)]
    own_grads, blocks = middle(place, taps, ups, parts, local_tok)
    nears = [swap(own, "depth", 1) for own in own_grads]
    blocks = [block if k == 0 else swap(block, "col", k) for k, block in enumerate(blocks)]
    beside = nears + blocks[1:]
    chunks = 4
    grads = [None] * n_col
    ready = []
    sent = []
    lhs = [None] * n_col
    for k in reversed(range(n_col)):
        fars = [swap(after(own_grads[k], *ready) if ready else own_grads[k], "depth", r) for r in range(2, n_depth, 2)]
        ready = fars
        if k > 0:
            fars = [after(far, *beside) for far in fars]
        elif sent:
            fars = [after(far, sent[-1][1][-1]) for far in fars]
        grads[k] = [own_grads[k], nears[k]]
        for far in fars:
            grads[k] += [far, swap(far, "depth", 1)]
        lhs[k] = assemble(place, grads[k])
        if k > 0:
            parts_of = input_grad(lhs[k], w, 0, 1, chunks, width)
            parts_of += input_grad(after(lhs[k], *parts_of), w, 1, chunks, chunks, width)
            sent.append(([swap(part, "col", k) for part in parts_of[:3]], parts_of))
    held = [parts_of[3:] for _, parts_of in sent]
    sent = [of for of, _ in sent]
    own_part = input_grad(lhs[0], w, 0, chunks, chunks, width)
    outer = (row_at == 0) | (row_at == 3)
    line = lax.axis_size("row") == 4
    inward, across, summed, done = ([None] * chunks for _ in range(4))
    pair = cross = filled = None
    marks = []
    for slot in range(chunks + 3):
        if slot < chunks:
            total = after(own_part[slot], *marks).astype(jnp.float32)
            for of in sent:
                total = total + of[slot].astype(jnp.float32)
            inward[slot] = total.astype(jnp.bfloat16)
            marks = [inward[slot]]
        if not line:
            if slot < chunks:
                done[slot] = lax.psum(inward[slot], "row")
        else:
            if 0 <= slot - 1 < chunks:
                across[slot - 1] = added(after(inward[slot - 1], *marks), pair)
                marks = [across[slot - 1]]
            if 0 <= slot - 2 < chunks:
                summed[slot - 2] = added(after(across[slot - 2], *marks), cross)
                marks = [summed[slot - 2]]
            if 0 <= slot - 3 < chunks:
                done[slot - 3] = jnp.where(outer, pair, summed[slot - 3])
            if slot < chunks + 2:
                out = summed[slot - 2] if slot >= 2 else inward[slot]
                pair = swap(jnp.where(outer, inward[slot], out) if slot < chunks else out, "row", 1)
            if 0 <= slot - 1 < chunks:
                cross = lax.ppermute(across[slot - 1], "row", [(0, 0), (1, 2), (2, 1), (3, 3)])
        if slot == 0:
            for k, parts_of in enumerate(held):
                sent[k] += [swap(after(part, *marks), "col", k + 1) for part in parts_of]
        if slot in (2, 4):
            filled = weight_grad(filled, [after(lhs[0], *marks)] + lhs[1:], xs, slot // 2 - 1, 3, width)
            marks = [filled[1]]
        if slot == 4:
            marks += late
        if slot == 3:
            blocks = split_rows(place, [after(blocks[0], *marks)] + blocks[1:], n_depth)
            blocks = [block if r == 0 else swap(block, "depth", r) for r, block in enumerate(blocks)]
            late = blocks[1:]
    grad_tokens = jnp.concatenate(done, axis=1)
    output, grad_taps = join(place, filled[1], [after(blocks[0], *marks)] + blocks[1:], taps.shape[1])
    grad_weight = jnp.transpose(filled[0], (1, 0, 2))
    return (output, grad_tokens, grad_weight, grad_taps)


def solution(mesh):
    in_specs = (
        P("col", "depth"),
        P(("row", "col"), None, "depth"),
        P(None, "row"),
        P(("col", "depth"), "row"),
    )
    out_specs = (
        P(("col", "depth"), "row"),
        P("col", "depth"),
        P(("row", "col"), None, "depth"),
        P(None, "row"),
    )
    return jax.shard_map(
        on_device, mesh=mesh, in_specs=in_specs, out_specs=out_specs, check_vma=False
    )
```

```python
import functools

import jax
import jax.numpy as jnp
from jax import lax
from jax.experimental import pallas as pl
from jax.experimental.pallas import tpu as pltpu
from jax.sharding import PartitionSpec as P

GROUP = 16
KT = 7
PAD = 8
LANES = 128
MIB = 1024 * 1024
SMALL = pl.CostEstimate(flops=1, bytes_accessed=1, transcendentals=0)


def swap(value, axis, flip):
    count = lax.axis_size(axis)
    return lax.ppermute(value, axis, [(i, i ^ flip) for i in range(count)])


def after(value, *earlier):
    return lax.optimization_barrier((value, *earlier))[0]


def resident(shape, width):
    if width % LANES == 0:
        return pl.BlockSpec(memory_space=pltpu.VMEM)
    return pl.BlockSpec(tuple(shape), lambda *_: (0,) * len(shape), pipeline_mode=pl.Buffered(1))


def params(mib, width):
    return pltpu.CompilerParams(vmem_limit_bytes=(mib if width % LANES == 0 else 56) * MIB)


def project_kernel(place, *refs, pieces, mode, count, width):
    x_refs = refs[:pieces]
    w_ref, keep_ref, send_ref = refs[pieces : pieces + 3]
    stream = pl.program_id(0)
    core = place[0] % 2
    x = x_refs[0][...]
    if mode == "cut":
        last_ref = refs[pieces + 3]

        @pl.when(stream == 0)
        def _():
            last_ref[...] = x_refs[0][x.shape[0] - last_ref.shape[0] :, :]

    if mode == "join":
        joined, rest = refs[pieces + 3 :]
        third = x.shape[0]
        parity = place[2] % 2

        @pl.when(stream == 0)
        def _():
            joined[pl.ds(pl.multiple_of(parity * third, third), third), :] = x_refs[0][...]
            joined[pl.ds(pl.multiple_of((1 - parity) * third, third), third), :] = x_refs[1][...]
            joined[2 * third :, :] = x_refs[2][...]
            rest[0:third, :] = x_refs[1][...]
            rest[third:, :] = x_refs[2][...]

        x = rest[...]
    nt = (((1,), (1,)), ((), ()))
    if width % LANES == 0:
        whole = lax.dot_general(x, w_ref[stream], nt, preferred_element_type=jnp.float32).astype(jnp.bfloat16)
        blocks = [whole[:, j * width : (j + 1) * width] for j in range(count)]
    else:
        blocks = [
            lax.dot_general(
                x, w_ref[0, j * width : (j + 1) * width, :], nt, preferred_element_type=jnp.float32
            ).astype(jnp.bfloat16)
            for j in range(count)
        ]
    for mine in range(2):

        @pl.when(core == mine)
        def _():
            for j in range(count):
                at = (j ^ place[0]) // 2
                if j % 2 == mine:
                    keep_ref[at, stream] = blocks[j]
                else:
                    send_ref[at, stream] = blocks[j]


def project(place, xs, w, count, mode="plain"):
    feat = xs[0].shape[1]
    all_tok = sum(x.shape[0] for x in xs)
    tok = all_tok - xs[0].shape[0] if mode == "join" else all_tok
    streams, channels, _ = w.shape
    width = channels // count
    part = jax.ShapeDtypeStruct((count // 2, streams, tok, width), jnp.bfloat16)
    wide = width % LANES == 0
    spec = resident(part.shape, width)
    more = {"plain": [], "cut": [(tok // 3, feat)], "join": [(all_tok, feat)]}[mode]
    return pl.pallas_call(
        functools.partial(project_kernel, pieces=len(xs), mode=mode, count=count, width=width),
        grid_spec=pltpu.PrefetchScalarGridSpec(
            num_scalar_prefetch=1,
            grid=(streams,),
            in_specs=[resident(x.shape, width) for x in xs]
            + [resident(w.shape, width) if wide else pl.BlockSpec((1, channels, feat), lambda s, _: (s, 0, 0))],
            out_specs=[spec, spec] + [resident(shape, width) for shape in more],
            scratch_shapes=[pltpu.VMEM((tok, feat), jnp.bfloat16)] if mode == "join" else [],
        ),
        out_shape=[part, part] + [jax.ShapeDtypeStruct(shape, jnp.bfloat16) for shape in more],
        compiler_params=params(10, width),
        cost_estimate=SMALL,
        name="project",
    )(place, *xs, w)


def in_three(value):
    terms = []
    for _ in range(3):
        term = value.astype(jnp.bfloat16)
        value = value - term.astype(jnp.float32)
        terms.append(term)
    return terms


def split_lanes_kernel(place, up_ref, *out_refs):
    n_depth, width = len(out_refs), out_refs[0].shape[2]
    for r, ref in enumerate(out_refs):
        for k in range(ref.shape[0]):
            at = ((place[1] ^ k) * n_depth + (place[0] ^ r)) * width
            ref[k] = up_ref[:, pl.ds(pl.multiple_of(at, width), width)]


def merge_rows_kernel(place, *refs, n_depth):
    in_refs, out_refs = refs[:n_depth], refs[n_depth:]
    local = in_refs[0].shape[1]
    for r, ref in enumerate(in_refs):
        for k, out_ref in enumerate(out_refs):
            out_ref[pl.ds(pl.multiple_of((place[0] ^ r) * local, 16), local), :] = ref[k]


def split_rows_kernel(place, *refs, n_col):
    in_refs, out_refs = refs[:n_col], refs[n_col:]
    local = out_refs[0].shape[1] - 32
    for r, ref in enumerate(out_refs):
        rows = pl.ds(pl.multiple_of((place[0] ^ r) * local, 16), local)
        for k in range(n_col):
            ref[k, 0:local] = in_refs[k][rows, :]
            ref[k, local:] = in_refs[k][-32:, :]


def rearrange(kernel, place, arrays, count, shape, name):
    width = shape[-1]
    return pl.pallas_call(
        kernel,
        grid_spec=pltpu.PrefetchScalarGridSpec(
            num_scalar_prefetch=1,
            grid=(1,),
            in_specs=[resident(value.shape, width) for value in arrays],
            out_specs=[resident(shape, width)] * count,
        ),
        out_shape=[jax.ShapeDtypeStruct(shape, jnp.bfloat16)] * count,
        compiler_params=params(4, width),
        cost_estimate=SMALL,
        name=name,
    )(place, *arrays)


def split_lanes(place, up, n_col, n_depth):
    local, width = up.shape[0], up.shape[1] // (n_col * n_depth)
    if width % LANES:
        blocks = up.reshape(local, n_col, n_depth, width)[:, place[1] ^ jnp.arange(n_col)]
        return [
            jnp.transpose(lax.dynamic_index_in_dim(blocks, place[0] ^ r, 2, keepdims=False), (1, 0, 2))
            for r in range(n_depth)
        ]
    return rearrange(split_lanes_kernel, place, [up], n_depth, (n_col, local, width), "split")


def merge_rows(place, pieces):
    n_depth = len(pieces)
    n_col, local, width = pieces[0].shape
    if width % LANES:
        whole = jnp.stack(pieces)[place[0] ^ jnp.arange(n_depth)]
        return list(jnp.transpose(whole, (1, 0, 2, 3)).reshape(n_col, n_depth * local, width))
    kernel = functools.partial(merge_rows_kernel, n_depth=n_depth)
    return list(rearrange(kernel, place, pieces, n_col, (n_depth * local, width), "merge"))


def split_rows(place, arrays, n_depth):
    local, width = (arrays[0].shape[0] - 32) // n_depth, arrays[0].shape[1]
    if width % LANES:
        whole = jnp.stack(arrays)
        return [
            jnp.concatenate(
                [lax.dynamic_slice_in_dim(whole, (place[0] ^ r) * local, local, axis=1), whole[:, -32:]], axis=1
            )
            for r in range(n_depth)
        ]
    kernel = functools.partial(split_rows_kernel, n_col=len(arrays))
    return rearrange(kernel, place, arrays, n_depth, (len(arrays), local + 32, width), "split")


def join_kernel(place, _, *refs):
    block_refs, (out_ref, grad_taps_ref) = refs[:-2], refs[-2:]
    n_depth = len(block_refs)
    n_col, _, width = block_refs[0].shape
    local, groups = out_ref.shape[0], grad_taps_ref.shape[1]
    lane_group = lax.broadcasted_iota(jnp.int32, (width, groups), 0) // GROUP
    group = lax.broadcasted_iota(jnp.int32, (width, groups), 1)
    total = jnp.zeros((24, groups), jnp.float32)
    for r, ref in enumerate(block_refs):
        for k in range(n_col):
            at = (place[1] ^ k) * n_depth + (place[0] ^ r)
            out_ref[:, pl.ds(pl.multiple_of(at * width, width), width)] = ref[k, 0:local, :]
            spread = (lane_group + at * (width // GROUP) == group).astype(jnp.bfloat16)
            total = total + jnp.dot(ref[k, local : local + 24, :], spread, preferred_element_type=jnp.float32)
    grad_taps_ref[...] = (total[0:8] + total[8:16] + total[16:24])[:KT]


def join(place, mark, blocks, groups):
    n_depth = len(blocks)
    n_col, rows, width = blocks[0].shape
    local = rows - 32
    if width % LANES:
        whole = jnp.stack(blocks)[place[0] ^ jnp.arange(n_depth)][:, place[1] ^ jnp.arange(n_col)]
        sums = whole[:, :, local : local + 24].astype(jnp.float32)
        sums = sums.reshape(n_depth, n_col, 3, 8, width // GROUP, GROUP).sum(axis=(2, 5))[:, :, :KT]
        return (
            jnp.transpose(whole[:, :, :local], (2, 1, 0, 3)).reshape(local, -1),
            jnp.transpose(sums, (2, 1, 0, 3)).reshape(KT, -1),
        )
    channels = n_depth * n_col * width
    return pl.pallas_call(
        join_kernel,
        grid_spec=pltpu.PrefetchScalarGridSpec(
            num_scalar_prefetch=1,
            grid=(1,),
            in_specs=[pl.BlockSpec(memory_space=pl.ANY)] + [resident(blocks[0].shape, width)] * n_depth,
            out_specs=[resident((local, channels), width), resident((KT, groups), width)],
        ),
        out_shape=[
            jax.ShapeDtypeStruct((local, channels), jnp.bfloat16),
            jax.ShapeDtypeStruct((KT, groups), jnp.float32),
        ],
        compiler_params=params(4, width),
        cost_estimate=SMALL,
        name="join",
    )(place, mark, *blocks)


def middle_kernel(place, taps_ref, *refs, pieces, groups, terms, tile):
    up_refs, refs = refs[:groups], refs[groups:]
    part_refs, refs = refs[: len(pieces) * terms], refs[len(pieces) * terms :]
    grad_refs, out_refs = refs[:groups], refs[groups : 2 * groups]
    up_s, out_s, q_s, k_s, v_s, mixed_s, gf_s, far_s = refs[2 * groups :]
    col = place[1]
    tok, width = up_refs[0].shape
    parity = place[2] % 2
    total = groups * tok
    tap_groups = taps_ref.shape[1]
    for k, ref in enumerate(up_refs):
        up_s[pl.ds(pl.multiple_of((col ^ k) * tok, tok), tok), :] = ref[...]
    lane_group = lax.broadcasted_iota(jnp.int32, (tap_groups, width), 1) // GROUP
    group = lax.broadcasted_iota(jnp.int32, (tap_groups, width), 0)
    spread = (lane_group + place[3] * (width // GROUP) == group).astype(jnp.bfloat16)
    taps = sum(jnp.dot(term, spread, preferred_element_type=jnp.float32) for term in in_three(taps_ref[...]))
    mixed_s[0:PAD, :] = jnp.zeros((PAD, width), jnp.float32)
    gf_s[total : total + PAD, :] = jnp.zeros((PAD, width), jnp.float32)
    step = 64
    for piece, (k, thirds) in enumerate(pieces):
        refs_of = part_refs[piece * terms : (piece + 1) * terms]
        rows_of = refs_of[0].shape[2]
        length = rows_of // len(thirds)
        for i in range(rows_of // step):
            third = thirds[i * step // length]
            at = {"own": parity, "other": 1 - parity, "last": 2, "all": 0}[third] * length
            start = (col ^ k) * tok + at + i * step % length
            inside = slice(i * step, (i + 1) * step)
            rows = pl.ds(pl.multiple_of(start, step), step)
            streams = []
            for s in range(3):
                acc = None
                for ref in refs_of:
                    term = ref[0, s, inside, :].astype(jnp.float32)
                    acc = term if acc is None else acc + term
                streams.append(acc.astype(jnp.bfloat16))
            q_s[rows, :], k_s[rows, :], v_s[rows, :] = streams
            query, key, value = [stream.astype(jnp.float32) for stream in streams]
            mixed_s[pl.ds(pl.multiple_of(start + PAD, PAD), step), :] = key * value
            gf_s[rows, :] = up_s[rows, :].astype(jnp.float32) * query
    sums = [jnp.zeros((8, width), jnp.float32) for _ in range(KT)]
    for a in range(groups):
        for i in range(tok // tile):
            first = a * tok + i * tile
            rows = slice(first, first + tile)
            inside = slice(i * tile, (i + 1) * tile)
            gf = gf_s[rows, :]
            filtered = jnp.zeros((tile, width), jnp.float32)
            grad_mixed = jnp.zeros((tile, width), jnp.float32)
            for j in range(KT):
                shifted = mixed_s[first + PAD - j : first + PAD - j + tile, :]
                filtered = filtered + taps[j : j + 1, :] * shifted
                sums[j] = sums[j] + (gf * shifted).reshape(tile // 8, 8, width).sum(axis=0)
                grad_mixed = grad_mixed + taps[j : j + 1, :] * gf_s[first + j : first + j + tile, :]
            out_s[a, inside, :] = (q_s[rows, :].astype(jnp.float32) * filtered).astype(jnp.bfloat16)
            at = col ^ a
            far_s[at, 0, inside, :] = (up_s[rows, :].astype(jnp.float32) * filtered).astype(jnp.bfloat16)
            far_s[at, 1, inside, :] = (grad_mixed * v_s[rows, :].astype(jnp.float32)).astype(jnp.bfloat16)
            far_s[at, 2, inside, :] = (grad_mixed * k_s[rows, :].astype(jnp.float32)).astype(jnp.bfloat16)
    for k in range(groups):
        grad_refs[k][...] = far_s[k]
    rest = jnp.concatenate(
        [sums[j].sum(axis=0, keepdims=True) for j in range(KT)] + [jnp.zeros((1, width), jnp.float32)], axis=0
    )
    terms_of = [term.astype(jnp.float32) for term in in_three(rest)]
    packed = jnp.concatenate(terms_of + [jnp.zeros((8, width), jnp.float32)], axis=0).astype(jnp.bfloat16)
    for k, ref in enumerate(out_refs):
        ref[0:tok, :] = out_s[col ^ k]
        ref[tok : tok + 32, :] = packed


def middle(place, taps, ups, pieces, parts, tile):
    groups, terms = len(ups), len(parts[0])
    tok, width = ups[0].shape
    total = groups * tok
    whole = lambda *shape: resident(shape, width)
    ones = [whole(1, 3, terms_of[0].shape[2], width) for terms_of in parts for _ in terms_of]
    outs = pl.pallas_call(
        functools.partial(middle_kernel, pieces=pieces, groups=groups, terms=terms, tile=tile),
        grid_spec=pltpu.PrefetchScalarGridSpec(
            num_scalar_prefetch=1,
            grid=(1,),
            in_specs=[whole(*taps.shape)] + [whole(tok, width)] * groups + ones,
            out_specs=[whole(3, tok, width)] * groups + [whole(tok + 32, width)] * groups,
            scratch_shapes=[
                pltpu.VMEM((total, width), jnp.bfloat16),
                pltpu.VMEM((groups, tok, width), jnp.bfloat16),
            ]
            + [pltpu.VMEM((total, width), jnp.bfloat16)] * 3
            + [pltpu.VMEM((total + PAD, width), jnp.float32)] * 2
            + [pltpu.VMEM((groups, 3, tok, width), jnp.bfloat16)],
        ),
        out_shape=[jax.ShapeDtypeStruct((3, tok, width), jnp.bfloat16)] * groups
        + [jax.ShapeDtypeStruct((tok + 32, width), jnp.bfloat16)] * groups,
        compiler_params=params(10, width),
        cost_estimate=SMALL,
        name="middle",
    )(place, taps, *ups, *[term for terms_of in parts for term in terms_of])
    return outs[:groups], outs[groups:]


def assemble_kernel(place, *refs):
    grad_refs, out_ref = refs[:-1], refs[-1]
    width = grad_refs[0].shape[2]
    for r, ref in enumerate(grad_refs):
        for s in range(3):
            at = pl.multiple_of((s * len(grad_refs) + (place[0] ^ r)) * width, width)
            out_ref[:, pl.ds(at, width)] = ref[s]


def assemble(place, grads):
    streams, tok, width = grads[0].shape
    out = jax.ShapeDtypeStruct((tok, streams * width * len(grads)), jnp.bfloat16)
    if width % LANES:
        whole = jnp.stack(grads)[place[0] ^ jnp.arange(len(grads))]
        return jnp.transpose(whole, (2, 1, 0, 3)).reshape(out.shape)
    return pl.pallas_call(
        assemble_kernel,
        grid_spec=pltpu.PrefetchScalarGridSpec(
            num_scalar_prefetch=1,
            grid=(1,),
            in_specs=[resident(grads[0].shape, width)] * len(grads),
            out_specs=resident(out.shape, width),
        ),
        out_shape=out,
        compiler_params=params(4, width),
        cost_estimate=SMALL,
        name="assemble",
    )(place, *grads)


def input_grad_kernel(grad_ref, w_ref, out_ref, *, first):
    step = out_ref.shape[1]
    rows = w_ref[:, :, first * step : (first + 1) * step].reshape(-1, step)
    out_ref[...] = jnp.dot(grad_ref[...], rows, preferred_element_type=jnp.float32).astype(jnp.bfloat16)


def input_grads_kernel(grad_ref, w_ref, *refs, first):
    out_refs, (slots, sems) = refs[:-2], refs[-2:]
    step = out_refs[0].shape[1]

    def fetch(i):
        columns = pl.ds((first + i) * step, step)
        return pltpu.make_async_copy(w_ref.at[:, :, columns], slots.at[i % 2], sems.at[i % 2])

    fetch(0).start()
    for i, out_ref in enumerate(out_refs):
        if i + 1 < len(out_refs):
            fetch(i + 1).start()
        fetch(i).wait()
        rows = slots[i % 2].reshape(-1, step)
        out_ref[...] = jnp.dot(grad_ref[...], rows, preferred_element_type=jnp.float32).astype(jnp.bfloat16)


def input_grad(grad, w, first, last, chunks, width):
    tok = grad.shape[0]
    streams, channels, feat = w.shape
    step = feat // chunks
    count = last - first
    if width % LANES:
        rows = w[:, :, first * step : last * step].reshape(streams * channels, count * step)
        whole = jnp.dot(grad, rows, preferred_element_type=jnp.float32).astype(jnp.bfloat16)
        return [whole[:, i * step : (i + 1) * step] for i in range(count)]
    single = count == 1
    return list(
        pl.pallas_call(
            functools.partial(input_grad_kernel if single else input_grads_kernel, first=first),
            in_specs=[
                resident(grad.shape, width),
                pl.BlockSpec(memory_space=pltpu.VMEM if single else pltpu.HBM),
            ],
            out_specs=[resident((tok, step), width)] * count,
            out_shape=[jax.ShapeDtypeStruct((tok, step), jnp.bfloat16)] * count,
            scratch_shapes=[]
            if single
            else [pltpu.VMEM((2, streams, channels, step), jnp.bfloat16), pltpu.SemaphoreType.DMA((2,))],
            compiler_params=params(8, width),
            cost_estimate=SMALL,
            name="input_grad",
        )(grad, w)
    )


def weight_grad_kernel(*refs, chained, groups, half):
    refs = refs[2 * chained :]
    grad_refs, x_refs = refs[:groups], refs[groups : 2 * groups]
    out_ref, mark_ref, turned = refs[2 * groups :]
    mark_ref[...] = jnp.zeros(mark_ref.shape, jnp.float32)
    streams, channels, step = out_ref.shape
    tok = x_refs[0].shape[0]

    @pl.when(pl.program_id(0) == 0)
    def _():
        for k in range(groups):
            for s in range(streams):
                at = (2 * s + half) * channels
                block = grad_refs[k][:, at : at + channels]
                turned[s * channels : (s + 1) * channels, k * tok : (k + 1) * tok] = block.T

    columns = pl.ds(pl.multiple_of(pl.program_id(0) * step, step), step)
    acc = None
    for k in range(groups):
        term = jnp.dot(turned[:, k * tok : (k + 1) * tok], x_refs[k][:, columns], preferred_element_type=jnp.float32)
        acc = term if acc is None else acc + term
    for s in range(streams):
        out_ref[s] = acc[s * channels : (s + 1) * channels, :]


def weight_grad(filled, grads, xs, half, streams, width):
    groups = len(xs)
    tok, feat = xs[0].shape
    channels = grads[0].shape[1] // streams
    chained = filled is not None
    if width % LANES:
        if chained:
            return filled
        terms = [
            lax.dot_general(grad, x, (((0,), (0,)), ((), ())), preferred_element_type=jnp.float32)
            for grad, x in zip(grads, xs)
        ]
        return sum(terms).reshape(streams, channels, feat), jnp.zeros((8, LANES), jnp.float32)
    step = min(512, feat)
    return pl.pallas_call(
        functools.partial(weight_grad_kernel, chained=chained, groups=groups, half=half),
        grid=(feat // step,),
        in_specs=[pl.BlockSpec(memory_space=pl.ANY)] * (2 * chained)
        + [resident(grads[0].shape, width)] * groups
        + [resident((tok, feat), width)] * groups,
        out_specs=[
            pl.BlockSpec((streams, channels // 2, step), lambda i: (0, half, i)),
            resident((8, LANES), width),
        ],
        scratch_shapes=[pltpu.VMEM((streams * channels // 2, groups * tok), jnp.bfloat16)],
        out_shape=[
            jax.ShapeDtypeStruct((streams, channels, feat), jnp.float32),
            jax.ShapeDtypeStruct((8, LANES), jnp.float32),
        ],
        input_output_aliases={0: 0} if chained else {},
        compiler_params=params(14, width),
        cost_estimate=SMALL,
        name="weight_grad",
    )(*(filled if chained else []), *grads, *xs)


def added(first, second):
    return (first.astype(jnp.float32) + second.astype(jnp.float32)).astype(jnp.bfloat16)


def on_device(tokens, weight, taps, upstream):
    n_col = lax.axis_size("col")
    n_depth = lax.axis_size("depth")
    local_tok = upstream.shape[0]
    depth_at = lax.axis_index("depth")
    col_at = lax.axis_index("col")
    row_at = lax.axis_index("row")
    place = jnp.stack([depth_at, col_at, row_at, col_at * n_depth + depth_at]).astype(jnp.int32)
    w = jnp.transpose(weight, (1, 0, 2))
    width = w.shape[1] // n_depth
    def sum_over_depth(keep, send, near_after=(), far_after=()):
        near = swap(after(send, *near_after) if near_after else send, "depth", 1)
        pairs = [added(keep[r // 2], near[r // 2])[None] for r in range(2, n_depth, 2)]
        held = [after(pair, *far_after) if far_after else pair for pair in pairs]
        fars = [swap(pair, "depth", 2 * i + 2) for i, pair in enumerate(held)]
        return [keep, near] + fars, pairs, fars

    tok = tokens.shape[0]
    third = tok // 3
    cut = tok % 192 == 0 and lax.axis_size("row") % 2 == 0
    sent_first = lax.dynamic_slice_in_dim(tokens, row_at % 2 * third, third, axis=0) if cut else tokens
    first = [swap(sent_first, "col", k) for k in range(1, n_col)]
    ups = split_lanes(place, upstream, n_col, n_depth)
    ups = [up if r == 0 else swap(up, "depth", r) for r, up in enumerate(ups)]
    keep, send, *last = project(place, [tokens], w, n_depth, "cut" if cut else "plain")
    terms, pairs, fars = sum_over_depth(keep, send, first + ups[1:])
    xs, pieces, parts = [tokens], [(0, ("all",))], [terms]
    for k in range(1, n_col):
        mine = first[k - 1]
        if not cut:
            keep, send = project(place, [after(mine, *fars)], w, n_depth)
            terms, pairs, fars = sum_over_depth(keep, send)
            xs.append(mine)
            pieces.append((k, ("all",)))
            parts.append(terms)
            continue
        other = swap(mine, "row", 1)
        rest = swap(after(last[0], mine), "col", k)
        keep, send = project(place, [after(mine, *pairs)], w, n_depth)
        terms, ahead, ahead_fars = sum_over_depth(keep, send)
        pieces.append((k, ("own",)))
        parts.append(terms)
        keep, send, x = project(place, [mine, other, after(rest, *fars, *ahead)], w, n_depth, "join")
        terms, pairs, fars = sum_over_depth(keep, send, (), ahead_fars)
        pieces.append((k, ("other", "last")))
        parts.append(terms)
        xs.append(x)
    ups = merge_rows(place, [after(ups[0], *pairs)] + ups[1:])
    ups = [up if k == 0 else swap(up, "col", k) for k, up in enumerate(ups)]
    own_grads, blocks = middle(place, taps, ups, pieces, parts, local_tok)
    nears = [swap(own, "depth", 1) for own in own_grads]
    blocks = [block if k == 0 else swap(block, "col", k) for k, block in enumerate(blocks)]
    beside = nears + blocks[1:]
    chunks = 4
    grads = [None] * n_col
    ready = []
    sent = []
    lhs = [None] * n_col
    for k in reversed(range(n_col)):
        fars = [swap(after(own_grads[k], *ready) if ready else own_grads[k], "depth", r) for r in range(2, n_depth, 2)]
        ready = fars
        if k > 0:
            fars = [after(far, *beside) for far in fars]
        elif sent:
            fars = [after(far, sent[-1][1][-1]) for far in fars]
        grads[k] = [own_grads[k], nears[k]]
        for far in fars:
            grads[k] += [far, swap(far, "depth", 1)]
        lhs[k] = assemble(place, grads[k])
        if k > 0:
            parts_of = input_grad(lhs[k], w, 0, 1, chunks, width)
            parts_of += input_grad(after(lhs[k], *parts_of), w, 1, chunks, chunks, width)
            sent.append(([swap(part, "col", k) for part in parts_of[:3]], parts_of))
    held = [parts_of[3:] for _, parts_of in sent]
    sent = [of for of, _ in sent]
    own_part = input_grad(lhs[0], w, 0, 1, chunks, width)
    outer = (row_at == 0) | (row_at == 3)
    line = lax.axis_size("row") == 4
    inward, across, summed, done = ([None] * chunks for _ in range(4))
    pair = cross = filled = None
    marks = []
    for slot in range(chunks + 3):
        if slot < chunks:
            total = after(own_part[slot], *marks).astype(jnp.float32)
            for of in sent:
                total = total + of[slot].astype(jnp.float32)
            inward[slot] = total.astype(jnp.bfloat16)
            marks = [inward[slot]]
        if not line:
            if slot < chunks:
                done[slot] = lax.psum(inward[slot], "row")
        else:
            if 0 <= slot - 1 < chunks:
                across[slot - 1] = added(after(inward[slot - 1], *marks), pair)
                marks = [across[slot - 1]]
            if 0 <= slot - 2 < chunks:
                summed[slot - 2] = added(after(across[slot - 2], *marks), cross)
                marks = [summed[slot - 2]]
            if 0 <= slot - 3 < chunks:
                done[slot - 3] = jnp.where(outer, pair, summed[slot - 3])
            if slot < chunks + 2:
                out = summed[slot - 2] if slot >= 2 else inward[slot]
                pair = swap(jnp.where(outer, inward[slot], out) if slot < chunks else out, "row", 1)
            if 0 <= slot - 1 < chunks:
                cross = lax.ppermute(across[slot - 1], "row", [(0, 0), (1, 2), (2, 1), (3, 3)])
        if slot == 0:
            own_part += input_grad(after(lhs[0], *marks), w, 1, chunks, chunks, width)
            marks = [own_part[1]]
            for k, parts_of in enumerate(held):
                sent[k] += [swap(after(part, *marks), "col", k + 1) for part in parts_of]
        if slot in (2, 4):
            filled = weight_grad(filled, [after(lhs[0], *marks)] + lhs[1:], xs, slot // 2 - 1, 3, width)
            marks = [filled[1]]
        if slot == 4:
            marks += late
        if slot == 3:
            blocks = split_rows(place, [after(blocks[0], *marks)] + blocks[1:], n_depth)
            blocks = [block if r == 0 else swap(block, "depth", r) for r, block in enumerate(blocks)]
            late = blocks[1:]
    grad_tokens = jnp.concatenate(done, axis=1)
    output, grad_taps = join(place, filled[1], [after(blocks[0], *marks)] + blocks[1:], taps.shape[1])
    grad_weight = jnp.transpose(filled[0], (1, 0, 2))
    return (output, grad_tokens, grad_weight, grad_taps)


def solution(mesh):
    in_specs = (
        P("col", "depth"),
        P(("row", "col"), None, "depth"),
        P(None, "row"),
        P(("col", "depth"), "row"),
    )
    out_specs = (
        P(("col", "depth"), "row"),
        P("col", "depth"),
        P(("row", "col"), None, "depth"),
        P(None, "row"),
    )
    return jax.shard_map(
        on_device, mesh=mesh, in_specs=in_specs, out_specs=out_specs, check_vma=False
    )
```

```python
import functools

import jax
import jax.numpy as jnp
from jax import lax
from jax.experimental import pallas as pl
from jax.experimental.pallas import tpu as pltpu
from jax.sharding import PartitionSpec as P

GROUP = 16
KT = 7
PAD = 8
LANES = 128
MIB = 1024 * 1024
SMALL = pl.CostEstimate(flops=1, bytes_accessed=1, transcendentals=0)


def swap(value, axis, flip):
    count = lax.axis_size(axis)
    return lax.ppermute(value, axis, [(i, i ^ flip) for i in range(count)])


def after(value, *earlier):
    return lax.optimization_barrier((value, *earlier))[0]


def resident(shape, width):
    if width % LANES == 0:
        return pl.BlockSpec(memory_space=pltpu.VMEM)
    return pl.BlockSpec(tuple(shape), lambda *_: (0,) * len(shape), pipeline_mode=pl.Buffered(1))


def params(mib, width):
    return pltpu.CompilerParams(vmem_limit_bytes=(mib if width % LANES == 0 else 56) * MIB)


def project_kernel(place, *refs, pieces, mode, count, width):
    x_refs = refs[:pieces]
    w_ref, keep_ref, send_ref = refs[pieces : pieces + 3]
    stream = pl.program_id(0)
    core = place[0] % 2
    x = x_refs[0][...]
    if mode == "cut":
        last_ref = refs[pieces + 3]

        @pl.when(stream == 0)
        def _():
            last_ref[...] = x_refs[0][x.shape[0] - last_ref.shape[0] :, :]

    if mode == "join":
        joined, rest = refs[pieces + 3 :]
        third = x.shape[0]
        parity = place[2] % 2

        @pl.when(stream == 0)
        def _():
            joined[pl.ds(pl.multiple_of(parity * third, third), third), :] = x_refs[0][...]
            joined[pl.ds(pl.multiple_of((1 - parity) * third, third), third), :] = x_refs[1][...]
            joined[2 * third :, :] = x_refs[2][...]
            rest[0:third, :] = x_refs[1][...]
            rest[third:, :] = x_refs[2][...]

        x = rest[...]
    nt = (((1,), (1,)), ((), ()))
    if width % LANES == 0:
        whole = lax.dot_general(x, w_ref[stream], nt, preferred_element_type=jnp.float32).astype(jnp.bfloat16)
        blocks = [whole[:, j * width : (j + 1) * width] for j in range(count)]
    else:
        blocks = [
            lax.dot_general(
                x, w_ref[0, j * width : (j + 1) * width, :], nt, preferred_element_type=jnp.float32
            ).astype(jnp.bfloat16)
            for j in range(count)
        ]
    for mine in range(2):

        @pl.when(core == mine)
        def _():
            for j in range(count):
                at = (j ^ place[0]) // 2
                if j % 2 == mine:
                    keep_ref[at, stream] = blocks[j]
                else:
                    send_ref[at, stream] = blocks[j]


def project(place, xs, w, count, mode="plain"):
    feat = xs[0].shape[1]
    all_tok = sum(x.shape[0] for x in xs)
    tok = all_tok - xs[0].shape[0] if mode == "join" else all_tok
    streams, channels, _ = w.shape
    width = channels // count
    part = jax.ShapeDtypeStruct((count // 2, streams, tok, width), jnp.bfloat16)
    wide = width % LANES == 0
    spec = resident(part.shape, width)
    more = {"plain": [], "cut": [(tok // 3, feat)], "join": [(all_tok, feat)]}[mode]
    return pl.pallas_call(
        functools.partial(project_kernel, pieces=len(xs), mode=mode, count=count, width=width),
        grid_spec=pltpu.PrefetchScalarGridSpec(
            num_scalar_prefetch=1,
            grid=(streams,),
            in_specs=[resident(x.shape, width) for x in xs]
            + [resident(w.shape, width) if wide else pl.BlockSpec((1, channels, feat), lambda s, _: (s, 0, 0))],
            out_specs=[spec, spec] + [resident(shape, width) for shape in more],
            scratch_shapes=[pltpu.VMEM((tok, feat), jnp.bfloat16)] if mode == "join" else [],
        ),
        out_shape=[part, part] + [jax.ShapeDtypeStruct(shape, jnp.bfloat16) for shape in more],
        compiler_params=params(10, width),
        cost_estimate=SMALL,
        name="project",
    )(place, *xs, w)


def in_three(value):
    terms = []
    for _ in range(3):
        term = value.astype(jnp.bfloat16)
        value = value - term.astype(jnp.float32)
        terms.append(term)
    return terms


def split_lanes_kernel(place, up_ref, *out_refs):
    n_depth, width = len(out_refs), out_refs[0].shape[2]
    for r, ref in enumerate(out_refs):
        for k in range(ref.shape[0]):
            at = ((place[1] ^ k) * n_depth + (place[0] ^ r)) * width
            ref[k] = up_ref[:, pl.ds(pl.multiple_of(at, width), width)]


def merge_rows_kernel(place, *refs, n_depth):
    in_refs, out_refs = refs[:n_depth], refs[n_depth:]
    local = in_refs[0].shape[1]
    for r, ref in enumerate(in_refs):
        for k, out_ref in enumerate(out_refs):
            out_ref[pl.ds(pl.multiple_of((place[0] ^ r) * local, 16), local), :] = ref[k]


def split_rows_kernel(place, *refs, n_col):
    in_refs, out_refs = refs[:n_col], refs[n_col:]
    local = out_refs[0].shape[1] - 32
    for r, ref in enumerate(out_refs):
        rows = pl.ds(pl.multiple_of((place[0] ^ r) * local, 16), local)
        for k in range(n_col):
            ref[k, 0:local] = in_refs[k][rows, :]
            ref[k, local:] = in_refs[k][-32:, :]


def rearrange(kernel, place, arrays, count, shape, name):
    width = shape[-1]
    return pl.pallas_call(
        kernel,
        grid_spec=pltpu.PrefetchScalarGridSpec(
            num_scalar_prefetch=1,
            grid=(1,),
            in_specs=[resident(value.shape, width) for value in arrays],
            out_specs=[resident(shape, width)] * count,
        ),
        out_shape=[jax.ShapeDtypeStruct(shape, jnp.bfloat16)] * count,
        compiler_params=params(4, width),
        cost_estimate=SMALL,
        name=name,
    )(place, *arrays)


def split_lanes(place, up, n_col, n_depth):
    local, width = up.shape[0], up.shape[1] // (n_col * n_depth)
    if width % LANES:
        blocks = up.reshape(local, n_col, n_depth, width)[:, place[1] ^ jnp.arange(n_col)]
        return [
            jnp.transpose(lax.dynamic_index_in_dim(blocks, place[0] ^ r, 2, keepdims=False), (1, 0, 2))
            for r in range(n_depth)
        ]
    return rearrange(split_lanes_kernel, place, [up], n_depth, (n_col, local, width), "split")


def merge_rows(place, pieces):
    n_depth = len(pieces)
    n_col, local, width = pieces[0].shape
    if width % LANES:
        whole = jnp.stack(pieces)[place[0] ^ jnp.arange(n_depth)]
        return list(jnp.transpose(whole, (1, 0, 2, 3)).reshape(n_col, n_depth * local, width))
    kernel = functools.partial(merge_rows_kernel, n_depth=n_depth)
    return list(rearrange(kernel, place, pieces, n_col, (n_depth * local, width), "merge"))


def split_rows(place, arrays, n_depth):
    local, width = (arrays[0].shape[0] - 32) // n_depth, arrays[0].shape[1]
    if width % LANES:
        whole = jnp.stack(arrays)
        return [
            jnp.concatenate(
                [lax.dynamic_slice_in_dim(whole, (place[0] ^ r) * local, local, axis=1), whole[:, -32:]], axis=1
            )
            for r in range(n_depth)
        ]
    kernel = functools.partial(split_rows_kernel, n_col=len(arrays))
    return rearrange(kernel, place, arrays, n_depth, (len(arrays), local + 32, width), "split")


def join_kernel(place, _, *refs):
    block_refs, (out_ref, grad_taps_ref) = refs[:-2], refs[-2:]
    n_depth = len(block_refs)
    n_col, _, width = block_refs[0].shape
    local, groups = out_ref.shape[0], grad_taps_ref.shape[1]
    lane_group = lax.broadcasted_iota(jnp.int32, (width, groups), 0) // GROUP
    group = lax.broadcasted_iota(jnp.int32, (width, groups), 1)
    total = jnp.zeros((24, groups), jnp.float32)
    for r, ref in enumerate(block_refs):
        for k in range(n_col):
            at = (place[1] ^ k) * n_depth + (place[0] ^ r)
            out_ref[:, pl.ds(pl.multiple_of(at * width, width), width)] = ref[k, 0:local, :]
            spread = (lane_group + at * (width // GROUP) == group).astype(jnp.bfloat16)
            total = total + jnp.dot(ref[k, local : local + 24, :], spread, preferred_element_type=jnp.float32)
    grad_taps_ref[...] = (total[0:8] + total[8:16] + total[16:24])[:KT]


def join(place, mark, blocks, groups):
    n_depth = len(blocks)
    n_col, rows, width = blocks[0].shape
    local = rows - 32
    if width % LANES:
        whole = jnp.stack(blocks)[place[0] ^ jnp.arange(n_depth)][:, place[1] ^ jnp.arange(n_col)]
        sums = whole[:, :, local : local + 24].astype(jnp.float32)
        sums = sums.reshape(n_depth, n_col, 3, 8, width // GROUP, GROUP).sum(axis=(2, 5))[:, :, :KT]
        return (
            jnp.transpose(whole[:, :, :local], (2, 1, 0, 3)).reshape(local, -1),
            jnp.transpose(sums, (2, 1, 0, 3)).reshape(KT, -1),
        )
    channels = n_depth * n_col * width
    return pl.pallas_call(
        join_kernel,
        grid_spec=pltpu.PrefetchScalarGridSpec(
            num_scalar_prefetch=1,
            grid=(1,),
            in_specs=[pl.BlockSpec(memory_space=pl.ANY)] + [resident(blocks[0].shape, width)] * n_depth,
            out_specs=[resident((local, channels), width), resident((KT, groups), width)],
        ),
        out_shape=[
            jax.ShapeDtypeStruct((local, channels), jnp.bfloat16),
            jax.ShapeDtypeStruct((KT, groups), jnp.float32),
        ],
        compiler_params=params(4, width),
        cost_estimate=SMALL,
        name="join",
    )(place, mark, *blocks)


def middle_kernel(place, taps_ref, *refs, pieces, groups, terms, tile):
    up_refs, refs = refs[:groups], refs[groups:]
    part_refs, refs = refs[: len(pieces) * terms], refs[len(pieces) * terms :]
    grad_refs, out_refs = refs[:groups], refs[groups : 2 * groups]
    up_s, out_s, q_s, k_s, v_s, mixed_s, gf_s, far_s = refs[2 * groups :]
    col = place[1]
    tok, width = up_refs[0].shape
    parity = place[2] % 2
    total = groups * tok
    tap_groups = taps_ref.shape[1]
    for k, ref in enumerate(up_refs):
        up_s[pl.ds(pl.multiple_of((col ^ k) * tok, tok), tok), :] = ref[...]
    lane_group = lax.broadcasted_iota(jnp.int32, (tap_groups, width), 1) // GROUP
    group = lax.broadcasted_iota(jnp.int32, (tap_groups, width), 0)
    spread = (lane_group + place[3] * (width // GROUP) == group).astype(jnp.bfloat16)
    taps = sum(jnp.dot(term, spread, preferred_element_type=jnp.float32) for term in in_three(taps_ref[...]))
    mixed_s[0:PAD, :] = jnp.zeros((PAD, width), jnp.float32)
    gf_s[total : total + PAD, :] = jnp.zeros((PAD, width), jnp.float32)
    step = 64
    for piece, (k, thirds) in enumerate(pieces):
        refs_of = part_refs[piece * terms : (piece + 1) * terms]
        rows_of = refs_of[0].shape[2]
        length = rows_of // len(thirds)
        for i in range(rows_of // step):
            third = thirds[i * step // length]
            at = {"own": parity, "other": 1 - parity, "last": 2, "all": 0}[third] * length
            start = (col ^ k) * tok + at + i * step % length
            inside = slice(i * step, (i + 1) * step)
            rows = pl.ds(pl.multiple_of(start, step), step)
            streams = []
            for s in range(3):
                acc = None
                for ref in refs_of:
                    term = ref[0, s, inside, :].astype(jnp.float32)
                    acc = term if acc is None else acc + term
                streams.append(acc.astype(jnp.bfloat16))
            q_s[rows, :], k_s[rows, :], v_s[rows, :] = streams
            query, key, value = [stream.astype(jnp.float32) for stream in streams]
            mixed_s[pl.ds(pl.multiple_of(start + PAD, PAD), step), :] = key * value
            gf_s[rows, :] = up_s[rows, :].astype(jnp.float32) * query
    sums = [jnp.zeros((8, width), jnp.float32) for _ in range(KT)]
    for a in range(groups):
        for i in range(tok // tile):
            first = a * tok + i * tile
            rows = slice(first, first + tile)
            inside = slice(i * tile, (i + 1) * tile)
            gf = gf_s[rows, :]
            filtered = jnp.zeros((tile, width), jnp.float32)
            grad_mixed = jnp.zeros((tile, width), jnp.float32)
            for j in range(KT):
                shifted = mixed_s[first + PAD - j : first + PAD - j + tile, :]
                filtered = filtered + taps[j : j + 1, :] * shifted
                sums[j] = sums[j] + (gf * shifted).reshape(tile // 8, 8, width).sum(axis=0)
                grad_mixed = grad_mixed + taps[j : j + 1, :] * gf_s[first + j : first + j + tile, :]
            out_s[a, inside, :] = (q_s[rows, :].astype(jnp.float32) * filtered).astype(jnp.bfloat16)
            at = col ^ a
            far_s[at, 0, inside, :] = (up_s[rows, :].astype(jnp.float32) * filtered).astype(jnp.bfloat16)
            far_s[at, 1, inside, :] = (grad_mixed * v_s[rows, :].astype(jnp.float32)).astype(jnp.bfloat16)
            far_s[at, 2, inside, :] = (grad_mixed * k_s[rows, :].astype(jnp.float32)).astype(jnp.bfloat16)
    for k in range(groups):
        grad_refs[k][...] = far_s[k]
    rest = jnp.concatenate(
        [sums[j].sum(axis=0, keepdims=True) for j in range(KT)] + [jnp.zeros((1, width), jnp.float32)], axis=0
    )
    terms_of = [term.astype(jnp.float32) for term in in_three(rest)]
    packed = jnp.concatenate(terms_of + [jnp.zeros((8, width), jnp.float32)], axis=0).astype(jnp.bfloat16)
    for k, ref in enumerate(out_refs):
        ref[0:tok, :] = out_s[col ^ k]
        ref[tok : tok + 32, :] = packed


def middle(place, taps, ups, pieces, parts, tile):
    groups, terms = len(ups), len(parts[0])
    tok, width = ups[0].shape
    total = groups * tok
    whole = lambda *shape: resident(shape, width)
    ones = [whole(1, 3, terms_of[0].shape[2], width) for terms_of in parts for _ in terms_of]
    outs = pl.pallas_call(
        functools.partial(middle_kernel, pieces=pieces, groups=groups, terms=terms, tile=tile),
        grid_spec=pltpu.PrefetchScalarGridSpec(
            num_scalar_prefetch=1,
            grid=(1,),
            in_specs=[whole(*taps.shape)] + [whole(tok, width)] * groups + ones,
            out_specs=[whole(3, tok, width)] * groups + [whole(tok + 32, width)] * groups,
            scratch_shapes=[
                pltpu.VMEM((total, width), jnp.bfloat16),
                pltpu.VMEM((groups, tok, width), jnp.bfloat16),
            ]
            + [pltpu.VMEM((total, width), jnp.bfloat16)] * 3
            + [pltpu.VMEM((total + PAD, width), jnp.float32)] * 2
            + [pltpu.VMEM((groups, 3, tok, width), jnp.bfloat16)],
        ),
        out_shape=[jax.ShapeDtypeStruct((3, tok, width), jnp.bfloat16)] * groups
        + [jax.ShapeDtypeStruct((tok + 32, width), jnp.bfloat16)] * groups,
        compiler_params=params(10, width),
        cost_estimate=SMALL,
        name="middle",
    )(place, taps, *ups, *[term for terms_of in parts for term in terms_of])
    return outs[:groups], outs[groups:]


def assemble_kernel(place, *refs):
    grad_refs, out_ref = refs[:-1], refs[-1]
    width = grad_refs[0].shape[2]
    for r, ref in enumerate(grad_refs):
        for s in range(3):
            at = pl.multiple_of((s * len(grad_refs) + (place[0] ^ r)) * width, width)
            out_ref[:, pl.ds(at, width)] = ref[s]


def assemble(place, grads):
    streams, tok, width = grads[0].shape
    out = jax.ShapeDtypeStruct((tok, streams * width * len(grads)), jnp.bfloat16)
    if width % LANES:
        whole = jnp.stack(grads)[place[0] ^ jnp.arange(len(grads))]
        return jnp.transpose(whole, (2, 1, 0, 3)).reshape(out.shape)
    return pl.pallas_call(
        assemble_kernel,
        grid_spec=pltpu.PrefetchScalarGridSpec(
            num_scalar_prefetch=1,
            grid=(1,),
            in_specs=[resident(grads[0].shape, width)] * len(grads),
            out_specs=resident(out.shape, width),
        ),
        out_shape=out,
        compiler_params=params(4, width),
        cost_estimate=SMALL,
        name="assemble",
    )(place, *grads)


def input_grad_kernel(grad_ref, w_ref, out_ref, *, first):
    step = out_ref.shape[1]
    rows = w_ref[:, :, first * step : (first + 1) * step].reshape(-1, step)
    out_ref[...] = jnp.dot(grad_ref[...], rows, preferred_element_type=jnp.float32).astype(jnp.bfloat16)


def input_grads_kernel(grad_ref, w_ref, *refs, first):
    out_refs, (slots, sems) = refs[:-2], refs[-2:]
    step = out_refs[0].shape[1]

    def fetch(i):
        columns = pl.ds((first + i) * step, step)
        return pltpu.make_async_copy(w_ref.at[:, :, columns], slots.at[i % 2], sems.at[i % 2])

    fetch(0).start()
    for i, out_ref in enumerate(out_refs):
        if i + 1 < len(out_refs):
            fetch(i + 1).start()
        fetch(i).wait()
        rows = slots[i % 2].reshape(-1, step)
        out_ref[...] = jnp.dot(grad_ref[...], rows, preferred_element_type=jnp.float32).astype(jnp.bfloat16)


def input_grad(grad, w, first, last, chunks, width):
    tok = grad.shape[0]
    streams, channels, feat = w.shape
    step = feat // chunks
    count = last - first
    if width % LANES:
        rows = w[:, :, first * step : last * step].reshape(streams * channels, count * step)
        whole = jnp.dot(grad, rows, preferred_element_type=jnp.float32).astype(jnp.bfloat16)
        return [whole[:, i * step : (i + 1) * step] for i in range(count)]
    single = count == 1
    return list(
        pl.pallas_call(
            functools.partial(input_grad_kernel if single else input_grads_kernel, first=first),
            in_specs=[
                resident(grad.shape, width),
                pl.BlockSpec(memory_space=pltpu.VMEM if single else pltpu.HBM),
            ],
            out_specs=[resident((tok, step), width)] * count,
            out_shape=[jax.ShapeDtypeStruct((tok, step), jnp.bfloat16)] * count,
            scratch_shapes=[]
            if single
            else [pltpu.VMEM((2, streams, channels, step), jnp.bfloat16), pltpu.SemaphoreType.DMA((2,))],
            compiler_params=params(8, width),
            cost_estimate=SMALL,
            name="input_grad",
        )(grad, w)
    )


def weight_grad_kernel(*refs, chained, groups, half):
    refs = refs[2 * chained :]
    grad_refs, x_refs = refs[:groups], refs[groups : 2 * groups]
    out_ref, mark_ref, turned = refs[2 * groups :]
    mark_ref[...] = jnp.zeros(mark_ref.shape, jnp.float32)
    streams, channels, step = out_ref.shape
    tok = x_refs[0].shape[0]

    @pl.when(pl.program_id(0) == 0)
    def _():
        for k in range(groups):
            for s in range(streams):
                at = (2 * s + half) * channels
                block = grad_refs[k][:, at : at + channels]
                turned[s * channels : (s + 1) * channels, k * tok : (k + 1) * tok] = block.T

    columns = pl.ds(pl.multiple_of(pl.program_id(0) * step, step), step)
    acc = None
    for k in range(groups):
        term = jnp.dot(turned[:, k * tok : (k + 1) * tok], x_refs[k][:, columns], preferred_element_type=jnp.float32)
        acc = term if acc is None else acc + term
    for s in range(streams):
        out_ref[s] = acc[s * channels : (s + 1) * channels, :]


def weight_grad(filled, grads, xs, half, streams, width):
    groups = len(xs)
    tok, feat = xs[0].shape
    channels = grads[0].shape[1] // streams
    chained = filled is not None
    if width % LANES:
        if chained:
            return filled
        terms = [
            lax.dot_general(grad, x, (((0,), (0,)), ((), ())), preferred_element_type=jnp.float32)
            for grad, x in zip(grads, xs)
        ]
        return sum(terms).reshape(streams, channels, feat), jnp.zeros((8, LANES), jnp.float32)
    step = min(512, feat)
    return pl.pallas_call(
        functools.partial(weight_grad_kernel, chained=chained, groups=groups, half=half),
        grid=(feat // step,),
        in_specs=[pl.BlockSpec(memory_space=pl.ANY)] * (2 * chained)
        + [resident(grads[0].shape, width)] * groups
        + [resident((tok, feat), width)] * groups,
        out_specs=[
            pl.BlockSpec((streams, channels // 2, step), lambda i: (0, half, i)),
            resident((8, LANES), width),
        ],
        scratch_shapes=[pltpu.VMEM((streams * channels // 2, groups * tok), jnp.bfloat16)],
        out_shape=[
            jax.ShapeDtypeStruct((streams, channels, feat), jnp.float32),
            jax.ShapeDtypeStruct((8, LANES), jnp.float32),
        ],
        input_output_aliases={0: 0} if chained else {},
        compiler_params=params(14, width),
        cost_estimate=SMALL,
        name="weight_grad",
    )(*(filled if chained else []), *grads, *xs)


def added(first, second):
    return (first.astype(jnp.float32) + second.astype(jnp.float32)).astype(jnp.bfloat16)


def on_device(tokens, weight, taps, upstream):
    n_col = lax.axis_size("col")
    n_depth = lax.axis_size("depth")
    local_tok = upstream.shape[0]
    depth_at = lax.axis_index("depth")
    col_at = lax.axis_index("col")
    row_at = lax.axis_index("row")
    place = jnp.stack([depth_at, col_at, row_at, col_at * n_depth + depth_at]).astype(jnp.int32)
    w = jnp.transpose(weight, (1, 0, 2))
    width = w.shape[1] // n_depth
    def sum_over_depth(keep, send, near_after=(), far_after=()):
        near = swap(after(send, *near_after) if near_after else send, "depth", 1)
        pairs = [added(keep[r // 2], near[r // 2])[None] for r in range(2, n_depth, 2)]
        held = [after(pair, *far_after) if far_after else pair for pair in pairs]
        fars = [swap(pair, "depth", 2 * i + 2) for i, pair in enumerate(held)]
        return [keep, near] + fars, pairs, fars

    tok = tokens.shape[0]
    third = tok // 3
    cut = tok % 192 == 0 and lax.axis_size("row") % 2 == 0
    sent_first = lax.dynamic_slice_in_dim(tokens, row_at % 2 * third, third, axis=0) if cut else tokens
    first = [swap(sent_first, "col", k) for k in range(1, n_col)]
    ups = split_lanes(place, upstream, n_col, n_depth)
    ups = [up if r == 0 else swap(up, "depth", r) for r, up in enumerate(ups)]
    outer = (row_at == 0) | (row_at == 3)
    keep, send, *last = project(place, [after(tokens, outer)], w, n_depth, "cut" if cut else "plain")
    terms, pairs, fars = sum_over_depth(keep, send, first + ups[1:])
    xs, pieces, parts = [tokens], [(0, ("all",))], [terms]
    for k in range(1, n_col):
        mine = first[k - 1]
        if not cut:
            keep, send = project(place, [after(mine, *fars)], w, n_depth)
            terms, pairs, fars = sum_over_depth(keep, send)
            xs.append(mine)
            pieces.append((k, ("all",)))
            parts.append(terms)
            continue
        other = swap(mine, "row", 1)
        rest = swap(after(last[0], mine), "col", k)
        keep, send = project(place, [after(mine, *pairs)], w, n_depth)
        terms, ahead, ahead_fars = sum_over_depth(keep, send)
        pieces.append((k, ("own",)))
        parts.append(terms)
        keep, send, x = project(place, [mine, other, after(rest, *fars, *ahead)], w, n_depth, "join")
        terms, pairs, fars = sum_over_depth(keep, send, (), ahead_fars)
        pieces.append((k, ("other", "last")))
        parts.append(terms)
        xs.append(x)
    ups = merge_rows(place, [after(ups[0], *pairs)] + ups[1:])
    ups = [up if k == 0 else swap(up, "col", k) for k, up in enumerate(ups)]
    own_grads, blocks = middle(place, taps, ups, pieces, parts, local_tok)
    nears = [swap(own, "depth", 1) for own in own_grads]
    blocks = [block if k == 0 else swap(block, "col", k) for k, block in enumerate(blocks)]
    beside = nears + blocks[1:]
    chunks = 4
    grads = [None] * n_col
    ready = []
    sent = []
    lhs = [None] * n_col
    for k in reversed(range(n_col)):
        fars = [swap(after(own_grads[k], *ready) if ready else own_grads[k], "depth", r) for r in range(2, n_depth, 2)]
        ready = fars
        if k > 0:
            fars = [after(far, *beside) for far in fars]
        elif sent:
            fars = [after(far, sent[-1][1][-1]) for far in fars]
        grads[k] = [own_grads[k], nears[k]]
        for far in fars:
            grads[k] += [far, swap(far, "depth", 1)]
        lhs[k] = assemble(place, grads[k])
        if k > 0:
            parts_of = input_grad(lhs[k], w, 0, 1, chunks, width)
            parts_of += input_grad(after(lhs[k], *parts_of), w, 1, chunks, chunks, width)
            sent.append(([swap(part, "col", k) for part in parts_of[:3]], parts_of))
    held = [parts_of[3:] for _, parts_of in sent]
    sent = [of for of, _ in sent]
    own_part = input_grad(lhs[0], w, 0, 1, chunks, width)
    line = lax.axis_size("row") == 4
    inward, across, summed, done = ([None] * chunks for _ in range(4))
    pair = cross = filled = None
    marks = []
    for slot in range(chunks + 3):
        if slot < chunks:
            total = after(own_part[slot], *marks).astype(jnp.float32)
            for of in sent:
                total = total + of[slot].astype(jnp.float32)
            inward[slot] = total.astype(jnp.bfloat16)
            marks = [inward[slot]]
        if not line:
            if slot < chunks:
                done[slot] = lax.psum(inward[slot], "row")
        else:
            if 0 <= slot - 1 < chunks:
                across[slot - 1] = added(after(inward[slot - 1], *marks), pair)
                marks = [across[slot - 1]]
            if 0 <= slot - 2 < chunks:
                summed[slot - 2] = added(after(across[slot - 2], *marks), cross)
                marks = [summed[slot - 2]]
            if 0 <= slot - 3 < chunks:
                done[slot - 3] = jnp.where(outer, pair, summed[slot - 3])
            if slot < chunks + 2:
                out = summed[slot - 2] if slot >= 2 else inward[slot]
                pair = swap(jnp.where(outer, inward[slot], out) if slot < chunks else out, "row", 1)
            if 0 <= slot - 1 < chunks:
                cross = lax.ppermute(across[slot - 1], "row", [(0, 0), (1, 2), (2, 1), (3, 3)])
        if slot == 0:
            own_part += input_grad(after(lhs[0], *marks), w, 1, chunks, chunks, width)
            marks = [own_part[1]]
            for k, parts_of in enumerate(held):
                sent[k] += [swap(after(part, *marks), "col", k + 1) for part in parts_of]
        if slot in (2, 4):
            filled = weight_grad(filled, [after(lhs[0], *marks)] + lhs[1:], xs, slot // 2 - 1, 3, width)
            marks = [filled[1]]
        if slot == 4:
            marks += late
        if slot == 3:
            blocks = split_rows(place, [after(blocks[0], *marks)] + blocks[1:], n_depth)
            blocks = [block if r == 0 else swap(block, "depth", r) for r, block in enumerate(blocks)]
            late = blocks[1:]
    grad_tokens = jnp.concatenate(done, axis=1)
    output, grad_taps = join(place, filled[1], [after(blocks[0], *marks)] + blocks[1:], taps.shape[1])
    grad_weight = jnp.transpose(filled[0], (1, 0, 2))
    return (output, grad_tokens, grad_weight, grad_taps)


def solution(mesh):
    in_specs = (
        P("col", "depth"),
        P(("row", "col"), None, "depth"),
        P(None, "row"),
        P(("col", "depth"), "row"),
    )
    out_specs = (
        P(("col", "depth"), "row"),
        P("col", "depth"),
        P(("row", "col"), None, "depth"),
        P(None, "row"),
    )
    return jax.shard_map(
        on_device, mesh=mesh, in_specs=in_specs, out_specs=out_specs, check_vma=False
    )
```

```python
import functools

import jax
import jax.numpy as jnp
from jax import lax
from jax.experimental import pallas as pl
from jax.experimental.pallas import tpu as pltpu
from jax.sharding import PartitionSpec as P

GROUP = 16
KT = 7
PAD = 8
LANES = 128
MIB = 1024 * 1024
SMALL = pl.CostEstimate(flops=1, bytes_accessed=1, transcendentals=0)


def swap(value, axis, flip):
    count = lax.axis_size(axis)
    return lax.ppermute(value, axis, [(i, i ^ flip) for i in range(count)])


def after(value, *earlier):
    return lax.optimization_barrier((value, *earlier))[0]


def resident(shape, width):
    if width % LANES == 0:
        return pl.BlockSpec(memory_space=pltpu.VMEM)
    return pl.BlockSpec(tuple(shape), lambda *_: (0,) * len(shape), pipeline_mode=pl.Buffered(1))


def params(mib, width):
    return pltpu.CompilerParams(vmem_limit_bytes=(mib if width % LANES == 0 else 56) * MIB)


def project_kernel(place, *refs, pieces, mode, count, width):
    x_refs = refs[:pieces]
    w_ref, keep_ref, send_ref = refs[pieces : pieces + 3]
    stream = pl.program_id(0)
    core = place[0] % 2
    x = x_refs[0][...]
    if mode == "cut":
        last_ref = refs[pieces + 3]

        @pl.when(stream == 0)
        def _():
            last_ref[...] = x_refs[0][x.shape[0] - last_ref.shape[0] :, :]

    if mode == "join":
        joined, rest = refs[pieces + 3 :]
        third = x.shape[0]
        parity = place[2] % 2

        @pl.when(stream == 0)
        def _():
            joined[pl.ds(pl.multiple_of(parity * third, third), third), :] = x_refs[0][...]
            joined[pl.ds(pl.multiple_of((1 - parity) * third, third), third), :] = x_refs[1][...]
            joined[2 * third :, :] = x_refs[2][...]
            rest[0:third, :] = x_refs[1][...]
            rest[third:, :] = x_refs[2][...]

        x = rest[...]
    nt = (((1,), (1,)), ((), ()))
    if width % LANES == 0:
        whole = lax.dot_general(x, w_ref[stream], nt, preferred_element_type=jnp.float32).astype(jnp.bfloat16)
        blocks = [whole[:, j * width : (j + 1) * width] for j in range(count)]
    else:
        blocks = [
            lax.dot_general(
                x, w_ref[0, j * width : (j + 1) * width, :], nt, preferred_element_type=jnp.float32
            ).astype(jnp.bfloat16)
            for j in range(count)
        ]
    for mine in range(2):

        @pl.when(core == mine)
        def _():
            for j in range(count):
                at = (j ^ place[0]) // 2
                if j % 2 == mine:
                    keep_ref[at, stream] = blocks[j]
                else:
                    send_ref[at, stream] = blocks[j]


def project(place, xs, w, count, mode="plain"):
    feat = xs[0].shape[1]
    all_tok = sum(x.shape[0] for x in xs)
    tok = all_tok - xs[0].shape[0] if mode == "join" else all_tok
    streams, channels, _ = w.shape
    width = channels // count
    part = jax.ShapeDtypeStruct((count // 2, streams, tok, width), jnp.bfloat16)
    wide = width % LANES == 0
    spec = resident(part.shape, width)
    more = {"plain": [], "cut": [(tok // 3, feat)], "join": [(all_tok, feat)]}[mode]
    return pl.pallas_call(
        functools.partial(project_kernel, pieces=len(xs), mode=mode, count=count, width=width),
        grid_spec=pltpu.PrefetchScalarGridSpec(
            num_scalar_prefetch=1,
            grid=(streams,),
            in_specs=[resident(x.shape, width) for x in xs]
            + [resident(w.shape, width) if wide else pl.BlockSpec((1, channels, feat), lambda s, _: (s, 0, 0))],
            out_specs=[spec, spec] + [resident(shape, width) for shape in more],
            scratch_shapes=[pltpu.VMEM((tok, feat), jnp.bfloat16)] if mode == "join" else [],
        ),
        out_shape=[part, part] + [jax.ShapeDtypeStruct(shape, jnp.bfloat16) for shape in more],
        compiler_params=params(10, width),
        cost_estimate=SMALL,
        name="project",
    )(place, *xs, w)


def in_three(value):
    terms = []
    for _ in range(3):
        term = value.astype(jnp.bfloat16)
        value = value - term.astype(jnp.float32)
        terms.append(term)
    return terms


def split_lanes_kernel(place, up_ref, *out_refs):
    n_depth, width = len(out_refs), out_refs[0].shape[2]
    for r, ref in enumerate(out_refs):
        for k in range(ref.shape[0]):
            at = ((place[1] ^ k) * n_depth + (place[0] ^ r)) * width
            ref[k] = up_ref[:, pl.ds(pl.multiple_of(at, width), width)]


def merge_rows_kernel(place, *refs, n_depth):
    in_refs, out_refs = refs[:n_depth], refs[n_depth:]
    local = in_refs[0].shape[1]
    for r, ref in enumerate(in_refs):
        for k, out_ref in enumerate(out_refs):
            out_ref[pl.ds(pl.multiple_of((place[0] ^ r) * local, 16), local), :] = ref[k]


def split_rows_kernel(place, *refs, n_col):
    in_refs, out_refs = refs[:n_col], refs[n_col:]
    local = out_refs[0].shape[1] - 32
    for r, ref in enumerate(out_refs):
        rows = pl.ds(pl.multiple_of((place[0] ^ r) * local, 16), local)
        for k in range(n_col):
            ref[k, 0:local] = in_refs[k][rows, :]
            ref[k, local:] = in_refs[k][-32:, :]


def rearrange(kernel, place, arrays, count, shape, name):
    width = shape[-1]
    return pl.pallas_call(
        kernel,
        grid_spec=pltpu.PrefetchScalarGridSpec(
            num_scalar_prefetch=1,
            grid=(1,),
            in_specs=[resident(value.shape, width) for value in arrays],
            out_specs=[resident(shape, width)] * count,
        ),
        out_shape=[jax.ShapeDtypeStruct(shape, jnp.bfloat16)] * count,
        compiler_params=params(4, width),
        cost_estimate=SMALL,
        name=name,
    )(place, *arrays)


def split_lanes(place, up, n_col, n_depth):
    local, width = up.shape[0], up.shape[1] // (n_col * n_depth)
    if width % LANES:
        blocks = up.reshape(local, n_col, n_depth, width)[:, place[1] ^ jnp.arange(n_col)]
        return [
            jnp.transpose(lax.dynamic_index_in_dim(blocks, place[0] ^ r, 2, keepdims=False), (1, 0, 2))
            for r in range(n_depth)
        ]
    return rearrange(split_lanes_kernel, place, [up], n_depth, (n_col, local, width), "split")


def merge_rows(place, pieces):
    n_depth = len(pieces)
    n_col, local, width = pieces[0].shape
    if width % LANES:
        whole = jnp.stack(pieces)[place[0] ^ jnp.arange(n_depth)]
        return list(jnp.transpose(whole, (1, 0, 2, 3)).reshape(n_col, n_depth * local, width))
    kernel = functools.partial(merge_rows_kernel, n_depth=n_depth)
    return list(rearrange(kernel, place, pieces, n_col, (n_depth * local, width), "merge"))


def split_rows(place, arrays, n_depth):
    local, width = (arrays[0].shape[0] - 32) // n_depth, arrays[0].shape[1]
    if width % LANES:
        whole = jnp.stack(arrays)
        return [
            jnp.concatenate(
                [lax.dynamic_slice_in_dim(whole, (place[0] ^ r) * local, local, axis=1), whole[:, -32:]], axis=1
            )
            for r in range(n_depth)
        ]
    kernel = functools.partial(split_rows_kernel, n_col=len(arrays))
    return rearrange(kernel, place, arrays, n_depth, (len(arrays), local + 32, width), "split")


def join_kernel(place, _, *refs):
    block_refs, (out_ref, grad_taps_ref) = refs[:-2], refs[-2:]
    n_depth = len(block_refs)
    n_col, _, width = block_refs[0].shape
    local, groups = out_ref.shape[0], grad_taps_ref.shape[1]
    lane_group = lax.broadcasted_iota(jnp.int32, (width, groups), 0) // GROUP
    group = lax.broadcasted_iota(jnp.int32, (width, groups), 1)
    total = jnp.zeros((24, groups), jnp.float32)
    for r, ref in enumerate(block_refs):
        for k in range(n_col):
            at = (place[1] ^ k) * n_depth + (place[0] ^ r)
            out_ref[:, pl.ds(pl.multiple_of(at * width, width), width)] = ref[k, 0:local, :]
            spread = (lane_group + at * (width // GROUP) == group).astype(jnp.bfloat16)
            total = total + jnp.dot(ref[k, local : local + 24, :], spread, preferred_element_type=jnp.float32)
    grad_taps_ref[...] = (total[0:8] + total[8:16] + total[16:24])[:KT]


def join(place, mark, blocks, groups):
    n_depth = len(blocks)
    n_col, rows, width = blocks[0].shape
    local = rows - 32
    if width % LANES:
        whole = jnp.stack(blocks)[place[0] ^ jnp.arange(n_depth)][:, place[1] ^ jnp.arange(n_col)]
        sums = whole[:, :, local : local + 24].astype(jnp.float32)
        sums = sums.reshape(n_depth, n_col, 3, 8, width // GROUP, GROUP).sum(axis=(2, 5))[:, :, :KT]
        return (
            jnp.transpose(whole[:, :, :local], (2, 1, 0, 3)).reshape(local, -1),
            jnp.transpose(sums, (2, 1, 0, 3)).reshape(KT, -1),
        )
    channels = n_depth * n_col * width
    return pl.pallas_call(
        join_kernel,
        grid_spec=pltpu.PrefetchScalarGridSpec(
            num_scalar_prefetch=1,
            grid=(1,),
            in_specs=[pl.BlockSpec(memory_space=pl.ANY)] + [resident(blocks[0].shape, width)] * n_depth,
            out_specs=[resident((local, channels), width), resident((KT, groups), width)],
        ),
        out_shape=[
            jax.ShapeDtypeStruct((local, channels), jnp.bfloat16),
            jax.ShapeDtypeStruct((KT, groups), jnp.float32),
        ],
        compiler_params=params(4, width),
        cost_estimate=SMALL,
        name="join",
    )(place, mark, *blocks)


def middle_kernel(place, taps_ref, *refs, pieces, groups, terms, tile):
    up_refs, refs = refs[:groups], refs[groups:]
    part_refs, refs = refs[: len(pieces) * terms], refs[len(pieces) * terms :]
    grad_refs, out_refs = refs[:groups], refs[groups : 2 * groups]
    up_s, out_s, q_s, k_s, v_s, mixed_s, gf_s, far_s = refs[2 * groups :]
    col = place[1]
    tok, width = up_refs[0].shape
    parity = place[2] % 2
    total = groups * tok
    tap_groups = taps_ref.shape[1]
    for k, ref in enumerate(up_refs):
        up_s[pl.ds(pl.multiple_of((col ^ k) * tok, tok), tok), :] = ref[...]
    lane_group = lax.broadcasted_iota(jnp.int32, (tap_groups, width), 1) // GROUP
    group = lax.broadcasted_iota(jnp.int32, (tap_groups, width), 0)
    spread = (lane_group + place[3] * (width // GROUP) == group).astype(jnp.bfloat16)
    taps = sum(jnp.dot(term, spread, preferred_element_type=jnp.float32) for term in in_three(taps_ref[...]))
    mixed_s[0:PAD, :] = jnp.zeros((PAD, width), jnp.float32)
    gf_s[total : total + PAD, :] = jnp.zeros((PAD, width), jnp.float32)
    step = 64
    for piece, (k, thirds) in enumerate(pieces):
        refs_of = part_refs[piece * terms : (piece + 1) * terms]
        rows_of = refs_of[0].shape[2]
        length = rows_of // len(thirds)
        for i in range(rows_of // step):
            third = thirds[i * step // length]
            at = {"own": parity, "other": 1 - parity, "last": 2, "all": 0}[third] * length
            start = (col ^ k) * tok + at + i * step % length
            inside = slice(i * step, (i + 1) * step)
            rows = pl.ds(pl.multiple_of(start, step), step)
            streams = []
            for s in range(3):
                acc = None
                for ref in refs_of:
                    term = ref[0, s, inside, :].astype(jnp.float32)
                    acc = term if acc is None else acc + term
                streams.append(acc.astype(jnp.bfloat16))
            q_s[rows, :], k_s[rows, :], v_s[rows, :] = streams
            query, key, value = [stream.astype(jnp.float32) for stream in streams]
            mixed_s[pl.ds(pl.multiple_of(start + PAD, PAD), step), :] = key * value
            gf_s[rows, :] = up_s[rows, :].astype(jnp.float32) * query
    sums = [jnp.zeros((8, width), jnp.float32) for _ in range(KT)]
    for a in range(groups):
        for i in range(tok // tile):
            first = a * tok + i * tile
            rows = slice(first, first + tile)
            inside = slice(i * tile, (i + 1) * tile)
            gf = gf_s[rows, :]
            filtered = jnp.zeros((tile, width), jnp.float32)
            grad_mixed = jnp.zeros((tile, width), jnp.float32)
            for j in range(KT):
                shifted = mixed_s[first + PAD - j : first + PAD - j + tile, :]
                filtered = filtered + taps[j : j + 1, :] * shifted
                sums[j] = sums[j] + (gf * shifted).reshape(tile // 8, 8, width).sum(axis=0)
                grad_mixed = grad_mixed + taps[j : j + 1, :] * gf_s[first + j : first + j + tile, :]
            out_s[a, inside, :] = (q_s[rows, :].astype(jnp.float32) * filtered).astype(jnp.bfloat16)
            at = col ^ a
            far_s[at, 0, inside, :] = (up_s[rows, :].astype(jnp.float32) * filtered).astype(jnp.bfloat16)
            far_s[at, 1, inside, :] = (grad_mixed * v_s[rows, :].astype(jnp.float32)).astype(jnp.bfloat16)
            far_s[at, 2, inside, :] = (grad_mixed * k_s[rows, :].astype(jnp.float32)).astype(jnp.bfloat16)
    for k in range(groups):
        grad_refs[k][...] = far_s[k]
    rest = jnp.concatenate(
        [sums[j].sum(axis=0, keepdims=True) for j in range(KT)] + [jnp.zeros((1, width), jnp.float32)], axis=0
    )
    terms_of = [term.astype(jnp.float32) for term in in_three(rest)]
    packed = jnp.concatenate(terms_of + [jnp.zeros((8, width), jnp.float32)], axis=0).astype(jnp.bfloat16)
    for k, ref in enumerate(out_refs):
        ref[0:tok, :] = out_s[col ^ k]
        ref[tok : tok + 32, :] = packed


def middle(place, taps, ups, pieces, parts, tile):
    groups, terms = len(ups), len(parts[0])
    tok, width = ups[0].shape
    total = groups * tok
    whole = lambda *shape: resident(shape, width)
    ones = [whole(1, 3, terms_of[0].shape[2], width) for terms_of in parts for _ in terms_of]
    outs = pl.pallas_call(
        functools.partial(middle_kernel, pieces=pieces, groups=groups, terms=terms, tile=tile),
        grid_spec=pltpu.PrefetchScalarGridSpec(
            num_scalar_prefetch=1,
            grid=(1,),
            in_specs=[whole(*taps.shape)] + [whole(tok, width)] * groups + ones,
            out_specs=[whole(3, tok, width)] * groups + [whole(tok + 32, width)] * groups,
            scratch_shapes=[
                pltpu.VMEM((total, width), jnp.bfloat16),
                pltpu.VMEM((groups, tok, width), jnp.bfloat16),
            ]
            + [pltpu.VMEM((total, width), jnp.bfloat16)] * 3
            + [pltpu.VMEM((total + PAD, width), jnp.float32)] * 2
            + [pltpu.VMEM((groups, 3, tok, width), jnp.bfloat16)],
        ),
        out_shape=[jax.ShapeDtypeStruct((3, tok, width), jnp.bfloat16)] * groups
        + [jax.ShapeDtypeStruct((tok + 32, width), jnp.bfloat16)] * groups,
        compiler_params=params(10, width),
        cost_estimate=SMALL,
        name="middle",
    )(place, taps, *ups, *[term for terms_of in parts for term in terms_of])
    return outs[:groups], outs[groups:]


def assemble_kernel(place, *refs):
    grad_refs, out_ref = refs[:-1], refs[-1]
    width = grad_refs[0].shape[2]
    for r, ref in enumerate(grad_refs):
        for s in range(3):
            at = pl.multiple_of((s * len(grad_refs) + (place[0] ^ r)) * width, width)
            out_ref[:, pl.ds(at, width)] = ref[s]


def assemble(place, grads):
    streams, tok, width = grads[0].shape
    out = jax.ShapeDtypeStruct((tok, streams * width * len(grads)), jnp.bfloat16)
    if width % LANES:
        whole = jnp.stack(grads)[place[0] ^ jnp.arange(len(grads))]
        return jnp.transpose(whole, (2, 1, 0, 3)).reshape(out.shape)
    return pl.pallas_call(
        assemble_kernel,
        grid_spec=pltpu.PrefetchScalarGridSpec(
            num_scalar_prefetch=1,
            grid=(1,),
            in_specs=[resident(grads[0].shape, width)] * len(grads),
            out_specs=resident(out.shape, width),
        ),
        out_shape=out,
        compiler_params=params(4, width),
        cost_estimate=SMALL,
        name="assemble",
    )(place, *grads)


def input_grad_kernel(grad_ref, w_ref, out_ref, *, first):
    step = out_ref.shape[1]
    rows = w_ref[:, :, first * step : (first + 1) * step].reshape(-1, step)
    out_ref[...] = jnp.dot(grad_ref[...], rows, preferred_element_type=jnp.float32).astype(jnp.bfloat16)


def input_grads_kernel(grad_ref, w_ref, *refs, first):
    out_refs, (slots, sems) = refs[:-2], refs[-2:]
    step = out_refs[0].shape[1]

    def fetch(i):
        columns = pl.ds((first + i) * step, step)
        return pltpu.make_async_copy(w_ref.at[:, :, columns], slots.at[i % 2], sems.at[i % 2])

    fetch(0).start()
    for i, out_ref in enumerate(out_refs):
        if i + 1 < len(out_refs):
            fetch(i + 1).start()
        fetch(i).wait()
        rows = slots[i % 2].reshape(-1, step)
        out_ref[...] = jnp.dot(grad_ref[...], rows, preferred_element_type=jnp.float32).astype(jnp.bfloat16)


def input_grad(grad, w, first, last, chunks, width):
    tok = grad.shape[0]
    streams, channels, feat = w.shape
    step = feat // chunks
    count = last - first
    if width % LANES:
        rows = w[:, :, first * step : last * step].reshape(streams * channels, count * step)
        whole = jnp.dot(grad, rows, preferred_element_type=jnp.float32).astype(jnp.bfloat16)
        return [whole[:, i * step : (i + 1) * step] for i in range(count)]
    single = count == 1
    return list(
        pl.pallas_call(
            functools.partial(input_grad_kernel if single else input_grads_kernel, first=first),
            in_specs=[
                resident(grad.shape, width),
                pl.BlockSpec(memory_space=pltpu.VMEM if single else pltpu.HBM),
            ],
            out_specs=[resident((tok, step), width)] * count,
            out_shape=[jax.ShapeDtypeStruct((tok, step), jnp.bfloat16)] * count,
            scratch_shapes=[]
            if single
            else [pltpu.VMEM((2, streams, channels, step), jnp.bfloat16), pltpu.SemaphoreType.DMA((2,))],
            compiler_params=params(8, width),
            cost_estimate=SMALL,
            name="input_grad",
        )(grad, w)
    )


def weight_grad_kernel(*refs, chained, groups, half):
    refs = refs[2 * chained :]
    grad_refs, x_refs = refs[:groups], refs[groups : 2 * groups]
    out_ref, mark_ref, turned = refs[2 * groups :]
    mark_ref[...] = jnp.zeros(mark_ref.shape, jnp.float32)
    streams, channels, step = out_ref.shape
    tok = x_refs[0].shape[0]

    @pl.when(pl.program_id(0) == 0)
    def _():
        for k in range(groups):
            for s in range(streams):
                at = (2 * s + half) * channels
                block = grad_refs[k][:, at : at + channels]
                turned[s * channels : (s + 1) * channels, k * tok : (k + 1) * tok] = block.T

    columns = pl.ds(pl.multiple_of(pl.program_id(0) * step, step), step)
    acc = None
    for k in range(groups):
        term = jnp.dot(turned[:, k * tok : (k + 1) * tok], x_refs[k][:, columns], preferred_element_type=jnp.float32)
        acc = term if acc is None else acc + term
    for s in range(streams):
        out_ref[s] = acc[s * channels : (s + 1) * channels, :]


def weight_grad(filled, grads, xs, half, streams, width):
    groups = len(xs)
    tok, feat = xs[0].shape
    channels = grads[0].shape[1] // streams
    chained = filled is not None
    if width % LANES:
        if chained:
            return filled
        terms = [
            lax.dot_general(grad, x, (((0,), (0,)), ((), ())), preferred_element_type=jnp.float32)
            for grad, x in zip(grads, xs)
        ]
        return sum(terms).reshape(streams, channels, feat), jnp.zeros((8, LANES), jnp.float32)
    step = min(512, feat)
    return pl.pallas_call(
        functools.partial(weight_grad_kernel, chained=chained, groups=groups, half=half),
        grid=(feat // step,),
        in_specs=[pl.BlockSpec(memory_space=pl.ANY)] * (2 * chained)
        + [resident(grads[0].shape, width)] * groups
        + [resident((tok, feat), width)] * groups,
        out_specs=[
            pl.BlockSpec((streams, channels // 2, step), lambda i: (0, half, i)),
            resident((8, LANES), width),
        ],
        scratch_shapes=[pltpu.VMEM((streams * channels // 2, groups * tok), jnp.bfloat16)],
        out_shape=[
            jax.ShapeDtypeStruct((streams, channels, feat), jnp.float32),
            jax.ShapeDtypeStruct((8, LANES), jnp.float32),
        ],
        input_output_aliases={0: 0} if chained else {},
        compiler_params=params(14, width),
        cost_estimate=SMALL,
        name="weight_grad",
    )(*(filled if chained else []), *grads, *xs)


def added(first, second):
    return (first.astype(jnp.float32) + second.astype(jnp.float32)).astype(jnp.bfloat16)


def on_device(tokens, weight, taps, upstream):
    n_col = lax.axis_size("col")
    n_depth = lax.axis_size("depth")
    local_tok = upstream.shape[0]
    depth_at = lax.axis_index("depth")
    col_at = lax.axis_index("col")
    row_at = lax.axis_index("row")
    place = jnp.stack([depth_at, col_at, row_at, col_at * n_depth + depth_at]).astype(jnp.int32)
    w = jnp.transpose(weight, (1, 0, 2))
    width = w.shape[1] // n_depth
    def sum_over_depth(keep, send, near_after=(), far_after=()):
        near = swap(after(send, *near_after) if near_after else send, "depth", 1)
        pairs = [added(keep[r // 2], near[r // 2])[None] for r in range(2, n_depth, 2)]
        held = [after(pair, *far_after) if far_after else pair for pair in pairs]
        fars = [swap(pair, "depth", 2 * i + 2) for i, pair in enumerate(held)]
        return [keep, near] + fars, pairs, fars

    tok = tokens.shape[0]
    third = tok // 3
    cut = tok % 192 == 0 and lax.axis_size("row") % 2 == 0
    sent_first = lax.dynamic_slice_in_dim(tokens, row_at % 2 * third, third, axis=0) if cut else tokens
    first = [swap(sent_first, "col", k) for k in range(1, n_col)]
    ups = split_lanes(place, upstream, n_col, n_depth)
    ups = [up if r == 0 else swap(up, "depth", r) for r, up in enumerate(ups)]
    outer = (row_at == 0) | (row_at == 3)
    keep, send, *last = project(place, [after(tokens, outer)], w, n_depth, "cut" if cut else "plain")
    terms, pairs, fars = sum_over_depth(keep, send, first + ups[1:])
    xs, pieces, parts = [tokens], [(0, ("all",))], [terms]
    for k in range(1, n_col):
        mine = first[k - 1]
        if not cut:
            keep, send = project(place, [after(mine, *fars)], w, n_depth)
            terms, pairs, fars = sum_over_depth(keep, send)
            xs.append(mine)
            pieces.append((k, ("all",)))
            parts.append(terms)
            continue
        other = swap(mine, "row", 1)
        rest = swap(after(last[0], mine), "col", k)
        keep, send = project(place, [after(mine, *pairs)], w, n_depth)
        terms, ahead, ahead_fars = sum_over_depth(keep, send)
        pieces.append((k, ("own",)))
        parts.append(terms)
        keep, send, x = project(place, [mine, other, after(rest, *fars, *ahead)], w, n_depth, "join")
        terms, pairs, fars = sum_over_depth(keep, send, (), ahead_fars)
        pieces.append((k, ("other", "last")))
        parts.append(terms)
        xs.append(x)
    ups = merge_rows(place, [after(ups[0], *pairs)] + ups[1:])
    ups = [up if k == 0 else swap(up, "col", k) for k, up in enumerate(ups)]
    own_grads, blocks = middle(place, taps, ups, pieces, parts, local_tok)
    nears = [swap(own, "depth", 1) for own in own_grads]
    blocks = [block if k == 0 else swap(block, "col", k) for k, block in enumerate(blocks)]
    beside = nears + blocks[1:]
    chunks = 4
    grads = [None] * n_col
    ready = []
    sent = []
    lhs = [None] * n_col
    for k in reversed(range(n_col)):
        fars = [swap(after(own_grads[k], *ready) if ready else own_grads[k], "depth", r) for r in range(2, n_depth, 2)]
        ready = fars
        if k > 0:
            fars = [after(far, *beside) for far in fars]
        elif sent:
            fars = [after(far, sent[-1][1][-1]) for far in fars]
        grads[k] = [own_grads[k], nears[k]]
        for far in fars:
            grads[k] += [far, swap(far, "depth", 1)]
        lhs[k] = assemble(place, grads[k])
        if k > 0:
            parts_of = input_grad(lhs[k], w, 0, 1, chunks, width)
            parts_of += input_grad(after(lhs[k], *parts_of), w, 1, chunks, chunks, width)
            sent.append(([swap(part, "col", k) for part in parts_of[:3]], parts_of))
    held = [parts_of[3:] for _, parts_of in sent]
    sent = [of for of, _ in sent]
    own_part = input_grad(lhs[0], w, 0, 1, chunks, width)
    line = lax.axis_size("row") == 4
    inward, across, summed, done = ([None] * chunks for _ in range(4))
    pair = cross = filled = None
    marks, late = [], []
    for slot in range(chunks + 3):
        if slot < chunks:
            total = after(own_part[slot], *marks).astype(jnp.float32)
            for of in sent:
                total = total + of[slot].astype(jnp.float32)
            inward[slot] = total.astype(jnp.bfloat16)
            marks = [inward[slot]] + late
            late = []
        if not line:
            if slot < chunks:
                done[slot] = lax.psum(inward[slot], "row")
        else:
            if 0 <= slot - 2 < chunks:
                summed[slot - 2] = added(after(across[slot - 2], *marks), cross)
                marks = [summed[slot - 2]]
            if 0 <= slot - 1 < chunks:
                across[slot - 1] = added(after(inward[slot - 1], *marks), pair)
                marks = [across[slot - 1]]
            if 0 <= slot - 3 < chunks:
                done[slot - 3] = jnp.where(outer, pair, summed[slot - 3])
            if slot < chunks + 2:
                out = summed[slot - 2] if slot >= 2 else inward[slot]
                pair = swap(jnp.where(outer, inward[slot], out) if slot < chunks else out, "row", 1)
            if 0 <= slot - 1 < chunks:
                cross = lax.ppermute(across[slot - 1], "row", [(0, 0), (1, 2), (2, 1), (3, 3)])
        if slot == 0:
            own_part += input_grad(after(lhs[0], *marks), w, 1, chunks, chunks, width)
            marks = [own_part[1]]
            for k, parts_of in enumerate(held):
                sent[k] += [swap(after(part, *marks), "col", k + 1) for part in parts_of]
        if slot in (2, 3):
            filled = weight_grad(filled, [after(lhs[0], *marks)] + lhs[1:], xs, slot - 2, 3, width)
            marks = [filled[1]]
        if slot == 1:
            blocks = split_rows(place, [after(blocks[0], *marks)] + blocks[1:], n_depth)
            blocks = [block if r == 0 else swap(block, "depth", r) for r, block in enumerate(blocks)]
            late = blocks[1:]
    grad_tokens = jnp.concatenate(done, axis=1)
    output, grad_taps = join(place, filled[1], [after(blocks[0], *marks)] + blocks[1:], taps.shape[1])
    grad_weight = jnp.transpose(filled[0], (1, 0, 2))
    return (output, grad_tokens, grad_weight, grad_taps)


def solution(mesh):
    in_specs = (
        P("col", "depth"),
        P(("row", "col"), None, "depth"),
        P(None, "row"),
        P(("col", "depth"), "row"),
    )
    out_specs = (
        P(("col", "depth"), "row"),
        P("col", "depth"),
        P(("row", "col"), None, "depth"),
        P(None, "row"),
    )
    return jax.shard_map(
        on_device, mesh=mesh, in_specs=in_specs, out_specs=out_specs, check_vma=False
    )
```

```python
import functools

import jax
import jax.numpy as jnp
from jax import lax
from jax.experimental import pallas as pl
from jax.experimental.pallas import tpu as pltpu
from jax.sharding import PartitionSpec as P

GROUP = 16
KT = 7
PAD = 8
LANES = 128
MIB = 1024 * 1024
SMALL = pl.CostEstimate(flops=1, bytes_accessed=1, transcendentals=0)


def swap(value, axis, flip):
    count = lax.axis_size(axis)
    return lax.ppermute(value, axis, [(i, i ^ flip) for i in range(count)])


def after(value, *earlier):
    return lax.optimization_barrier((value, *earlier))[0]


def resident(shape, width):
    if width % LANES == 0:
        return pl.BlockSpec(memory_space=pltpu.VMEM)
    return pl.BlockSpec(tuple(shape), lambda *_: (0,) * len(shape), pipeline_mode=pl.Buffered(1))


def params(mib, width):
    return pltpu.CompilerParams(vmem_limit_bytes=(mib if width % LANES == 0 else 56) * MIB)


def project_kernel(place, *refs, pieces, mode, count, width):
    x_refs = refs[:pieces]
    w_ref, keep_ref, send_ref = refs[pieces : pieces + 3]
    stream = pl.program_id(0)
    core = place[0] % 2
    x = x_refs[0][...]
    if mode == "cut":
        last_ref = refs[pieces + 3]

        @pl.when(stream == 0)
        def _():
            last_ref[...] = x_refs[0][x.shape[0] - last_ref.shape[0] :, :]

    if mode == "join":
        joined, rest = refs[pieces + 3 :]
        third = x.shape[0]
        parity = place[2] % 2

        @pl.when(stream == 0)
        def _():
            joined[pl.ds(pl.multiple_of(parity * third, third), third), :] = x_refs[0][...]
            joined[pl.ds(pl.multiple_of((1 - parity) * third, third), third), :] = x_refs[1][...]
            joined[2 * third :, :] = x_refs[2][...]
            rest[0:third, :] = x_refs[1][...]
            rest[third:, :] = x_refs[2][...]

        x = rest[...]
    nt = (((1,), (1,)), ((), ()))
    if width % LANES == 0:
        whole = lax.dot_general(x, w_ref[stream], nt, preferred_element_type=jnp.float32).astype(jnp.bfloat16)
        blocks = [whole[:, j * width : (j + 1) * width] for j in range(count)]
    else:
        blocks = [
            lax.dot_general(
                x, w_ref[0, j * width : (j + 1) * width, :], nt, preferred_element_type=jnp.float32
            ).astype(jnp.bfloat16)
            for j in range(count)
        ]
    for mine in range(2):

        @pl.when(core == mine)
        def _():
            for j in range(count):
                at = (j ^ place[0]) // 2
                if j % 2 == mine:
                    keep_ref[at, stream] = blocks[j]
                else:
                    send_ref[at, stream] = blocks[j]


def project(place, xs, w, count, mode="plain"):
    feat = xs[0].shape[1]
    all_tok = sum(x.shape[0] for x in xs)
    tok = all_tok - xs[0].shape[0] if mode == "join" else all_tok
    streams, channels, _ = w.shape
    width = channels // count
    part = jax.ShapeDtypeStruct((count // 2, streams, tok, width), jnp.bfloat16)
    wide = width % LANES == 0
    spec = resident(part.shape, width)
    more = {"plain": [], "cut": [(tok // 3, feat)], "join": [(all_tok, feat)]}[mode]
    return pl.pallas_call(
        functools.partial(project_kernel, pieces=len(xs), mode=mode, count=count, width=width),
        grid_spec=pltpu.PrefetchScalarGridSpec(
            num_scalar_prefetch=1,
            grid=(streams,),
            in_specs=[resident(x.shape, width) for x in xs]
            + [resident(w.shape, width) if wide else pl.BlockSpec((1, channels, feat), lambda s, _: (s, 0, 0))],
            out_specs=[spec, spec] + [resident(shape, width) for shape in more],
            scratch_shapes=[pltpu.VMEM((tok, feat), jnp.bfloat16)] if mode == "join" else [],
        ),
        out_shape=[part, part] + [jax.ShapeDtypeStruct(shape, jnp.bfloat16) for shape in more],
        compiler_params=params(10, width),
        cost_estimate=SMALL,
        name="project",
    )(place, *xs, w)


def in_three(value):
    terms = []
    for _ in range(3):
        term = value.astype(jnp.bfloat16)
        value = value - term.astype(jnp.float32)
        terms.append(term)
    return terms


def split_lanes_kernel(place, up_ref, *out_refs):
    n_depth, width = len(out_refs), out_refs[0].shape[2]
    for r, ref in enumerate(out_refs):
        for k in range(ref.shape[0]):
            at = ((place[1] ^ k) * n_depth + (place[0] ^ r)) * width
            ref[k] = up_ref[:, pl.ds(pl.multiple_of(at, width), width)]


def merge_rows_kernel(place, *refs, n_depth):
    in_refs, out_refs = refs[:n_depth], refs[n_depth:]
    local = in_refs[0].shape[1]
    for r, ref in enumerate(in_refs):
        for k, out_ref in enumerate(out_refs):
            out_ref[pl.ds(pl.multiple_of((place[0] ^ r) * local, 16), local), :] = ref[k]


def split_rows_kernel(place, *refs, n_col):
    in_refs, out_refs = refs[:n_col], refs[n_col:]
    local = out_refs[0].shape[1] - 32
    for r, ref in enumerate(out_refs):
        rows = pl.ds(pl.multiple_of((place[0] ^ r) * local, 16), local)
        for k in range(n_col):
            ref[k, 0:local] = in_refs[k][rows, :]
            ref[k, local:] = in_refs[k][-32:, :]


def rearrange(kernel, place, arrays, count, shape, name):
    width = shape[-1]
    return pl.pallas_call(
        kernel,
        grid_spec=pltpu.PrefetchScalarGridSpec(
            num_scalar_prefetch=1,
            grid=(1,),
            in_specs=[resident(value.shape, width) for value in arrays],
            out_specs=[resident(shape, width)] * count,
        ),
        out_shape=[jax.ShapeDtypeStruct(shape, jnp.bfloat16)] * count,
        compiler_params=params(4, width),
        cost_estimate=SMALL,
        name=name,
    )(place, *arrays)


def split_lanes(place, up, n_col, n_depth):
    local, width = up.shape[0], up.shape[1] // (n_col * n_depth)
    if width % LANES:
        blocks = up.reshape(local, n_col, n_depth, width)[:, place[1] ^ jnp.arange(n_col)]
        return [
            jnp.transpose(lax.dynamic_index_in_dim(blocks, place[0] ^ r, 2, keepdims=False), (1, 0, 2))
            for r in range(n_depth)
        ]
    return rearrange(split_lanes_kernel, place, [up], n_depth, (n_col, local, width), "split")


def merge_rows(place, pieces):
    n_depth = len(pieces)
    n_col, local, width = pieces[0].shape
    if width % LANES:
        whole = jnp.stack(pieces)[place[0] ^ jnp.arange(n_depth)]
        return list(jnp.transpose(whole, (1, 0, 2, 3)).reshape(n_col, n_depth * local, width))
    kernel = functools.partial(merge_rows_kernel, n_depth=n_depth)
    return list(rearrange(kernel, place, pieces, n_col, (n_depth * local, width), "merge"))


def split_rows(place, arrays, n_depth):
    local, width = (arrays[0].shape[0] - 32) // n_depth, arrays[0].shape[1]
    if width % LANES:
        whole = jnp.stack(arrays)
        return [
            jnp.concatenate(
                [lax.dynamic_slice_in_dim(whole, (place[0] ^ r) * local, local, axis=1), whole[:, -32:]], axis=1
            )
            for r in range(n_depth)
        ]
    kernel = functools.partial(split_rows_kernel, n_col=len(arrays))
    return rearrange(kernel, place, arrays, n_depth, (len(arrays), local + 32, width), "split")


def join_kernel(place, _, *refs):
    block_refs, (out_ref, grad_taps_ref) = refs[:-2], refs[-2:]
    n_depth = len(block_refs)
    n_col, _, width = block_refs[0].shape
    local, groups = out_ref.shape[0], grad_taps_ref.shape[1]
    lane_group = lax.broadcasted_iota(jnp.int32, (width, groups), 0) // GROUP
    group = lax.broadcasted_iota(jnp.int32, (width, groups), 1)
    total = jnp.zeros((24, groups), jnp.float32)
    for r, ref in enumerate(block_refs):
        for k in range(n_col):
            at = (place[1] ^ k) * n_depth + (place[0] ^ r)
            out_ref[:, pl.ds(pl.multiple_of(at * width, width), width)] = ref[k, 0:local, :]
            spread = (lane_group + at * (width // GROUP) == group).astype(jnp.bfloat16)
            total = total + jnp.dot(ref[k, local : local + 24, :], spread, preferred_element_type=jnp.float32)
    grad_taps_ref[...] = (total[0:8] + total[8:16] + total[16:24])[:KT]


def join(place, mark, blocks, groups):
    n_depth = len(blocks)
    n_col, rows, width = blocks[0].shape
    local = rows - 32
    if width % LANES:
        whole = jnp.stack(blocks)[place[0] ^ jnp.arange(n_depth)][:, place[1] ^ jnp.arange(n_col)]
        sums = whole[:, :, local : local + 24].astype(jnp.float32)
        sums = sums.reshape(n_depth, n_col, 3, 8, width // GROUP, GROUP).sum(axis=(2, 5))[:, :, :KT]
        return (
            jnp.transpose(whole[:, :, :local], (2, 1, 0, 3)).reshape(local, -1),
            jnp.transpose(sums, (2, 1, 0, 3)).reshape(KT, -1),
        )
    channels = n_depth * n_col * width
    return pl.pallas_call(
        join_kernel,
        grid_spec=pltpu.PrefetchScalarGridSpec(
            num_scalar_prefetch=1,
            grid=(1,),
            in_specs=[pl.BlockSpec(memory_space=pl.ANY)] + [resident(blocks[0].shape, width)] * n_depth,
            out_specs=[resident((local, channels), width), resident((KT, groups), width)],
        ),
        out_shape=[
            jax.ShapeDtypeStruct((local, channels), jnp.bfloat16),
            jax.ShapeDtypeStruct((KT, groups), jnp.float32),
        ],
        compiler_params=params(4, width),
        cost_estimate=SMALL,
        name="join",
    )(place, mark, *blocks)


def middle_kernel(place, taps_ref, *refs, pieces, groups, terms, tile):
    up_refs, refs = refs[:groups], refs[groups:]
    part_refs, refs = refs[: len(pieces) * terms], refs[len(pieces) * terms :]
    grad_refs, out_refs = refs[:groups], refs[groups : 2 * groups]
    up_s, out_s, q_s, k_s, v_s, mixed_s, gf_s, far_s = refs[2 * groups :]
    col = place[1]
    tok, width = up_refs[0].shape
    parity = place[2] % 2
    total = groups * tok
    tap_groups = taps_ref.shape[1]
    for k, ref in enumerate(up_refs):
        up_s[pl.ds(pl.multiple_of((col ^ k) * tok, tok), tok), :] = ref[...]
    lane_group = lax.broadcasted_iota(jnp.int32, (tap_groups, width), 1) // GROUP
    group = lax.broadcasted_iota(jnp.int32, (tap_groups, width), 0)
    spread = (lane_group + place[3] * (width // GROUP) == group).astype(jnp.bfloat16)
    taps = sum(jnp.dot(term, spread, preferred_element_type=jnp.float32) for term in in_three(taps_ref[...]))
    mixed_s[0:PAD, :] = jnp.zeros((PAD, width), jnp.float32)
    gf_s[total : total + PAD, :] = jnp.zeros((PAD, width), jnp.float32)
    step = 64
    for piece, (k, thirds) in enumerate(pieces):
        refs_of = part_refs[piece * terms : (piece + 1) * terms]
        rows_of = refs_of[0].shape[2]
        length = rows_of // len(thirds)
        for i in range(rows_of // step):
            third = thirds[i * step // length]
            at = {"own": parity, "other": 1 - parity, "last": 2, "all": 0}[third] * length
            start = (col ^ k) * tok + at + i * step % length
            inside = slice(i * step, (i + 1) * step)
            rows = pl.ds(pl.multiple_of(start, step), step)
            streams = []
            for s in range(3):
                acc = None
                for ref in refs_of:
                    term = ref[0, s, inside, :].astype(jnp.float32)
                    acc = term if acc is None else acc + term
                streams.append(acc.astype(jnp.bfloat16))
            q_s[rows, :], k_s[rows, :], v_s[rows, :] = streams
            query, key, value = [stream.astype(jnp.float32) for stream in streams]
            mixed_s[pl.ds(pl.multiple_of(start + PAD, PAD), step), :] = key * value
            gf_s[rows, :] = up_s[rows, :].astype(jnp.float32) * query
    sums = [jnp.zeros((8, width), jnp.float32) for _ in range(KT)]
    for a in range(groups):
        for i in range(tok // tile):
            first = a * tok + i * tile
            rows = slice(first, first + tile)
            inside = slice(i * tile, (i + 1) * tile)
            gf = gf_s[rows, :]
            filtered = jnp.zeros((tile, width), jnp.float32)
            grad_mixed = jnp.zeros((tile, width), jnp.float32)
            for j in range(KT):
                shifted = mixed_s[first + PAD - j : first + PAD - j + tile, :]
                filtered = filtered + taps[j : j + 1, :] * shifted
                sums[j] = sums[j] + (gf * shifted).reshape(tile // 8, 8, width).sum(axis=0)
                grad_mixed = grad_mixed + taps[j : j + 1, :] * gf_s[first + j : first + j + tile, :]
            out_s[a, inside, :] = (q_s[rows, :].astype(jnp.float32) * filtered).astype(jnp.bfloat16)
            at = col ^ a
            far_s[at, 0, inside, :] = (up_s[rows, :].astype(jnp.float32) * filtered).astype(jnp.bfloat16)
            far_s[at, 1, inside, :] = (grad_mixed * v_s[rows, :].astype(jnp.float32)).astype(jnp.bfloat16)
            far_s[at, 2, inside, :] = (grad_mixed * k_s[rows, :].astype(jnp.float32)).astype(jnp.bfloat16)
    for k in range(groups):
        grad_refs[k][...] = far_s[k]
    rest = jnp.concatenate(
        [sums[j].sum(axis=0, keepdims=True) for j in range(KT)] + [jnp.zeros((1, width), jnp.float32)], axis=0
    )
    terms_of = [term.astype(jnp.float32) for term in in_three(rest)]
    packed = jnp.concatenate(terms_of + [jnp.zeros((8, width), jnp.float32)], axis=0).astype(jnp.bfloat16)
    for k, ref in enumerate(out_refs):
        ref[0:tok, :] = out_s[col ^ k]
        ref[tok : tok + 32, :] = packed


def middle(place, taps, ups, pieces, parts, tile):
    groups, terms = len(ups), len(parts[0])
    tok, width = ups[0].shape
    total = groups * tok
    whole = lambda *shape: resident(shape, width)
    ones = [whole(1, 3, terms_of[0].shape[2], width) for terms_of in parts for _ in terms_of]
    outs = pl.pallas_call(
        functools.partial(middle_kernel, pieces=pieces, groups=groups, terms=terms, tile=tile),
        grid_spec=pltpu.PrefetchScalarGridSpec(
            num_scalar_prefetch=1,
            grid=(1,),
            in_specs=[whole(*taps.shape)] + [whole(tok, width)] * groups + ones,
            out_specs=[whole(3, tok, width)] * groups + [whole(tok + 32, width)] * groups,
            scratch_shapes=[
                pltpu.VMEM((total, width), jnp.bfloat16),
                pltpu.VMEM((groups, tok, width), jnp.bfloat16),
            ]
            + [pltpu.VMEM((total, width), jnp.bfloat16)] * 3
            + [pltpu.VMEM((total + PAD, width), jnp.float32)] * 2
            + [pltpu.VMEM((groups, 3, tok, width), jnp.bfloat16)],
        ),
        out_shape=[jax.ShapeDtypeStruct((3, tok, width), jnp.bfloat16)] * groups
        + [jax.ShapeDtypeStruct((tok + 32, width), jnp.bfloat16)] * groups,
        compiler_params=params(10, width),
        cost_estimate=SMALL,
        name="middle",
    )(place, taps, *ups, *[term for terms_of in parts for term in terms_of])
    return outs[:groups], outs[groups:]


def assemble_kernel(place, *refs):
    grad_refs, out_ref = refs[:-1], refs[-1]
    width = grad_refs[0].shape[2]
    for r, ref in enumerate(grad_refs):
        for s in range(3):
            at = pl.multiple_of((s * len(grad_refs) + (place[0] ^ r)) * width, width)
            out_ref[:, pl.ds(at, width)] = ref[s]


def assemble(place, grads):
    streams, tok, width = grads[0].shape
    out = jax.ShapeDtypeStruct((tok, streams * width * len(grads)), jnp.bfloat16)
    if width % LANES:
        whole = jnp.stack(grads)[place[0] ^ jnp.arange(len(grads))]
        return jnp.transpose(whole, (2, 1, 0, 3)).reshape(out.shape)
    return pl.pallas_call(
        assemble_kernel,
        grid_spec=pltpu.PrefetchScalarGridSpec(
            num_scalar_prefetch=1,
            grid=(1,),
            in_specs=[resident(grads[0].shape, width)] * len(grads),
            out_specs=resident(out.shape, width),
        ),
        out_shape=out,
        compiler_params=params(4, width),
        cost_estimate=SMALL,
        name="assemble",
    )(place, *grads)


def input_grad_kernel(grad_ref, w_ref, out_ref, *, first):
    step = out_ref.shape[1]
    rows = w_ref[:, :, first * step : (first + 1) * step].reshape(-1, step)
    out_ref[...] = jnp.dot(grad_ref[...], rows, preferred_element_type=jnp.float32).astype(jnp.bfloat16)


def input_grads_kernel(grad_ref, w_ref, *refs, first):
    out_refs, (slots, sems) = refs[:-2], refs[-2:]
    step = out_refs[0].shape[1]

    def fetch(i):
        columns = pl.ds((first + i) * step, step)
        return pltpu.make_async_copy(w_ref.at[:, :, columns], slots.at[i % 2], sems.at[i % 2])

    fetch(0).start()
    for i, out_ref in enumerate(out_refs):
        if i + 1 < len(out_refs):
            fetch(i + 1).start()
        fetch(i).wait()
        rows = slots[i % 2].reshape(-1, step)
        out_ref[...] = jnp.dot(grad_ref[...], rows, preferred_element_type=jnp.float32).astype(jnp.bfloat16)


def input_grad(grad, w, first, last, chunks, width):
    tok = grad.shape[0]
    streams, channels, feat = w.shape
    step = feat // chunks
    count = last - first
    if width % LANES:
        rows = w[:, :, first * step : last * step].reshape(streams * channels, count * step)
        whole = jnp.dot(grad, rows, preferred_element_type=jnp.float32).astype(jnp.bfloat16)
        return [whole[:, i * step : (i + 1) * step] for i in range(count)]
    single = count == 1
    return list(
        pl.pallas_call(
            functools.partial(input_grad_kernel if single else input_grads_kernel, first=first),
            in_specs=[
                resident(grad.shape, width),
                pl.BlockSpec(memory_space=pltpu.VMEM if single else pltpu.HBM),
            ],
            out_specs=[resident((tok, step), width)] * count,
            out_shape=[jax.ShapeDtypeStruct((tok, step), jnp.bfloat16)] * count,
            scratch_shapes=[]
            if single
            else [pltpu.VMEM((2, streams, channels, step), jnp.bfloat16), pltpu.SemaphoreType.DMA((2,))],
            compiler_params=params(8, width),
            cost_estimate=SMALL,
            name="input_grad",
        )(grad, w)
    )


def weight_grad_kernel(*refs, chained, groups, half):
    refs = refs[2 * chained :]
    grad_refs, x_refs = refs[:groups], refs[groups : 2 * groups]
    out_ref, mark_ref, turned = refs[2 * groups :]
    mark_ref[...] = jnp.zeros(mark_ref.shape, jnp.float32)
    streams, channels, step = out_ref.shape
    tok = x_refs[0].shape[0]

    @pl.when(pl.program_id(0) == 0)
    def _():
        for k in range(groups):
            for s in range(streams):
                at = (2 * s + half) * channels
                block = grad_refs[k][:, at : at + channels]
                turned[s * channels : (s + 1) * channels, k * tok : (k + 1) * tok] = block.T

    columns = pl.ds(pl.multiple_of(pl.program_id(0) * step, step), step)
    acc = None
    for k in range(groups):
        term = jnp.dot(turned[:, k * tok : (k + 1) * tok], x_refs[k][:, columns], preferred_element_type=jnp.float32)
        acc = term if acc is None else acc + term
    for s in range(streams):
        out_ref[s] = acc[s * channels : (s + 1) * channels, :]


def weight_grad(filled, grads, xs, half, streams, width):
    groups = len(xs)
    tok, feat = xs[0].shape
    channels = grads[0].shape[1] // streams
    chained = filled is not None
    if width % LANES:
        if chained:
            return filled
        terms = [
            lax.dot_general(grad, x, (((0,), (0,)), ((), ())), preferred_element_type=jnp.float32)
            for grad, x in zip(grads, xs)
        ]
        return sum(terms).reshape(streams, channels, feat), jnp.zeros((8, LANES), jnp.float32)
    step = min(512, feat)
    return pl.pallas_call(
        functools.partial(weight_grad_kernel, chained=chained, groups=groups, half=half),
        grid=(feat // step,),
        in_specs=[pl.BlockSpec(memory_space=pl.ANY)] * (2 * chained)
        + [resident(grads[0].shape, width)] * groups
        + [resident((tok, feat), width)] * groups,
        out_specs=[
            pl.BlockSpec((streams, channels // 2, step), lambda i: (0, half, i)),
            resident((8, LANES), width),
        ],
        scratch_shapes=[pltpu.VMEM((streams * channels // 2, groups * tok), jnp.bfloat16)],
        out_shape=[
            jax.ShapeDtypeStruct((streams, channels, feat), jnp.float32),
            jax.ShapeDtypeStruct((8, LANES), jnp.float32),
        ],
        input_output_aliases={0: 0} if chained else {},
        compiler_params=params(14, width),
        cost_estimate=SMALL,
        name="weight_grad",
    )(*(filled if chained else []), *grads, *xs)


def added(first, second):
    return (first.astype(jnp.float32) + second.astype(jnp.float32)).astype(jnp.bfloat16)


def on_device(tokens, weight, taps, upstream):
    n_col = lax.axis_size("col")
    n_depth = lax.axis_size("depth")
    local_tok = upstream.shape[0]
    depth_at = lax.axis_index("depth")
    col_at = lax.axis_index("col")
    row_at = lax.axis_index("row")
    place = jnp.stack([depth_at, col_at, row_at, col_at * n_depth + depth_at]).astype(jnp.int32)
    w = jnp.transpose(weight, (1, 0, 2))
    width = w.shape[1] // n_depth
    def sum_over_depth(keep, send, near_after=(), far_after=()):
        near = swap(after(send, *near_after) if near_after else send, "depth", 1)
        pairs = [added(keep[r // 2], near[r // 2])[None] for r in range(2, n_depth, 2)]
        held = [after(pair, *far_after) if far_after else pair for pair in pairs]
        fars = [swap(pair, "depth", 2 * i + 2) for i, pair in enumerate(held)]
        return [keep, near] + fars, pairs, fars

    tok = tokens.shape[0]
    third = tok // 3
    cut = tok % 192 == 0 and lax.axis_size("row") % 2 == 0
    sent_first = lax.dynamic_slice_in_dim(tokens, row_at % 2 * third, third, axis=0) if cut else tokens
    first = [swap(sent_first, "col", k) for k in range(1, n_col)]
    ups = split_lanes(place, upstream, n_col, n_depth)
    ups = [up if r == 0 else swap(up, "depth", r) for r, up in enumerate(ups)]
    outer = (row_at == 0) | (row_at == 3)
    keep, send, *last = project(place, [after(tokens, outer)], w, n_depth, "cut" if cut else "plain")
    terms, pairs, fars = sum_over_depth(keep, send, first + ups[1:])
    xs, pieces, parts = [tokens], [(0, ("all",))], [terms]
    for k in range(1, n_col):
        mine = first[k - 1]
        if not cut:
            keep, send = project(place, [after(mine, *fars)], w, n_depth)
            terms, pairs, fars = sum_over_depth(keep, send)
            xs.append(mine)
            pieces.append((k, ("all",)))
            parts.append(terms)
            continue
        other = swap(mine, "row", 1)
        rest = swap(after(last[0], mine), "col", k)
        keep, send = project(place, [after(mine, *pairs)], w, n_depth)
        terms, ahead, ahead_fars = sum_over_depth(keep, send)
        pieces.append((k, ("own",)))
        parts.append(terms)
        keep, send, x = project(place, [mine, other, after(rest, *fars, *ahead)], w, n_depth, "join")
        terms, pairs, fars = sum_over_depth(keep, send, (), ahead_fars)
        pieces.append((k, ("other", "last")))
        parts.append(terms)
        xs.append(x)
    ups = merge_rows(place, [after(ups[0], *pairs)] + ups[1:])
    ups = [up if k == 0 else swap(up, "col", k) for k, up in enumerate(ups)]
    own_grads, blocks = middle(place, taps, ups, pieces, parts, local_tok)
    nears = [swap(own, "depth", 1) for own in own_grads]
    blocks = [block if k == 0 else swap(block, "col", k) for k, block in enumerate(blocks)]
    beside = nears + blocks[1:]
    chunks = 4
    grads = [None] * n_col
    ready = []
    sent = []
    lhs = [None] * n_col
    for k in reversed(range(n_col)):
        fars = [swap(after(own_grads[k], *ready) if ready else own_grads[k], "depth", r) for r in range(2, n_depth, 2)]
        ready = fars
        if k > 0:
            fars = [after(far, *beside) for far in fars]
        elif sent:
            fars = [after(far, sent[-1][1][-1]) for far in fars]
        grads[k] = [own_grads[k], nears[k]]
        for far in fars:
            grads[k] += [far, swap(far, "depth", 1)]
        lhs[k] = assemble(place, grads[k])
        if k > 0:
            parts_of = input_grad(lhs[k], w, 0, 1, chunks, width)
            parts_of += input_grad(after(lhs[k], *parts_of), w, 1, chunks, chunks, width)
            sent.append(([swap(part, "col", k) for part in parts_of[:3]], parts_of))
    held = [parts_of[3:] for _, parts_of in sent]
    sent = [of for of, _ in sent]
    own_part = input_grad(lhs[0], w, 0, 1, chunks, width)
    line = lax.axis_size("row") == 4
    inward, across, summed, done = ([None] * chunks for _ in range(4))
    pair = cross = filled = None
    marks, late = [], []
    for slot in range(chunks + 3):
        if slot < chunks:
            total = after(own_part[slot], *marks).astype(jnp.float32)
            for of in sent:
                total = total + of[slot].astype(jnp.float32)
            inward[slot] = total.astype(jnp.bfloat16)
            marks = [inward[slot]] + late
            late = []
        if not line:
            if slot < chunks:
                done[slot] = lax.psum(inward[slot], "row")
        else:
            if 0 <= slot - 1 < chunks:
                across[slot - 1] = added(after(inward[slot - 1], *marks), pair)
                marks = [across[slot - 1]]
            if 0 <= slot - 2 < chunks:
                summed[slot - 2] = added(after(across[slot - 2], *marks), cross)
                marks = [summed[slot - 2]]
            if 0 <= slot - 3 < chunks:
                done[slot - 3] = jnp.where(outer, pair, summed[slot - 3])
            if slot < chunks + 2:
                out = summed[slot - 2] if slot >= 2 else inward[slot]
                pair = swap(jnp.where(outer, inward[slot], out) if slot < chunks else out, "row", 1)
            if 0 <= slot - 1 < chunks:
                cross = lax.ppermute(across[slot - 1], "row", [(0, 0), (1, 2), (2, 1), (3, 3)])
        if slot == 0:
            own_part += input_grad(after(lhs[0], *marks), w, 1, chunks, chunks, width)
            marks = [own_part[1]]
            for k, parts_of in enumerate(held):
                sent[k] += [swap(after(part, *marks), "col", k + 1) for part in parts_of]
        if slot in (2, 3):
            filled = weight_grad(filled, [after(lhs[0], *marks)] + lhs[1:], xs, slot - 2, 3, width)
            marks = [filled[1]]
        if slot == 1:
            blocks = split_rows(place, [after(blocks[0], *marks)] + blocks[1:], n_depth)
            blocks = [block if r == 0 else swap(block, "depth", r) for r, block in enumerate(blocks)]
            late = blocks[1:]
    grad_tokens = jnp.concatenate(done, axis=1)
    output, grad_taps = join(place, filled[1], [after(blocks[0], *marks)] + blocks[1:], taps.shape[1])
    grad_weight = jnp.transpose(filled[0], (1, 0, 2))
    return (output, grad_tokens, grad_weight, grad_taps)


def solution(mesh):
    in_specs = (
        P("col", "depth"),
        P(("row", "col"), None, "depth"),
        P(None, "row"),
        P(("col", "depth"), "row"),
    )
    out_specs = (
        P(("col", "depth"), "row"),
        P("col", "depth"),
        P(("row", "col"), None, "depth"),
        P(None, "row"),
    )
    return jax.shard_map(
        on_device, mesh=mesh, in_specs=in_specs, out_specs=out_specs, check_vma=False
    )
```

```python
import functools

import jax
import jax.numpy as jnp
from jax import lax
from jax.experimental import pallas as pl
from jax.experimental.pallas import tpu as pltpu
from jax.sharding import PartitionSpec as P

GROUP = 16
KT = 7
PAD = 8
LANES = 128
MIB = 1024 * 1024
SMALL = pl.CostEstimate(flops=1, bytes_accessed=1, transcendentals=0)


def swap(value, axis, flip):
    count = lax.axis_size(axis)
    return lax.ppermute(value, axis, [(i, i ^ flip) for i in range(count)])


def after(value, *earlier):
    return lax.optimization_barrier((value, *earlier))[0]


def resident(shape, width):
    if width % LANES == 0:
        return pl.BlockSpec(memory_space=pltpu.VMEM)
    return pl.BlockSpec(tuple(shape), lambda *_: (0,) * len(shape), pipeline_mode=pl.Buffered(1))


def params(mib, width):
    return pltpu.CompilerParams(vmem_limit_bytes=(mib if width % LANES == 0 else 56) * MIB)


def project_kernel(place, *refs, pieces, mode, count, width):
    x_refs = refs[:pieces]
    w_ref, keep_ref, send_ref = refs[pieces : pieces + 3]
    stream = pl.program_id(0)
    core = place[0] % 2
    x = x_refs[0][...]
    if mode == "cut":
        last_ref = refs[pieces + 3]

        @pl.when(stream == 0)
        def _():
            last_ref[...] = x_refs[0][x.shape[0] - last_ref.shape[0] :, :]

    if mode == "join":
        joined, rest = refs[pieces + 3 :]
        third = x.shape[0]
        parity = place[2] % 2

        @pl.when(stream == 0)
        def _():
            joined[pl.ds(pl.multiple_of(parity * third, third), third), :] = x_refs[0][...]
            joined[pl.ds(pl.multiple_of((1 - parity) * third, third), third), :] = x_refs[1][...]
            joined[2 * third :, :] = x_refs[2][...]
            rest[0:third, :] = x_refs[1][...]
            rest[third:, :] = x_refs[2][...]

        x = rest[...]
    nt = (((1,), (1,)), ((), ()))
    if width % LANES == 0:
        whole = lax.dot_general(x, w_ref[stream], nt, preferred_element_type=jnp.float32).astype(jnp.bfloat16)
        blocks = [whole[:, j * width : (j + 1) * width] for j in range(count)]
    else:
        blocks = [
            lax.dot_general(
                x, w_ref[0, j * width : (j + 1) * width, :], nt, preferred_element_type=jnp.float32
            ).astype(jnp.bfloat16)
            for j in range(count)
        ]
    for mine in range(2):

        @pl.when(core == mine)
        def _():
            for j in range(count):
                at = (j ^ place[0]) // 2
                if j % 2 == mine:
                    keep_ref[at, stream] = blocks[j]
                else:
                    send_ref[at, stream] = blocks[j]


def project(place, xs, w, count, mode="plain"):
    feat = xs[0].shape[1]
    all_tok = sum(x.shape[0] for x in xs)
    tok = all_tok - xs[0].shape[0] if mode == "join" else all_tok
    streams, channels, _ = w.shape
    width = channels // count
    part = jax.ShapeDtypeStruct((count // 2, streams, tok, width), jnp.bfloat16)
    wide = width % LANES == 0
    spec = resident(part.shape, width)
    more = {"plain": [], "cut": [(tok // 3, feat)], "join": [(all_tok, feat)]}[mode]
    return pl.pallas_call(
        functools.partial(project_kernel, pieces=len(xs), mode=mode, count=count, width=width),
        grid_spec=pltpu.PrefetchScalarGridSpec(
            num_scalar_prefetch=1,
            grid=(streams,),
            in_specs=[resident(x.shape, width) for x in xs]
            + [resident(w.shape, width) if wide else pl.BlockSpec((1, channels, feat), lambda s, _: (s, 0, 0))],
            out_specs=[spec, spec] + [resident(shape, width) for shape in more],
            scratch_shapes=[pltpu.VMEM((tok, feat), jnp.bfloat16)] if mode == "join" else [],
        ),
        out_shape=[part, part] + [jax.ShapeDtypeStruct(shape, jnp.bfloat16) for shape in more],
        compiler_params=params(10, width),
        cost_estimate=SMALL,
        name="project",
    )(place, *xs, w)


def in_three(value):
    terms = []
    for _ in range(3):
        term = value.astype(jnp.bfloat16)
        value = value - term.astype(jnp.float32)
        terms.append(term)
    return terms


def split_lanes_kernel(place, up_ref, *out_refs):
    n_depth, width = len(out_refs), out_refs[0].shape[2]
    for r, ref in enumerate(out_refs):
        for k in range(ref.shape[0]):
            at = ((place[1] ^ k) * n_depth + (place[0] ^ r)) * width
            ref[k] = up_ref[:, pl.ds(pl.multiple_of(at, width), width)]


def merge_rows_kernel(place, *refs, n_depth):
    in_refs, out_refs = refs[:n_depth], refs[n_depth:]
    local = in_refs[0].shape[1]
    for r, ref in enumerate(in_refs):
        for k, out_ref in enumerate(out_refs):
            out_ref[pl.ds(pl.multiple_of((place[0] ^ r) * local, 16), local), :] = ref[k]


def split_rows_kernel(place, *refs, n_col):
    in_refs, out_refs = refs[:n_col], refs[n_col:]
    local = out_refs[0].shape[1] - 32
    for r, ref in enumerate(out_refs):
        rows = pl.ds(pl.multiple_of((place[0] ^ r) * local, 16), local)
        for k in range(n_col):
            ref[k, 0:local] = in_refs[k][rows, :]
            ref[k, local:] = in_refs[k][-32:, :]


def rearrange(kernel, place, arrays, count, shape, name):
    width = shape[-1]
    return pl.pallas_call(
        kernel,
        grid_spec=pltpu.PrefetchScalarGridSpec(
            num_scalar_prefetch=1,
            grid=(1,),
            in_specs=[resident(value.shape, width) for value in arrays],
            out_specs=[resident(shape, width)] * count,
        ),
        out_shape=[jax.ShapeDtypeStruct(shape, jnp.bfloat16)] * count,
        compiler_params=params(4, width),
        cost_estimate=SMALL,
        name=name,
    )(place, *arrays)


def split_lanes(place, up, n_col, n_depth):
    local, width = up.shape[0], up.shape[1] // (n_col * n_depth)
    if width % LANES:
        blocks = up.reshape(local, n_col, n_depth, width)[:, place[1] ^ jnp.arange(n_col)]
        return [
            jnp.transpose(lax.dynamic_index_in_dim(blocks, place[0] ^ r, 2, keepdims=False), (1, 0, 2))
            for r in range(n_depth)
        ]
    return rearrange(split_lanes_kernel, place, [up], n_depth, (n_col, local, width), "split")


def merge_rows(place, pieces):
    n_depth = len(pieces)
    n_col, local, width = pieces[0].shape
    if width % LANES:
        whole = jnp.stack(pieces)[place[0] ^ jnp.arange(n_depth)]
        return list(jnp.transpose(whole, (1, 0, 2, 3)).reshape(n_col, n_depth * local, width))
    kernel = functools.partial(merge_rows_kernel, n_depth=n_depth)
    return list(rearrange(kernel, place, pieces, n_col, (n_depth * local, width), "merge"))


def split_rows(place, arrays, n_depth):
    local, width = (arrays[0].shape[0] - 32) // n_depth, arrays[0].shape[1]
    if width % LANES:
        whole = jnp.stack(arrays)
        return [
            jnp.concatenate(
                [lax.dynamic_slice_in_dim(whole, (place[0] ^ r) * local, local, axis=1), whole[:, -32:]], axis=1
            )
            for r in range(n_depth)
        ]
    kernel = functools.partial(split_rows_kernel, n_col=len(arrays))
    return rearrange(kernel, place, arrays, n_depth, (len(arrays), local + 32, width), "split")


def join_kernel(place, _, *refs):
    block_refs, (out_ref, grad_taps_ref) = refs[:-2], refs[-2:]
    n_depth = len(block_refs)
    n_col, _, width = block_refs[0].shape
    local, groups = out_ref.shape[0], grad_taps_ref.shape[1]
    lane_group = lax.broadcasted_iota(jnp.int32, (width, groups), 0) // GROUP
    group = lax.broadcasted_iota(jnp.int32, (width, groups), 1)
    total = jnp.zeros((24, groups), jnp.float32)
    for r, ref in enumerate(block_refs):
        for k in range(n_col):
            at = (place[1] ^ k) * n_depth + (place[0] ^ r)
            out_ref[:, pl.ds(pl.multiple_of(at * width, width), width)] = ref[k, 0:local, :]
            spread = (lane_group + at * (width // GROUP) == group).astype(jnp.bfloat16)
            total = total + jnp.dot(ref[k, local : local + 24, :], spread, preferred_element_type=jnp.float32)
    grad_taps_ref[...] = (total[0:8] + total[8:16] + total[16:24])[:KT]


def join(place, mark, blocks, groups):
    n_depth = len(blocks)
    n_col, rows, width = blocks[0].shape
    local = rows - 32
    if width % LANES:
        whole = jnp.stack(blocks)[place[0] ^ jnp.arange(n_depth)][:, place[1] ^ jnp.arange(n_col)]
        sums = whole[:, :, local : local + 24].astype(jnp.float32)
        sums = sums.reshape(n_depth, n_col, 3, 8, width // GROUP, GROUP).sum(axis=(2, 5))[:, :, :KT]
        return (
            jnp.transpose(whole[:, :, :local], (2, 1, 0, 3)).reshape(local, -1),
            jnp.transpose(sums, (2, 1, 0, 3)).reshape(KT, -1),
        )
    channels = n_depth * n_col * width
    return pl.pallas_call(
        join_kernel,
        grid_spec=pltpu.PrefetchScalarGridSpec(
            num_scalar_prefetch=1,
            grid=(1,),
            in_specs=[pl.BlockSpec(memory_space=pl.ANY)] + [resident(blocks[0].shape, width)] * n_depth,
            out_specs=[resident((local, channels), width), resident((KT, groups), width)],
        ),
        out_shape=[
            jax.ShapeDtypeStruct((local, channels), jnp.bfloat16),
            jax.ShapeDtypeStruct((KT, groups), jnp.float32),
        ],
        compiler_params=params(4, width),
        cost_estimate=SMALL,
        name="join",
    )(place, mark, *blocks)


def middle_kernel(place, taps_ref, *refs, pieces, groups, terms, tile):
    up_refs, refs = refs[:groups], refs[groups:]
    part_refs, refs = refs[: len(pieces) * terms], refs[len(pieces) * terms :]
    grad_refs, out_refs = refs[:groups], refs[groups : 2 * groups]
    up_s, out_s, q_s, k_s, v_s, mixed_s, gf_s, far_s = refs[2 * groups :]
    col = place[1]
    tok, width = up_refs[0].shape
    parity = place[2] % 2
    total = groups * tok
    tap_groups = taps_ref.shape[1]
    for k, ref in enumerate(up_refs):
        up_s[pl.ds(pl.multiple_of((col ^ k) * tok, tok), tok), :] = ref[...]
    lane_group = lax.broadcasted_iota(jnp.int32, (tap_groups, width), 1) // GROUP
    group = lax.broadcasted_iota(jnp.int32, (tap_groups, width), 0)
    spread = (lane_group + place[3] * (width // GROUP) == group).astype(jnp.bfloat16)
    taps = sum(jnp.dot(term, spread, preferred_element_type=jnp.float32) for term in in_three(taps_ref[...]))
    mixed_s[0:PAD, :] = jnp.zeros((PAD, width), jnp.float32)
    gf_s[total : total + PAD, :] = jnp.zeros((PAD, width), jnp.float32)
    step = 64
    for piece, (k, thirds) in enumerate(pieces):
        refs_of = part_refs[piece * terms : (piece + 1) * terms]
        rows_of = refs_of[0].shape[2]
        length = rows_of // len(thirds)
        for i in range(rows_of // step):
            third = thirds[i * step // length]
            at = {"own": parity, "other": 1 - parity, "last": 2, "all": 0}[third] * length
            start = (col ^ k) * tok + at + i * step % length
            inside = slice(i * step, (i + 1) * step)
            rows = pl.ds(pl.multiple_of(start, step), step)
            streams = []
            for s in range(3):
                acc = None
                for ref in refs_of:
                    term = ref[0, s, inside, :].astype(jnp.float32)
                    acc = term if acc is None else acc + term
                streams.append(acc.astype(jnp.bfloat16))
            q_s[rows, :], k_s[rows, :], v_s[rows, :] = streams
            query, key, value = [stream.astype(jnp.float32) for stream in streams]
            mixed_s[pl.ds(pl.multiple_of(start + PAD, PAD), step), :] = key * value
            gf_s[rows, :] = up_s[rows, :].astype(jnp.float32) * query
    sums = [jnp.zeros((8, width), jnp.float32) for _ in range(KT)]
    for a in range(groups):
        for i in range(tok // tile):
            first = a * tok + i * tile
            rows = slice(first, first + tile)
            inside = slice(i * tile, (i + 1) * tile)
            gf = gf_s[rows, :]
            filtered = jnp.zeros((tile, width), jnp.float32)
            grad_mixed = jnp.zeros((tile, width), jnp.float32)
            for j in range(KT):
                shifted = mixed_s[first + PAD - j : first + PAD - j + tile, :]
                filtered = filtered + taps[j : j + 1, :] * shifted
                sums[j] = sums[j] + (gf * shifted).reshape(tile // 8, 8, width).sum(axis=0)
                grad_mixed = grad_mixed + taps[j : j + 1, :] * gf_s[first + j : first + j + tile, :]
            out_s[a, inside, :] = (q_s[rows, :].astype(jnp.float32) * filtered).astype(jnp.bfloat16)
            at = col ^ a
            far_s[at, 0, inside, :] = (up_s[rows, :].astype(jnp.float32) * filtered).astype(jnp.bfloat16)
            far_s[at, 1, inside, :] = (grad_mixed * v_s[rows, :].astype(jnp.float32)).astype(jnp.bfloat16)
            far_s[at, 2, inside, :] = (grad_mixed * k_s[rows, :].astype(jnp.float32)).astype(jnp.bfloat16)
    for k in range(groups):
        grad_refs[k][...] = far_s[k]
    rest = jnp.concatenate(
        [sums[j].sum(axis=0, keepdims=True) for j in range(KT)] + [jnp.zeros((1, width), jnp.float32)], axis=0
    )
    terms_of = [term.astype(jnp.float32) for term in in_three(rest)]
    packed = jnp.concatenate(terms_of + [jnp.zeros((8, width), jnp.float32)], axis=0).astype(jnp.bfloat16)
    for k, ref in enumerate(out_refs):
        ref[0:tok, :] = out_s[col ^ k]
        ref[tok : tok + 32, :] = packed


def middle(place, taps, ups, pieces, parts, tile):
    groups, terms = len(ups), len(parts[0])
    tok, width = ups[0].shape
    total = groups * tok
    whole = lambda *shape: resident(shape, width)
    ones = [whole(1, 3, terms_of[0].shape[2], width) for terms_of in parts for _ in terms_of]
    outs = pl.pallas_call(
        functools.partial(middle_kernel, pieces=pieces, groups=groups, terms=terms, tile=tile),
        grid_spec=pltpu.PrefetchScalarGridSpec(
            num_scalar_prefetch=1,
            grid=(1,),
            in_specs=[whole(*taps.shape)] + [whole(tok, width)] * groups + ones,
            out_specs=[whole(3, tok, width)] * groups + [whole(tok + 32, width)] * groups,
            scratch_shapes=[
                pltpu.VMEM((total, width), jnp.bfloat16),
                pltpu.VMEM((groups, tok, width), jnp.bfloat16),
            ]
            + [pltpu.VMEM((total, width), jnp.bfloat16)] * 3
            + [pltpu.VMEM((total + PAD, width), jnp.float32)] * 2
            + [pltpu.VMEM((groups, 3, tok, width), jnp.bfloat16)],
        ),
        out_shape=[jax.ShapeDtypeStruct((3, tok, width), jnp.bfloat16)] * groups
        + [jax.ShapeDtypeStruct((tok + 32, width), jnp.bfloat16)] * groups,
        compiler_params=params(10, width),
        cost_estimate=SMALL,
        name="middle",
    )(place, taps, *ups, *[term for terms_of in parts for term in terms_of])
    return outs[:groups], outs[groups:]


def assemble_kernel(place, *refs):
    grad_refs, out_ref = refs[:-1], refs[-1]
    width = grad_refs[0].shape[2]
    for r, ref in enumerate(grad_refs):
        for s in range(3):
            at = pl.multiple_of((s * len(grad_refs) + (place[0] ^ r)) * width, width)
            out_ref[:, pl.ds(at, width)] = ref[s]


def assemble(place, grads):
    streams, tok, width = grads[0].shape
    out = jax.ShapeDtypeStruct((tok, streams * width * len(grads)), jnp.bfloat16)
    if width % LANES:
        whole = jnp.stack(grads)[place[0] ^ jnp.arange(len(grads))]
        return jnp.transpose(whole, (2, 1, 0, 3)).reshape(out.shape)
    return pl.pallas_call(
        assemble_kernel,
        grid_spec=pltpu.PrefetchScalarGridSpec(
            num_scalar_prefetch=1,
            grid=(1,),
            in_specs=[resident(grads[0].shape, width)] * len(grads),
            out_specs=resident(out.shape, width),
        ),
        out_shape=out,
        compiler_params=params(4, width),
        cost_estimate=SMALL,
        name="assemble",
    )(place, *grads)


def input_grad_kernel(grad_ref, w_ref, out_ref, *, first):
    step = out_ref.shape[1]
    rows = w_ref[:, :, first * step : (first + 1) * step].reshape(-1, step)
    out_ref[...] = jnp.dot(grad_ref[...], rows, preferred_element_type=jnp.float32).astype(jnp.bfloat16)


def input_grads_kernel(grad_ref, w_ref, *refs, first):
    out_refs, (slots, sems) = refs[:-2], refs[-2:]
    step = out_refs[0].shape[1]

    def fetch(i):
        columns = pl.ds((first + i) * step, step)
        return pltpu.make_async_copy(w_ref.at[:, :, columns], slots.at[i % 2], sems.at[i % 2])

    fetch(0).start()
    for i, out_ref in enumerate(out_refs):
        if i + 1 < len(out_refs):
            fetch(i + 1).start()
        fetch(i).wait()
        rows = slots[i % 2].reshape(-1, step)
        out_ref[...] = jnp.dot(grad_ref[...], rows, preferred_element_type=jnp.float32).astype(jnp.bfloat16)


def input_grad(grad, w, first, last, chunks, width):
    tok = grad.shape[0]
    streams, channels, feat = w.shape
    step = feat // chunks
    count = last - first
    if width % LANES:
        rows = w[:, :, first * step : last * step].reshape(streams * channels, count * step)
        whole = jnp.dot(grad, rows, preferred_element_type=jnp.float32).astype(jnp.bfloat16)
        return [whole[:, i * step : (i + 1) * step] for i in range(count)]
    single = count == 1
    return list(
        pl.pallas_call(
            functools.partial(input_grad_kernel if single else input_grads_kernel, first=first),
            in_specs=[
                resident(grad.shape, width),
                pl.BlockSpec(memory_space=pltpu.VMEM if single else pltpu.HBM),
            ],
            out_specs=[resident((tok, step), width)] * count,
            out_shape=[jax.ShapeDtypeStruct((tok, step), jnp.bfloat16)] * count,
            scratch_shapes=[]
            if single
            else [pltpu.VMEM((2, streams, channels, step), jnp.bfloat16), pltpu.SemaphoreType.DMA((2,))],
            compiler_params=params(8, width),
            cost_estimate=SMALL,
            name="input_grad",
        )(grad, w)
    )


def weight_grad_kernel(*refs, chained, groups, half):
    refs = refs[2 * chained :]
    grad_refs, x_refs = refs[:groups], refs[groups : 2 * groups]
    out_ref, mark_ref, turned = refs[2 * groups :]
    mark_ref[...] = jnp.zeros(mark_ref.shape, jnp.float32)
    streams, channels, step = out_ref.shape
    tok = x_refs[0].shape[0]

    @pl.when(pl.program_id(0) == 0)
    def _():
        for k in range(groups):
            for s in range(streams):
                at = (2 * s + half) * channels
                block = grad_refs[k][:, at : at + channels]
                turned[s * channels : (s + 1) * channels, k * tok : (k + 1) * tok] = block.T

    columns = pl.ds(pl.multiple_of(pl.program_id(0) * step, step), step)
    acc = None
    for k in range(groups):
        term = jnp.dot(turned[:, k * tok : (k + 1) * tok], x_refs[k][:, columns], preferred_element_type=jnp.float32)
        acc = term if acc is None else acc + term
    for s in range(streams):
        out_ref[s] = acc[s * channels : (s + 1) * channels, :]


def weight_grad(filled, grads, xs, half, streams, width):
    groups = len(xs)
    tok, feat = xs[0].shape
    channels = grads[0].shape[1] // streams
    chained = filled is not None
    if width % LANES:
        if chained:
            return filled
        terms = [
            lax.dot_general(grad, x, (((0,), (0,)), ((), ())), preferred_element_type=jnp.float32)
            for grad, x in zip(grads, xs)
        ]
        return sum(terms).reshape(streams, channels, feat), jnp.zeros((8, LANES), jnp.float32)
    step = min(512, feat)
    return pl.pallas_call(
        functools.partial(weight_grad_kernel, chained=chained, groups=groups, half=half),
        grid=(feat // step,),
        in_specs=[pl.BlockSpec(memory_space=pl.ANY)] * (2 * chained)
        + [resident(grads[0].shape, width)] * groups
        + [resident((tok, feat), width)] * groups,
        out_specs=[
            pl.BlockSpec((streams, channels // 2, step), lambda i: (0, half, i)),
            resident((8, LANES), width),
        ],
        scratch_shapes=[pltpu.VMEM((streams * channels // 2, groups * tok), jnp.bfloat16)],
        out_shape=[
            jax.ShapeDtypeStruct((streams, channels, feat), jnp.float32),
            jax.ShapeDtypeStruct((8, LANES), jnp.float32),
        ],
        input_output_aliases={0: 0} if chained else {},
        compiler_params=params(14, width),
        cost_estimate=SMALL,
        name="weight_grad",
    )(*(filled if chained else []), *grads, *xs)


def added(first, second):
    return (first.astype(jnp.float32) + second.astype(jnp.float32)).astype(jnp.bfloat16)


def on_device(tokens, weight, taps, upstream):
    n_col = lax.axis_size("col")
    n_depth = lax.axis_size("depth")
    local_tok = upstream.shape[0]
    depth_at = lax.axis_index("depth")
    col_at = lax.axis_index("col")
    row_at = lax.axis_index("row")
    place = jnp.stack([depth_at, col_at, row_at, col_at * n_depth + depth_at]).astype(jnp.int32)
    w = jnp.transpose(weight, (1, 0, 2))
    width = w.shape[1] // n_depth
    def sum_over_depth(keep, send, near_after=(), far_after=()):
        near = swap(after(send, *near_after) if near_after else send, "depth", 1)
        pairs = [added(keep[r // 2], near[r // 2])[None] for r in range(2, n_depth, 2)]
        held = [after(pair, *far_after) if far_after else pair for pair in pairs]
        fars = [swap(pair, "depth", 2 * i + 2) for i, pair in enumerate(held)]
        return [keep, near] + fars, pairs, fars

    tok = tokens.shape[0]
    third = tok // 3
    cut = tok % 192 == 0 and lax.axis_size("row") % 2 == 0
    sent_first = lax.dynamic_slice_in_dim(tokens, row_at % 2 * third, third, axis=0) if cut else tokens
    first = [swap(sent_first, "col", k) for k in range(1, n_col)]
    ups = split_lanes(place, upstream, n_col, n_depth)
    ups = [up if r == 0 else swap(up, "depth", r) for r, up in enumerate(ups)]
    outer = (row_at == 0) | (row_at == 3)
    keep, send, *last = project(place, [after(tokens, outer)], w, n_depth, "cut" if cut else "plain")
    terms, pairs, fars = sum_over_depth(keep, send, first + ups[1:])
    xs, pieces, parts = [tokens], [(0, ("all",))], [terms]
    for k in range(1, n_col):
        mine = first[k - 1]
        if not cut:
            keep, send = project(place, [after(mine, *fars)], w, n_depth)
            terms, pairs, fars = sum_over_depth(keep, send)
            xs.append(mine)
            pieces.append((k, ("all",)))
            parts.append(terms)
            continue
        other = swap(mine, "row", 1)
        rest = swap(after(last[0], mine), "col", k)
        keep, send = project(place, [after(mine, *pairs)], w, n_depth)
        terms, ahead, ahead_fars = sum_over_depth(keep, send)
        pieces.append((k, ("own",)))
        parts.append(terms)
        keep, send, x = project(place, [mine, other, after(rest, *fars, *ahead)], w, n_depth, "join")
        terms, pairs, fars = sum_over_depth(keep, send, (), ahead_fars)
        pieces.append((k, ("other", "last")))
        parts.append(terms)
        xs.append(x)
    ups = merge_rows(place, [after(ups[0], *pairs)] + ups[1:])
    ups = [up if k == 0 else swap(up, "col", k) for k, up in enumerate(ups)]
    own_grads, blocks = middle(place, taps, ups, pieces, parts, local_tok)
    nears = [swap(own, "depth", 1) for own in own_grads]
    blocks = [block if k == 0 else swap(block, "col", k) for k, block in enumerate(blocks)]
    beside = nears + blocks[1:]
    chunks = 4
    grads = [None] * n_col
    ready = []
    sent = []
    lhs = [None] * n_col
    for k in reversed(range(n_col)):
        fars = [swap(after(own_grads[k], *ready) if ready else own_grads[k], "depth", r) for r in range(2, n_depth, 2)]
        ready = fars
        if k > 0:
            fars = [after(far, *beside) for far in fars]
        elif sent:
            fars = [after(far, sent[-1][1][-1]) for far in fars]
        grads[k] = [own_grads[k], nears[k]]
        for far in fars:
            grads[k] += [far, swap(far, "depth", 1)]
        lhs[k] = assemble(place, grads[k])
        if k > 0:
            parts_of = input_grad(lhs[k], w, 0, 1, chunks, width)
            parts_of += input_grad(after(lhs[k], *parts_of), w, 1, chunks, chunks, width)
            sent.append(([swap(part, "col", k) for part in parts_of[:3]], parts_of))
    held = [parts_of[3:] for _, parts_of in sent]
    sent = [of for of, _ in sent]
    own_part = input_grad(lhs[0], w, 0, 1, chunks, width)
    line = lax.axis_size("row") == 4
    inward, across, summed, done = ([None] * chunks for _ in range(4))
    pair = cross = filled = None
    marks = []
    for slot in range(chunks + 3):
        if slot < chunks:
            total = after(own_part[slot], *marks).astype(jnp.float32)
            for of in sent:
                total = total + of[slot].astype(jnp.float32)
            inward[slot] = total.astype(jnp.bfloat16)
            marks = [inward[slot]]
        if not line:
            if slot < chunks:
                done[slot] = lax.psum(inward[slot], "row")
        else:
            if 0 <= slot - 1 < chunks:
                across[slot - 1] = added(after(inward[slot - 1], *marks), pair)
                marks = [across[slot - 1]]
            if 0 <= slot - 2 < chunks:
                summed[slot - 2] = added(after(across[slot - 2], *marks), cross)
                marks = [summed[slot - 2]]
            if 0 <= slot - 3 < chunks:
                done[slot - 3] = jnp.where(outer, pair, summed[slot - 3])
            if slot < 2:
                pair = lax.ppermute(inward[slot], "row", [(0, 1), (3, 2)])
            elif slot < chunks + 2:
                out = summed[slot - 2]
                pair = swap(jnp.where(outer, inward[slot], out) if slot < chunks else out, "row", 1)
            if 0 <= slot - 1 < chunks:
                cross = lax.ppermute(across[slot - 1], "row", [(0, 0), (1, 2), (2, 1), (3, 3)])
        if slot == 0:
            own_part += input_grad(after(lhs[0], *marks), w, 1, chunks, chunks, width)
            marks = [own_part[1]]
            for k, parts_of in enumerate(held):
                sent[k] += [swap(after(part, *marks), "col", k + 1) for part in parts_of]
        if slot in (2, 4):
            filled = weight_grad(filled, [after(lhs[0], *marks)] + lhs[1:], xs, slot // 2 - 1, 3, width)
            marks = [filled[1]]
        if slot == 4:
            marks += late
        if slot == 3:
            blocks = split_rows(place, [after(blocks[0], *marks)] + blocks[1:], n_depth)
            blocks = [block if r == 0 else swap(block, "depth", r) for r, block in enumerate(blocks)]
            late = blocks[1:]
    grad_tokens = jnp.concatenate(done, axis=1)
    output, grad_taps = join(place, filled[1], [after(blocks[0], *marks)] + blocks[1:], taps.shape[1])
    grad_weight = jnp.transpose(filled[0], (1, 0, 2))
    return (output, grad_tokens, grad_weight, grad_taps)


def solution(mesh):
    in_specs = (
        P("col", "depth"),
        P(("row", "col"), None, "depth"),
        P(None, "row"),
        P(("col", "depth"), "row"),
    )
    out_specs = (
        P(("col", "depth"), "row"),
        P("col", "depth"),
        P(("row", "col"), None, "depth"),
        P(None, "row"),
    )
    return jax.shard_map(
        on_device, mesh=mesh, in_specs=in_specs, out_specs=out_specs, check_vma=False
    )
```

```python
import functools

import jax
import jax.numpy as jnp
from jax import lax
from jax.experimental import pallas as pl
from jax.experimental.pallas import tpu as pltpu
from jax.sharding import PartitionSpec as P

GROUP = 16
KT = 7
PAD = 8
LANES = 128
MIB = 1024 * 1024
SMALL = pl.CostEstimate(flops=1, bytes_accessed=1, transcendentals=0)


def swap(value, axis, flip):
    count = lax.axis_size(axis)
    return lax.ppermute(value, axis, [(i, i ^ flip) for i in range(count)])


def after(value, *earlier):
    return lax.optimization_barrier((value, *earlier))[0]


def resident(shape, width):
    if width % LANES == 0:
        return pl.BlockSpec(memory_space=pltpu.VMEM)
    return pl.BlockSpec(tuple(shape), lambda *_: (0,) * len(shape), pipeline_mode=pl.Buffered(1))


def params(mib, width):
    return pltpu.CompilerParams(vmem_limit_bytes=(mib if width % LANES == 0 else 56) * MIB)


def project_kernel(place, *refs, pieces, mode, count, width):
    x_refs = refs[:pieces]
    w_ref, keep_ref, send_ref = refs[pieces : pieces + 3]
    stream = pl.program_id(0)
    core = place[0] % 2
    x = x_refs[0][...]
    if mode == "cut":
        last_ref = refs[pieces + 3]

        @pl.when(stream == 0)
        def _():
            last_ref[...] = x_refs[0][x.shape[0] - last_ref.shape[0] :, :]

    if mode == "join":
        joined, rest = refs[pieces + 3 :]
        third = x.shape[0]
        parity = place[2] % 2

        @pl.when(stream == 0)
        def _():
            joined[pl.ds(pl.multiple_of(parity * third, third), third), :] = x_refs[0][...]
            joined[pl.ds(pl.multiple_of((1 - parity) * third, third), third), :] = x_refs[1][...]
            joined[2 * third :, :] = x_refs[2][...]
            rest[0:third, :] = x_refs[1][...]
            rest[third:, :] = x_refs[2][...]

        x = rest[...]
    nt = (((1,), (1,)), ((), ()))
    if width % LANES == 0:
        whole = lax.dot_general(x, w_ref[stream], nt, preferred_element_type=jnp.float32).astype(jnp.bfloat16)
        blocks = [whole[:, j * width : (j + 1) * width] for j in range(count)]
    else:
        blocks = [
            lax.dot_general(
                x, w_ref[0, j * width : (j + 1) * width, :], nt, preferred_element_type=jnp.float32
            ).astype(jnp.bfloat16)
            for j in range(count)
        ]
    for mine in range(2):

        @pl.when(core == mine)
        def _():
            for j in range(count):
                at = (j ^ place[0]) // 2
                if j % 2 == mine:
                    keep_ref[at, stream] = blocks[j]
                else:
                    send_ref[at, stream] = blocks[j]


def project(place, xs, w, count, mode="plain"):
    feat = xs[0].shape[1]
    all_tok = sum(x.shape[0] for x in xs)
    tok = all_tok - xs[0].shape[0] if mode == "join" else all_tok
    streams, channels, _ = w.shape
    width = channels // count
    part = jax.ShapeDtypeStruct((count // 2, streams, tok, width), jnp.bfloat16)
    wide = width % LANES == 0
    spec = resident(part.shape, width)
    more = {"plain": [], "cut": [(tok // 3, feat)], "join": [(all_tok, feat)]}[mode]
    return pl.pallas_call(
        functools.partial(project_kernel, pieces=len(xs), mode=mode, count=count, width=width),
        grid_spec=pltpu.PrefetchScalarGridSpec(
            num_scalar_prefetch=1,
            grid=(streams,),
            in_specs=[resident(x.shape, width) for x in xs]
            + [resident(w.shape, width) if wide else pl.BlockSpec((1, channels, feat), lambda s, _: (s, 0, 0))],
            out_specs=[spec, spec] + [resident(shape, width) for shape in more],
            scratch_shapes=[pltpu.VMEM((tok, feat), jnp.bfloat16)] if mode == "join" else [],
        ),
        out_shape=[part, part] + [jax.ShapeDtypeStruct(shape, jnp.bfloat16) for shape in more],
        compiler_params=params(10, width),
        cost_estimate=SMALL,
        name="project",
    )(place, *xs, w)


def in_three(value):
    terms = []
    for _ in range(3):
        term = value.astype(jnp.bfloat16)
        value = value - term.astype(jnp.float32)
        terms.append(term)
    return terms


def split_lanes_kernel(place, up_ref, *out_refs):
    n_depth, width = len(out_refs), out_refs[0].shape[2]
    for r, ref in enumerate(out_refs):
        for k in range(ref.shape[0]):
            at = ((place[1] ^ k) * n_depth + (place[0] ^ r)) * width
            ref[k] = up_ref[:, pl.ds(pl.multiple_of(at, width), width)]


def merge_rows_kernel(place, *refs, n_depth):
    in_refs, out_refs = refs[:n_depth], refs[n_depth:]
    local = in_refs[0].shape[1]
    for r, ref in enumerate(in_refs):
        for k, out_ref in enumerate(out_refs):
            out_ref[pl.ds(pl.multiple_of((place[0] ^ r) * local, 16), local), :] = ref[k]


def split_rows_kernel(place, *refs, n_col):
    in_refs, out_refs = refs[:n_col], refs[n_col:]
    local = out_refs[0].shape[1] - 32
    for r, ref in enumerate(out_refs):
        rows = pl.ds(pl.multiple_of((place[0] ^ r) * local, 16), local)
        for k in range(n_col):
            ref[k, 0:local] = in_refs[k][rows, :]
            ref[k, local:] = in_refs[k][-32:, :]


def rearrange(kernel, place, arrays, count, shape, name):
    width = shape[-1]
    return pl.pallas_call(
        kernel,
        grid_spec=pltpu.PrefetchScalarGridSpec(
            num_scalar_prefetch=1,
            grid=(1,),
            in_specs=[resident(value.shape, width) for value in arrays],
            out_specs=[resident(shape, width)] * count,
        ),
        out_shape=[jax.ShapeDtypeStruct(shape, jnp.bfloat16)] * count,
        compiler_params=params(4, width),
        cost_estimate=SMALL,
        name=name,
    )(place, *arrays)


def split_lanes(place, up, n_col, n_depth):
    local, width = up.shape[0], up.shape[1] // (n_col * n_depth)
    if width % LANES:
        blocks = up.reshape(local, n_col, n_depth, width)[:, place[1] ^ jnp.arange(n_col)]
        return [
            jnp.transpose(lax.dynamic_index_in_dim(blocks, place[0] ^ r, 2, keepdims=False), (1, 0, 2))
            for r in range(n_depth)
        ]
    return rearrange(split_lanes_kernel, place, [up], n_depth, (n_col, local, width), "split")


def merge_rows(place, pieces):
    n_depth = len(pieces)
    n_col, local, width = pieces[0].shape
    if width % LANES:
        whole = jnp.stack(pieces)[place[0] ^ jnp.arange(n_depth)]
        return list(jnp.transpose(whole, (1, 0, 2, 3)).reshape(n_col, n_depth * local, width))
    kernel = functools.partial(merge_rows_kernel, n_depth=n_depth)
    return list(rearrange(kernel, place, pieces, n_col, (n_depth * local, width), "merge"))


def split_rows(place, arrays, n_depth):
    local, width = (arrays[0].shape[0] - 32) // n_depth, arrays[0].shape[1]
    if width % LANES:
        whole = jnp.stack(arrays)
        return [
            jnp.concatenate(
                [lax.dynamic_slice_in_dim(whole, (place[0] ^ r) * local, local, axis=1), whole[:, -32:]], axis=1
            )
            for r in range(n_depth)
        ]
    kernel = functools.partial(split_rows_kernel, n_col=len(arrays))
    return rearrange(kernel, place, arrays, n_depth, (len(arrays), local + 32, width), "split")


def join_kernel(place, _, *refs):
    block_refs, (out_ref, grad_taps_ref) = refs[:-2], refs[-2:]
    n_depth = len(block_refs)
    n_col, _, width = block_refs[0].shape
    local, groups = out_ref.shape[0], grad_taps_ref.shape[1]
    lane_group = lax.broadcasted_iota(jnp.int32, (width, groups), 0) // GROUP
    group = lax.broadcasted_iota(jnp.int32, (width, groups), 1)
    total = jnp.zeros((24, groups), jnp.float32)
    for r, ref in enumerate(block_refs):
        for k in range(n_col):
            at = (place[1] ^ k) * n_depth + (place[0] ^ r)
            out_ref[:, pl.ds(pl.multiple_of(at * width, width), width)] = ref[k, 0:local, :]
            spread = (lane_group + at * (width // GROUP) == group).astype(jnp.bfloat16)
            total = total + jnp.dot(ref[k, local : local + 24, :], spread, preferred_element_type=jnp.float32)
    grad_taps_ref[...] = (total[0:8] + total[8:16] + total[16:24])[:KT]


def join(place, mark, blocks, groups):
    n_depth = len(blocks)
    n_col, rows, width = blocks[0].shape
    local = rows - 32
    if width % LANES:
        whole = jnp.stack(blocks)[place[0] ^ jnp.arange(n_depth)][:, place[1] ^ jnp.arange(n_col)]
        sums = whole[:, :, local : local + 24].astype(jnp.float32)
        sums = sums.reshape(n_depth, n_col, 3, 8, width // GROUP, GROUP).sum(axis=(2, 5))[:, :, :KT]
        return (
            jnp.transpose(whole[:, :, :local], (2, 1, 0, 3)).reshape(local, -1),
            jnp.transpose(sums, (2, 1, 0, 3)).reshape(KT, -1),
        )
    channels = n_depth * n_col * width
    return pl.pallas_call(
        join_kernel,
        grid_spec=pltpu.PrefetchScalarGridSpec(
            num_scalar_prefetch=1,
            grid=(1,),
            in_specs=[pl.BlockSpec(memory_space=pl.ANY)] + [resident(blocks[0].shape, width)] * n_depth,
            out_specs=[resident((local, channels), width), resident((KT, groups), width)],
        ),
        out_shape=[
            jax.ShapeDtypeStruct((local, channels), jnp.bfloat16),
            jax.ShapeDtypeStruct((KT, groups), jnp.float32),
        ],
        compiler_params=params(4, width),
        cost_estimate=SMALL,
        name="join",
    )(place, mark, *blocks)


def middle_kernel(place, taps_ref, *refs, pieces, groups, terms, tile):
    up_refs, refs = refs[:groups], refs[groups:]
    part_refs, refs = refs[: len(pieces) * terms], refs[len(pieces) * terms :]
    grad_refs, out_refs = refs[:groups], refs[groups : 2 * groups]
    up_s, out_s, q_s, k_s, v_s, mixed_s, gf_s, far_s = refs[2 * groups :]
    col = place[1]
    tok, width = up_refs[0].shape
    parity = place[2] % 2
    total = groups * tok
    tap_groups = taps_ref.shape[1]
    for k, ref in enumerate(up_refs):
        up_s[pl.ds(pl.multiple_of((col ^ k) * tok, tok), tok), :] = ref[...]
    lane_group = lax.broadcasted_iota(jnp.int32, (tap_groups, width), 1) // GROUP
    group = lax.broadcasted_iota(jnp.int32, (tap_groups, width), 0)
    spread = (lane_group + place[3] * (width // GROUP) == group).astype(jnp.bfloat16)
    taps = sum(jnp.dot(term, spread, preferred_element_type=jnp.float32) for term in in_three(taps_ref[...]))
    mixed_s[0:PAD, :] = jnp.zeros((PAD, width), jnp.float32)
    gf_s[total : total + PAD, :] = jnp.zeros((PAD, width), jnp.float32)
    step = 64
    for piece, (k, thirds) in enumerate(pieces):
        refs_of = part_refs[piece * terms : (piece + 1) * terms]
        rows_of = refs_of[0].shape[2]
        length = rows_of // len(thirds)
        for i in range(rows_of // step):
            third = thirds[i * step // length]
            at = {"own": parity, "other": 1 - parity, "last": 2, "all": 0}[third] * length
            start = (col ^ k) * tok + at + i * step % length
            inside = slice(i * step, (i + 1) * step)
            rows = pl.ds(pl.multiple_of(start, step), step)
            streams = []
            for s in range(3):
                acc = None
                for ref in refs_of:
                    term = ref[0, s, inside, :].astype(jnp.float32)
                    acc = term if acc is None else acc + term
                streams.append(acc.astype(jnp.bfloat16))
            q_s[rows, :], k_s[rows, :], v_s[rows, :] = streams
            query, key, value = [stream.astype(jnp.float32) for stream in streams]
            mixed_s[pl.ds(pl.multiple_of(start + PAD, PAD), step), :] = key * value
            gf_s[rows, :] = up_s[rows, :].astype(jnp.float32) * query
    sums = [jnp.zeros((8, width), jnp.float32) for _ in range(KT)]
    for a in range(groups):
        for i in range(tok // tile):
            first = a * tok + i * tile
            rows = slice(first, first + tile)
            inside = slice(i * tile, (i + 1) * tile)
            gf = gf_s[rows, :]
            filtered = jnp.zeros((tile, width), jnp.float32)
            grad_mixed = jnp.zeros((tile, width), jnp.float32)
            for j in range(KT):
                shifted = mixed_s[first + PAD - j : first + PAD - j + tile, :]
                filtered = filtered + taps[j : j + 1, :] * shifted
                sums[j] = sums[j] + (gf * shifted).reshape(tile // 8, 8, width).sum(axis=0)
                grad_mixed = grad_mixed + taps[j : j + 1, :] * gf_s[first + j : first + j + tile, :]
            out_s[a, inside, :] = (q_s[rows, :].astype(jnp.float32) * filtered).astype(jnp.bfloat16)
            at = col ^ a
            far_s[at, 0, inside, :] = (up_s[rows, :].astype(jnp.float32) * filtered).astype(jnp.bfloat16)
            far_s[at, 1, inside, :] = (grad_mixed * v_s[rows, :].astype(jnp.float32)).astype(jnp.bfloat16)
            far_s[at, 2, inside, :] = (grad_mixed * k_s[rows, :].astype(jnp.float32)).astype(jnp.bfloat16)
    for k in range(groups):
        grad_refs[k][...] = far_s[k]
    rest = jnp.concatenate(
        [sums[j].sum(axis=0, keepdims=True) for j in range(KT)] + [jnp.zeros((1, width), jnp.float32)], axis=0
    )
    terms_of = [term.astype(jnp.float32) for term in in_three(rest)]
    packed = jnp.concatenate(terms_of + [jnp.zeros((8, width), jnp.float32)], axis=0).astype(jnp.bfloat16)
    for k, ref in enumerate(out_refs):
        ref[0:tok, :] = out_s[col ^ k]
        ref[tok : tok + 32, :] = packed


def middle(place, taps, ups, pieces, parts, tile):
    groups, terms = len(ups), len(parts[0])
    tok, width = ups[0].shape
    total = groups * tok
    whole = lambda *shape: resident(shape, width)
    ones = [whole(1, 3, terms_of[0].shape[2], width) for terms_of in parts for _ in terms_of]
    outs = pl.pallas_call(
        functools.partial(middle_kernel, pieces=pieces, groups=groups, terms=terms, tile=tile),
        grid_spec=pltpu.PrefetchScalarGridSpec(
            num_scalar_prefetch=1,
            grid=(1,),
            in_specs=[whole(*taps.shape)] + [whole(tok, width)] * groups + ones,
            out_specs=[whole(3, tok, width)] * groups + [whole(tok + 32, width)] * groups,
            scratch_shapes=[
                pltpu.VMEM((total, width), jnp.bfloat16),
                pltpu.VMEM((groups, tok, width), jnp.bfloat16),
            ]
            + [pltpu.VMEM((total, width), jnp.bfloat16)] * 3
            + [pltpu.VMEM((total + PAD, width), jnp.float32)] * 2
            + [pltpu.VMEM((groups, 3, tok, width), jnp.bfloat16)],
        ),
        out_shape=[jax.ShapeDtypeStruct((3, tok, width), jnp.bfloat16)] * groups
        + [jax.ShapeDtypeStruct((tok + 32, width), jnp.bfloat16)] * groups,
        compiler_params=params(10, width),
        cost_estimate=SMALL,
        name="middle",
    )(place, taps, *ups, *[term for terms_of in parts for term in terms_of])
    return outs[:groups], outs[groups:]


def assemble_kernel(place, *refs):
    grad_refs, out_ref = refs[:-1], refs[-1]
    width = grad_refs[0].shape[2]
    for r, ref in enumerate(grad_refs):
        for s in range(3):
            at = pl.multiple_of((s * len(grad_refs) + (place[0] ^ r)) * width, width)
            out_ref[:, pl.ds(at, width)] = ref[s]


def assemble(place, grads):
    streams, tok, width = grads[0].shape
    out = jax.ShapeDtypeStruct((tok, streams * width * len(grads)), jnp.bfloat16)
    if width % LANES:
        whole = jnp.stack(grads)[place[0] ^ jnp.arange(len(grads))]
        return jnp.transpose(whole, (2, 1, 0, 3)).reshape(out.shape)
    return pl.pallas_call(
        assemble_kernel,
        grid_spec=pltpu.PrefetchScalarGridSpec(
            num_scalar_prefetch=1,
            grid=(1,),
            in_specs=[resident(grads[0].shape, width)] * len(grads),
            out_specs=resident(out.shape, width),
        ),
        out_shape=out,
        compiler_params=params(4, width),
        cost_estimate=SMALL,
        name="assemble",
    )(place, *grads)


def input_grad_kernel(grad_ref, w_ref, out_ref, *, first):
    step = out_ref.shape[1]
    rows = w_ref[:, :, first * step : (first + 1) * step].reshape(-1, step)
    out_ref[...] = jnp.dot(grad_ref[...], rows, preferred_element_type=jnp.float32).astype(jnp.bfloat16)


def input_grads_kernel(grad_ref, w_ref, *refs, first):
    out_refs, (slots, sems) = refs[:-2], refs[-2:]
    step = out_refs[0].shape[1]

    def fetch(i):
        columns = pl.ds((first + i) * step, step)
        return pltpu.make_async_copy(w_ref.at[:, :, columns], slots.at[i % 2], sems.at[i % 2])

    fetch(0).start()
    for i, out_ref in enumerate(out_refs):
        if i + 1 < len(out_refs):
            fetch(i + 1).start()
        fetch(i).wait()
        rows = slots[i % 2].reshape(-1, step)
        out_ref[...] = jnp.dot(grad_ref[...], rows, preferred_element_type=jnp.float32).astype(jnp.bfloat16)


def input_grad(grad, w, first, last, chunks, width):
    tok = grad.shape[0]
    streams, channels, feat = w.shape
    step = feat // chunks
    count = last - first
    if width % LANES:
        rows = w[:, :, first * step : last * step].reshape(streams * channels, count * step)
        whole = jnp.dot(grad, rows, preferred_element_type=jnp.float32).astype(jnp.bfloat16)
        return [whole[:, i * step : (i + 1) * step] for i in range(count)]
    single = count == 1
    return list(
        pl.pallas_call(
            functools.partial(input_grad_kernel if single else input_grads_kernel, first=first),
            in_specs=[
                resident(grad.shape, width),
                pl.BlockSpec(memory_space=pltpu.VMEM if single else pltpu.HBM),
            ],
            out_specs=[resident((tok, step), width)] * count,
            out_shape=[jax.ShapeDtypeStruct((tok, step), jnp.bfloat16)] * count,
            scratch_shapes=[]
            if single
            else [pltpu.VMEM((2, streams, channels, step), jnp.bfloat16), pltpu.SemaphoreType.DMA((2,))],
            compiler_params=params(8, width),
            cost_estimate=SMALL,
            name="input_grad",
        )(grad, w)
    )


def weight_grad_kernel(*refs, chained, groups, half):
    refs = refs[2 * chained :]
    grad_refs, x_refs = refs[:groups], refs[groups : 2 * groups]
    out_ref, mark_ref, turned = refs[2 * groups :]
    mark_ref[...] = jnp.zeros(mark_ref.shape, jnp.float32)
    streams, channels, step = out_ref.shape
    tok = x_refs[0].shape[0]

    @pl.when(pl.program_id(0) == 0)
    def _():
        for k in range(groups):
            for s in range(streams):
                at = (2 * s + half) * channels
                block = grad_refs[k][:, at : at + channels]
                turned[s * channels : (s + 1) * channels, k * tok : (k + 1) * tok] = block.T

    columns = pl.ds(pl.multiple_of(pl.program_id(0) * step, step), step)
    acc = None
    for k in range(groups):
        term = jnp.dot(turned[:, k * tok : (k + 1) * tok], x_refs[k][:, columns], preferred_element_type=jnp.float32)
        acc = term if acc is None else acc + term
    for s in range(streams):
        out_ref[s] = acc[s * channels : (s + 1) * channels, :]


def weight_grad(filled, grads, xs, half, streams, width):
    groups = len(xs)
    tok, feat = xs[0].shape
    channels = grads[0].shape[1] // streams
    chained = filled is not None
    if width % LANES:
        if chained:
            return filled
        terms = [
            lax.dot_general(grad, x, (((0,), (0,)), ((), ())), preferred_element_type=jnp.float32)
            for grad, x in zip(grads, xs)
        ]
        return sum(terms).reshape(streams, channels, feat), jnp.zeros((8, LANES), jnp.float32)
    step = min(512, feat)
    return pl.pallas_call(
        functools.partial(weight_grad_kernel, chained=chained, groups=groups, half=half),
        grid=(feat // step,),
        in_specs=[pl.BlockSpec(memory_space=pl.ANY)] * (2 * chained)
        + [resident(grads[0].shape, width)] * groups
        + [resident((tok, feat), width)] * groups,
        out_specs=[
            pl.BlockSpec((streams, channels // 2, step), lambda i: (0, half, i)),
            resident((8, LANES), width),
        ],
        scratch_shapes=[pltpu.VMEM((streams * channels // 2, groups * tok), jnp.bfloat16)],
        out_shape=[
            jax.ShapeDtypeStruct((streams, channels, feat), jnp.float32),
            jax.ShapeDtypeStruct((8, LANES), jnp.float32),
        ],
        input_output_aliases={0: 0} if chained else {},
        compiler_params=params(14, width),
        cost_estimate=SMALL,
        name="weight_grad",
    )(*(filled if chained else []), *grads, *xs)


def added(first, second):
    return (first.astype(jnp.float32) + second.astype(jnp.float32)).astype(jnp.bfloat16)


def on_device(tokens, weight, taps, upstream):
    n_col = lax.axis_size("col")
    n_depth = lax.axis_size("depth")
    local_tok = upstream.shape[0]
    depth_at = lax.axis_index("depth")
    col_at = lax.axis_index("col")
    row_at = lax.axis_index("row")
    place = jnp.stack([depth_at, col_at, row_at, col_at * n_depth + depth_at]).astype(jnp.int32)
    w = jnp.transpose(weight, (1, 0, 2))
    width = w.shape[1] // n_depth
    def sum_over_depth(keep, send, near_after=(), far_after=()):
        near = swap(after(send, *near_after) if near_after else send, "depth", 1)
        pairs = [added(keep[r // 2], near[r // 2])[None] for r in range(2, n_depth, 2)]
        held = [after(pair, *far_after) if far_after else pair for pair in pairs]
        fars = [swap(pair, "depth", 2 * i + 2) for i, pair in enumerate(held)]
        return [keep, near] + fars, pairs, fars

    tok = tokens.shape[0]
    third = tok // 3
    cut = tok % 192 == 0 and lax.axis_size("row") % 2 == 0
    sent_first = lax.dynamic_slice_in_dim(tokens, row_at % 2 * third, third, axis=0) if cut else tokens
    first = [swap(sent_first, "col", k) for k in range(1, n_col)]
    ups = split_lanes(place, upstream, n_col, n_depth)
    ups = [up if r == 0 else swap(up, "depth", r) for r, up in enumerate(ups)]
    outer = (row_at == 0) | (row_at == 3)
    keep, send, *last = project(place, [after(tokens, outer)], w, n_depth, "cut" if cut else "plain")
    terms, pairs, fars = sum_over_depth(keep, send, first + ups[1:])
    xs, pieces, parts = [tokens], [(0, ("all",))], [terms]
    for k in range(1, n_col):
        mine = first[k - 1]
        if not cut:
            keep, send = project(place, [after(mine, *fars)], w, n_depth)
            terms, pairs, fars = sum_over_depth(keep, send)
            xs.append(mine)
            pieces.append((k, ("all",)))
            parts.append(terms)
            continue
        other = swap(mine, "row", 1)
        rest = swap(after(last[0], mine), "col", k)
        keep, send = project(place, [after(mine, *pairs)], w, n_depth)
        terms, ahead, _ = sum_over_depth(keep, send)
        pieces.append((k, ("own",)))
        parts.append(terms)
        keep, send, x = project(place, [mine, other, after(rest, *fars, *ahead)], w, n_depth, "join")
        terms, pairs, fars = sum_over_depth(keep, send)
        pieces.append((k, ("other", "last")))
        parts.append(terms)
        xs.append(x)
    ups = merge_rows(place, [after(ups[0], *pairs)] + ups[1:])
    ups = [up if k == 0 else swap(up, "col", k) for k, up in enumerate(ups)]
    own_grads, blocks = middle(place, taps, ups, pieces, parts, local_tok)
    nears = [swap(own, "depth", 1) for own in own_grads]
    blocks = [block if k == 0 else swap(block, "col", k) for k, block in enumerate(blocks)]
    beside = nears + blocks[1:]
    chunks = 4
    grads = [None] * n_col
    ready = []
    sent = []
    lhs = [None] * n_col
    for k in reversed(range(n_col)):
        fars = [swap(after(own_grads[k], *ready) if ready else own_grads[k], "depth", r) for r in range(2, n_depth, 2)]
        ready = fars
        if k > 0:
            fars = [after(far, *beside) for far in fars]
        elif sent:
            fars = [after(far, sent[-1][1][-1]) for far in fars]
        grads[k] = [own_grads[k], nears[k]]
        for far in fars:
            grads[k] += [far, swap(far, "depth", 1)]
        lhs[k] = assemble(place, grads[k])
        if k > 0:
            parts_of = input_grad(lhs[k], w, 0, 1, chunks, width)
            parts_of += input_grad(after(lhs[k], *parts_of), w, 1, chunks, chunks, width)
            sent.append(([swap(part, "col", k) for part in parts_of[:3]], parts_of))
    held = [parts_of[3:] for _, parts_of in sent]
    sent = [of for of, _ in sent]
    own_part = input_grad(lhs[0], w, 0, 1, chunks, width)
    line = lax.axis_size("row") == 4
    inward, across, summed, done = ([None] * chunks for _ in range(4))
    pair = cross = filled = None
    marks, late = [], []
    for slot in range(chunks + 3):
        if slot < chunks:
            total = after(own_part[slot], *marks).astype(jnp.float32)
            for of in sent:
                total = total + of[slot].astype(jnp.float32)
            inward[slot] = total.astype(jnp.bfloat16)
            marks = [inward[slot]] + late
            late = []
        if not line:
            if slot < chunks:
                done[slot] = lax.psum(inward[slot], "row")
        else:
            if 0 <= slot - 1 < chunks:
                across[slot - 1] = added(after(inward[slot - 1], *marks), pair)
                marks = [across[slot - 1]]
            if 0 <= slot - 2 < chunks:
                summed[slot - 2] = added(after(across[slot - 2], *marks), cross)
                marks = [summed[slot - 2]]
            if 0 <= slot - 3 < chunks:
                done[slot - 3] = jnp.where(outer, pair, summed[slot - 3])
            if slot < chunks + 2:
                out = summed[slot - 2] if slot >= 2 else inward[slot]
                pair = swap(jnp.where(outer, inward[slot], out) if slot < chunks else out, "row", 1)
            if 0 <= slot - 1 < chunks:
                cross = lax.ppermute(across[slot - 1], "row", [(0, 0), (1, 2), (2, 1), (3, 3)])
        if slot == 0:
            own_part += input_grad(after(lhs[0], *marks), w, 1, chunks, chunks, width)
            marks = [own_part[1]]
            for k, parts_of in enumerate(held):
                sent[k] += [swap(after(part, *marks), "col", k + 1) for part in parts_of]
        if slot in (3, 4):
            filled = weight_grad(filled, [after(lhs[0], *marks)] + lhs[1:], xs, slot - 3, 3, width)
            marks = [filled[1]]
        if slot == 2:
            blocks = split_rows(place, [after(blocks[0], *marks)] + blocks[1:], n_depth)
            blocks = [block if r == 0 else swap(block, "depth", r) for r, block in enumerate(blocks)]
            late = blocks[1:]
    grad_tokens = jnp.concatenate(done, axis=1)
    output, grad_taps = join(place, filled[1], [after(blocks[0], *marks)] + blocks[1:], taps.shape[1])
    grad_weight = jnp.transpose(filled[0], (1, 0, 2))
    return (output, grad_tokens, grad_weight, grad_taps)


def solution(mesh):
    in_specs = (
        P("col", "depth"),
        P(("row", "col"), None, "depth"),
        P(None, "row"),
        P(("col", "depth"), "row"),
    )
    out_specs = (
        P(("col", "depth"), "row"),
        P("col", "depth"),
        P(("row", "col"), None, "depth"),
        P(None, "row"),
    )
    return jax.shard_map(
        on_device, mesh=mesh, in_specs=in_specs, out_specs=out_specs, check_vma=False
    )
```

```python
import functools

import jax
import jax.numpy as jnp
from jax import lax
from jax.experimental import pallas as pl
from jax.experimental.pallas import tpu as pltpu
from jax.sharding import PartitionSpec as P

GROUP = 16
KT = 7
PAD = 8
LANES = 128
MIB = 1024 * 1024
SMALL = pl.CostEstimate(flops=1, bytes_accessed=1, transcendentals=0)


def swap(value, axis, flip):
    count = lax.axis_size(axis)
    return lax.ppermute(value, axis, [(i, i ^ flip) for i in range(count)])


def after(value, *earlier):
    return lax.optimization_barrier((value, *earlier))[0]


def resident(shape, width):
    if width % LANES == 0:
        return pl.BlockSpec(memory_space=pltpu.VMEM)
    return pl.BlockSpec(tuple(shape), lambda *_: (0,) * len(shape), pipeline_mode=pl.Buffered(1))


def params(mib, width):
    return pltpu.CompilerParams(vmem_limit_bytes=(mib if width % LANES == 0 else 56) * MIB)


def project_kernel(place, *refs, pieces, mode, count, width):
    x_refs = refs[:pieces]
    w_ref, keep_ref, send_ref = refs[pieces : pieces + 3]
    stream = pl.program_id(0)
    core = place[0] % 2
    x = x_refs[0][...]
    if mode == "cut":
        last_ref = refs[pieces + 3]

        @pl.when(stream == 0)
        def _():
            last_ref[...] = x_refs[0][x.shape[0] - last_ref.shape[0] :, :]

    if mode == "join":
        joined, rest = refs[pieces + 3 :]
        third = x.shape[0]
        parity = place[2] % 2

        @pl.when(stream == 0)
        def _():
            joined[pl.ds(pl.multiple_of(parity * third, third), third), :] = x_refs[0][...]
            joined[pl.ds(pl.multiple_of((1 - parity) * third, third), third), :] = x_refs[1][...]
            joined[2 * third :, :] = x_refs[2][...]
            rest[0:third, :] = x_refs[1][...]
            rest[third:, :] = x_refs[2][...]

        x = rest[...]
    nt = (((1,), (1,)), ((), ()))
    if width % LANES == 0:
        whole = lax.dot_general(x, w_ref[stream], nt, preferred_element_type=jnp.float32).astype(jnp.bfloat16)
        blocks = [whole[:, j * width : (j + 1) * width] for j in range(count)]
    else:
        blocks = [
            lax.dot_general(
                x, w_ref[0, j * width : (j + 1) * width, :], nt, preferred_element_type=jnp.float32
            ).astype(jnp.bfloat16)
            for j in range(count)
        ]
    for mine in range(2):

        @pl.when(core == mine)
        def _():
            for j in range(count):
                at = (j ^ place[0]) // 2
                if j % 2 == mine:
                    keep_ref[at, stream] = blocks[j]
                else:
                    send_ref[at, stream] = blocks[j]


def project(place, xs, w, count, mode="plain"):
    feat = xs[0].shape[1]
    all_tok = sum(x.shape[0] for x in xs)
    tok = all_tok - xs[0].shape[0] if mode == "join" else all_tok
    streams, channels, _ = w.shape
    width = channels // count
    part = jax.ShapeDtypeStruct((count // 2, streams, tok, width), jnp.bfloat16)
    wide = width % LANES == 0
    spec = resident(part.shape, width)
    more = {"plain": [], "cut": [(tok // 3, feat)], "join": [(all_tok, feat)]}[mode]
    return pl.pallas_call(
        functools.partial(project_kernel, pieces=len(xs), mode=mode, count=count, width=width),
        grid_spec=pltpu.PrefetchScalarGridSpec(
            num_scalar_prefetch=1,
            grid=(streams,),
            in_specs=[resident(x.shape, width) for x in xs]
            + [resident(w.shape, width) if wide else pl.BlockSpec((1, channels, feat), lambda s, _: (s, 0, 0))],
            out_specs=[spec, spec] + [resident(shape, width) for shape in more],
            scratch_shapes=[pltpu.VMEM((tok, feat), jnp.bfloat16)] if mode == "join" else [],
        ),
        out_shape=[part, part] + [jax.ShapeDtypeStruct(shape, jnp.bfloat16) for shape in more],
        compiler_params=params(10, width),
        cost_estimate=SMALL,
        name="project",
    )(place, *xs, w)


def in_three(value):
    terms = []
    for _ in range(3):
        term = value.astype(jnp.bfloat16)
        value = value - term.astype(jnp.float32)
        terms.append(term)
    return terms


def split_lanes_kernel(place, up_ref, *out_refs):
    n_depth, width = len(out_refs), out_refs[0].shape[2]
    for r, ref in enumerate(out_refs):
        for k in range(ref.shape[0]):
            at = ((place[1] ^ k) * n_depth + (place[0] ^ r)) * width
            ref[k] = up_ref[:, pl.ds(pl.multiple_of(at, width), width)]


def merge_rows_kernel(place, *refs, n_depth):
    in_refs, out_refs = refs[:n_depth], refs[n_depth:]
    local = in_refs[0].shape[1]
    for r, ref in enumerate(in_refs):
        for k, out_ref in enumerate(out_refs):
            out_ref[pl.ds(pl.multiple_of((place[0] ^ r) * local, 16), local), :] = ref[k]


def split_rows_kernel(place, *refs, n_col):
    in_refs, out_refs = refs[:n_col], refs[n_col:]
    local = out_refs[0].shape[1] - 32
    for r, ref in enumerate(out_refs):
        rows = pl.ds(pl.multiple_of((place[0] ^ r) * local, 16), local)
        for k in range(n_col):
            ref[k, 0:local] = in_refs[k][rows, :]
            ref[k, local:] = in_refs[k][-32:, :]


def rearrange(kernel, place, arrays, count, shape, name):
    width = shape[-1]
    return pl.pallas_call(
        kernel,
        grid_spec=pltpu.PrefetchScalarGridSpec(
            num_scalar_prefetch=1,
            grid=(1,),
            in_specs=[resident(value.shape, width) for value in arrays],
            out_specs=[resident(shape, width)] * count,
        ),
        out_shape=[jax.ShapeDtypeStruct(shape, jnp.bfloat16)] * count,
        compiler_params=params(4, width),
        cost_estimate=SMALL,
        name=name,
    )(place, *arrays)


def split_lanes(place, up, n_col, n_depth):
    local, width = up.shape[0], up.shape[1] // (n_col * n_depth)
    if width % LANES:
        blocks = up.reshape(local, n_col, n_depth, width)[:, place[1] ^ jnp.arange(n_col)]
        return [
            jnp.transpose(lax.dynamic_index_in_dim(blocks, place[0] ^ r, 2, keepdims=False), (1, 0, 2))
            for r in range(n_depth)
        ]
    return rearrange(split_lanes_kernel, place, [up], n_depth, (n_col, local, width), "split")


def merge_rows(place, pieces):
    n_depth = len(pieces)
    n_col, local, width = pieces[0].shape
    if width % LANES:
        whole = jnp.stack(pieces)[place[0] ^ jnp.arange(n_depth)]
        return list(jnp.transpose(whole, (1, 0, 2, 3)).reshape(n_col, n_depth * local, width))
    kernel = functools.partial(merge_rows_kernel, n_depth=n_depth)
    return list(rearrange(kernel, place, pieces, n_col, (n_depth * local, width), "merge"))


def split_rows(place, arrays, n_depth):
    local, width = (arrays[0].shape[0] - 32) // n_depth, arrays[0].shape[1]
    if width % LANES:
        whole = jnp.stack(arrays)
        return [
            jnp.concatenate(
                [lax.dynamic_slice_in_dim(whole, (place[0] ^ r) * local, local, axis=1), whole[:, -32:]], axis=1
            )
            for r in range(n_depth)
        ]
    kernel = functools.partial(split_rows_kernel, n_col=len(arrays))
    return rearrange(kernel, place, arrays, n_depth, (len(arrays), local + 32, width), "split")


def join_kernel(place, _, *refs):
    block_refs, (out_ref, grad_taps_ref) = refs[:-2], refs[-2:]
    n_depth = len(block_refs)
    n_col, _, width = block_refs[0].shape
    local, groups = out_ref.shape[0], grad_taps_ref.shape[1]
    lane_group = lax.broadcasted_iota(jnp.int32, (width, groups), 0) // GROUP
    group = lax.broadcasted_iota(jnp.int32, (width, groups), 1)
    total = jnp.zeros((24, groups), jnp.float32)
    for r, ref in enumerate(block_refs):
        for k in range(n_col):
            at = (place[1] ^ k) * n_depth + (place[0] ^ r)
            out_ref[:, pl.ds(pl.multiple_of(at * width, width), width)] = ref[k, 0:local, :]
            spread = (lane_group + at * (width // GROUP) == group).astype(jnp.bfloat16)
            total = total + jnp.dot(ref[k, local : local + 24, :], spread, preferred_element_type=jnp.float32)
    grad_taps_ref[...] = (total[0:8] + total[8:16] + total[16:24])[:KT]


def join(place, mark, blocks, groups):
    n_depth = len(blocks)
    n_col, rows, width = blocks[0].shape
    local = rows - 32
    if width % LANES:
        whole = jnp.stack(blocks)[place[0] ^ jnp.arange(n_depth)][:, place[1] ^ jnp.arange(n_col)]
        sums = whole[:, :, local : local + 24].astype(jnp.float32)
        sums = sums.reshape(n_depth, n_col, 3, 8, width // GROUP, GROUP).sum(axis=(2, 5))[:, :, :KT]
        return (
            jnp.transpose(whole[:, :, :local], (2, 1, 0, 3)).reshape(local, -1),
            jnp.transpose(sums, (2, 1, 0, 3)).reshape(KT, -1),
        )
    channels = n_depth * n_col * width
    return pl.pallas_call(
        join_kernel,
        grid_spec=pltpu.PrefetchScalarGridSpec(
            num_scalar_prefetch=1,
            grid=(1,),
            in_specs=[pl.BlockSpec(memory_space=pl.ANY)] + [resident(blocks[0].shape, width)] * n_depth,
            out_specs=[resident((local, channels), width), resident((KT, groups), width)],
        ),
        out_shape=[
            jax.ShapeDtypeStruct((local, channels), jnp.bfloat16),
            jax.ShapeDtypeStruct((KT, groups), jnp.float32),
        ],
        compiler_params=params(4, width),
        cost_estimate=SMALL,
        name="join",
    )(place, mark, *blocks)


def middle_kernel(place, taps_ref, *refs, pieces, groups, terms, tile):
    up_refs, refs = refs[:groups], refs[groups:]
    part_refs, refs = refs[: len(pieces) * terms], refs[len(pieces) * terms :]
    grad_refs, out_refs = refs[:groups], refs[groups : 2 * groups]
    up_s, out_s, q_s, k_s, v_s, mixed_s, gf_s, far_s = refs[2 * groups :]
    col = place[1]
    tok, width = up_refs[0].shape
    parity = place[2] % 2
    total = groups * tok
    tap_groups = taps_ref.shape[1]
    for k, ref in enumerate(up_refs):
        up_s[pl.ds(pl.multiple_of((col ^ k) * tok, tok), tok), :] = ref[...]
    lane_group = lax.broadcasted_iota(jnp.int32, (tap_groups, width), 1) // GROUP
    group = lax.broadcasted_iota(jnp.int32, (tap_groups, width), 0)
    spread = (lane_group + place[3] * (width // GROUP) == group).astype(jnp.bfloat16)
    taps = sum(jnp.dot(term, spread, preferred_element_type=jnp.float32) for term in in_three(taps_ref[...]))
    mixed_s[0:PAD, :] = jnp.zeros((PAD, width), jnp.float32)
    gf_s[total : total + PAD, :] = jnp.zeros((PAD, width), jnp.float32)
    step = 64
    for piece, (k, thirds) in enumerate(pieces):
        refs_of = part_refs[piece * terms : (piece + 1) * terms]
        rows_of = refs_of[0].shape[2]
        length = rows_of // len(thirds)
        for i in range(rows_of // step):
            third = thirds[i * step // length]
            at = {"own": parity, "other": 1 - parity, "last": 2, "all": 0}[third] * length
            start = (col ^ k) * tok + at + i * step % length
            inside = slice(i * step, (i + 1) * step)
            rows = pl.ds(pl.multiple_of(start, step), step)
            streams = []
            for s in range(3):
                acc = None
                for ref in refs_of:
                    term = ref[0, s, inside, :].astype(jnp.float32)
                    acc = term if acc is None else acc + term
                streams.append(acc.astype(jnp.bfloat16))
            q_s[rows, :], k_s[rows, :], v_s[rows, :] = streams
            query, key, value = [stream.astype(jnp.float32) for stream in streams]
            mixed_s[pl.ds(pl.multiple_of(start + PAD, PAD), step), :] = key * value
            gf_s[rows, :] = up_s[rows, :].astype(jnp.float32) * query
    sums = [jnp.zeros((8, width), jnp.float32) for _ in range(KT)]
    for a in range(groups):
        for i in range(tok // tile):
            first = a * tok + i * tile
            rows = slice(first, first + tile)
            inside = slice(i * tile, (i + 1) * tile)
            gf = gf_s[rows, :]
            filtered = jnp.zeros((tile, width), jnp.float32)
            grad_mixed = jnp.zeros((tile, width), jnp.float32)
            for j in range(KT):
                shifted = mixed_s[first + PAD - j : first + PAD - j + tile, :]
                filtered = filtered + taps[j : j + 1, :] * shifted
                sums[j] = sums[j] + (gf * shifted).reshape(tile // 8, 8, width).sum(axis=0)
                grad_mixed = grad_mixed + taps[j : j + 1, :] * gf_s[first + j : first + j + tile, :]
            out_s[a, inside, :] = (q_s[rows, :].astype(jnp.float32) * filtered).astype(jnp.bfloat16)
            at = col ^ a
            far_s[at, 0, inside, :] = (up_s[rows, :].astype(jnp.float32) * filtered).astype(jnp.bfloat16)
            far_s[at, 1, inside, :] = (grad_mixed * v_s[rows, :].astype(jnp.float32)).astype(jnp.bfloat16)
            far_s[at, 2, inside, :] = (grad_mixed * k_s[rows, :].astype(jnp.float32)).astype(jnp.bfloat16)
    for k in range(groups):
        grad_refs[k][...] = far_s[k]
    rest = jnp.concatenate(
        [sums[j].sum(axis=0, keepdims=True) for j in range(KT)] + [jnp.zeros((1, width), jnp.float32)], axis=0
    )
    terms_of = [term.astype(jnp.float32) for term in in_three(rest)]
    packed = jnp.concatenate(terms_of + [jnp.zeros((8, width), jnp.float32)], axis=0).astype(jnp.bfloat16)
    for k, ref in enumerate(out_refs):
        ref[0:tok, :] = out_s[col ^ k]
        ref[tok : tok + 32, :] = packed


def middle(place, taps, ups, pieces, parts, tile):
    groups, terms = len(ups), len(parts[0])
    tok, width = ups[0].shape
    total = groups * tok
    whole = lambda *shape: resident(shape, width)
    ones = [whole(1, 3, terms_of[0].shape[2], width) for terms_of in parts for _ in terms_of]
    outs = pl.pallas_call(
        functools.partial(middle_kernel, pieces=pieces, groups=groups, terms=terms, tile=tile),
        grid_spec=pltpu.PrefetchScalarGridSpec(
            num_scalar_prefetch=1,
            grid=(1,),
            in_specs=[whole(*taps.shape)] + [whole(tok, width)] * groups + ones,
            out_specs=[whole(3, tok, width)] * groups + [whole(tok + 32, width)] * groups,
            scratch_shapes=[
                pltpu.VMEM((total, width), jnp.bfloat16),
                pltpu.VMEM((groups, tok, width), jnp.bfloat16),
            ]
            + [pltpu.VMEM((total, width), jnp.bfloat16)] * 3
            + [pltpu.VMEM((total + PAD, width), jnp.float32)] * 2
            + [pltpu.VMEM((groups, 3, tok, width), jnp.bfloat16)],
        ),
        out_shape=[jax.ShapeDtypeStruct((3, tok, width), jnp.bfloat16)] * groups
        + [jax.ShapeDtypeStruct((tok + 32, width), jnp.bfloat16)] * groups,
        compiler_params=params(10, width),
        cost_estimate=SMALL,
        name="middle",
    )(place, taps, *ups, *[term for terms_of in parts for term in terms_of])
    return outs[:groups], outs[groups:]


def assemble_kernel(place, *refs):
    grad_refs, out_ref = refs[:-1], refs[-1]
    width = grad_refs[0].shape[2]
    for r, ref in enumerate(grad_refs):
        for s in range(3):
            at = pl.multiple_of((s * len(grad_refs) + (place[0] ^ r)) * width, width)
            out_ref[:, pl.ds(at, width)] = ref[s]


def assemble(place, grads):
    streams, tok, width = grads[0].shape
    out = jax.ShapeDtypeStruct((tok, streams * width * len(grads)), jnp.bfloat16)
    if width % LANES:
        whole = jnp.stack(grads)[place[0] ^ jnp.arange(len(grads))]
        return jnp.transpose(whole, (2, 1, 0, 3)).reshape(out.shape)
    return pl.pallas_call(
        assemble_kernel,
        grid_spec=pltpu.PrefetchScalarGridSpec(
            num_scalar_prefetch=1,
            grid=(1,),
            in_specs=[resident(grads[0].shape, width)] * len(grads),
            out_specs=resident(out.shape, width),
        ),
        out_shape=out,
        compiler_params=params(4, width),
        cost_estimate=SMALL,
        name="assemble",
    )(place, *grads)


def input_grad_kernel(grad_ref, w_ref, out_ref, *, first):
    step = out_ref.shape[1]
    rows = w_ref[:, :, first * step : (first + 1) * step].reshape(-1, step)
    out_ref[...] = jnp.dot(grad_ref[...], rows, preferred_element_type=jnp.float32).astype(jnp.bfloat16)


def input_grads_kernel(grad_ref, w_ref, *refs, first):
    out_refs, (slots, sems) = refs[:-2], refs[-2:]
    step = out_refs[0].shape[1]

    def fetch(i):
        columns = pl.ds((first + i) * step, step)
        return pltpu.make_async_copy(w_ref.at[:, :, columns], slots.at[i % 2], sems.at[i % 2])

    fetch(0).start()
    for i, out_ref in enumerate(out_refs):
        if i + 1 < len(out_refs):
            fetch(i + 1).start()
        fetch(i).wait()
        rows = slots[i % 2].reshape(-1, step)
        out_ref[...] = jnp.dot(grad_ref[...], rows, preferred_element_type=jnp.float32).astype(jnp.bfloat16)


def input_grad(grad, w, first, last, chunks, width):
    tok = grad.shape[0]
    streams, channels, feat = w.shape
    step = feat // chunks
    count = last - first
    if width % LANES:
        rows = w[:, :, first * step : last * step].reshape(streams * channels, count * step)
        whole = jnp.dot(grad, rows, preferred_element_type=jnp.float32).astype(jnp.bfloat16)
        return [whole[:, i * step : (i + 1) * step] for i in range(count)]
    single = count == 1
    return list(
        pl.pallas_call(
            functools.partial(input_grad_kernel if single else input_grads_kernel, first=first),
            in_specs=[
                resident(grad.shape, width),
                pl.BlockSpec(memory_space=pltpu.VMEM if single else pltpu.HBM),
            ],
            out_specs=[resident((tok, step), width)] * count,
            out_shape=[jax.ShapeDtypeStruct((tok, step), jnp.bfloat16)] * count,
            scratch_shapes=[]
            if single
            else [pltpu.VMEM((2, streams, channels, step), jnp.bfloat16), pltpu.SemaphoreType.DMA((2,))],
            compiler_params=params(8, width),
            cost_estimate=SMALL,
            name="input_grad",
        )(grad, w)
    )


def weight_grad_kernel(*refs, chained, groups, half):
    refs = refs[2 * chained :]
    grad_refs, x_refs = refs[:groups], refs[groups : 2 * groups]
    out_ref, mark_ref, turned = refs[2 * groups :]
    mark_ref[...] = jnp.zeros(mark_ref.shape, jnp.float32)
    streams, channels, step = out_ref.shape
    tok = x_refs[0].shape[0]

    @pl.when(pl.program_id(0) == 0)
    def _():
        for k in range(groups):
            for s in range(streams):
                at = (2 * s + half) * channels
                block = grad_refs[k][:, at : at + channels]
                turned[s * channels : (s + 1) * channels, k * tok : (k + 1) * tok] = block.T

    columns = pl.ds(pl.multiple_of(pl.program_id(0) * step, step), step)
    acc = None
    for k in range(groups):
        term = jnp.dot(turned[:, k * tok : (k + 1) * tok], x_refs[k][:, columns], preferred_element_type=jnp.float32)
        acc = term if acc is None else acc + term
    for s in range(streams):
        out_ref[s] = acc[s * channels : (s + 1) * channels, :]


def weight_grad(filled, grads, xs, half, streams, width):
    groups = len(xs)
    tok, feat = xs[0].shape
    channels = grads[0].shape[1] // streams
    chained = filled is not None
    if width % LANES:
        if chained:
            return filled
        terms = [
            lax.dot_general(grad, x, (((0,), (0,)), ((), ())), preferred_element_type=jnp.float32)
            for grad, x in zip(grads, xs)
        ]
        return sum(terms).reshape(streams, channels, feat), jnp.zeros((8, LANES), jnp.float32)
    step = min(512, feat)
    return pl.pallas_call(
        functools.partial(weight_grad_kernel, chained=chained, groups=groups, half=half),
        grid=(feat // step,),
        in_specs=[pl.BlockSpec(memory_space=pl.ANY)] * (2 * chained)
        + [resident(grads[0].shape, width)] * groups
        + [resident((tok, feat), width)] * groups,
        out_specs=[
            pl.BlockSpec((streams, channels // 2, step), lambda i: (0, half, i)),
            resident((8, LANES), width),
        ],
        scratch_shapes=[pltpu.VMEM((streams * channels // 2, groups * tok), jnp.bfloat16)],
        out_shape=[
            jax.ShapeDtypeStruct((streams, channels, feat), jnp.float32),
            jax.ShapeDtypeStruct((8, LANES), jnp.float32),
        ],
        input_output_aliases={0: 0} if chained else {},
        compiler_params=params(14, width),
        cost_estimate=SMALL,
        name="weight_grad",
    )(*(filled if chained else []), *grads, *xs)


def added(first, second):
    return (first.astype(jnp.float32) + second.astype(jnp.float32)).astype(jnp.bfloat16)


def on_device(tokens, weight, taps, upstream):
    n_col = lax.axis_size("col")
    n_depth = lax.axis_size("depth")
    local_tok = upstream.shape[0]
    depth_at = lax.axis_index("depth")
    col_at = lax.axis_index("col")
    row_at = lax.axis_index("row")
    place = jnp.stack([depth_at, col_at, row_at, col_at * n_depth + depth_at]).astype(jnp.int32)
    w = jnp.transpose(weight, (1, 0, 2))
    width = w.shape[1] // n_depth
    def sum_over_depth(keep, send, near_after=()):
        near = swap(after(send, *near_after) if near_after else send, "depth", 1)
        pairs = [added(keep[r // 2], near[r // 2])[None] for r in range(2, n_depth, 2)]
        fars = [swap(pair, "depth", 2 * i + 2) for i, pair in enumerate(pairs)]
        return [keep, near] + fars, pairs, fars

    tok = tokens.shape[0]
    third = tok // 3
    cut = tok % 192 == 0 and lax.axis_size("row") % 2 == 0
    sent_first = lax.dynamic_slice_in_dim(tokens, row_at % 2 * third, third, axis=0) if cut else tokens
    first = [swap(sent_first, "col", k) for k in range(1, n_col)]
    ups = split_lanes(place, upstream, n_col, n_depth)
    ups = [up if r == 0 else swap(up, "depth", r) for r, up in enumerate(ups)]
    outer = (row_at == 0) | (row_at == 3)
    keep, send, *last = project(place, [after(tokens, outer)], w, n_depth, "cut" if cut else "plain")
    terms, pairs, fars = sum_over_depth(keep, send, first + ups[1:])
    xs, pieces, parts = [tokens], [(0, ("all",))], [terms]
    for k in range(1, n_col):
        mine = first[k - 1]
        if not cut:
            keep, send = project(place, [after(mine, *fars)], w, n_depth)
            terms, pairs, fars = sum_over_depth(keep, send)
            xs.append(mine)
            pieces.append((k, ("all",)))
            parts.append(terms)
            continue
        other = swap(mine, "row", 1)
        rest = swap(after(last[0], mine), "col", k)
        keep, send = project(place, [after(mine, *pairs)], w, n_depth)
        terms, ahead, _ = sum_over_depth(keep, send)
        pieces.append((k, ("own",)))
        parts.append(terms)
        keep, send, x = project(place, [mine, other, after(rest, *fars, *ahead)], w, n_depth, "join")
        terms, pairs, fars = sum_over_depth(keep, send)
        pieces.append((k, ("other", "last")))
        parts.append(terms)
        xs.append(x)
    ups = merge_rows(place, [after(ups[0], *pairs)] + ups[1:])
    ups = [up if k == 0 else swap(up, "col", k) for k, up in enumerate(ups)]
    own_grads, blocks = middle(place, taps, ups, pieces, parts, local_tok)
    nears = [swap(own, "depth", 1) for own in own_grads]
    blocks = [block if k == 0 else swap(block, "col", k) for k, block in enumerate(blocks)]
    beside = nears + blocks[1:]
    chunks = 4
    grads = [None] * n_col
    ready = []
    sent = []
    lhs = [None] * n_col
    for k in reversed(range(n_col)):
        fars = [swap(after(own_grads[k], *ready) if ready else own_grads[k], "depth", r) for r in range(2, n_depth, 2)]
        ready = fars
        if k > 0:
            fars = [after(far, *beside) for far in fars]
        elif sent:
            fars = [after(far, sent[-1][1][-1]) for far in fars]
        grads[k] = [own_grads[k], nears[k]]
        for far in fars:
            grads[k] += [far, swap(far, "depth", 1)]
        lhs[k] = assemble(place, grads[k])
        if k > 0:
            parts_of = input_grad(lhs[k], w, 0, 1, chunks, width)
            parts_of += input_grad(after(lhs[k], *parts_of), w, 1, chunks, chunks, width)
            sent.append(([swap(part, "col", k) for part in parts_of[:3]], parts_of))
    held = [parts_of[3:] for _, parts_of in sent]
    sent = [of for of, _ in sent]
    own_part = input_grad(lhs[0], w, 0, 1, chunks, width)
    line = lax.axis_size("row") == 4
    inward, across, summed, done = ([None] * chunks for _ in range(4))
    pair = cross = filled = None
    marks = []
    for slot in range(chunks + 3):
        if slot < chunks:
            total = after(own_part[slot], *marks).astype(jnp.float32)
            for of in sent:
                total = total + of[slot].astype(jnp.float32)
            inward[slot] = total.astype(jnp.bfloat16)
            marks = [inward[slot]]
        if not line:
            if slot < chunks:
                done[slot] = lax.psum(inward[slot], "row")
        else:
            if 0 <= slot - 1 < chunks:
                across[slot - 1] = added(after(inward[slot - 1], *marks), pair)
                marks = [across[slot - 1]]
            if 0 <= slot - 2 < chunks:
                summed[slot - 2] = added(after(across[slot - 2], *marks), cross)
                marks = [summed[slot - 2]]
            if 0 <= slot - 3 < chunks:
                done[slot - 3] = jnp.where(outer, pair, summed[slot - 3])
            if slot < chunks + 2:
                out = summed[slot - 2] if slot >= 2 else inward[slot]
                pair = swap(jnp.where(outer, inward[slot], out) if slot < chunks else out, "row", 1)
            if 0 <= slot - 1 < chunks:
                cross = lax.ppermute(across[slot - 1], "row", [(0, 0), (1, 2), (2, 1), (3, 3)])
        if slot == 0:
            own_part += input_grad(after(lhs[0], *marks), w, 1, chunks, chunks, width)
            marks = [own_part[1]]
            for k, parts_of in enumerate(held):
                sent[k] += [swap(after(part, *marks), "col", k + 1) for part in parts_of]
        if slot in (2, 4):
            filled = weight_grad(filled, [after(lhs[0], *marks)] + lhs[1:], xs, slot // 2 - 1, 3, width)
            marks = [filled[1]]
        if slot == 4:
            marks += late
        if slot == 3:
            blocks = split_rows(place, [after(blocks[0], *marks)] + blocks[1:], n_depth)
            blocks = [block if r == 0 else swap(block, "depth", r) for r, block in enumerate(blocks)]
            late = blocks[1:]
    grad_tokens = jnp.concatenate(done, axis=1)
    output, grad_taps = join(place, filled[1], [after(blocks[0], *marks)] + blocks[1:], taps.shape[1])
    grad_weight = jnp.transpose(filled[0], (1, 0, 2))
    return (output, grad_tokens, grad_weight, grad_taps)


def solution(mesh):
    in_specs = (
        P("col", "depth"),
        P(("row", "col"), None, "depth"),
        P(None, "row"),
        P(("col", "depth"), "row"),
    )
    out_specs = (
        P(("col", "depth"), "row"),
        P("col", "depth"),
        P(("row", "col"), None, "depth"),
        P(None, "row"),
    )
    return jax.shard_map(
        on_device, mesh=mesh, in_specs=in_specs, out_specs=out_specs, check_vma=False
    )
```
